32 devices in a mesh: batch: 8 (over z, core), mp: 4 (over y, x).
Axes of the slice: x: 2, y: 2, z: 4, core: 2. Of those that a mesh axis runs over, the one named last changes fastest.
Arguments:
- queries: bfloat16 [128, 4096], P('batch', 'mp'), may hold values from -384 to 384, as said below
- prompt_cache: bfloat16 [8, 4, 4096, 256], P('batch', 'mp'), may hold values from -48 to 48, as said below
- pool: bfloat16 [256, 4, 64, 256], P('batch', 'mp'), may hold values from -48 to 48, as said below
- block_table: int32 [128, 4], replicated, may hold values from 0 to 255, as said below
- parents: int32 [128], replicated, may hold values from 0 to 127, as said below
- lengths: int32 [8], P('batch'), may hold values from 2048 to 8192, as said below
Outputs:
- attended: float32 [128, 4096], P('batch', 'mp')
The draws below stay inside these ranges and needn't reach their ends.
Inputs may be any that keep to these rules, and one draw needn't show every extreme that they name: `queries`: custom float draw of activations; entries stay within the range. `prompt_cache`: keys are of order one and values about eight times larger. `pool`: keys are of order one and values larger, as in prompt_cache. `block_table`: block b is held by batch index b // 32. A row's 4 entries are distinct. The rows of one request name at most 4 distinct blocks held by any one batch index, and exactly 4 held by some index. parents[i] // 16 == i // 16: a row continues a beam of its own request. `lengths`: some request has 8192 valid prompt tokens.
All inputs are finite; a program needn't handle non-finite values.
Results may differ from the reference program's by a relative error of at most 0.007.
Values may be sent and summed in bfloat16 or wider, within the bound.
No kernel may reach another device: no remote copies, remote signals or barrier semaphores. Data moves between devices by JAX's collectives and lax.ppermute only.
A program may use at most 64 MiB of HBM per device.

```python
import jax
import jax.numpy as jnp
from jax import lax

HD = 128
GROUP = 16
KVH = 2
NH = 32
BT = 128
PT = 8192
BEAMS = 16
SUF = 4
POOL_DEV = 32
REQ = 8
ROWS = 128


VALUE_SCALE = 8.0


def draw_queries(key, part):
    key = jax.random.fold_in(key, 11)
    first = jax.random.fold_in(key, 0)
    values = jnp.clip(jax.random.normal(first, (ROWS, NH * HD), jnp.float32), -6.0, 6.0)
    return values.astype(jnp.bfloat16)


def draw_prompt_cache(key, part):
    key = jax.random.fold_in(key, 12)
    shape = (REQ, 2 * KVH, PT // 2, 2 * HD)
    entries = jnp.clip(jax.random.normal(key, shape, jnp.float32), -6.0, 6.0)
    column = jnp.arange(2 * HD)
    return (entries * jnp.where(column < HD, 1.0, VALUE_SCALE)).astype(jnp.bfloat16)


def draw_pool(key, part):
    key = jax.random.fold_in(key, 13)
    shape = (REQ * POOL_DEV, 2 * KVH, BT // 2, 2 * HD)
    entries = jnp.clip(jax.random.normal(key, shape, jnp.float32), -6.0, 6.0)
    column = jnp.arange(2 * HD)
    return (entries * jnp.where(column < HD, 1.0, VALUE_SCALE)).astype(jnp.bfloat16)


def draw_block_table(key, part):
    key = jax.random.fold_in(key, 14)
    first, second, third = jax.random.split(key, 3)
    owner_perm = jax.random.permutation(first, REQ)
    slot_perm = jax.vmap(lambda k: jax.random.permutation(k, POOL_DEV))(jax.random.split(second, REQ))
    beam_perm = jax.vmap(lambda k: jax.random.permutation(k, BEAMS))(jax.random.split(third, REQ))
    request = jnp.arange(REQ, dtype=jnp.int32)[:, None]
    columns = []
    for level in range(SUF):
        width = BEAMS // 2 ** (level + 1)
        branch = beam_perm // width
        distinct = 2 ** (level + 1) - 2 + branch
        pair = distinct // 2
        owner = owner_perm[(pair + request) % REQ]
        slot = slot_perm[owner, 2 * pair + distinct % 2]
        columns.append(owner * POOL_DEV + slot)
    table = jnp.stack(columns, axis=-1)
    return table.reshape(ROWS, SUF).astype(jnp.int32)


def draw_parents(key, part):
    key = jax.random.fold_in(key, 15)
    base = jnp.arange(REQ, dtype=jnp.int32)[:, None] * BEAMS
    offset = jax.random.randint(key, (REQ, BEAMS), 0, BEAMS, jnp.int32)
    return (base + offset).reshape(ROWS).astype(jnp.int32)


def draw_lengths(key, part):
    key = jax.random.fold_in(key, 16)
    first, second = jax.random.split(key)
    counts = jax.random.randint(first, (REQ,), PT // 4, PT + 1, jnp.int32)
    longest = jax.random.randint(second, (), 0, REQ, jnp.int32)
    return jnp.where(jnp.arange(REQ, dtype=jnp.int32) == longest, PT, counts).astype(jnp.int32)


def setup_inputs(seed: int = 0) -> dict:
    splits = jax.random.split(jax.random.key(seed), 7)
    return {
        "queries": draw_queries(jax.random.fold_in(splits[6], 71), 0),
        "prompt_cache": draw_prompt_cache(jax.random.fold_in(splits[6], 71), 0),
        "pool": draw_pool(jax.random.fold_in(splits[6], 71), 0),
        "block_table": draw_block_table(jax.random.fold_in(splits[6], 71), 0),
        "parents": draw_parents(jax.random.fold_in(splits[6], 71), 0),
        "lengths": draw_lengths(jax.random.fold_in(splits[6], 71), 0),
    }


big_negative = -1.0e30


def reference(queries, prompt_cache, pool, block_table, parents, lengths):
    half = BT // 2
    scale = HD ** -0.5
    referenced = block_table[parents]
    token = jnp.arange(PT // 2, dtype=jnp.int32)
    side = jnp.arange(2, dtype=jnp.int32)

    def one_request(items):
        rows_q, prompt_r, refs, length = items
        qf = rows_q.astype(jnp.float32).reshape(BEAMS, KVH, GROUP, HD)
        prompt_g = prompt_r.astype(jnp.float32).reshape(KVH, 2, PT // 2, 2 * HD)
        keys_p = prompt_g[..., :HD].reshape(KVH, PT, HD)
        vals_p = prompt_g[..., HD:].reshape(KVH, PT, HD)
        position = (token[None, :] // half) * BT + side[:, None] * half + token[None, :] % half
        valid = (position < length).reshape(PT)
        blocks = pool[refs].astype(jnp.float32)
        blocks = blocks.reshape(BEAMS, SUF, KVH, 2, half, 2 * HD)
        blocks = blocks.transpose(0, 2, 1, 3, 4, 5).reshape(BEAMS, KVH, SUF * BT, 2 * HD)
        keys_s = blocks[..., :HD]
        vals_s = blocks[..., HD:]
        score_p = jnp.einsum('bghd,gtd->bght', qf, keys_p) * scale
        score_p = jnp.where(valid[None, None, None, :], score_p, big_negative)
        score_s = jnp.einsum('bghd,bgtd->bght', qf, keys_s) * scale
        scores = jnp.concatenate([score_p, score_s], axis=-1)
        top = jnp.max(scores, axis=-1, keepdims=True)
        weights = jnp.exp(scores - top)
        total = jnp.sum(weights, axis=-1)
        rounded = lax.optimization_barrier(weights.astype(jnp.bfloat16)).astype(jnp.float32)
        summed = jnp.einsum('bght,gtd->bghd', rounded[..., :PT], vals_p)
        summed = summed + jnp.einsum('bght,bgtd->bghd', rounded[..., PT:], vals_s)
        return (summed / total[..., None]).reshape(BEAMS, KVH * GROUP * HD)

    result = lax.map(one_request, (queries.reshape(REQ, BEAMS, KVH * GROUP * HD), prompt_cache,
                                   referenced.reshape(REQ, BEAMS, SUF), lengths))
    return result.reshape(ROWS, KVH * GROUP * HD)
```

```python
import functools

import jax
import jax.numpy as jnp
from jax import lax
from jax.experimental import pallas as pl
from jax.experimental.pallas import tpu as pltpu
from jax.sharding import PartitionSpec as P

HD = 128
GROUP = 16
BEAMS = 16
SUF = 4
HEADS = GROUP // 2
VECS = HEADS * BEAMS
STAT_ROWS = 16
UNIT_ROWS = HD + STAT_ROWS
CHUNK = 512

big_negative = -1e30
to_exp2 = HD ** (-0.5) * 1.4426950408889634


def exchanged(value, z_mask, pair_mask, core_mask=0):
    n_mp = lax.axis_size("mp")
    n_batch = lax.axis_size("batch")
    pairs = []
    for b in range(n_batch):
        for m in range(n_mp):
            other = (b ^ (2 * z_mask + core_mask)) * n_mp + (m ^ pair_mask)
            pairs.append((b * n_mp + m, other))
    return lax.ppermute(value, ("batch", "mp"), pairs)


def stacked_heads(q):
    return jnp.concatenate([q[:, h * HD : (h + 1) * HD] for h in range(HEADS)], axis=0)


def scores_of(keys, vectors):
    return lax.dot_general(
        keys, vectors, (((1,), (1,)), ((), ())), preferred_element_type=jnp.float32
    )


def summed_of(values, weights):
    return lax.dot_general(
        values,
        weights.astype(jnp.bfloat16),
        (((0,), (0,)), ((), ())),
        preferred_element_type=jnp.float32,
    )


def merged(parts):
    top = functools.reduce(jnp.maximum, [p[0] for p in parts])
    total = 0.0
    summed = 0.0
    for part_top, part_total, part_summed in parts:
        factor = jnp.exp2((part_top - top) * to_exp2)
        total = total + part_total * factor
        summed = summed + part_summed * factor
    return top, total, summed


def softmax_part(scores, values):
    top = jnp.max(scores, axis=0, keepdims=True)
    weights = jnp.exp2((scores - top) * to_exp2)
    total = jnp.sum(weights, axis=0, keepdims=True)
    return top, total, summed_of(values, weights)


def three_pieces(x):
    first = x.astype(jnp.bfloat16).astype(jnp.float32)
    rest = x - first
    second = rest.astype(jnp.bfloat16).astype(jnp.float32)
    return [first, second, rest - second]


def store_unit(ref, top, total, summed):
    ref[:HD, :] = summed.astype(jnp.bfloat16)
    rows = three_pieces(top) + three_pieces(total)
    rows.append(jnp.zeros((STAT_ROWS - len(rows), VECS), jnp.float32))
    ref[HD:, :] = jnp.concatenate(rows, axis=0).astype(jnp.bfloat16)


def load_unit(ref):
    stats = ref[HD:, :].astype(jnp.float32)
    top = stats[0:1] + stats[1:2] + stats[2:3]
    total = stats[3:4] + stats[4:5] + stats[5:6]
    return top, total, ref[:HD, :].astype(jnp.float32)


def prompt_kernel(valid_ref, own_ref, pair_ref, prompt_ref, summed_ref, stats_ref):
    vectors = jnp.concatenate([stacked_heads(own_ref[...]), stacked_heads(pair_ref[...])], axis=0)
    valid = valid_ref[0]
    tokens = prompt_ref.shape[0]
    parts = []
    for start in range(0, tokens, CHUNK):
        scores = scores_of(prompt_ref[start : start + CHUNK, :HD], vectors)
        token = lax.broadcasted_iota(jnp.int32, scores.shape, 0)
        scores = jnp.where(token < valid - start, scores, big_negative)
        parts.append(softmax_part(scores, prompt_ref[start : start + CHUNK, HD:]))
        if len(parts) == 2:
            parts = [merged(parts)]
    top, total, summed = merged(parts)
    summed_ref[...] = summed
    stats_ref[...] = jnp.concatenate(
        [top, total, jnp.zeros((6, 2 * VECS), jnp.float32)], axis=0
    )


def gather_kernel(meta_ref, ids_ref, near_ref, far_ref, out_ref, sem):
    n_req, n_slots, half, _ = out_ref.shape
    capacity = n_slots // 2
    z, core = meta_ref[0], meta_ref[1]
    copies = []
    for d in range(n_req):
        request = (z ^ d) * 2 + core
        for k in range(n_slots):
            slot = jnp.maximum(ids_ref[request, k], 0)
            pool = near_ref if k < capacity else far_ref
            copy = pltpu.make_async_copy(pool.at[slot], out_ref.at[d, k], sem.at[d, k])
            copy.start()
            copies.append(copy)
    for copy in copies:
        copy.wait()


def request_part(d, meta_ref, ids_ref, refs_ref, blocks_ref, vectors):
    _, n_slots, half, width = blocks_ref.shape
    capacity = n_slots // 2
    z, core, slots = meta_ref[0], meta_ref[1], meta_ref[2]
    request = (z ^ d) * 2 + core
    wanted = refs_ref[request]
    blocks = blocks_ref[d].reshape(n_slots * half, width)
    scores = scores_of(blocks[:, :HD], vectors)
    pieces = []
    for k in range(n_slots):
        slot = ids_ref[request, k]
        holder = z * 2 + (core if k < capacity else 1 - core)
        block = jnp.where(slot < 0, -1, holder * slots + slot)
        member = jnp.max((wanted == block).astype(jnp.int32), axis=0, keepdims=True) > 0
        piece = scores[k * half : (k + 1) * half]
        pieces.append(jnp.where(member, piece, big_negative))
    scores = jnp.concatenate(pieces, axis=0)
    return softmax_part(scores, blocks[:, HD:])


def away_kernel(n_req, meta_ref, ids_ref, refs_ref, blocks_ref, *rest):
    queries, outs = rest[: 2 * (n_req - 1)], rest[2 * (n_req - 1) :]
    for d in range(1, n_req):
        own_ref, pair_ref = queries[2 * (d - 1) : 2 * d]
        vectors = jnp.concatenate(
            [stacked_heads(own_ref[...]), stacked_heads(pair_ref[...])], axis=0
        )
        top, total, summed = request_part(d, meta_ref, ids_ref, refs_ref, blocks_ref, vectors)
        for side in range(2):
            lanes = slice(side * VECS, (side + 1) * VECS)
            store_unit(
                outs[2 * (d - 1) + side], top[:, lanes], total[:, lanes], summed[:, lanes]
            )


def home_kernel(
    meta_ref, ids_ref, refs_ref, blocks_ref, own_ref, pair_ref, summed_ref, stats_ref,
    kept_ref, kept_stats_ref, given_ref,
):
    vectors = jnp.concatenate([stacked_heads(own_ref[...]), stacked_heads(pair_ref[...])], axis=0)
    suffix = request_part(0, meta_ref, ids_ref, refs_ref, blocks_ref, vectors)
    prompt = (stats_ref[0:1], stats_ref[1:2], summed_ref[...])
    top, total, summed = merged([prompt, suffix])
    kept_ref[...] = summed[:, :VECS]
    kept_stats_ref[...] = jnp.concatenate(
        [top[:, :VECS], total[:, :VECS], jnp.zeros((6, VECS), jnp.float32)], axis=0
    )
    store_unit(given_ref, top[:, VECS:], total[:, VECS:], summed[:, VECS:])


def final_kernel(kept_ref, kept_stats_ref, *rest):
    units, out_ref = rest[:-1], rest[-1]
    parts = [(kept_stats_ref[0:1], kept_stats_ref[1:2], kept_ref[...])]
    parts += [load_unit(unit) for unit in units]
    _, total, summed = merged(parts)
    attended = (summed / total).T
    for h in range(HEADS):
        out_ref[:, h * HD : (h + 1) * HD] = attended[h * BEAMS : (h + 1) * BEAMS]


def slots_of(block_table, n_batch, slots, capacity, z, core):
    entries = block_table.reshape(n_batch, 1, 1, BEAMS * SUF)
    holder = jnp.stack([z * 2 + core, z * 2 + 1 - core]).reshape(1, 2, 1, 1)
    slot = jnp.arange(slots, dtype=jnp.int32).reshape(1, 1, slots, 1)
    hit = jnp.any(entries == holder * slots + slot, axis=3)
    order = jnp.arange(slots, dtype=jnp.int32)
    before = (order[None, :] < order[:, None])[None, None]
    rank = jnp.sum((hit[:, :, None, :] & before).astype(jnp.int32), axis=3)
    index = jnp.arange(capacity, dtype=jnp.int32).reshape(1, 1, capacity, 1)
    chosen = hit[:, :, None, :] & (rank[:, :, None, :] == index)
    found = jnp.sum(jnp.where(chosen, order + 1, 0), axis=3) - 1
    return found.reshape(n_batch, 2 * capacity)


def on_device(queries, prompt_cache, pool, block_table, parents, lengths):
    n_batch = lax.axis_size("batch")
    myself = lax.axis_index("batch")
    parity = lax.axis_index("mp") % 2
    z, core = myself // 2, myself % 2
    n_req = n_batch // 2
    ndist = 2 ** (SUF + 1) - 2
    capacity = 2 * ((ndist // 2 + n_batch - 1) // n_batch)
    slots, _, half, width = pool.shape
    tokens = prompt_cache.shape[2]
    smem = pl.BlockSpec(memory_space=pltpu.SMEM)
    vmem = pl.BlockSpec(memory_space=pltpu.VMEM)
    anywhere = pl.BlockSpec(memory_space=pl.ANY)
    params = pltpu.CompilerParams(vmem_limit_bytes=40 * 2**20)
    unit = jax.ShapeDtypeStruct((UNIT_ROWS, VECS), jnp.bfloat16)

    other = exchanged(queries, 0, 1)
    sent = []
    for d in range(1, n_req):
        sent += [exchanged(queries, d, 0), exchanged(queries, d, 1)]
    near = pool.reshape(slots, half, width)
    far = exchanged(near, 0, 0, 1)

    meta = jnp.stack([z, core, jnp.int32(slots)]).astype(jnp.int32)
    ids = slots_of(block_table, n_batch, slots, capacity, z, core)
    wanted = block_table[parents].reshape(n_batch, BEAMS, SUF).transpose(0, 2, 1)
    wanted = jnp.tile(wanted, (1, 1, GROUP))

    length = lengths[0]
    valid = length // (2 * half) * half + jnp.clip(length % (2 * half) - parity * half, 0, half)
    summed, stats = pl.pallas_call(
        prompt_kernel,
        out_shape=(
            jax.ShapeDtypeStruct((HD, 2 * VECS), jnp.float32),
            jax.ShapeDtypeStruct((8, 2 * VECS), jnp.float32),
        ),
        in_specs=[smem, vmem, vmem, vmem],
        out_specs=(vmem, vmem),
        compiler_params=params,
        name="prompt_part",
    )(valid.reshape(1), queries, other, prompt_cache.reshape(tokens, width))

    blocks = pl.pallas_call(
        gather_kernel,
        out_shape=jax.ShapeDtypeStruct((n_req, 2 * capacity, half, width), jnp.bfloat16),
        in_specs=[smem, smem, anywhere, anywhere],
        out_specs=anywhere,
        scratch_shapes=[pltpu.SemaphoreType.DMA((n_req, 2 * capacity))],
        name="named_blocks",
    )(meta, ids, near, far)

    units = pl.pallas_call(
        functools.partial(away_kernel, n_req),
        out_shape=(unit,) * (2 * (n_req - 1)),
        in_specs=[smem, smem] + [vmem] * (2 + 2 * (n_req - 1)),
        out_specs=(vmem,) * (2 * (n_req - 1)),
        compiler_params=params,
        name="suffix_away",
    )(meta, ids, wanted, blocks, *sent)
    received = []
    for d in range(1, n_req):
        for side in range(2):
            received.append(exchanged(units[2 * (d - 1) + side], d, side))

    kept, kept_stats, given = pl.pallas_call(
        home_kernel,
        out_shape=(
            jax.ShapeDtypeStruct((HD, VECS), jnp.float32),
            jax.ShapeDtypeStruct((8, VECS), jnp.float32),
            unit,
        ),
        in_specs=[smem, smem] + [vmem] * 6,
        out_specs=(vmem,) * 3,
        compiler_params=params,
        name="suffix_home",
    )(meta, ids, wanted, blocks, queries, other, summed, stats)
    received.append(exchanged(given, 0, 1))

    return pl.pallas_call(
        final_kernel,
        out_shape=jax.ShapeDtypeStruct((BEAMS, HEADS * HD), jnp.float32),
        in_specs=[vmem] * (2 + len(received)),
        out_specs=vmem,
        compiler_params=params,
        name="combine",
    )(kept, kept_stats, *received)


def solution(mesh):
    return jax.shard_map(
        on_device,
        mesh=mesh,
        in_specs=(
            P("batch", "mp"),
            P("batch", "mp", None, None),
            P("batch", "mp", None, None),
            P(),
            P(),
            P("batch"),
        ),
        out_specs=P("batch", "mp"),
        check_vma=False,
    )
```

```python
import functools

import jax
import jax.numpy as jnp
from jax import lax
from jax.experimental import pallas as pl
from jax.experimental.pallas import tpu as pltpu
from jax.sharding import PartitionSpec as P

HD = 128
GROUP = 16
BEAMS = 16
SUF = 4
HEADS = GROUP // 2
VECS = HEADS * BEAMS
STAT_ROWS = 16
UNIT_ROWS = HD + STAT_ROWS
CHUNK = 512

big_negative = -1e30
to_exp2 = HD ** (-0.5) * 1.4426950408889634


def swapped(value, axis):
    return lax.ppermute(value, axis, [(0, 1), (1, 0)])


def stacked_heads(q):
    return jnp.concatenate([q[:, h * HD : (h + 1) * HD] for h in range(HEADS)], axis=0)


def scores_of(keys, vectors):
    return lax.dot_general(
        keys, vectors, (((1,), (1,)), ((), ())), preferred_element_type=jnp.float32
    )


def summed_of(values, weights):
    return lax.dot_general(
        values,
        weights.astype(jnp.bfloat16),
        (((0,), (0,)), ((), ())),
        preferred_element_type=jnp.float32,
    )


def merged(parts):
    top = functools.reduce(jnp.maximum, [p[0] for p in parts])
    total = 0.0
    summed = 0.0
    for part_top, part_total, part_summed in parts:
        factor = jnp.exp2((part_top - top) * to_exp2)
        total = total + part_total * factor
        summed = summed + part_summed * factor
    return top, total, summed


def softmax_part(scores, values):
    top = jnp.max(scores, axis=0, keepdims=True)
    weights = jnp.exp2((scores - top) * to_exp2)
    total = jnp.sum(weights, axis=0, keepdims=True)
    return top, total, summed_of(values, weights)


def three_pieces(x):
    first = x.astype(jnp.bfloat16).astype(jnp.float32)
    rest = x - first
    second = rest.astype(jnp.bfloat16).astype(jnp.float32)
    return [first, second, rest - second]


def store_unit(ref, top, total, summed):
    ref[:HD, :] = summed.astype(jnp.bfloat16)
    rows = three_pieces(top) + three_pieces(total)
    rows.append(jnp.zeros((STAT_ROWS - len(rows), VECS), jnp.float32))
    ref[HD:, :] = jnp.concatenate(rows, axis=0).astype(jnp.bfloat16)


def load_unit(ref):
    stats = ref[HD:, :].astype(jnp.float32)
    top = stats[0:1] + stats[1:2] + stats[2:3]
    total = stats[3:4] + stats[4:5] + stats[5:6]
    return top, total, ref[:HD, :].astype(jnp.float32)


def prompt_kernel(valid_ref, own_ref, pair_ref, prompt_ref, summed_ref, stats_ref):
    vectors = jnp.concatenate([stacked_heads(own_ref[...]), stacked_heads(pair_ref[...])], axis=0)
    valid = valid_ref[0]
    tokens = prompt_ref.shape[0]
    parts = []
    for start in range(0, tokens, CHUNK):
        scores = scores_of(prompt_ref[start : start + CHUNK, :HD], vectors)
        token = lax.broadcasted_iota(jnp.int32, scores.shape, 0)
        scores = jnp.where(token < valid - start, scores, big_negative)
        parts.append(softmax_part(scores, prompt_ref[start : start + CHUNK, HD:]))
        if len(parts) == 2:
            parts = [merged(parts)]
    top, total, summed = merged(parts)
    summed_ref[...] = summed
    stats_ref[...] = jnp.concatenate(
        [top, total, jnp.zeros((6, 2 * VECS), jnp.float32)], axis=0
    )


def suffix_kernel(
    meta_ref, ids_ref, refs_ref, near_ref, far_ref, queries_ref, summed_ref, stats_ref, out_ref
):
    n_req = queries_ref.shape[0]
    n_slots = ids_ref.shape[1]
    capacity = n_slots // 2
    slots, half, _ = near_ref.shape
    z, core, parity = meta_ref[0], meta_ref[1], meta_ref[2]
    for d in range(n_req):
        target = z ^ d
        request = target * 2 + core
        vectors = jnp.concatenate(
            [
                stacked_heads(queries_ref[target, parity]),
                stacked_heads(queries_ref[target, 1 - parity]),
            ],
            axis=0,
        )
        wanted = refs_ref[request]
        blocks, biases = [], []
        for k in range(n_slots):
            slot = ids_ref[request, k]
            pool_ref = near_ref if k < capacity else far_ref
            blocks.append(pool_ref[jnp.maximum(slot, 0)])
            holder = z * 2 + (core if k < capacity else 1 - core)
            block = jnp.where(slot < 0, -1, holder * slots + slot)
            member = jnp.max((wanted == block).astype(jnp.int32), axis=0, keepdims=True) > 0
            biases.append(member)
        blocks = jnp.concatenate(blocks, axis=0)
        scores = scores_of(blocks[:, :HD], vectors)
        scores = jnp.concatenate(
            [
                jnp.where(member, scores[k * half : (k + 1) * half], big_negative)
                for k, member in enumerate(biases)
            ],
            axis=0,
        )
        part = softmax_part(scores, blocks[:, HD:])
        if d == 0:
            part = merged([part, (stats_ref[0:1], stats_ref[1:2], summed_ref[...])])
        top, total, summed = part
        for side in range(2):
            lanes = slice(side * VECS, (side + 1) * VECS)
            owner = parity if side == 0 else 1 - parity
            store_unit(
                out_ref.at[target, owner], top[:, lanes], total[:, lanes], summed[:, lanes]
            )


def final_kernel(units_ref, out_ref):
    n_req, n_pair = units_ref.shape[:2]
    parts = [load_unit(units_ref.at[r, p]) for r in range(n_req) for p in range(n_pair)]
    _, total, summed = merged(parts)
    attended = (summed / total).T
    for h in range(HEADS):
        out_ref[:, h * HD : (h + 1) * HD] = attended[h * BEAMS : (h + 1) * BEAMS]


def slots_of(block_table, n_batch, slots, capacity, z, core):
    entries = block_table.reshape(n_batch, 1, 1, BEAMS * SUF)
    holder = jnp.stack([z * 2 + core, z * 2 + 1 - core]).reshape(1, 2, 1, 1)
    slot = jnp.arange(slots, dtype=jnp.int32).reshape(1, 1, slots, 1)
    hit = jnp.any(entries == holder * slots + slot, axis=3)
    order = jnp.arange(slots, dtype=jnp.int32)
    before = (order[None, :] < order[:, None])[None, None]
    rank = jnp.sum((hit[:, :, None, :] & before).astype(jnp.int32), axis=3)
    index = jnp.arange(capacity, dtype=jnp.int32).reshape(1, 1, capacity, 1)
    chosen = hit[:, :, None, :] & (rank[:, :, None, :] == index)
    found = jnp.sum(jnp.where(chosen, order + 1, 0), axis=3) - 1
    return found.reshape(n_batch, 2 * capacity)


def on_device(queries, prompt_cache, pool, block_table, parents, lengths):
    n_req = lax.axis_size("z")
    n_batch = 2 * n_req
    z, core, parity = lax.axis_index("z"), lax.axis_index("core"), lax.axis_index("pair")
    ndist = 2 ** (SUF + 1) - 2
    capacity = 2 * ((ndist // 2 + n_batch - 1) // n_batch)
    slots, _, half, width = pool.shape
    tokens = prompt_cache.shape[2]
    smem = pl.BlockSpec(memory_space=pltpu.SMEM)
    vmem = pl.BlockSpec(memory_space=pltpu.VMEM)
    params = pltpu.CompilerParams(vmem_limit_bytes=40 * 2**20)

    gathered = lax.all_gather(queries, ("z", "pair"), axis=0)
    gathered = gathered.reshape(n_req, 2, BEAMS, HEADS * HD)
    other = swapped(queries, "pair")
    near = pool.reshape(slots, half, width)
    far = swapped(near, "core")

    meta = jnp.stack([z, core, parity]).astype(jnp.int32)
    ids = slots_of(block_table, n_batch, slots, capacity, z, core)
    wanted = block_table[parents].reshape(n_batch, BEAMS, SUF).transpose(0, 2, 1)
    wanted = jnp.tile(wanted, (1, 1, GROUP))

    length = lengths[0]
    valid = length // (2 * half) * half + jnp.clip(length % (2 * half) - parity * half, 0, half)
    summed, stats = pl.pallas_call(
        prompt_kernel,
        out_shape=(
            jax.ShapeDtypeStruct((HD, 2 * VECS), jnp.float32),
            jax.ShapeDtypeStruct((8, 2 * VECS), jnp.float32),
        ),
        in_specs=[smem, vmem, vmem, vmem],
        out_specs=(vmem, vmem),
        compiler_params=params,
        name="prompt_part",
    )(valid.reshape(1), queries, other, prompt_cache.reshape(tokens, width))

    units = pl.pallas_call(
        suffix_kernel,
        out_shape=jax.ShapeDtypeStruct((n_req, 2, UNIT_ROWS, VECS), jnp.bfloat16),
        in_specs=[smem, smem] + [vmem] * 6,
        out_specs=vmem,
        compiler_params=params,
        name="suffix_parts",
    )(meta, ids, wanted, near, far, gathered, summed, stats)
    units = units.reshape(2 * n_req, UNIT_ROWS, VECS)
    units = lax.all_to_all(units, ("z", "pair"), split_axis=0, concat_axis=0, tiled=True)

    return pl.pallas_call(
        final_kernel,
        out_shape=jax.ShapeDtypeStruct((BEAMS, HEADS * HD), jnp.float32),
        in_specs=[vmem],
        out_specs=vmem,
        compiler_params=params,
        name="combine",
    )(units.reshape(n_req, 2, UNIT_ROWS, VECS))


def solution(mesh):
    n_batch, n_mp = mesh.devices.shape
    split = jax.sharding.Mesh(
        mesh.devices.reshape(n_batch // 2, 2, n_mp // 2, 2), ("z", "core", "group", "pair")
    )
    batch, mp = ("z", "core"), ("group", "pair")
    return jax.shard_map(
        on_device,
        mesh=split,
        in_specs=(
            P(batch, mp),
            P(batch, mp, None, None),
            P(batch, mp, None, None),
            P(),
            P(),
            P(batch),
        ),
        out_specs=P(batch, mp),
        check_vma=False,
    )
```

```python
import functools

import jax
import jax.numpy as jnp
from jax import lax
from jax.experimental import pallas as pl
from jax.experimental.pallas import tpu as pltpu
from jax.sharding import PartitionSpec as P

HD = 128
GROUP = 16
BEAMS = 16
SUF = 4
HEADS = GROUP // 2
VECS = HEADS * BEAMS
STAT_ROWS = 16
UNIT_ROWS = HD + STAT_ROWS
CHUNK = 512

big_negative = -1e30
to_exp2 = HD ** (-0.5) * 1.4426950408889634


def swapped(value, axis):
    return lax.ppermute(value, axis, [(0, 1), (1, 0)])


def stacked_heads(q):
    return jnp.concatenate([q[:, h * HD : (h + 1) * HD] for h in range(HEADS)], axis=0)


def scores_of(keys, vectors):
    return lax.dot_general(
        keys, vectors, (((1,), (1,)), ((), ())), preferred_element_type=jnp.float32
    )


def summed_of(values, weights):
    return lax.dot_general(
        values,
        weights.astype(jnp.bfloat16),
        (((0,), (0,)), ((), ())),
        preferred_element_type=jnp.float32,
    )


def merged(parts):
    top = functools.reduce(jnp.maximum, [p[0] for p in parts])
    total = 0.0
    summed = 0.0
    for part_top, part_total, part_summed in parts:
        factor = jnp.exp2((part_top - top) * to_exp2)
        total = total + part_total * factor
        summed = summed + part_summed * factor
    return top, total, summed


def softmax_part(scores, values):
    top = jnp.max(scores, axis=0, keepdims=True)
    weights = jnp.exp2((scores - top) * to_exp2)
    total = jnp.sum(weights, axis=0, keepdims=True)
    return top, total, summed_of(values, weights)


def three_pieces(x):
    first = x.astype(jnp.bfloat16).astype(jnp.float32)
    rest = x - first
    second = rest.astype(jnp.bfloat16).astype(jnp.float32)
    return [first, second, rest - second]


def store_unit(ref, top, total, summed):
    ref[:HD, :] = summed.astype(jnp.bfloat16)
    rows = three_pieces(top) + three_pieces(total)
    rows.append(jnp.zeros((STAT_ROWS - len(rows), VECS), jnp.float32))
    ref[HD:, :] = jnp.concatenate(rows, axis=0).astype(jnp.bfloat16)


def load_unit(ref):
    stats = ref[HD:, :].astype(jnp.float32)
    top = stats[0:1] + stats[1:2] + stats[2:3]
    total = stats[3:4] + stats[4:5] + stats[5:6]
    return top, total, ref[:HD, :].astype(jnp.float32)


def prompt_kernel(valid_ref, own_ref, pair_ref, prompt_ref, summed_ref, stats_ref):
    vectors = jnp.concatenate([stacked_heads(own_ref[...]), stacked_heads(pair_ref[...])], axis=0)
    valid = valid_ref[0]
    tokens = prompt_ref.shape[0]
    parts = []
    for start in range(0, tokens, CHUNK):
        scores = scores_of(prompt_ref[start : start + CHUNK, :HD], vectors)
        token = lax.broadcasted_iota(jnp.int32, scores.shape, 0)
        scores = jnp.where(token < valid - start, scores, big_negative)
        parts.append(softmax_part(scores, prompt_ref[start : start + CHUNK, HD:]))
        if len(parts) == 2:
            parts = [merged(parts)]
    top, total, summed = merged(parts)
    summed_ref[...] = summed
    stats_ref[...] = jnp.concatenate(
        [top, total, jnp.zeros((6, 2 * VECS), jnp.float32)], axis=0
    )


def suffix_kernel(
    meta_ref, ids_ref, refs_ref, near_ref, far_ref, queries_ref, summed_ref, stats_ref, out_ref
):
    n_req = queries_ref.shape[0]
    n_slots = ids_ref.shape[1]
    capacity = n_slots // 2
    slots, half, _ = near_ref.shape
    z, core, parity = meta_ref[0], meta_ref[1], meta_ref[2]
    for d in range(n_req):
        target = z ^ d
        request = target * 2 + core
        vectors = jnp.concatenate(
            [
                stacked_heads(queries_ref[target, parity]),
                stacked_heads(queries_ref[target, 1 - parity]),
            ],
            axis=0,
        )
        wanted = refs_ref[request]
        blocks, biases = [], []
        for k in range(n_slots):
            slot = ids_ref[request, k]
            pool_ref = near_ref if k < capacity else far_ref
            blocks.append(pool_ref[jnp.maximum(slot, 0)])
            holder = z * 2 + (core if k < capacity else 1 - core)
            block = jnp.where(slot < 0, -1, holder * slots + slot)
            member = jnp.max((wanted == block).astype(jnp.int32), axis=0, keepdims=True) > 0
            biases.append(member)
        blocks = jnp.concatenate(blocks, axis=0)
        scores = scores_of(blocks[:, :HD], vectors)
        scores = jnp.concatenate(
            [
                jnp.where(member, scores[k * half : (k + 1) * half], big_negative)
                for k, member in enumerate(biases)
            ],
            axis=0,
        )
        part = softmax_part(scores, blocks[:, HD:])
        if d == 0:
            part = merged([part, (stats_ref[0:1], stats_ref[1:2], summed_ref[...])])
        top, total, summed = part
        for side in range(2):
            lanes = slice(side * VECS, (side + 1) * VECS)
            owner = parity if side == 0 else 1 - parity
            store_unit(
                out_ref.at[target, owner], top[:, lanes], total[:, lanes], summed[:, lanes]
            )


def final_kernel(units_ref, out_ref):
    n_req, n_pair = units_ref.shape[:2]
    parts = [load_unit(units_ref.at[r, p]) for r in range(n_req) for p in range(n_pair)]
    _, total, summed = merged(parts)
    attended = (summed / total).T
    for h in range(HEADS):
        out_ref[:, h * HD : (h + 1) * HD] = attended[h * BEAMS : (h + 1) * BEAMS]


def slots_of(block_table, n_batch, slots, capacity, z, core):
    entries = block_table.reshape(n_batch, 1, 1, BEAMS * SUF)
    holder = jnp.stack([z * 2 + core, z * 2 + 1 - core]).reshape(1, 2, 1, 1)
    slot = jnp.arange(slots, dtype=jnp.int32).reshape(1, 1, slots, 1)
    hit = jnp.any(entries == holder * slots + slot, axis=3)
    order = jnp.arange(slots, dtype=jnp.int32)
    before = (order[None, :] < order[:, None])[None, None]
    rank = jnp.sum((hit[:, :, None, :] & before).astype(jnp.int32), axis=3)
    index = jnp.arange(capacity, dtype=jnp.int32).reshape(1, 1, capacity, 1)
    chosen = hit[:, :, None, :] & (rank[:, :, None, :] == index)
    found = jnp.sum(jnp.where(chosen, order + 1, 0), axis=3) - 1
    return found.reshape(n_batch, 2 * capacity)


def on_device(queries, prompt_cache, pool, block_table, parents, lengths):
    n_req = lax.axis_size("z")
    n_batch = 2 * n_req
    z, core, parity = lax.axis_index("z"), lax.axis_index("core"), lax.axis_index("pair")
    ndist = 2 ** (SUF + 1) - 2
    capacity = 2 * ((ndist // 2 + n_batch - 1) // n_batch)
    slots, _, half, width = pool.shape
    tokens = prompt_cache.shape[2]
    smem = pl.BlockSpec(memory_space=pltpu.SMEM)
    vmem = pl.BlockSpec(memory_space=pltpu.VMEM)
    params = pltpu.CompilerParams(vmem_limit_bytes=40 * 2**20)

    copies = jnp.broadcast_to(queries[None], (2 * n_req,) + queries.shape)
    gathered = lax.all_to_all(copies, ("z", "pair"), split_axis=0, concat_axis=0, tiled=True)
    gathered = gathered.reshape(n_req, 2, BEAMS, HEADS * HD)
    other = swapped(queries, "pair")
    near = pool.reshape(slots, half, width)
    far = swapped(near, "core")

    meta = jnp.stack([z, core, parity]).astype(jnp.int32)
    ids = slots_of(block_table, n_batch, slots, capacity, z, core)
    wanted = block_table[parents].reshape(n_batch, BEAMS, SUF).transpose(0, 2, 1)
    wanted = jnp.tile(wanted, (1, 1, GROUP))

    length = lengths[0]
    valid = length // (2 * half) * half + jnp.clip(length % (2 * half) - parity * half, 0, half)
    summed, stats = pl.pallas_call(
        prompt_kernel,
        out_shape=(
            jax.ShapeDtypeStruct((HD, 2 * VECS), jnp.float32),
            jax.ShapeDtypeStruct((8, 2 * VECS), jnp.float32),
        ),
        in_specs=[smem, vmem, vmem, vmem],
        out_specs=(vmem, vmem),
        compiler_params=params,
        name="prompt_part",
    )(valid.reshape(1), queries, other, prompt_cache.reshape(tokens, width))

    units = pl.pallas_call(
        suffix_kernel,
        out_shape=jax.ShapeDtypeStruct((n_req, 2, UNIT_ROWS, VECS), jnp.bfloat16),
        in_specs=[smem, smem] + [vmem] * 6,
        out_specs=vmem,
        compiler_params=params,
        name="suffix_parts",
    )(meta, ids, wanted, near, far, gathered, summed, stats)
    units = units.reshape(2 * n_req, UNIT_ROWS, VECS)
    units = lax.all_to_all(units, ("z", "pair"), split_axis=0, concat_axis=0, tiled=True)

    return pl.pallas_call(
        final_kernel,
        out_shape=jax.ShapeDtypeStruct((BEAMS, HEADS * HD), jnp.float32),
        in_specs=[vmem],
        out_specs=vmem,
        compiler_params=params,
        name="combine",
    )(units.reshape(n_req, 2, UNIT_ROWS, VECS))


def solution(mesh):
    n_batch, n_mp = mesh.devices.shape
    split = jax.sharding.Mesh(
        mesh.devices.reshape(n_batch // 2, 2, n_mp // 2, 2), ("z", "core", "group", "pair")
    )
    batch, mp = ("z", "core"), ("group", "pair")
    return jax.shard_map(
        on_device,
        mesh=split,
        in_specs=(
            P(batch, mp),
            P(batch, mp, None, None),
            P(batch, mp, None, None),
            P(),
            P(),
            P(batch),
        ),
        out_specs=P(batch, mp),
        check_vma=False,
    )
```

```python
import functools

import jax
import jax.numpy as jnp
from jax import lax
from jax.experimental import pallas as pl
from jax.experimental.pallas import tpu as pltpu
from jax.sharding import PartitionSpec as P

HD = 128
GROUP = 16
BEAMS = 16
SUF = 4
HEADS = GROUP // 2
VECS = HEADS * BEAMS
STAT_ROWS = 16
UNIT_ROWS = HD + STAT_ROWS
CHUNK = 512

big_negative = -1e30
to_exp2 = HD ** (-0.5) * 1.4426950408889634


def swapped(value, axis):
    return lax.ppermute(value, axis, [(0, 1), (1, 0)])


def stacked_heads(q):
    return jnp.concatenate([q[:, h * HD : (h + 1) * HD] for h in range(HEADS)], axis=0)


def scores_of(keys, vectors):
    return lax.dot_general(
        keys, vectors, (((1,), (1,)), ((), ())), preferred_element_type=jnp.float32
    )


def summed_of(values, weights):
    return lax.dot_general(
        values,
        weights.astype(jnp.bfloat16),
        (((0,), (0,)), ((), ())),
        preferred_element_type=jnp.float32,
    )


def merged(parts):
    top = functools.reduce(jnp.maximum, [p[0] for p in parts])
    total = 0.0
    summed = 0.0
    for part_top, part_total, part_summed in parts:
        factor = jnp.exp2((part_top - top) * to_exp2)
        total = total + part_total * factor
        summed = summed + part_summed * factor
    return top, total, summed


def weighted(scores):
    top = jnp.max(scores, axis=0, keepdims=True)
    weights = jnp.exp2((scores - top) * to_exp2)
    return top, jnp.sum(weights, axis=0, keepdims=True), weights


def three_pieces(x):
    first = x.astype(jnp.bfloat16).astype(jnp.float32)
    rest = x - first
    second = rest.astype(jnp.bfloat16).astype(jnp.float32)
    return [first, second, rest - second]


def store_unit(ref, top, total, summed):
    ref[:HD, :] = summed.astype(jnp.bfloat16)
    rows = three_pieces(top) + three_pieces(total)
    rows.append(jnp.zeros((STAT_ROWS - len(rows), VECS), jnp.float32))
    ref[HD:, :] = jnp.concatenate(rows, axis=0).astype(jnp.bfloat16)


def load_unit(ref):
    stats = ref[HD:, :].astype(jnp.float32)
    top = stats[0:1] + stats[1:2] + stats[2:3]
    total = stats[3:4] + stats[4:5] + stats[5:6]
    return top, total, ref[:HD, :].astype(jnp.float32)


def count(left, right):
    return jnp.dot(
        left.astype(jnp.bfloat16), right.astype(jnp.bfloat16), preferred_element_type=jnp.float32
    )


def iota(shape, axis):
    return lax.broadcasted_iota(jnp.int32, shape, axis)


def prepare_kernel(
    capacity, length_ref, own_ref, pair_ref, prompt_ref, table_ref, parents_ref, near_ref, far_ref,
    summed_ref, stats_ref, keys_ref, values_ref, member_ref, rows_ref,
):
    n_req = keys_ref.shape[0]
    slots, half, _ = near_ref.shape
    rows = table_ref.shape[1]
    n_batch = rows // BEAMS
    z, core, parity = lax.axis_index("z"), lax.axis_index("core"), lax.axis_index("pair")

    slot = iota((2 * slots, rows), 0)
    mine = slot < slots
    block = jnp.where(mine, slot, slot - slots) + jnp.where(mine, 2 * z + core, 2 * z + 1 - core) * slots
    named = functools.reduce(
        jnp.logical_or, [table_ref[j : j + 1, :] == block for j in range(SUF)]
    ).astype(jnp.float32)
    group = (iota((rows, n_batch), 0) // BEAMS == iota((rows, n_batch), 1)).astype(jnp.float32)
    hit = jnp.where(count(named, group) > 0.0, 1.0, 0.0)
    left, right = iota((2 * slots, 2 * slots), 0), iota((2 * slots, 2 * slots), 1)
    before = (left // slots == right // slots) & (right < left)
    rank = count(before.astype(jnp.float32), hit)
    taken = (iota((rows, rows), 0) == parents_ref[...]).astype(jnp.float32)
    continued = count(named, taken)

    place = iota((2 * slots, n_batch), 0)
    found = []
    for k in range(2 * capacity):
        holder = k // capacity
        chosen = (hit > 0.0) & (rank == float(k % capacity)) & (place // slots == holder)
        found.append(jnp.sum(jnp.where(chosen, place + 1, 0), axis=0, keepdims=True))
    found = jnp.concatenate(found, axis=0)

    for d in range(n_req):
        request = (z ^ d) * 2 + core
        lane = iota((rows, 2 * VECS), 1)
        spread = iota((rows, 2 * VECS), 0) == request * BEAMS + lane % BEAMS
        rows_ref[: 2 * slots, :] = count(continued, spread.astype(jnp.float32))
        rows_ref[2 * slots :, :] = jnp.zeros((8, 2 * VECS), jnp.float32)
        mask = iota(found.shape, 1) == request
        picked = jnp.sum(jnp.where(mask, found, 0), axis=1, keepdims=True)
        values = []
        for k in range(2 * capacity):
            index = picked[k, 0]
            row = jnp.where(index > 0, index - 1, 2 * slots)
            member_ref[d, k : k + 1, :] = rows_ref[pl.ds(row, 1), :]
            pool_ref = near_ref if k < capacity else far_ref
            base = 0 if k < capacity else slots
            content = pool_ref[jnp.maximum(index - 1 - base, 0)]
            keys_ref[d, k * half : (k + 1) * half, :] = content[:, :HD]
            values.append(content[:, HD:])
        values_ref[d] = jnp.concatenate(values, axis=0).T

    vectors = jnp.concatenate([stacked_heads(own_ref[...]), stacked_heads(pair_ref[...])], axis=0)
    length = length_ref[0]
    whole = lax.div(length, 2 * half)
    valid = whole * half + jnp.clip(length - whole * (2 * half) - parity * half, 0, half)
    parts = []
    for start in range(0, prompt_ref.shape[0], CHUNK):
        scores = scores_of(prompt_ref[start : start + CHUNK, :HD], vectors)
        token = iota(scores.shape, 0)
        scores = jnp.where(token < valid - start, scores, big_negative)
        top, total, weights = weighted(scores)
        parts.append((top, total, summed_of(prompt_ref[start : start + CHUNK, HD:], weights)))
        if len(parts) == 2:
            parts = [merged(parts)]
    top, total, summed = merged(parts)
    summed_ref[...] = summed
    stats_ref[...] = jnp.concatenate(
        [top, total, jnp.zeros((6, 2 * VECS), jnp.float32)], axis=0
    )


def suffix_kernel(keys_ref, values_ref, member_ref, queries_ref, summed_ref, stats_ref, out_ref):
    n_req = queries_ref.shape[0]
    n_slots = member_ref.shape[1]
    half = keys_ref.shape[1] // n_slots
    z, parity = lax.axis_index("z"), lax.axis_index("pair")
    for d in range(n_req):
        target = z ^ d
        vectors = jnp.concatenate(
            [
                stacked_heads(queries_ref[target, parity]),
                stacked_heads(queries_ref[target, 1 - parity]),
            ],
            axis=0,
        )
        scores = scores_of(keys_ref[d], vectors)
        scores = jnp.concatenate(
            [
                jnp.where(
                    member_ref[d, k : k + 1, :] > 0.0,
                    scores[k * half : (k + 1) * half],
                    big_negative,
                )
                for k in range(n_slots)
            ],
            axis=0,
        )
        top, total, weights = weighted(scores)
        summed = jnp.dot(
            values_ref[d], weights.astype(jnp.bfloat16), preferred_element_type=jnp.float32
        )
        if d == 0:
            prompt = (stats_ref[0:1], stats_ref[1:2], summed_ref[...])
            top, total, summed = merged([(top, total, summed), prompt])
        for side in range(2):
            lanes = slice(side * VECS, (side + 1) * VECS)
            owner = parity if side == 0 else 1 - parity
            store_unit(
                out_ref.at[target, owner], top[:, lanes], total[:, lanes], summed[:, lanes]
            )


def final_kernel(units_ref, out_ref):
    n_req, n_pair = units_ref.shape[:2]
    parts = [load_unit(units_ref.at[r, p]) for r in range(n_req) for p in range(n_pair)]
    _, total, summed = merged(parts)
    attended = (summed / total).T
    for h in range(HEADS):
        out_ref[:, h * HD : (h + 1) * HD] = attended[h * BEAMS : (h + 1) * BEAMS]


def on_device(queries, prompt_cache, pool, block_table, parents, lengths):
    n_req = lax.axis_size("z")
    n_batch = 2 * n_req
    ndist = 2 ** (SUF + 1) - 2
    capacity = 2 * ((ndist // 2 + n_batch - 1) // n_batch)
    slots, _, half, width = pool.shape
    tokens = prompt_cache.shape[2]
    rows = block_table.shape[0]
    smem = pl.BlockSpec(memory_space=pltpu.SMEM)
    vmem = pl.BlockSpec(memory_space=pltpu.VMEM)
    params = pltpu.CompilerParams(vmem_limit_bytes=40 * 2**20)

    copies = jnp.broadcast_to(queries[None], (2 * n_req,) + queries.shape)
    gathered = lax.all_to_all(copies, ("z", "pair"), split_axis=0, concat_axis=0, tiled=True)
    gathered = gathered.reshape(n_req, 2, BEAMS, HEADS * HD)
    other = swapped(queries, "pair")
    near = pool.reshape(slots, half, width)
    far = swapped(near, "core")

    summed, stats, keys, values, member = pl.pallas_call(
        functools.partial(prepare_kernel, capacity),
        out_shape=(
            jax.ShapeDtypeStruct((HD, 2 * VECS), jnp.float32),
            jax.ShapeDtypeStruct((8, 2 * VECS), jnp.float32),
            jax.ShapeDtypeStruct((n_req, 2 * capacity * half, HD), jnp.bfloat16),
            jax.ShapeDtypeStruct((n_req, HD, 2 * capacity * half), jnp.bfloat16),
            jax.ShapeDtypeStruct((n_req, 2 * capacity, 2 * VECS), jnp.float32),
        ),
        in_specs=[smem] + [vmem] * 7,
        out_specs=(vmem,) * 5,
        scratch_shapes=[pltpu.VMEM((2 * slots + 8, 2 * VECS), jnp.float32)],
        compiler_params=params,
        name="prepare",
    )(
        lengths,
        queries,
        other,
        prompt_cache.reshape(tokens, width),
        block_table.T,
        parents.reshape(1, rows),
        near,
        far,
    )

    units = pl.pallas_call(
        suffix_kernel,
        out_shape=jax.ShapeDtypeStruct((n_req, 2, UNIT_ROWS, VECS), jnp.bfloat16),
        in_specs=[vmem] * 6,
        out_specs=vmem,
        compiler_params=params,
        name="suffix_parts",
    )(keys, values, member, gathered, summed, stats)
    units = units.reshape(2 * n_req, UNIT_ROWS, VECS)
    units = lax.all_to_all(units, ("z", "pair"), split_axis=0, concat_axis=0, tiled=True)

    return pl.pallas_call(
        final_kernel,
        out_shape=jax.ShapeDtypeStruct((BEAMS, HEADS * HD), jnp.float32),
        in_specs=[vmem],
        out_specs=vmem,
        compiler_params=params,
        name="combine",
    )(units.reshape(n_req, 2, UNIT_ROWS, VECS))


def solution(mesh):
    n_batch, n_mp = mesh.devices.shape
    split = jax.sharding.Mesh(
        mesh.devices.reshape(n_batch // 2, 2, n_mp // 2, 2), ("z", "core", "group", "pair")
    )
    batch, mp = ("z", "core"), ("group", "pair")
    return jax.shard_map(
        on_device,
        mesh=split,
        in_specs=(
            P(batch, mp),
            P(batch, mp, None, None),
            P(batch, mp, None, None),
            P(),
            P(),
            P(batch),
        ),
        out_specs=P(batch, mp),
        check_vma=False,
    )
```

```python
import functools

import jax
import jax.numpy as jnp
from jax import lax
from jax.experimental import pallas as pl
from jax.experimental.pallas import tpu as pltpu
from jax.sharding import PartitionSpec as P

HD = 128
GROUP = 16
BEAMS = 16
SUF = 4
HEADS = GROUP // 2
VECS = HEADS * BEAMS
STAT_ROWS = 16
UNIT_ROWS = HD + STAT_ROWS
CHUNK = 512

big_negative = -1e30
to_exp2 = HD ** (-0.5) * 1.4426950408889634


def swapped(value, axis):
    return lax.ppermute(value, axis, [(0, 1), (1, 0)])


def stacked_heads(q):
    return jnp.concatenate([q[:, h * HD : (h + 1) * HD] for h in range(HEADS)], axis=0)


def scores_of(keys, vectors):
    return lax.dot_general(
        keys, vectors, (((1,), (1,)), ((), ())), preferred_element_type=jnp.float32
    )


def summed_of(values, weights):
    return lax.dot_general(
        values,
        weights.astype(jnp.bfloat16),
        (((0,), (0,)), ((), ())),
        preferred_element_type=jnp.float32,
    )


def merged(parts):
    top = functools.reduce(jnp.maximum, [p[0] for p in parts])
    total = 0.0
    summed = 0.0
    for part_top, part_total, part_summed in parts:
        factor = jnp.exp2((part_top - top) * to_exp2)
        total = total + part_total * factor
        summed = summed + part_summed * factor
    return top, total, summed


def weighted(scores):
    top = jnp.max(scores, axis=0, keepdims=True)
    weights = jnp.exp2((scores - top) * to_exp2)
    return top, jnp.sum(weights, axis=0, keepdims=True), weights


def three_pieces(x):
    first = x.astype(jnp.bfloat16).astype(jnp.float32)
    rest = x - first
    second = rest.astype(jnp.bfloat16).astype(jnp.float32)
    return [first, second, rest - second]


def store_unit(ref, top, total, summed):
    ref[:HD, :] = summed.astype(jnp.bfloat16)
    rows = three_pieces(top) + three_pieces(total)
    rows.append(jnp.zeros((STAT_ROWS - len(rows), VECS), jnp.float32))
    ref[HD:, :] = jnp.concatenate(rows, axis=0).astype(jnp.bfloat16)


def load_unit(ref):
    stats = ref[HD:, :].astype(jnp.float32)
    top = stats[0:1] + stats[1:2] + stats[2:3]
    total = stats[3:4] + stats[4:5] + stats[5:6]
    return top, total, ref[:HD, :].astype(jnp.float32)


def count(left, right):
    return jnp.dot(
        left.astype(jnp.bfloat16), right.astype(jnp.bfloat16), preferred_element_type=jnp.float32
    )


def iota(shape, axis):
    return lax.broadcasted_iota(jnp.int32, shape, axis)


def copies_kernel(queries_ref, out_ref, sems):
    copies = [
        pltpu.make_async_copy(queries_ref, out_ref.at[i], sems.at[i])
        for i in range(out_ref.shape[0])
    ]
    for copy in copies:
        copy.start()
    for copy in copies:
        copy.wait()


def prompt_chunks(prompt_ref, held_ref, sems):
    copies = []
    for i in range(held_ref.shape[0] // CHUNK):
        part = pl.ds(i * CHUNK, CHUNK)
        copies.append(pltpu.make_async_copy(prompt_ref.at[part], held_ref.at[part], sems.at[i]))
    return copies


def prompt_part(length, half, held_ref, copies, vectors):
    parity = lax.axis_index("pair")
    whole = lax.div(length, 2 * half)
    valid = whole * half + jnp.clip(length - whole * (2 * half) - parity * half, 0, half)
    parts = []
    for i, copy in enumerate(copies):
        copy.wait()
        part = slice(i * CHUNK, (i + 1) * CHUNK)
        scores = scores_of(held_ref[part, :HD], vectors)
        token = iota(scores.shape, 0)
        scores = jnp.where(token < valid - i * CHUNK, scores, big_negative)
        top, total, weights = weighted(scores)
        parts.append((top, total, summed_of(held_ref[part, HD:], weights)))
        if len(parts) == 2:
            parts = [merged(parts)]
    return merged(parts)


def prepare_kernel(
    capacity, length_ref, own_ref, prompt_ref, table_ref, parents_ref, near_ref, far_ref,
    summed_ref, stats_ref, keys_ref, values_ref, member_ref,
    rows_ref, own, held, table, parents, near, sems, prompt_sems,
):
    n_req = keys_ref.shape[0]
    slots, half, _ = near.shape
    rows = table.shape[1]
    n_batch = rows // BEAMS
    z, core = lax.axis_index("z"), lax.axis_index("core")

    small = [
        pltpu.make_async_copy(source, target, sems.at[i])
        for i, (source, target) in enumerate(
            [(table_ref, table), (parents_ref, parents), (near_ref, near), (own_ref, own)]
        )
    ]
    chunks = prompt_chunks(prompt_ref, held, prompt_sems)
    for copy in small + chunks:
        copy.start()

    small[0].wait()
    slot = iota((2 * slots, rows), 0)
    mine = slot < slots
    block = jnp.where(mine, slot, slot - slots) + jnp.where(mine, 2 * z + core, 2 * z + 1 - core) * slots
    named = functools.reduce(
        jnp.logical_or, [table[j : j + 1, :] == block for j in range(SUF)]
    ).astype(jnp.float32)
    group = (iota((rows, n_batch), 0) // BEAMS == iota((rows, n_batch), 1)).astype(jnp.float32)
    hit = jnp.where(count(named, group) > 0.0, 1.0, 0.0)
    left, right = iota((2 * slots, 2 * slots), 0), iota((2 * slots, 2 * slots), 1)
    before = (left // slots == right // slots) & (right < left)
    rank = count(before.astype(jnp.float32), hit)
    small[1].wait()
    taken = (iota((rows, rows), 0) == parents[...]).astype(jnp.float32)
    continued = count(named, taken)

    place = iota((2 * slots, n_batch), 0)
    found = []
    for k in range(2 * capacity):
        holder = k // capacity
        chosen = (hit > 0.0) & (rank == float(k % capacity)) & (place // slots == holder)
        found.append(jnp.sum(jnp.where(chosen, place + 1, 0), axis=0, keepdims=True))
    found = jnp.concatenate(found, axis=0)

    small[2].wait()
    for d in range(n_req):
        request = (z ^ d) * 2 + core
        lane = iota((rows, 2 * VECS), 1)
        spread = iota((rows, 2 * VECS), 0) == request * BEAMS + lane % BEAMS
        rows_ref[: 2 * slots, :] = count(continued, spread.astype(jnp.float32))
        rows_ref[2 * slots :, :] = jnp.zeros((8, 2 * VECS), jnp.float32)
        mask = iota(found.shape, 1) == request
        picked = jnp.sum(jnp.where(mask, found, 0), axis=1, keepdims=True)
        values = []
        for k in range(2 * capacity):
            index = picked[k, 0]
            row = jnp.where(index > 0, index - 1, 2 * slots)
            member_ref[d, k : k + 1, :] = rows_ref[pl.ds(row, 1), :]
            pool_ref = near if k < capacity else far_ref
            base = 0 if k < capacity else slots
            content = pool_ref[jnp.maximum(index - 1 - base, 0)]
            keys_ref[d, k * half : (k + 1) * half, :] = content[:, :HD]
            values.append(content[:, HD:])
        values_ref[d] = jnp.concatenate(values, axis=0).T

    small[3].wait()
    top, total, summed = prompt_part(length_ref[0], half, held, chunks, stacked_heads(own[...]))
    summed_ref[...] = summed
    stats_ref[...] = jnp.concatenate([top, total, jnp.zeros((6, VECS), jnp.float32)], axis=0)


def other_heads_kernel(half, length_ref, gathered_ref, prompt_ref, out_ref, held, prompt_sems):
    chunks = prompt_chunks(prompt_ref, held, prompt_sems)
    for copy in chunks:
        copy.start()
    z, parity = lax.axis_index("z"), lax.axis_index("pair")
    vectors = stacked_heads(gathered_ref[z, 1 - parity])
    store_unit(out_ref, *prompt_part(length_ref[0], half, held, chunks, vectors))


def suffix_kernel(keys_ref, values_ref, member_ref, queries_ref, summed_ref, stats_ref, out_ref):
    n_req = queries_ref.shape[0]
    n_slots = member_ref.shape[1]
    half = keys_ref.shape[1] // n_slots
    z, parity = lax.axis_index("z"), lax.axis_index("pair")
    for d in range(n_req):
        target = z ^ d
        vectors = jnp.concatenate(
            [
                stacked_heads(queries_ref[target, parity]),
                stacked_heads(queries_ref[target, 1 - parity]),
            ],
            axis=0,
        )
        scores = scores_of(keys_ref[d], vectors)
        scores = jnp.concatenate(
            [
                jnp.where(
                    member_ref[d, k : k + 1, :] > 0.0,
                    scores[k * half : (k + 1) * half],
                    big_negative,
                )
                for k in range(n_slots)
            ],
            axis=0,
        )
        top, total, weights = weighted(scores)
        summed = jnp.dot(
            values_ref[d], weights.astype(jnp.bfloat16), preferred_element_type=jnp.float32
        )
        for side in range(2):
            lanes = slice(side * VECS, (side + 1) * VECS)
            owner = parity if side == 0 else 1 - parity
            part = (top[:, lanes], total[:, lanes], summed[:, lanes])
            if d == 0 and side == 0:
                part = merged([part, (stats_ref[0:1], stats_ref[1:2], summed_ref[...])])
            store_unit(out_ref.at[target, owner], *part)


def final_kernel(units_ref, last_ref, out_ref):
    n_req, n_pair = units_ref.shape[:2]
    parts = [load_unit(units_ref.at[r, p]) for r in range(n_req) for p in range(n_pair)]
    parts.append(load_unit(last_ref))
    _, total, summed = merged(parts)
    attended = (summed / total).T
    for h in range(HEADS):
        out_ref[:, h * HD : (h + 1) * HD] = attended[h * BEAMS : (h + 1) * BEAMS]


def in_hbm(value):
    return pltpu.with_memory_space_constraint(value, pltpu.HBM)


def on_device(queries, prompt_cache, pool, block_table, parents, lengths):
    n_req = lax.axis_size("z")
    n_batch = 2 * n_req
    ndist = 2 ** (SUF + 1) - 2
    capacity = 2 * ((ndist // 2 + n_batch - 1) // n_batch)
    slots, _, half, width = pool.shape
    tokens = prompt_cache.shape[2]
    rows = block_table.shape[0]
    smem = pl.BlockSpec(memory_space=pltpu.SMEM)
    vmem = pl.BlockSpec(memory_space=pltpu.VMEM)
    params = pltpu.CompilerParams(vmem_limit_bytes=40 * 2**20)

    hbm = pl.BlockSpec(memory_space=pltpu.HBM)
    chunk_sems = pltpu.SemaphoreType.DMA((tokens // CHUNK,))
    prompt = in_hbm(prompt_cache.reshape(tokens, width))
    near = pool.reshape(slots, half, width)
    far = swapped(near, "core")

    copies = pl.pallas_call(
        copies_kernel,
        out_shape=jax.ShapeDtypeStruct((2 * n_req,) + queries.shape, jnp.bfloat16),
        in_specs=[hbm],
        out_specs=vmem,
        scratch_shapes=[pltpu.SemaphoreType.DMA((2 * n_req,))],
        name="query_copies",
    )(in_hbm(queries))
    gathered = lax.all_to_all(copies, ("z", "pair"), split_axis=0, concat_axis=0, tiled=True)
    gathered = gathered.reshape(n_req, 2, BEAMS, HEADS * HD)

    summed, stats, keys, values, member = pl.pallas_call(
        functools.partial(prepare_kernel, capacity),
        out_shape=(
            jax.ShapeDtypeStruct((HD, VECS), jnp.float32),
            jax.ShapeDtypeStruct((8, VECS), jnp.float32),
            jax.ShapeDtypeStruct((n_req, 2 * capacity * half, HD), jnp.bfloat16),
            jax.ShapeDtypeStruct((n_req, HD, 2 * capacity * half), jnp.bfloat16),
            jax.ShapeDtypeStruct((n_req, 2 * capacity, 2 * VECS), jnp.float32),
        ),
        in_specs=[smem] + [hbm] * 5 + [vmem],
        out_specs=(vmem,) * 5,
        scratch_shapes=[
            pltpu.VMEM((2 * slots + 8, 2 * VECS), jnp.float32),
            pltpu.VMEM(queries.shape, jnp.bfloat16),
            pltpu.VMEM((tokens, width), jnp.bfloat16),
            pltpu.VMEM((SUF, rows), jnp.int32),
            pltpu.VMEM((1, rows), jnp.int32),
            pltpu.VMEM((slots, half, width), jnp.bfloat16),
            pltpu.SemaphoreType.DMA((4,)),
            chunk_sems,
        ],
        compiler_params=params,
        cost_estimate=pl.CostEstimate(
            flops=4 * tokens * VECS * HD, bytes_accessed=4 * tokens * width, transcendentals=0
        ),
        name="prepare",
    )(
        lengths,
        in_hbm(queries),
        prompt,
        in_hbm(block_table.T),
        in_hbm(parents.reshape(1, rows)),
        in_hbm(near),
        far,
    )

    units = pl.pallas_call(
        suffix_kernel,
        out_shape=jax.ShapeDtypeStruct((n_req, 2, UNIT_ROWS, VECS), jnp.bfloat16),
        in_specs=[vmem] * 6,
        out_specs=vmem,
        compiler_params=params,
        name="suffix_parts",
    )(keys, values, member, gathered, summed, stats)
    units, gathered = lax.optimization_barrier((units, gathered))
    units = units.reshape(2 * n_req, UNIT_ROWS, VECS)
    units = lax.all_to_all(units, ("z", "pair"), split_axis=0, concat_axis=0, tiled=True)

    given = pl.pallas_call(
        functools.partial(other_heads_kernel, half),
        out_shape=jax.ShapeDtypeStruct((UNIT_ROWS, VECS), jnp.bfloat16),
        in_specs=[smem, vmem, hbm],
        out_specs=vmem,
        scratch_shapes=[pltpu.VMEM((tokens, width), jnp.bfloat16), chunk_sems],
        compiler_params=params,
        cost_estimate=pl.CostEstimate(
            flops=4 * tokens * VECS * HD, bytes_accessed=2 * tokens * width, transcendentals=0
        ),
        name="other_heads",
    )(lengths, gathered, prompt)
    last = swapped(given, "pair")

    return pl.pallas_call(
        final_kernel,
        out_shape=jax.ShapeDtypeStruct((BEAMS, HEADS * HD), jnp.float32),
        in_specs=[vmem, vmem],
        out_specs=vmem,
        compiler_params=params,
        name="combine",
    )(units.reshape(n_req, 2, UNIT_ROWS, VECS), last)


def solution(mesh):
    n_batch, n_mp = mesh.devices.shape
    split = jax.sharding.Mesh(
        mesh.devices.reshape(n_batch // 2, 2, n_mp // 2, 2), ("z", "core", "group", "pair")
    )
    batch, mp = ("z", "core"), ("group", "pair")
    return jax.shard_map(
        on_device,
        mesh=split,
        in_specs=(
            P(batch, mp),
            P(batch, mp, None, None),
            P(batch, mp, None, None),
            P(),
            P(),
            P(batch),
        ),
        out_specs=P(batch, mp),
        check_vma=False,
    )
```

```python
import functools

import jax
import jax.numpy as jnp
from jax import lax
from jax.experimental import pallas as pl
from jax.experimental.pallas import tpu as pltpu
from jax.sharding import PartitionSpec as P

HD = 128
GROUP = 16
BEAMS = 16
SUF = 4
HEADS = GROUP // 2
VECS = HEADS * BEAMS
STAT_ROWS = 16
UNIT_ROWS = HD + STAT_ROWS
CHUNK = 512

big_negative = -1e30
to_exp2 = HD ** (-0.5) * 1.4426950408889634


def swapped(value, axis, mask=1):
    return lax.ppermute(value, axis, [(i, i ^ mask) for i in range(lax.axis_size(axis))])


def stacked_heads(q):
    return jnp.concatenate([q[:, h * HD : (h + 1) * HD] for h in range(HEADS)], axis=0)


def scores_of(keys, vectors):
    return lax.dot_general(
        keys, vectors, (((1,), (1,)), ((), ())), preferred_element_type=jnp.float32
    )


def summed_of(values, weights):
    return lax.dot_general(
        values,
        weights.astype(jnp.bfloat16),
        (((0,), (0,)), ((), ())),
        preferred_element_type=jnp.float32,
    )


def merged(parts):
    top = functools.reduce(jnp.maximum, [p[0] for p in parts])
    total = 0.0
    summed = 0.0
    for part_top, part_total, part_summed in parts:
        factor = jnp.exp2((part_top - top) * to_exp2)
        total = total + part_total * factor
        summed = summed + part_summed * factor
    return top, total, summed


def weighted(scores):
    top = jnp.max(scores, axis=0, keepdims=True)
    weights = jnp.exp2((scores - top) * to_exp2)
    return top, jnp.sum(weights, axis=0, keepdims=True), weights


def three_pieces(x):
    first = x.astype(jnp.bfloat16).astype(jnp.float32)
    rest = x - first
    second = rest.astype(jnp.bfloat16).astype(jnp.float32)
    return [first, second, rest - second]


def store_unit(ref, top, total, summed):
    ref[:HD, :] = summed.astype(jnp.bfloat16)
    rows = three_pieces(top) + three_pieces(total)
    rows.append(jnp.zeros((STAT_ROWS - len(rows), VECS), jnp.float32))
    ref[HD:, :] = jnp.concatenate(rows, axis=0).astype(jnp.bfloat16)


def load_unit(ref):
    stats = ref[HD:, :].astype(jnp.float32)
    top = stats[0:1] + stats[1:2] + stats[2:3]
    total = stats[3:4] + stats[4:5] + stats[5:6]
    return top, total, ref[:HD, :].astype(jnp.float32)


def count(left, right):
    return jnp.dot(
        left.astype(jnp.bfloat16), right.astype(jnp.bfloat16), preferred_element_type=jnp.float32
    )


def iota(shape, axis):
    return lax.broadcasted_iota(jnp.int32, shape, axis)


def prompt_chunks(prompt_ref, held_ref, sems):
    copies = []
    for i in range(held_ref.shape[0] // CHUNK):
        part = pl.ds(i * CHUNK, CHUNK)
        copies.append(pltpu.make_async_copy(prompt_ref.at[part], held_ref.at[part], sems.at[i]))
    return copies


def prompt_part(length, half, held_ref, copies, vectors):
    parity = lax.axis_index("pair")
    whole = lax.div(length, 2 * half)
    valid = whole * half + jnp.clip(length - whole * (2 * half) - parity * half, 0, half)
    parts = []
    for i, copy in enumerate(copies):
        copy.wait()
        part = slice(i * CHUNK, (i + 1) * CHUNK)
        scores = scores_of(held_ref[part, :HD], vectors)
        token = iota(scores.shape, 0)
        scores = jnp.where(token < valid - i * CHUNK, scores, big_negative)
        top, total, weights = weighted(scores)
        parts.append((top, total, summed_of(held_ref[part, HD:], weights)))
        if len(parts) == 2:
            parts = [merged(parts)]
    return merged(parts)


def prepare_kernel(
    capacity, table_ref, parents_ref, near_ref, far_ref, keys_ref, values_ref, member_ref,
    rows_ref, table, parents, near, sems,
):
    n_req = keys_ref.shape[0]
    slots, half, _ = near.shape
    rows = table.shape[1]
    n_batch = rows // BEAMS
    z, core = lax.axis_index("z"), lax.axis_index("core")

    small = [
        pltpu.make_async_copy(source, target, sems.at[i])
        for i, (source, target) in enumerate(
            [(table_ref, table), (parents_ref, parents), (near_ref, near)]
        )
    ]
    for copy in small:
        copy.start()

    small[0].wait()
    slot = iota((2 * slots, rows), 0)
    mine = slot < slots
    block = jnp.where(mine, slot, slot - slots) + jnp.where(mine, 2 * z + core, 2 * z + 1 - core) * slots
    named = functools.reduce(
        jnp.logical_or, [table[j : j + 1, :] == block for j in range(SUF)]
    ).astype(jnp.float32)
    group = (iota((rows, n_batch), 0) // BEAMS == iota((rows, n_batch), 1)).astype(jnp.float32)
    hit = jnp.where(count(named, group) > 0.0, 1.0, 0.0)
    left, right = iota((2 * slots, 2 * slots), 0), iota((2 * slots, 2 * slots), 1)
    before = (left // slots == right // slots) & (right < left)
    rank = count(before.astype(jnp.float32), hit)
    small[1].wait()
    taken = (iota((rows, rows), 0) == parents[...]).astype(jnp.float32)
    continued = count(named, taken)

    place = iota((2 * slots, n_batch), 0)
    found = []
    for k in range(2 * capacity):
        holder = k // capacity
        chosen = (hit > 0.0) & (rank == float(k % capacity)) & (place // slots == holder)
        found.append(jnp.sum(jnp.where(chosen, place + 1, 0), axis=0, keepdims=True))
    found = jnp.concatenate(found, axis=0)

    small[2].wait()
    for d in range(n_req):
        request = (z ^ d) * 2 + core
        lane = iota((rows, 2 * VECS), 1)
        spread = iota((rows, 2 * VECS), 0) == request * BEAMS + lane % BEAMS
        rows_ref[: 2 * slots, :] = count(continued, spread.astype(jnp.float32))
        rows_ref[2 * slots :, :] = jnp.zeros((8, 2 * VECS), jnp.float32)
        mask = iota(found.shape, 1) == request
        picked = jnp.sum(jnp.where(mask, found, 0), axis=1, keepdims=True)
        values = []
        for k in range(2 * capacity):
            index = picked[k, 0]
            row = jnp.where(index > 0, index - 1, 2 * slots)
            member_ref[d, k : k + 1, :] = rows_ref[pl.ds(row, 1), :]
            pool_ref = near if k < capacity else far_ref
            base = 0 if k < capacity else slots
            content = pool_ref[jnp.maximum(index - 1 - base, 0)]
            keys_ref[d, k * half : (k + 1) * half, :] = content[:, :HD]
            values.append(content[:, HD:])
        values_ref[d] = jnp.concatenate(values, axis=0).T


def prompt_kernel(
    half, length_ref, own_ref, pair_ref, prompt_ref, summed_ref, stats_ref, out_ref,
    held, prompt_sems,
):
    chunks = prompt_chunks(prompt_ref, held, prompt_sems)
    for copy in chunks:
        copy.start()
    vectors = jnp.concatenate([stacked_heads(own_ref[...]), stacked_heads(pair_ref[...])], axis=0)
    top, total, summed = prompt_part(length_ref[0], half, held, chunks, vectors)
    summed_ref[...] = summed[:, :VECS]
    stats_ref[...] = jnp.concatenate(
        [top[:, :VECS], total[:, :VECS], jnp.zeros((6, VECS), jnp.float32)], axis=0
    )
    store_unit(out_ref, top[:, VECS:], total[:, VECS:], summed[:, VECS:])


def suffix_kernel(keys_ref, values_ref, member_ref, *rest):
    queries, out_ref = rest[:-1], rest[-1]
    n_req = keys_ref.shape[0]
    n_slots = member_ref.shape[1]
    half = keys_ref.shape[1] // n_slots
    z, parity = lax.axis_index("z"), lax.axis_index("pair")
    for d in range(n_req):
        target = z ^ d
        own_ref, pair_ref = queries[2 * d : 2 * d + 2]
        vectors = jnp.concatenate(
            [stacked_heads(own_ref[...]), stacked_heads(pair_ref[...])], axis=0
        )
        scores = scores_of(keys_ref[d], vectors)
        scores = jnp.concatenate(
            [
                jnp.where(
                    member_ref[d, k : k + 1, :] > 0.0,
                    scores[k * half : (k + 1) * half],
                    big_negative,
                )
                for k in range(n_slots)
            ],
            axis=0,
        )
        top, total, weights = weighted(scores)
        summed = jnp.dot(
            values_ref[d], weights.astype(jnp.bfloat16), preferred_element_type=jnp.float32
        )
        for side in range(2):
            lanes = slice(side * VECS, (side + 1) * VECS)
            owner = parity if side == 0 else 1 - parity
            store_unit(
                out_ref.at[target, owner], top[:, lanes], total[:, lanes], summed[:, lanes]
            )


def final_kernel(units_ref, last_ref, summed_ref, stats_ref, out_ref):
    n_req, n_pair = units_ref.shape[:2]
    parts = [load_unit(units_ref.at[r, p]) for r in range(n_req) for p in range(n_pair)]
    parts += [load_unit(last_ref), (stats_ref[0:1], stats_ref[1:2], summed_ref[...])]
    _, total, summed = merged(parts)
    attended = (summed / total).T
    for h in range(HEADS):
        out_ref[:, h * HD : (h + 1) * HD] = attended[h * BEAMS : (h + 1) * BEAMS]


def in_hbm(value):
    return pltpu.with_memory_space_constraint(value, pltpu.HBM)


def on_device(queries, prompt_cache, pool, block_table, parents, lengths):
    n_req = lax.axis_size("z")
    n_batch = 2 * n_req
    ndist = 2 ** (SUF + 1) - 2
    capacity = 2 * ((ndist // 2 + n_batch - 1) // n_batch)
    slots, _, half, width = pool.shape
    tokens = prompt_cache.shape[2]
    rows = block_table.shape[0]
    smem = pl.BlockSpec(memory_space=pltpu.SMEM)
    vmem = pl.BlockSpec(memory_space=pltpu.VMEM)
    params = pltpu.CompilerParams(vmem_limit_bytes=40 * 2**20)

    hbm = pl.BlockSpec(memory_space=pltpu.HBM)
    near = pool.reshape(slots, half, width)
    far = swapped(near, "core")
    sent = [queries, swapped(queries, "pair")]
    arrived = [swapped(queries, "z", d) for d in range(1, n_req)]
    for piece in arrived:
        sent += [piece, swapped(piece, "pair")]

    keys, values, member = pl.pallas_call(
        functools.partial(prepare_kernel, capacity),
        out_shape=(
            jax.ShapeDtypeStruct((n_req, 2 * capacity * half, HD), jnp.bfloat16),
            jax.ShapeDtypeStruct((n_req, HD, 2 * capacity * half), jnp.bfloat16),
            jax.ShapeDtypeStruct((n_req, 2 * capacity, 2 * VECS), jnp.float32),
        ),
        in_specs=[hbm] * 3 + [vmem],
        out_specs=(vmem,) * 3,
        scratch_shapes=[
            pltpu.VMEM((2 * slots + 8, 2 * VECS), jnp.float32),
            pltpu.VMEM((SUF, rows), jnp.int32),
            pltpu.VMEM((1, rows), jnp.int32),
            pltpu.VMEM((slots, half, width), jnp.bfloat16),
            pltpu.SemaphoreType.DMA((3,)),
        ],
        compiler_params=params,
        name="prepare",
    )(in_hbm(block_table.T), in_hbm(parents.reshape(1, rows)), in_hbm(near), far)

    units = pl.pallas_call(
        suffix_kernel,
        out_shape=jax.ShapeDtypeStruct((n_req, 2, UNIT_ROWS, VECS), jnp.bfloat16),
        in_specs=[vmem] * (3 + 2 * n_req),
        out_specs=vmem,
        compiler_params=params,
        name="suffix_parts",
    )(keys, values, member, *sent)
    units, other = lax.optimization_barrier((units, sent[1]))
    units = units.reshape(2 * n_req, UNIT_ROWS, VECS)
    units = lax.all_to_all(units, ("z", "pair"), split_axis=0, concat_axis=0, tiled=True)

    summed, stats, given = pl.pallas_call(
        functools.partial(prompt_kernel, half),
        out_shape=(
            jax.ShapeDtypeStruct((HD, VECS), jnp.float32),
            jax.ShapeDtypeStruct((8, VECS), jnp.float32),
            jax.ShapeDtypeStruct((UNIT_ROWS, VECS), jnp.bfloat16),
        ),
        in_specs=[smem, vmem, vmem, hbm],
        out_specs=(vmem,) * 3,
        scratch_shapes=[
            pltpu.VMEM((tokens, width), jnp.bfloat16),
            pltpu.SemaphoreType.DMA((tokens // CHUNK,)),
        ],
        compiler_params=params,
        cost_estimate=pl.CostEstimate(
            flops=8 * tokens * VECS * HD, bytes_accessed=2 * tokens * width, transcendentals=0
        ),
        name="prompt_part",
    )(lengths, queries, other, in_hbm(prompt_cache.reshape(tokens, width)))
    last = swapped(given, "pair")

    return pl.pallas_call(
        final_kernel,
        out_shape=jax.ShapeDtypeStruct((BEAMS, HEADS * HD), jnp.float32),
        in_specs=[vmem] * 4,
        out_specs=vmem,
        compiler_params=params,
        name="combine",
    )(units.reshape(n_req, 2, UNIT_ROWS, VECS), last, summed, stats)


def solution(mesh):
    n_batch, n_mp = mesh.devices.shape
    split = jax.sharding.Mesh(
        mesh.devices.reshape(n_batch // 2, 2, n_mp // 2, 2), ("z", "core", "group", "pair")
    )
    batch, mp = ("z", "core"), ("group", "pair")
    return jax.shard_map(
        on_device,
        mesh=split,
        in_specs=(
            P(batch, mp),
            P(batch, mp, None, None),
            P(batch, mp, None, None),
            P(),
            P(),
            P(batch),
        ),
        out_specs=P(batch, mp),
        check_vma=False,
    )
```

```python
import functools

import jax
import jax.numpy as jnp
from jax import lax
from jax.experimental import pallas as pl
from jax.experimental.pallas import tpu as pltpu
from jax.sharding import PartitionSpec as P

HD = 128
GROUP = 16
BEAMS = 16
SUF = 4
HEADS = GROUP // 2
VECS = HEADS * BEAMS
STAT_ROWS = 16
UNIT_ROWS = HD + STAT_ROWS
CHUNK = 512

big_negative = -1e30
to_exp2 = HD ** (-0.5) * 1.4426950408889634


def swapped(value, axis, mask=1):
    return lax.ppermute(value, axis, [(i, i ^ mask) for i in range(lax.axis_size(axis))])


def stacked_heads(q):
    return jnp.concatenate([q[:, h * HD : (h + 1) * HD] for h in range(HEADS)], axis=0)


def scores_of(keys, vectors):
    return lax.dot_general(
        keys, vectors, (((1,), (1,)), ((), ())), preferred_element_type=jnp.float32
    )


def summed_of(values, weights):
    return lax.dot_general(
        values,
        weights.astype(jnp.bfloat16),
        (((0,), (0,)), ((), ())),
        preferred_element_type=jnp.float32,
    )


def merged(parts):
    top = functools.reduce(jnp.maximum, [p[0] for p in parts])
    total = 0.0
    summed = 0.0
    for part_top, part_total, part_summed in parts:
        factor = jnp.exp2((part_top - top) * to_exp2)
        total = total + part_total * factor
        summed = summed + part_summed * factor
    return top, total, summed


def weighted(scores):
    top = jnp.max(scores, axis=0, keepdims=True)
    weights = jnp.exp2((scores - top) * to_exp2)
    return top, jnp.sum(weights, axis=0, keepdims=True), weights


def three_pieces(x):
    first = x.astype(jnp.bfloat16).astype(jnp.float32)
    rest = x - first
    second = rest.astype(jnp.bfloat16).astype(jnp.float32)
    return [first, second, rest - second]


def store_unit(ref, top, total, summed):
    ref[:HD, :] = summed.astype(jnp.bfloat16)
    rows = three_pieces(top) + three_pieces(total)
    rows.append(jnp.zeros((STAT_ROWS - len(rows), VECS), jnp.float32))
    ref[HD:, :] = jnp.concatenate(rows, axis=0).astype(jnp.bfloat16)


def empty_part():
    zeros = jnp.zeros((1, VECS), jnp.float32)
    return zeros + big_negative, zeros, jnp.zeros((HD, VECS), jnp.float32)


def load_unit(ref):
    stats = ref[HD:, :].astype(jnp.float32)
    top = stats[0:1] + stats[1:2] + stats[2:3]
    total = stats[3:4] + stats[4:5] + stats[5:6]
    return top, total, ref[:HD, :].astype(jnp.float32)


def count(left, right):
    return jnp.dot(
        left.astype(jnp.bfloat16), right.astype(jnp.bfloat16), preferred_element_type=jnp.float32
    )


def iota(shape, axis):
    return lax.broadcasted_iota(jnp.int32, shape, axis)


def prompt_part(valid, prompt_ref, vectors):
    parts = []
    for start in range(0, prompt_ref.shape[0], CHUNK):
        part = slice(start, start + CHUNK)
        scores = scores_of(prompt_ref[part, :HD], vectors)
        token = iota(scores.shape, 0)
        scores = jnp.where(token < valid - start, scores, big_negative)
        top, total, weights = weighted(scores)
        parts.append((top, total, summed_of(prompt_ref[part, HD:], weights)))
        if len(parts) == 2:
            parts = [merged(parts)]
    return merged(parts)


def prepare_kernel(
    capacity, length_ref, table_ref, parents_ref, near_ref, prompt_ref, far_ref,
    keys_ref, values_ref, member_ref, held_ref, valid_ref, rows_ref, table, parents, near, sems,
):
    n_req = keys_ref.shape[0]
    slots, half, _ = near.shape
    rows = table.shape[1]
    n_batch = rows // BEAMS
    z, core = lax.axis_index("z"), lax.axis_index("core")

    small = [
        pltpu.make_async_copy(source, target, sems.at[i])
        for i, (source, target) in enumerate(
            [(table_ref, table), (parents_ref, parents), (near_ref, near), (prompt_ref, held_ref)]
        )
    ]
    for copy in small:
        copy.start()

    length = length_ref[0]
    whole = lax.div(length, 2 * half)
    parity = lax.axis_index("pair")
    valid = whole * half + jnp.clip(length - whole * (2 * half) - parity * half, 0, half)
    valid_ref[...] = jnp.full(valid_ref.shape, valid, jnp.int32)

    small[0].wait()
    slot = iota((2 * slots, rows), 0)
    mine = slot < slots
    block = jnp.where(mine, slot, slot - slots) + jnp.where(mine, 2 * z + core, 2 * z + 1 - core) * slots
    named = functools.reduce(
        jnp.logical_or, [table[j : j + 1, :] == block for j in range(SUF)]
    ).astype(jnp.float32)
    group = (iota((rows, n_batch), 0) // BEAMS == iota((rows, n_batch), 1)).astype(jnp.float32)
    hit = jnp.where(count(named, group) > 0.0, 1.0, 0.0)
    left, right = iota((2 * slots, 2 * slots), 0), iota((2 * slots, 2 * slots), 1)
    before = (left // slots == right // slots) & (right < left)
    rank = count(before.astype(jnp.float32), hit)
    small[1].wait()
    taken = (iota((rows, rows), 0) == parents[...]).astype(jnp.float32)
    continued = count(named, taken)

    place = iota((2 * slots, n_batch), 0)
    found = []
    for k in range(2 * capacity):
        holder = k // capacity
        chosen = (hit > 0.0) & (rank == float(k % capacity)) & (place // slots == holder)
        found.append(jnp.sum(jnp.where(chosen, place + 1, 0), axis=0, keepdims=True))
    found = jnp.concatenate(found, axis=0)

    small[2].wait()
    for d in range(n_req):
        request = (z ^ d) * 2 + core
        lane = iota((rows, 2 * VECS), 1)
        spread = iota((rows, 2 * VECS), 0) == request * BEAMS + lane % BEAMS
        rows_ref[: 2 * slots, :] = count(continued, spread.astype(jnp.float32))
        rows_ref[2 * slots :, :] = jnp.zeros((8, 2 * VECS), jnp.float32)
        mask = iota(found.shape, 1) == request
        picked = jnp.sum(jnp.where(mask, found, 0), axis=1, keepdims=True)
        values = []
        for k in range(2 * capacity):
            index = picked[k, 0]
            row = jnp.where(index > 0, index - 1, 2 * slots)
            member_ref[d, k : k + 1, :] = rows_ref[pl.ds(row, 1), :]
            pool_ref = near if k < capacity else far_ref
            base = 0 if k < capacity else slots
            content = pool_ref[jnp.maximum(index - 1 - base, 0)]
            keys_ref[d, k * half : (k + 1) * half, :] = content[:, :HD]
            values.append(content[:, HD:])
        values_ref[d] = jnp.concatenate(values, axis=0).T
    small[3].wait()


def all_vectors(own_ref, pair_ref):
    return jnp.concatenate([stacked_heads(own_ref[...]), stacked_heads(pair_ref[...])], axis=0)


def suffix_parts(requests, queries, keys_ref, values_ref, member_ref):
    n_slots = member_ref.shape[1]
    half = keys_ref.shape[1] // n_slots
    scores = [
        scores_of(keys_ref[d], all_vectors(*queries[2 * i : 2 * i + 2]))
        for i, d in enumerate(requests)
    ]
    softmaxes = []
    for d, score in zip(requests, scores):
        pieces = [
            jnp.where(
                member_ref[d, k : k + 1, :] > 0.0,
                score[k * half : (k + 1) * half],
                big_negative,
            )
            for k in range(n_slots)
        ]
        softmaxes.append(weighted(jnp.concatenate(pieces, axis=0)))
    return [
        (
            top,
            total,
            jnp.dot(
                values_ref[d], weights.astype(jnp.bfloat16), preferred_element_type=jnp.float32
            ),
        )
        for d, (top, total, weights) in zip(requests, softmaxes)
    ]


def half_of(part, side):
    lanes = slice(side * VECS, (side + 1) * VECS)
    return [x[:, lanes] for x in part]


def away_kernel(keys_ref, values_ref, member_ref, *rest):
    queries, out_ref = rest[:-1], rest[-1]
    requests = tuple(reversed(range(1, keys_ref.shape[0])))
    z, parity = lax.axis_index("z"), lax.axis_index("pair")
    parts = suffix_parts(requests, queries, keys_ref, values_ref, member_ref)
    for d, part in zip(requests, parts):
        store_unit(out_ref.at[z ^ d, parity], *half_of(part, 0))
        store_unit(out_ref.at[z ^ d, 1 - parity], *half_of(part, 1))
    for side in range(2):
        store_unit(out_ref.at[z, side], *empty_part())


def home_kernel(
    keys_ref, values_ref, member_ref, own_ref, pair_ref, prompt_ref, valid_ref,
    summed_ref, stats_ref, out_ref,
):
    (suffix,) = suffix_parts((0,), (own_ref, pair_ref), keys_ref, values_ref, member_ref)
    prompt = prompt_part(valid_ref[0:1, :], prompt_ref, all_vectors(own_ref, pair_ref))
    part = merged([prompt, suffix])
    top, total, summed_ref[...] = half_of(part, 0)
    stats_ref[...] = jnp.concatenate([top, total, jnp.zeros((6, VECS), jnp.float32)], axis=0)
    store_unit(out_ref, *half_of(part, 1))


def final_kernel(units_ref, last_ref, summed_ref, stats_ref, out_ref):
    n_req, n_pair = units_ref.shape[:2]
    parts = [load_unit(units_ref.at[r, p]) for r in range(n_req) for p in range(n_pair)]
    parts += [load_unit(last_ref), (stats_ref[0:1], stats_ref[1:2], summed_ref[...])]
    _, total, summed = merged(parts)
    attended = (summed / total).T
    for h in range(HEADS):
        out_ref[:, h * HD : (h + 1) * HD] = attended[h * BEAMS : (h + 1) * BEAMS]


def in_hbm(value):
    return pltpu.with_memory_space_constraint(value, pltpu.HBM)


def on_device(queries, prompt_cache, pool, block_table, parents, lengths):
    n_req = lax.axis_size("z")
    n_batch = 2 * n_req
    ndist = 2 ** (SUF + 1) - 2
    capacity = 2 * ((ndist // 2 + n_batch - 1) // n_batch)
    slots, _, half, width = pool.shape
    tokens = prompt_cache.shape[2]
    rows = block_table.shape[0]
    vmem = pl.BlockSpec(memory_space=pltpu.VMEM)
    params = pltpu.CompilerParams(vmem_limit_bytes=40 * 2**20)

    hbm = pl.BlockSpec(memory_space=pltpu.HBM)
    near = pool.reshape(slots, half, width)
    far = swapped(near, "core")
    arrived = [swapped(queries, "z", d) for d in reversed(range(1, n_req))]
    sent = []
    for piece in arrived:
        sent += [piece, swapped(piece, "pair")]
    other = swapped(queries, "pair")

    keys, values, member, prompt, valid = pl.pallas_call(
        functools.partial(prepare_kernel, capacity),
        out_shape=(
            jax.ShapeDtypeStruct((n_req, 2 * capacity * half, HD), jnp.bfloat16),
            jax.ShapeDtypeStruct((n_req, HD, 2 * capacity * half), jnp.bfloat16),
            jax.ShapeDtypeStruct((n_req, 2 * capacity, 2 * VECS), jnp.float32),
            jax.ShapeDtypeStruct((tokens, width), jnp.bfloat16),
            jax.ShapeDtypeStruct((8, 2 * VECS), jnp.int32),
        ),
        in_specs=[pl.BlockSpec(memory_space=pltpu.SMEM)] + [hbm] * 4 + [vmem],
        out_specs=(vmem,) * 5,
        scratch_shapes=[
            pltpu.VMEM((2 * slots + 8, 2 * VECS), jnp.float32),
            pltpu.VMEM((SUF, rows), jnp.int32),
            pltpu.VMEM((1, rows), jnp.int32),
            pltpu.VMEM((slots, half, width), jnp.bfloat16),
            pltpu.SemaphoreType.DMA((4,)),
        ],
        compiler_params=params,
        name="prepare",
    )(
        lengths,
        in_hbm(block_table.T),
        in_hbm(parents.reshape(1, rows)),
        in_hbm(near),
        in_hbm(prompt_cache.reshape(tokens, width)),
        far,
    )

    units = pl.pallas_call(
        away_kernel,
        out_shape=jax.ShapeDtypeStruct((n_req, 2, UNIT_ROWS, VECS), jnp.bfloat16),
        in_specs=[vmem] * (3 + len(sent)),
        out_specs=vmem,
        compiler_params=params,
        name="suffix_away",
    )(keys, values, member, *sent)
    units, other = lax.optimization_barrier((units, other))
    units = units.reshape(2 * n_req, UNIT_ROWS, VECS)
    units = lax.all_to_all(units, ("z", "pair"), split_axis=0, concat_axis=0, tiled=True)

    summed, stats, given = pl.pallas_call(
        home_kernel,
        out_shape=(
            jax.ShapeDtypeStruct((HD, VECS), jnp.float32),
            jax.ShapeDtypeStruct((8, VECS), jnp.float32),
            jax.ShapeDtypeStruct((UNIT_ROWS, VECS), jnp.bfloat16),
        ),
        in_specs=[vmem] * 7,
        out_specs=(vmem,) * 3,
        compiler_params=params,
        cost_estimate=pl.CostEstimate(
            flops=8 * tokens * VECS * HD, bytes_accessed=2 * tokens * width, transcendentals=0
        ),
        name="home_part",
    )(keys, values, member, queries, other, prompt, valid)
    last = swapped(given, "pair")

    return pl.pallas_call(
        final_kernel,
        out_shape=jax.ShapeDtypeStruct((BEAMS, HEADS * HD), jnp.float32),
        in_specs=[vmem] * 4,
        out_specs=vmem,
        compiler_params=params,
        name="combine",
    )(units.reshape(n_req, 2, UNIT_ROWS, VECS), last, summed, stats)


def solution(mesh):
    n_batch, n_mp = mesh.devices.shape
    split = jax.sharding.Mesh(
        mesh.devices.reshape(n_batch // 2, 2, n_mp // 2, 2), ("z", "core", "group", "pair")
    )
    batch, mp = ("z", "core"), ("group", "pair")
    return jax.shard_map(
        on_device,
        mesh=split,
        in_specs=(
            P(batch, mp),
            P(batch, mp, None, None),
            P(batch, mp, None, None),
            P(),
            P(),
            P(batch),
        ),
        out_specs=P(batch, mp),
        check_vma=False,
    )
```

```python
import functools

import jax
import jax.numpy as jnp
from jax import lax
from jax.experimental import pallas as pl
from jax.experimental.pallas import tpu as pltpu
from jax.sharding import PartitionSpec as P

HD = 128
GROUP = 16
BEAMS = 16
SUF = 4
HEADS = GROUP // 2
VECS = HEADS * BEAMS
STAT_ROWS = 16
UNIT_ROWS = HD + STAT_ROWS
CHUNK = 512

big_negative = -1e30
to_exp2 = HD ** (-0.5) * 1.4426950408889634


def swapped(value, axis, mask=1):
    return lax.ppermute(value, axis, [(i, i ^ mask) for i in range(lax.axis_size(axis))])


def stacked_heads(q):
    return jnp.concatenate([q[:, h * HD : (h + 1) * HD] for h in range(HEADS)], axis=0)


def scores_of(keys, vectors):
    return lax.dot_general(
        keys, vectors, (((1,), (1,)), ((), ())), preferred_element_type=jnp.float32
    )


def summed_of(values, weights):
    return lax.dot_general(
        values,
        weights.astype(jnp.bfloat16),
        (((0,), (0,)), ((), ())),
        preferred_element_type=jnp.float32,
    )


def merged(parts):
    top = functools.reduce(jnp.maximum, [p[0] for p in parts])
    total = 0.0
    summed = 0.0
    for part_top, part_total, part_summed in parts:
        factor = jnp.exp2((part_top - top) * to_exp2)
        total = total + part_total * factor
        summed = summed + part_summed * factor
    return top, total, summed


def weighted(scores):
    top = jnp.max(scores, axis=0, keepdims=True)
    weights = jnp.exp2((scores - top) * to_exp2)
    return top, jnp.sum(weights, axis=0, keepdims=True), weights


def three_pieces(x):
    first = x.astype(jnp.bfloat16).astype(jnp.float32)
    rest = x - first
    second = rest.astype(jnp.bfloat16).astype(jnp.float32)
    return [first, second, rest - second]


def store_unit(ref, top, total, summed):
    ref[:HD, :] = summed.astype(jnp.bfloat16)
    rows = three_pieces(top) + three_pieces(total)
    rows.append(jnp.zeros((STAT_ROWS - len(rows), VECS), jnp.float32))
    ref[HD:, :] = jnp.concatenate(rows, axis=0).astype(jnp.bfloat16)


def empty_part():
    zeros = jnp.zeros((1, VECS), jnp.float32)
    return zeros + big_negative, zeros, jnp.zeros((HD, VECS), jnp.float32)


def load_unit(ref):
    stats = ref[HD:, :].astype(jnp.float32)
    top = stats[0:1] + stats[1:2] + stats[2:3]
    total = stats[3:4] + stats[4:5] + stats[5:6]
    return top, total, ref[:HD, :].astype(jnp.float32)


def count(left, right):
    return jnp.dot(
        left.astype(jnp.bfloat16), right.astype(jnp.bfloat16), preferred_element_type=jnp.float32
    )


def iota(shape, axis):
    return lax.broadcasted_iota(jnp.int32, shape, axis)


def prompt_part(length, half, prompt_ref, vectors):
    parity = lax.axis_index("pair")
    whole = lax.div(length, 2 * half)
    valid = whole * half + jnp.clip(length - whole * (2 * half) - parity * half, 0, half)
    parts = []
    for start in range(0, prompt_ref.shape[0], CHUNK):
        part = slice(start, start + CHUNK)
        scores = scores_of(prompt_ref[part, :HD], vectors)
        token = iota(scores.shape, 0)
        scores = jnp.where(token < valid - start, scores, big_negative)
        top, total, weights = weighted(scores)
        parts.append((top, total, summed_of(prompt_ref[part, HD:], weights)))
        if len(parts) == 2:
            parts = [merged(parts)]
    return merged(parts)


def prepare_kernel(
    capacity, table_ref, parents_ref, near_ref, prompt_ref, own_ref, far_ref,
    keys_ref, values_ref, member_ref, held_ref, own, rows_ref, table, parents, near, sems,
):
    n_req = keys_ref.shape[0]
    slots, half, _ = near.shape
    rows = table.shape[1]
    n_batch = rows // BEAMS
    z, core = lax.axis_index("z"), lax.axis_index("core")

    small = [
        pltpu.make_async_copy(source, target, sems.at[i])
        for i, (source, target) in enumerate(
            [
                (table_ref, table),
                (parents_ref, parents),
                (near_ref, near),
                (prompt_ref, held_ref),
                (own_ref, own),
            ]
        )
    ]
    for copy in small:
        copy.start()

    small[0].wait()
    slot = iota((2 * slots, rows), 0)
    mine = slot < slots
    block = jnp.where(mine, slot, slot - slots) + jnp.where(mine, 2 * z + core, 2 * z + 1 - core) * slots
    named = functools.reduce(
        jnp.logical_or, [table[j : j + 1, :] == block for j in range(SUF)]
    ).astype(jnp.float32)
    group = (iota((rows, n_batch), 0) // BEAMS == iota((rows, n_batch), 1)).astype(jnp.float32)
    hit = jnp.where(count(named, group) > 0.0, 1.0, 0.0)
    left, right = iota((2 * slots, 2 * slots), 0), iota((2 * slots, 2 * slots), 1)
    before = (left // slots == right // slots) & (right < left)
    rank = count(before.astype(jnp.float32), hit)
    small[1].wait()
    taken = (iota((rows, rows), 0) == parents[...]).astype(jnp.float32)
    continued = count(named, taken)

    place = iota((2 * slots, n_batch), 0)
    found = []
    for k in range(2 * capacity):
        holder = k // capacity
        chosen = (hit > 0.0) & (rank == float(k % capacity)) & (place // slots == holder)
        found.append(jnp.sum(jnp.where(chosen, place + 1, 0), axis=0, keepdims=True))
    found = jnp.concatenate(found, axis=0)

    small[2].wait()
    for d in range(n_req):
        request = (z ^ d) * 2 + core
        lane = iota((rows, 2 * VECS), 1)
        spread = iota((rows, 2 * VECS), 0) == request * BEAMS + lane % BEAMS
        rows_ref[: 2 * slots, :] = count(continued, spread.astype(jnp.float32))
        rows_ref[2 * slots :, :] = jnp.zeros((8, 2 * VECS), jnp.float32)
        mask = iota(found.shape, 1) == request
        picked = jnp.sum(jnp.where(mask, found, 0), axis=1, keepdims=True)
        values = []
        for k in range(2 * capacity):
            index = picked[k, 0]
            row = jnp.where(index > 0, index - 1, 2 * slots)
            member_ref[d, k : k + 1, :] = rows_ref[pl.ds(row, 1), :]
            pool_ref = near if k < capacity else far_ref
            base = 0 if k < capacity else slots
            content = pool_ref[jnp.maximum(index - 1 - base, 0)]
            keys_ref[d, k * half : (k + 1) * half, :] = content[:, :HD]
            values.append(content[:, HD:])
        values_ref[d] = jnp.concatenate(values, axis=0).T
    small[3].wait()
    small[4].wait()


def all_vectors(own_ref, pair_ref):
    return jnp.concatenate([stacked_heads(own_ref[...]), stacked_heads(pair_ref[...])], axis=0)


def suffix_parts(requests, queries, keys_ref, values_ref, member_ref):
    n_slots = member_ref.shape[1]
    half = keys_ref.shape[1] // n_slots
    scores = [
        scores_of(keys_ref[d], all_vectors(*queries[2 * i : 2 * i + 2]))
        for i, d in enumerate(requests)
    ]
    softmaxes = []
    for d, score in zip(requests, scores):
        pieces = [
            jnp.where(
                member_ref[d, k : k + 1, :] > 0.0,
                score[k * half : (k + 1) * half],
                big_negative,
            )
            for k in range(n_slots)
        ]
        softmaxes.append(weighted(jnp.concatenate(pieces, axis=0)))
    return [
        (
            top,
            total,
            jnp.dot(
                values_ref[d], weights.astype(jnp.bfloat16), preferred_element_type=jnp.float32
            ),
        )
        for d, (top, total, weights) in zip(requests, softmaxes)
    ]


def half_of(part, side):
    lanes = slice(side * VECS, (side + 1) * VECS)
    return [x[:, lanes] for x in part]


def away_kernel(keys_ref, values_ref, member_ref, *rest):
    queries, out_ref = rest[:-2], rest[-1]
    requests = tuple(reversed(range(1, keys_ref.shape[0])))
    z, parity = lax.axis_index("z"), lax.axis_index("pair")
    parts = suffix_parts(requests, queries, keys_ref, values_ref, member_ref)
    for d, part in zip(requests, parts):
        store_unit(out_ref.at[z ^ d, parity], *half_of(part, 0))
        store_unit(out_ref.at[z ^ d, 1 - parity], *half_of(part, 1))
    for side in range(2):
        store_unit(out_ref.at[z, side], *empty_part())


def home_kernel(
    half, length_ref, keys_ref, values_ref, member_ref, own_ref, pair_ref, prompt_ref, after_ref,
    summed_ref, stats_ref, out_ref,
):
    (suffix,) = suffix_parts((0,), (own_ref, pair_ref), keys_ref, values_ref, member_ref)
    prompt = prompt_part(length_ref[0], half, prompt_ref, all_vectors(own_ref, pair_ref))
    part = merged([prompt, suffix])
    top, total, summed_ref[...] = half_of(part, 0)
    stats_ref[...] = jnp.concatenate([top, total, jnp.zeros((6, VECS), jnp.float32)], axis=0)
    store_unit(out_ref, *half_of(part, 1))


def final_kernel(units_ref, last_ref, summed_ref, stats_ref, out_ref):
    n_req, n_pair = units_ref.shape[:2]
    parts = [load_unit(units_ref.at[r, p]) for r in range(n_req) for p in range(n_pair)]
    parts += [load_unit(last_ref), (stats_ref[0:1], stats_ref[1:2], summed_ref[...])]
    _, total, summed = merged(parts)
    attended = (summed / total).T
    for h in range(HEADS):
        out_ref[:, h * HD : (h + 1) * HD] = attended[h * BEAMS : (h + 1) * BEAMS]


def in_hbm(value):
    return pltpu.with_memory_space_constraint(value, pltpu.HBM)


def on_device(queries, prompt_cache, pool, block_table, parents, lengths):
    n_req = lax.axis_size("z")
    n_batch = 2 * n_req
    ndist = 2 ** (SUF + 1) - 2
    capacity = 2 * ((ndist // 2 + n_batch - 1) // n_batch)
    slots, _, half, width = pool.shape
    tokens = prompt_cache.shape[2]
    rows = block_table.shape[0]
    vmem = pl.BlockSpec(memory_space=pltpu.VMEM)
    params = pltpu.CompilerParams(vmem_limit_bytes=40 * 2**20)

    hbm = pl.BlockSpec(memory_space=pltpu.HBM)
    near = pool.reshape(slots, half, width)
    far = swapped(near, "core")
    arrived = [swapped(queries, "z", d) for d in reversed(range(1, n_req))]
    sent = []
    for piece in arrived:
        sent += [piece, swapped(piece, "pair")]
    other = swapped(queries, "pair")

    keys, values, member, prompt, own = pl.pallas_call(
        functools.partial(prepare_kernel, capacity),
        out_shape=(
            jax.ShapeDtypeStruct((n_req, 2 * capacity * half, HD), jnp.bfloat16),
            jax.ShapeDtypeStruct((n_req, HD, 2 * capacity * half), jnp.bfloat16),
            jax.ShapeDtypeStruct((n_req, 2 * capacity, 2 * VECS), jnp.float32),
            jax.ShapeDtypeStruct((tokens, width), jnp.bfloat16),
            jax.ShapeDtypeStruct(queries.shape, jnp.bfloat16),
        ),
        in_specs=[hbm] * 5 + [vmem],
        out_specs=(vmem,) * 5,
        scratch_shapes=[
            pltpu.VMEM((2 * slots + 8, 2 * VECS), jnp.float32),
            pltpu.VMEM((SUF, rows), jnp.int32),
            pltpu.VMEM((1, rows), jnp.int32),
            pltpu.VMEM((slots, half, width), jnp.bfloat16),
            pltpu.SemaphoreType.DMA((5,)),
        ],
        compiler_params=params,
        name="prepare",
    )(
        in_hbm(block_table.T),
        in_hbm(parents.reshape(1, rows)),
        in_hbm(near),
        in_hbm(prompt_cache.reshape(tokens, width)),
        in_hbm(queries),
        far,
    )

    units = pl.pallas_call(
        away_kernel,
        out_shape=jax.ShapeDtypeStruct((n_req, 2, UNIT_ROWS, VECS), jnp.bfloat16),
        in_specs=[vmem] * (4 + len(sent)),
        out_specs=vmem,
        compiler_params=params,
        name="suffix_away",
    )(keys, values, member, *sent, other)
    after = units
    units = units.reshape(2 * n_req, UNIT_ROWS, VECS)
    units = lax.all_to_all(units, ("z", "pair"), split_axis=0, concat_axis=0, tiled=True)

    summed, stats, given = pl.pallas_call(
        functools.partial(home_kernel, half),
        out_shape=(
            jax.ShapeDtypeStruct((HD, VECS), jnp.float32),
            jax.ShapeDtypeStruct((8, VECS), jnp.float32),
            jax.ShapeDtypeStruct((UNIT_ROWS, VECS), jnp.bfloat16),
        ),
        in_specs=[pl.BlockSpec(memory_space=pltpu.SMEM)] + [vmem] * 7,
        out_specs=(vmem,) * 3,
        compiler_params=params,
        cost_estimate=pl.CostEstimate(
            flops=8 * tokens * VECS * HD, bytes_accessed=2 * tokens * width, transcendentals=0
        ),
        name="home_part",
    )(lengths, keys, values, member, own, other, prompt, after)
    last = swapped(given, "pair")

    return pl.pallas_call(
        final_kernel,
        out_shape=jax.ShapeDtypeStruct((BEAMS, HEADS * HD), jnp.float32),
        in_specs=[vmem] * 4,
        out_specs=vmem,
        compiler_params=params,
        name="combine",
    )(units.reshape(n_req, 2, UNIT_ROWS, VECS), last, summed, stats)


def solution(mesh):
    n_batch, n_mp = mesh.devices.shape
    split = jax.sharding.Mesh(
        mesh.devices.reshape(n_batch // 2, 2, n_mp // 2, 2), ("z", "core", "group", "pair")
    )
    batch, mp = ("z", "core"), ("group", "pair")
    return jax.shard_map(
        on_device,
        mesh=split,
        in_specs=(
            P(batch, mp),
            P(batch, mp, None, None),
            P(batch, mp, None, None),
            P(),
            P(),
            P(batch),
        ),
        out_specs=P(batch, mp),
        check_vma=False,
    )
```

```python
import functools

import jax
import jax.numpy as jnp
from jax import lax
from jax.experimental import pallas as pl
from jax.experimental.pallas import tpu as pltpu
from jax.sharding import PartitionSpec as P

HD = 128
GROUP = 16
BEAMS = 16
SUF = 4
HEADS = GROUP // 2
VECS = HEADS * BEAMS
STAT_ROWS = 16
UNIT_ROWS = HD + STAT_ROWS
CHUNK = 512

big_negative = -1e30
to_exp2 = HD ** (-0.5) * 1.4426950408889634


def swapped(value, axis, mask=1):
    size = lax.axis_size(axis)
    return lax.ppermute(value, axis, [(i, i ^ mask) for i in range(size)])


def stacked_heads(q):
    return jnp.concatenate([q[:, h * HD : (h + 1) * HD] for h in range(HEADS)], axis=0)


def scores_of(keys, vectors):
    return lax.dot_general(
        keys, vectors, (((1,), (1,)), ((), ())), preferred_element_type=jnp.float32
    )


def summed_of(values, weights):
    return lax.dot_general(
        values,
        weights.astype(jnp.bfloat16),
        (((0,), (0,)), ((), ())),
        preferred_element_type=jnp.float32,
    )


def merged(parts):
    top = functools.reduce(jnp.maximum, [p[0] for p in parts])
    total = 0.0
    summed = 0.0
    for part_top, part_total, part_summed in parts:
        factor = jnp.exp2((part_top - top) * to_exp2)
        total = total + part_total * factor
        summed = summed + part_summed * factor
    return top, total, summed


def weighted(scores):
    top = jnp.max(scores, axis=0, keepdims=True)
    weights = jnp.exp2((scores - top) * to_exp2)
    return top, jnp.sum(weights, axis=0, keepdims=True), weights


def three_pieces(x):
    first = x.astype(jnp.bfloat16).astype(jnp.float32)
    rest = x - first
    second = rest.astype(jnp.bfloat16).astype(jnp.float32)
    return [first, second, rest - second]


def store_unit(ref, top, total, summed):
    ref[:HD, :] = summed.astype(jnp.bfloat16)
    rows = three_pieces(top) + three_pieces(total)
    rows.append(jnp.zeros((STAT_ROWS - len(rows), VECS), jnp.float32))
    ref[HD:, :] = jnp.concatenate(rows, axis=0).astype(jnp.bfloat16)


def empty_part():
    zeros = jnp.zeros((1, VECS), jnp.float32)
    return zeros + big_negative, zeros, jnp.zeros((HD, VECS), jnp.float32)


def load_unit(ref):
    stats = ref[HD:, :].astype(jnp.float32)
    top = stats[0:1] + stats[1:2] + stats[2:3]
    total = stats[3:4] + stats[4:5] + stats[5:6]
    return top, total, ref[:HD, :].astype(jnp.float32)


def count(left, right):
    return jnp.dot(
        left.astype(jnp.bfloat16), right.astype(jnp.bfloat16), preferred_element_type=jnp.float32
    )


def iota(shape, axis):
    return lax.broadcasted_iota(jnp.int32, shape, axis)


def prompt_part(length, half, prompt_ref, vectors):
    parity = lax.axis_index("pair")
    whole = lax.div(length, 2 * half)
    valid = whole * half + jnp.clip(length - whole * (2 * half) - parity * half, 0, half)
    parts = []
    for start in range(0, prompt_ref.shape[0], CHUNK):
        part = slice(start, start + CHUNK)
        scores = scores_of(prompt_ref[part, :HD], vectors)
        token = iota(scores.shape, 0)
        scores = jnp.where(token < valid - start, scores, big_negative)
        top, total, weights = weighted(scores)
        parts.append((top, total, summed_of(prompt_ref[part, HD:], weights)))
        if len(parts) == 2:
            parts = [merged(parts)]
    return merged(parts)


def prepare_kernel(
    capacity, table_ref, parents_ref, near_ref, prompt_ref, own_ref, far_ref,
    keys_ref, values_ref, member_ref, held_ref, own, rows_ref, table, parents, near, sems,
):
    n_req = keys_ref.shape[0]
    slots, half, _ = near.shape
    rows = table.shape[1]
    n_batch = rows // BEAMS
    z, core = lax.axis_index("z"), lax.axis_index("core")

    small = [
        pltpu.make_async_copy(source, target, sems.at[i])
        for i, (source, target) in enumerate(
            [
                (table_ref, table),
                (parents_ref, parents),
                (near_ref, near),
                (prompt_ref, held_ref),
                (own_ref, own),
            ]
        )
    ]
    for copy in small:
        copy.start()

    small[0].wait()
    slot = iota((2 * slots, rows), 0)
    mine = slot < slots
    block = jnp.where(mine, slot, slot - slots) + jnp.where(mine, 2 * z + core, 2 * z + 1 - core) * slots
    named = functools.reduce(
        jnp.logical_or, [table[j : j + 1, :] == block for j in range(SUF)]
    ).astype(jnp.float32)
    group = (iota((rows, n_batch), 0) // BEAMS == iota((rows, n_batch), 1)).astype(jnp.float32)
    hit = jnp.where(count(named, group) > 0.0, 1.0, 0.0)
    left, right = iota((2 * slots, 2 * slots), 0), iota((2 * slots, 2 * slots), 1)
    before = (left // slots == right // slots) & (right < left)
    rank = count(before.astype(jnp.float32), hit)
    small[1].wait()
    taken = (iota((rows, rows), 0) == parents[...]).astype(jnp.float32)
    continued = count(named, taken)

    place = iota((2 * slots, n_batch), 0)
    found = []
    for k in range(2 * capacity):
        holder = k // capacity
        chosen = (hit > 0.0) & (rank == float(k % capacity)) & (place // slots == holder)
        found.append(jnp.sum(jnp.where(chosen, place + 1, 0), axis=0, keepdims=True))
    found = jnp.concatenate(found, axis=0)

    small[2].wait()
    for d in range(n_req):
        request = (z ^ d) * 2 + core
        lane = iota((rows, 2 * VECS), 1)
        spread = iota((rows, 2 * VECS), 0) == request * BEAMS + lane % BEAMS
        rows_ref[: 2 * slots, :] = count(continued, spread.astype(jnp.float32))
        rows_ref[2 * slots :, :] = jnp.zeros((8, 2 * VECS), jnp.float32)
        mask = iota(found.shape, 1) == request
        picked = jnp.sum(jnp.where(mask, found, 0), axis=1, keepdims=True)
        values = []
        for k in range(2 * capacity):
            index = picked[k, 0]
            row = jnp.where(index > 0, index - 1, 2 * slots)
            member_ref[d, k : k + 1, :] = rows_ref[pl.ds(row, 1), :]
            pool_ref = near if k < capacity else far_ref
            base = 0 if k < capacity else slots
            content = pool_ref[jnp.maximum(index - 1 - base, 0)]
            keys_ref[d, k * half : (k + 1) * half, :] = content[:, :HD]
            values.append(content[:, HD:])
        values_ref[d] = jnp.concatenate(values, axis=0).T
    small[3].wait()
    small[4].wait()


def all_vectors(own_ref, pair_ref):
    return jnp.concatenate([stacked_heads(own_ref[...]), stacked_heads(pair_ref[...])], axis=0)


def suffix_parts(requests, queries, keys_ref, values_ref, member_ref):
    n_slots = member_ref.shape[1]
    half = keys_ref.shape[1] // n_slots
    scores = [
        scores_of(keys_ref[d], all_vectors(*queries[2 * i : 2 * i + 2]))
        for i, d in enumerate(requests)
    ]
    softmaxes = []
    for d, score in zip(requests, scores):
        pieces = [
            jnp.where(
                member_ref[d, k : k + 1, :] > 0.0,
                score[k * half : (k + 1) * half],
                big_negative,
            )
            for k in range(n_slots)
        ]
        softmaxes.append(weighted(jnp.concatenate(pieces, axis=0)))
    return [
        (
            top,
            total,
            jnp.dot(
                values_ref[d], weights.astype(jnp.bfloat16), preferred_element_type=jnp.float32
            ),
        )
        for d, (top, total, weights) in zip(requests, softmaxes)
    ]


def half_of(part, side):
    lanes = slice(side * VECS, (side + 1) * VECS)
    return [x[:, lanes] for x in part]


def away_kernel(keys_ref, values_ref, member_ref, *rest):
    queries, out_ref, after_ref = rest[:-3], rest[-2], rest[-1]
    after_ref[...] = jnp.zeros(after_ref.shape, jnp.float32)
    requests = tuple(reversed(range(1, keys_ref.shape[0])))
    z, parity = lax.axis_index("z"), lax.axis_index("pair")
    parts = suffix_parts(requests, queries, keys_ref, values_ref, member_ref)
    for d, part in zip(requests, parts):
        store_unit(out_ref.at[z ^ d, parity], *half_of(part, 0))
        store_unit(out_ref.at[z ^ d, 1 - parity], *half_of(part, 1))
    for side in range(2):
        store_unit(out_ref.at[z, side], *empty_part())


def home_kernel(
    half, length_ref, keys_ref, values_ref, member_ref, own_ref, pair_ref, prompt_ref, after_ref,
    summed_ref, stats_ref, out_ref,
):
    (suffix,) = suffix_parts((0,), (own_ref, pair_ref), keys_ref, values_ref, member_ref)
    prompt = prompt_part(length_ref[0], half, prompt_ref, all_vectors(own_ref, pair_ref))
    part = merged([prompt, suffix])
    top, total, summed_ref[...] = half_of(part, 0)
    stats_ref[...] = jnp.concatenate([top, total, jnp.zeros((6, VECS), jnp.float32)], axis=0)
    store_unit(out_ref, *half_of(part, 1))


def final_kernel(units_ref, last_ref, summed_ref, stats_ref, out_ref):
    n_req, n_pair = units_ref.shape[:2]
    parts = [load_unit(units_ref.at[r, p]) for r in range(n_req) for p in range(n_pair)]
    parts += [load_unit(last_ref), (stats_ref[0:1], stats_ref[1:2], summed_ref[...])]
    _, total, summed = merged(parts)
    attended = (summed / total).T
    for h in range(HEADS):
        out_ref[:, h * HD : (h + 1) * HD] = attended[h * BEAMS : (h + 1) * BEAMS]


def in_hbm(value):
    return pltpu.with_memory_space_constraint(value, pltpu.HBM)


def on_device(queries, prompt_cache, pool, block_table, parents, lengths):
    n_req = lax.axis_size("z")
    n_batch = 2 * n_req
    ndist = 2 ** (SUF + 1) - 2
    capacity = 2 * ((ndist // 2 + n_batch - 1) // n_batch)
    slots, _, half, width = pool.shape
    tokens = prompt_cache.shape[2]
    rows = block_table.shape[0]
    vmem = pl.BlockSpec(memory_space=pltpu.VMEM)
    params = pltpu.CompilerParams(vmem_limit_bytes=40 * 2**20)

    hbm = pl.BlockSpec(memory_space=pltpu.HBM)
    near = pool.reshape(slots, half, width)
    far = swapped(near, "core")
    sent = []
    for d in reversed(range(1, n_req)):
        sent += [swapped(queries, "z", d), swapped(queries, ("z", "pair"), 2 * d + 1)]
    other = swapped(queries, "pair")

    keys, values, member, prompt, own = pl.pallas_call(
        functools.partial(prepare_kernel, capacity),
        out_shape=(
            pltpu.VMEM((n_req, 2 * capacity * half, HD), jnp.bfloat16),
            pltpu.VMEM((n_req, HD, 2 * capacity * half), jnp.bfloat16),
            pltpu.VMEM((n_req, 2 * capacity, 2 * VECS), jnp.float32),
            pltpu.VMEM((tokens, width), jnp.bfloat16),
            pltpu.VMEM(queries.shape, jnp.bfloat16),
        ),
        in_specs=[hbm] * 5 + [vmem],
        out_specs=(vmem,) * 5,
        scratch_shapes=[
            pltpu.VMEM((2 * slots + 8, 2 * VECS), jnp.float32),
            pltpu.VMEM((SUF, rows), jnp.int32),
            pltpu.VMEM((1, rows), jnp.int32),
            pltpu.VMEM((slots, half, width), jnp.bfloat16),
            pltpu.SemaphoreType.DMA((5,)),
        ],
        compiler_params=params,
        name="prepare",
    )(
        in_hbm(block_table.T),
        in_hbm(parents.reshape(1, rows)),
        in_hbm(near),
        in_hbm(prompt_cache.reshape(tokens, width)),
        in_hbm(queries),
        far,
    )

    units, after = pl.pallas_call(
        away_kernel,
        out_shape=(
            pltpu.VMEM((n_req, 2, UNIT_ROWS, VECS), jnp.bfloat16),
            pltpu.VMEM((8, VECS), jnp.float32),
        ),
        in_specs=[vmem] * (4 + len(sent)),
        out_specs=(vmem,) * 2,
        compiler_params=params,
        name="suffix_away",
    )(keys, values, member, *sent, other)
    units = units.reshape(2 * n_req, UNIT_ROWS, VECS)
    units = lax.all_to_all(units, ("z", "pair"), split_axis=0, concat_axis=0, tiled=True)

    summed, stats, given = pl.pallas_call(
        functools.partial(home_kernel, half),
        out_shape=(
            pltpu.VMEM((HD, VECS), jnp.float32),
            pltpu.VMEM((8, VECS), jnp.float32),
            pltpu.VMEM((UNIT_ROWS, VECS), jnp.bfloat16),
        ),
        in_specs=[pl.BlockSpec(memory_space=pltpu.SMEM)] + [vmem] * 7,
        out_specs=(vmem,) * 3,
        compiler_params=params,
        cost_estimate=pl.CostEstimate(
            flops=8 * tokens * VECS * HD, bytes_accessed=2 * tokens * width, transcendentals=0
        ),
        name="home_part",
    )(lengths, keys, values, member, own, other, prompt, after)
    last = swapped(given, "pair")

    return pl.pallas_call(
        final_kernel,
        out_shape=jax.ShapeDtypeStruct((BEAMS, HEADS * HD), jnp.float32),
        in_specs=[vmem] * 4,
        out_specs=vmem,
        compiler_params=params,
        name="combine",
    )(units.reshape(n_req, 2, UNIT_ROWS, VECS), last, summed, stats)


def solution(mesh):
    n_batch, n_mp = mesh.devices.shape
    split = jax.sharding.Mesh(
        mesh.devices.reshape(n_batch // 2, 2, n_mp // 2, 2), ("z", "core", "group", "pair")
    )
    batch, mp = ("z", "core"), ("group", "pair")
    return jax.shard_map(
        on_device,
        mesh=split,
        in_specs=(
            P(batch, mp),
            P(batch, mp, None, None),
            P(batch, mp, None, None),
            P(),
            P(),
            P(batch),
        ),
        out_specs=P(batch, mp),
        check_vma=False,
    )
```

```python
import functools

import jax
import jax.numpy as jnp
from jax import lax
from jax.experimental import pallas as pl
from jax.experimental.pallas import tpu as pltpu
from jax.sharding import PartitionSpec as P

HD = 128
GROUP = 16
BEAMS = 16
SUF = 4
HEADS = GROUP // 2
VECS = HEADS * BEAMS
STAT_ROWS = 16
UNIT_ROWS = HD + STAT_ROWS
CHUNK = 512
PASSED_ON = (2,)

big_negative = -1e30
to_exp2 = HD ** (-0.5) * 1.4426950408889634


def swapped(value, axis, mask=1):
    size = lax.axis_size(axis)
    return lax.ppermute(value, axis, [(i, i ^ mask) for i in range(size)])


def routes(n_req):
    first = [(d, 0) for d in PASSED_ON if d < n_req]
    last = [(d, 1) for d, _ in first]
    direct = [(d, side) for d in range(n_req - 1, 0, -1) for side in (0, 1)]
    return first + [route for route in direct if route not in first + last] + last


def stacked_heads(q):
    return jnp.concatenate([q[:, h * HD : (h + 1) * HD] for h in range(HEADS)], axis=0)


def scores_of(keys, vectors):
    return lax.dot_general(
        keys, vectors, (((1,), (1,)), ((), ())), preferred_element_type=jnp.float32
    )


def summed_of(values, weights):
    return lax.dot_general(
        values,
        weights.astype(jnp.bfloat16),
        (((0,), (0,)), ((), ())),
        preferred_element_type=jnp.float32,
    )


def merged(parts):
    top = functools.reduce(jnp.maximum, [p[0] for p in parts])
    total = 0.0
    summed = 0.0
    for part_top, part_total, part_summed in parts:
        factor = jnp.exp2((part_top - top) * to_exp2)
        total = total + part_total * factor
        summed = summed + part_summed * factor
    return top, total, summed


def weighted(scores):
    top = jnp.max(scores, axis=0, keepdims=True)
    weights = jnp.exp2((scores - top) * to_exp2)
    return top, jnp.sum(weights, axis=0, keepdims=True), weights


def three_pieces(x):
    first = x.astype(jnp.bfloat16).astype(jnp.float32)
    rest = x - first
    second = rest.astype(jnp.bfloat16).astype(jnp.float32)
    return [first, second, rest - second]


def store_unit(ref, top, total, summed):
    ref[:HD, :] = summed.astype(jnp.bfloat16)
    rows = three_pieces(top) + three_pieces(total)
    rows.append(jnp.zeros((STAT_ROWS - len(rows), VECS), jnp.float32))
    ref[HD:, :] = jnp.concatenate(rows, axis=0).astype(jnp.bfloat16)


def empty_part():
    zeros = jnp.zeros((1, VECS), jnp.float32)
    return zeros + big_negative, zeros, jnp.zeros((HD, VECS), jnp.float32)


def load_unit(ref):
    stats = ref[HD:, :].astype(jnp.float32)
    top = stats[0:1] + stats[1:2] + stats[2:3]
    total = stats[3:4] + stats[4:5] + stats[5:6]
    return top, total, ref[:HD, :].astype(jnp.float32)


def count(left, right):
    return jnp.dot(
        left.astype(jnp.bfloat16), right.astype(jnp.bfloat16), preferred_element_type=jnp.float32
    )


def iota(shape, axis):
    return lax.broadcasted_iota(jnp.int32, shape, axis)


def prompt_part(length, half, prompt_ref, vectors):
    parity = lax.axis_index("pair")
    whole = lax.div(length, 2 * half)
    valid = whole * half + jnp.clip(length - whole * (2 * half) - parity * half, 0, half)
    parts = []
    for start in range(0, prompt_ref.shape[0], CHUNK):
        part = slice(start, start + CHUNK)
        scores = scores_of(prompt_ref[part, :HD], vectors)
        token = iota(scores.shape, 0)
        scores = jnp.where(token < valid - start, scores, big_negative)
        top, total, weights = weighted(scores)
        parts.append((top, total, summed_of(prompt_ref[part, HD:], weights)))
        if len(parts) == 2:
            parts = [merged(parts)]
    return merged(parts)


def prepare_kernel(
    capacity, table_ref, parents_ref, near_ref, prompt_ref, own_ref, far_ref,
    home_keys_ref, home_values_ref, keys_ref, values_ref, member_ref, held_ref, own, rows_ref, table, parents, near, sems,
):
    n_req = keys_ref.shape[0] + 1
    slots, half, _ = near.shape
    rows = table.shape[1]
    n_batch = rows // BEAMS
    z, core = lax.axis_index("z"), lax.axis_index("core")

    small = [
        pltpu.make_async_copy(source, target, sems.at[i])
        for i, (source, target) in enumerate(
            [
                (table_ref, table),
                (parents_ref, parents),
                (near_ref, near),
                (prompt_ref, held_ref),
                (own_ref, own),
            ]
        )
    ]
    for copy in small:
        copy.start()

    small[0].wait()
    slot = iota((2 * slots, rows), 0)
    mine = slot < slots
    block = jnp.where(mine, slot, slot - slots) + jnp.where(mine, 2 * z + core, 2 * z + 1 - core) * slots
    named = functools.reduce(
        jnp.logical_or, [table[j : j + 1, :] == block for j in range(SUF)]
    ).astype(jnp.float32)
    group = (iota((rows, n_batch), 0) // BEAMS == iota((rows, n_batch), 1)).astype(jnp.float32)
    hit = jnp.where(count(named, group) > 0.0, 1.0, 0.0)
    left, right = iota((2 * slots, 2 * slots), 0), iota((2 * slots, 2 * slots), 1)
    before = (left // slots == right // slots) & (right < left)
    rank = count(before.astype(jnp.float32), hit)
    small[1].wait()
    taken = (iota((rows, rows), 0) == parents[...]).astype(jnp.float32)
    continued = count(named, taken)

    place = iota((2 * slots, n_batch), 0)
    found = []
    for k in range(2 * capacity):
        holder = k // capacity
        chosen = (hit > 0.0) & (rank == float(k % capacity)) & (place // slots == holder)
        found.append(jnp.sum(jnp.where(chosen, place + 1, 0), axis=0, keepdims=True))
    found = jnp.concatenate(found, axis=0)

    small[2].wait()
    for d in range(n_req):
        request = (z ^ d) * 2 + core
        lane = iota((rows, 2 * VECS), 1)
        spread = iota((rows, 2 * VECS), 0) == request * BEAMS + lane % BEAMS
        rows_ref[: 2 * slots, :] = count(continued, spread.astype(jnp.float32))
        rows_ref[2 * slots :, :] = jnp.zeros((8, 2 * VECS), jnp.float32)
        mask = iota(found.shape, 1) == request
        picked = jnp.sum(jnp.where(mask, found, 0), axis=1, keepdims=True)
        values = []
        for k in range(2 * capacity):
            index = picked[k, 0]
            row = jnp.where(index > 0, index - 1, 2 * slots)
            member_ref[d, k : k + 1, :] = rows_ref[pl.ds(row, 1), :]
            pool_ref = near if k < capacity else far_ref
            base = 0 if k < capacity else slots
            content = pool_ref[jnp.maximum(index - 1 - base, 0)]
            tokens = slice(k * half, (k + 1) * half)
            if d == 0:
                home_keys_ref[0, tokens, :] = content[:, :HD]
            else:
                keys_ref[d - 1, tokens, :] = content[:, :HD]
            values.append(content[:, HD:])
        values = jnp.concatenate(values, axis=0).T
        if d == 0:
            home_values_ref[0] = values
        else:
            values_ref[d - 1] = values
    small[3].wait()
    small[4].wait()


def all_vectors(own_ref, pair_ref):
    return jnp.concatenate([stacked_heads(own_ref[...]), stacked_heads(pair_ref[...])], axis=0)


def suffix_parts(vectors, keys_ref, values_ref, members):
    n_slots = members[0].shape[0]
    half = keys_ref.shape[1] // n_slots
    scores = [scores_of(keys_ref[i], each) for i, each in enumerate(vectors)]
    softmaxes = []
    for member, score in zip(members, scores):
        pieces = [
            jnp.where(
                member[k : k + 1, :] > 0.0, score[k * half : (k + 1) * half], big_negative
            )
            for k in range(n_slots)
        ]
        softmaxes.append(weighted(jnp.concatenate(pieces, axis=0)))
    return [
        (
            top,
            total,
            jnp.dot(
                values_ref[i], weights.astype(jnp.bfloat16), preferred_element_type=jnp.float32
            ),
        )
        for i, (top, total, weights) in enumerate(softmaxes)
    ]


def half_of(part, side):
    lanes = slice(side * VECS, (side + 1) * VECS)
    return [x[:, lanes] for x in part]


def away_kernel(keys_ref, values_ref, member_ref, *rest):
    queries, out_ref, after_ref = rest[:-2], rest[-2], rest[-1]
    after_ref[...] = jnp.zeros(after_ref.shape, jnp.float32)
    requests = range(1, keys_ref.shape[0] + 1)
    z, parity = lax.axis_index("z"), lax.axis_index("pair")
    order = routes(len(requests) + 1)
    vectors = [
        all_vectors(queries[order.index((d, 0))], queries[order.index((d, 1))]) for d in requests
    ]
    parts = suffix_parts(vectors, keys_ref, values_ref, [member_ref[d] for d in requests])
    for d, part in zip(requests, parts):
        store_unit(out_ref.at[z ^ d, parity], *half_of(part, 0))
        store_unit(out_ref.at[z ^ d, 1 - parity], *half_of(part, 1))
    for side in range(2):
        store_unit(out_ref.at[z, side], *empty_part())


def home_kernel(
    half, length_ref, keys_ref, values_ref, member_ref, own_ref, pair_ref, prompt_ref, after_ref,
    summed_ref, stats_ref, out_ref,
):
    vectors = all_vectors(own_ref, pair_ref)
    (suffix,) = suffix_parts([vectors], keys_ref, values_ref, [member_ref[0]])
    prompt = prompt_part(length_ref[0], half, prompt_ref, vectors)
    part = merged([prompt, suffix])
    top, total, summed_ref[...] = half_of(part, 0)
    stats_ref[...] = jnp.concatenate([top, total, jnp.zeros((6, VECS), jnp.float32)], axis=0)
    store_unit(out_ref, *half_of(part, 1))


def final_kernel(units_ref, last_ref, summed_ref, stats_ref, out_ref):
    n_req, n_pair = units_ref.shape[:2]
    parts = [load_unit(units_ref.at[r, p]) for r in range(n_req) for p in range(n_pair)]
    parts += [load_unit(last_ref), (stats_ref[0:1], stats_ref[1:2], summed_ref[...])]
    _, total, summed = merged(parts)
    attended = (summed / total).T
    for h in range(HEADS):
        out_ref[:, h * HD : (h + 1) * HD] = attended[h * BEAMS : (h + 1) * BEAMS]


def in_hbm(value):
    return pltpu.with_memory_space_constraint(value, pltpu.HBM)


def on_device(queries, prompt_cache, pool, block_table, parents, lengths):
    n_req = lax.axis_size("z")
    n_batch = 2 * n_req
    ndist = 2 ** (SUF + 1) - 2
    capacity = 2 * ((ndist // 2 + n_batch - 1) // n_batch)
    slots, _, half, width = pool.shape
    tokens = prompt_cache.shape[2]
    rows = block_table.shape[0]
    vmem = pl.BlockSpec(memory_space=pltpu.VMEM)
    params = pltpu.CompilerParams(vmem_limit_bytes=40 * 2**20)

    hbm = pl.BlockSpec(memory_space=pltpu.HBM)
    near = pool.reshape(slots, half, width)
    far = swapped(near, "core")
    sent = {}
    for d, side in routes(n_req):
        if side == 0:
            sent[d, 0] = swapped(queries, "z", d)
        elif d in PASSED_ON:
            sent[d, 1] = swapped(sent[d, 0], "pair")
        else:
            sent[d, 1] = swapped(queries, ("z", "pair"), 2 * d + 1)
    other = swapped(queries, "pair")

    home_keys, home_values, keys, values, member, prompt, own = pl.pallas_call(
        functools.partial(prepare_kernel, capacity),
        out_shape=(
            pltpu.VMEM((1, 2 * capacity * half, HD), jnp.bfloat16),
            pltpu.VMEM((1, HD, 2 * capacity * half), jnp.bfloat16),
            pltpu.VMEM((n_req - 1, 2 * capacity * half, HD), jnp.bfloat16),
            pltpu.VMEM((n_req - 1, HD, 2 * capacity * half), jnp.bfloat16),
            pltpu.VMEM((n_req, 2 * capacity, 2 * VECS), jnp.float32),
            pltpu.VMEM((tokens, width), jnp.bfloat16),
            pltpu.VMEM(queries.shape, jnp.bfloat16),
        ),
        in_specs=[hbm] * 5 + [vmem],
        out_specs=(vmem,) * 7,
        scratch_shapes=[
            pltpu.VMEM((2 * slots + 8, 2 * VECS), jnp.float32),
            pltpu.VMEM((SUF, rows), jnp.int32),
            pltpu.VMEM((1, rows), jnp.int32),
            pltpu.VMEM((slots, half, width), jnp.bfloat16),
            pltpu.SemaphoreType.DMA((5,)),
        ],
        compiler_params=params,
        name="prepare",
    )(
        in_hbm(block_table.T),
        in_hbm(parents.reshape(1, rows)),
        in_hbm(near),
        in_hbm(prompt_cache.reshape(tokens, width)),
        in_hbm(queries),
        far,
    )

    units, after = pl.pallas_call(
        away_kernel,
        out_shape=(
            pltpu.VMEM((n_req, 2, UNIT_ROWS, VECS), jnp.bfloat16),
            pltpu.VMEM((8, VECS), jnp.float32),
        ),
        in_specs=[vmem] * (3 + len(sent)),
        out_specs=(vmem,) * 2,
        compiler_params=params,
        name="suffix_away",
    )(keys, values, member, *sent.values())
    units = units.reshape(2 * n_req, UNIT_ROWS, VECS)
    units = lax.all_to_all(units, ("z", "pair"), split_axis=0, concat_axis=0, tiled=True)

    summed, stats, given = pl.pallas_call(
        functools.partial(home_kernel, half),
        out_shape=(
            pltpu.VMEM((HD, VECS), jnp.float32),
            pltpu.VMEM((8, VECS), jnp.float32),
            pltpu.VMEM((UNIT_ROWS, VECS), jnp.bfloat16),
        ),
        in_specs=[pl.BlockSpec(memory_space=pltpu.SMEM)] + [vmem] * 7,
        out_specs=(vmem,) * 3,
        compiler_params=params,
        cost_estimate=pl.CostEstimate(
            flops=8 * tokens * VECS * HD, bytes_accessed=2 * tokens * width, transcendentals=0
        ),
        name="home_part",
    )(lengths, home_keys, home_values, member, own, other, prompt, after)
    last = swapped(given, "pair")

    return pl.pallas_call(
        final_kernel,
        out_shape=jax.ShapeDtypeStruct((BEAMS, HEADS * HD), jnp.float32),
        in_specs=[vmem] * 4,
        out_specs=vmem,
        compiler_params=params,
        name="combine",
    )(units.reshape(n_req, 2, UNIT_ROWS, VECS), last, summed, stats)


def solution(mesh):
    n_batch, n_mp = mesh.devices.shape
    split = jax.sharding.Mesh(
        mesh.devices.reshape(n_batch // 2, 2, n_mp // 2, 2), ("z", "core", "group", "pair")
    )
    batch, mp = ("z", "core"), ("group", "pair")
    return jax.shard_map(
        on_device,
        mesh=split,
        in_specs=(
            P(batch, mp),
            P(batch, mp, None, None),
            P(batch, mp, None, None),
            P(),
            P(),
            P(batch),
        ),
        out_specs=P(batch, mp),
        check_vma=False,
    )
```

```python
import functools

import jax
import jax.numpy as jnp
from jax import lax
from jax.experimental import pallas as pl
from jax.experimental.pallas import tpu as pltpu
from jax.sharding import PartitionSpec as P

HD = 128
GROUP = 16
BEAMS = 16
SUF = 4
HEADS = GROUP // 2
VECS = HEADS * BEAMS
STAT_ROWS = 16
UNIT_ROWS = HD + STAT_ROWS
CHUNK = 512

big_negative = -1e30
to_exp2 = HD ** (-0.5) * 1.4426950408889634


def swapped(value, axis, mask=1):
    size = lax.axis_size(axis)
    return lax.ppermute(value, axis, [(i, i ^ mask) for i in range(size)])


def request_order(n_req):
    masks = list(range(n_req - 1, 0, -1))
    return [2, 3, 1] if masks == [3, 2, 1] else masks


def stacked_heads(q):
    return jnp.concatenate([q[:, h * HD : (h + 1) * HD] for h in range(HEADS)], axis=0)


def scores_of(keys, vectors):
    return lax.dot_general(
        keys, vectors, (((1,), (1,)), ((), ())), preferred_element_type=jnp.float32
    )


def summed_of(values, weights):
    return lax.dot_general(
        values,
        weights.astype(jnp.bfloat16),
        (((0,), (0,)), ((), ())),
        preferred_element_type=jnp.float32,
    )


def merged(parts):
    top = functools.reduce(jnp.maximum, [p[0] for p in parts])
    total = 0.0
    summed = 0.0
    for part_top, part_total, part_summed in parts:
        factor = jnp.exp2((part_top - top) * to_exp2)
        total = total + part_total * factor
        summed = summed + part_summed * factor
    return top, total, summed


def weighted(scores):
    top = jnp.max(scores, axis=0, keepdims=True)
    weights = jnp.exp2((scores - top) * to_exp2)
    return top, jnp.sum(weights, axis=0, keepdims=True), weights


def three_pieces(x):
    first = x.astype(jnp.bfloat16).astype(jnp.float32)
    rest = x - first
    second = rest.astype(jnp.bfloat16).astype(jnp.float32)
    return [first, second, rest - second]


def store_unit(ref, top, total, summed):
    ref[:HD, :] = summed.astype(jnp.bfloat16)
    rows = three_pieces(top) + three_pieces(total)
    rows.append(jnp.zeros((STAT_ROWS - len(rows), VECS), jnp.float32))
    ref[HD:, :] = jnp.concatenate(rows, axis=0).astype(jnp.bfloat16)


def load_unit(ref):
    stats = ref[HD:, :].astype(jnp.float32)
    top = stats[0:1] + stats[1:2] + stats[2:3]
    total = stats[3:4] + stats[4:5] + stats[5:6]
    return top, total, ref[:HD, :].astype(jnp.float32)


def count(left, right):
    return jnp.dot(
        left.astype(jnp.bfloat16), right.astype(jnp.bfloat16), preferred_element_type=jnp.float32
    )


def iota(shape, axis):
    return lax.broadcasted_iota(jnp.int32, shape, axis)


def prompt_part(length, half, prompt_ref, vectors):
    parity = lax.axis_index("pair")
    whole = lax.div(length, 2 * half)
    valid = whole * half + jnp.clip(length - whole * (2 * half) - parity * half, 0, half)
    parts = []
    for start in range(0, prompt_ref.shape[0], CHUNK):
        part = slice(start, start + CHUNK)
        scores = scores_of(prompt_ref[part, :HD], vectors)
        token = iota(scores.shape, 0)
        scores = jnp.where(token < valid - start, scores, big_negative)
        top, total, weights = weighted(scores)
        parts.append((top, total, summed_of(prompt_ref[part, HD:], weights)))
        if len(parts) == 2:
            parts = [merged(parts)]
    return merged(parts)


def prepare_kernel(
    capacity, table_ref, parents_ref, near_ref, prompt_ref, own_ref, far_ref,
    home_keys_ref, home_values_ref, keys_ref, values_ref, member_ref, held_ref, own, rows_ref, table, parents, near, sems,
):
    n_req = keys_ref.shape[0] + 1
    slots, half, _ = near.shape
    rows = table.shape[1]
    n_batch = rows // BEAMS
    z, core = lax.axis_index("z"), lax.axis_index("core")

    small = [
        pltpu.make_async_copy(source, target, sems.at[i])
        for i, (source, target) in enumerate(
            [
                (table_ref, table),
                (parents_ref, parents),
                (near_ref, near),
                (prompt_ref, held_ref),
                (own_ref, own),
            ]
        )
    ]
    for copy in small:
        copy.start()

    small[0].wait()
    slot = iota((2 * slots, rows), 0)
    mine = slot < slots
    block = jnp.where(mine, slot, slot - slots) + jnp.where(mine, 2 * z + core, 2 * z + 1 - core) * slots
    named = functools.reduce(
        jnp.logical_or, [table[j : j + 1, :] == block for j in range(SUF)]
    ).astype(jnp.float32)
    group = (iota((rows, n_batch), 0) // BEAMS == iota((rows, n_batch), 1)).astype(jnp.float32)
    hit = jnp.where(count(named, group) > 0.0, 1.0, 0.0)
    left, right = iota((2 * slots, 2 * slots), 0), iota((2 * slots, 2 * slots), 1)
    before = (left // slots == right // slots) & (right < left)
    rank = count(before.astype(jnp.float32), hit)
    small[1].wait()
    taken = (iota((rows, rows), 0) == parents[...]).astype(jnp.float32)
    continued = count(named, taken)

    place = iota((2 * slots, n_batch), 0)
    found = []
    for k in range(2 * capacity):
        holder = k // capacity
        chosen = (hit > 0.0) & (rank == float(k % capacity)) & (place // slots == holder)
        found.append(jnp.sum(jnp.where(chosen, place + 1, 0), axis=0, keepdims=True))
    found = jnp.concatenate(found, axis=0)

    small[2].wait()
    for d in range(n_req):
        request = (z ^ d) * 2 + core
        lane = iota((rows, 2 * VECS), 1)
        spread = iota((rows, 2 * VECS), 0) == request * BEAMS + lane % BEAMS
        rows_ref[: 2 * slots, :] = count(continued, spread.astype(jnp.float32))
        rows_ref[2 * slots :, :] = jnp.zeros((8, 2 * VECS), jnp.float32)
        mask = iota(found.shape, 1) == request
        picked = jnp.sum(jnp.where(mask, found, 0), axis=1, keepdims=True)
        values = []
        for k in range(2 * capacity):
            index = picked[k, 0]
            row = jnp.where(index > 0, index - 1, 2 * slots)
            member_ref[d, k : k + 1, :] = rows_ref[pl.ds(row, 1), :]
            pool_ref = near if k < capacity else far_ref
            base = 0 if k < capacity else slots
            content = pool_ref[jnp.maximum(index - 1 - base, 0)]
            tokens = slice(k * half, (k + 1) * half)
            if d == 0:
                home_keys_ref[0, tokens, :] = content[:, :HD]
            else:
                keys_ref[d - 1, tokens, :] = content[:, :HD]
            values.append(content[:, HD:])
        values = jnp.concatenate(values, axis=0).T
        if d == 0:
            home_values_ref[0] = values
        else:
            values_ref[d - 1] = values
    small[3].wait()
    small[4].wait()


def all_vectors(own_ref, pair_ref):
    return jnp.concatenate([stacked_heads(own_ref[...]), stacked_heads(pair_ref[...])], axis=0)


def suffix_parts(vectors, keys_ref, values_ref, members, places):
    n_slots = members[0].shape[0]
    half = keys_ref.shape[1] // n_slots
    scores = [scores_of(keys_ref[i], each) for i, each in zip(places, vectors)]
    softmaxes = []
    for member, score in zip(members, scores):
        pieces = [
            jnp.where(
                member[k : k + 1, :] > 0.0, score[k * half : (k + 1) * half], big_negative
            )
            for k in range(n_slots)
        ]
        softmaxes.append(weighted(jnp.concatenate(pieces, axis=0)))
    return [
        (
            top,
            total,
            jnp.dot(
                values_ref[i], weights.astype(jnp.bfloat16), preferred_element_type=jnp.float32
            ),
        )
        for i, (top, total, weights) in zip(places, softmaxes)
    ]


def half_of(part, side):
    lanes = slice(side * VECS, (side + 1) * VECS)
    return [x[:, lanes] for x in part]


def away_kernel(keys_ref, values_ref, member_ref, *rest):
    queries, (_, out_ref, after_ref, units, sems) = rest[:-5], rest[-5:]
    after_ref[...] = jnp.zeros(after_ref.shape, jnp.float32)
    requests = request_order(keys_ref.shape[0] + 1)
    z, parity = lax.axis_index("z"), lax.axis_index("pair")
    vectors = [all_vectors(*queries[2 * i : 2 * i + 2]) for i in range(len(requests))]
    members = [member_ref[d] for d in requests]
    copies = []
    parts = suffix_parts(vectors, keys_ref, values_ref, members, [d - 1 for d in requests])
    for i, (d, part) in enumerate(zip(requests, parts)):
        for side in range(2):
            store_unit(units.at[i, side], *half_of(part, side))
            owner = parity if side == 0 else 1 - parity
            copy = pltpu.make_async_copy(
                units.at[i, side], out_ref.at[z ^ d, owner], sems.at[i, side]
            )
            copy.start()
            copies.append(copy)
    for copy in copies:
        copy.wait()


def home_kernel(
    half, length_ref, keys_ref, values_ref, member_ref, own_ref, pair_ref, prompt_ref, after_ref,
    summed_ref, stats_ref, out_ref,
):
    vectors = all_vectors(own_ref, pair_ref)
    (suffix,) = suffix_parts([vectors], keys_ref, values_ref, [member_ref[0]], [0])
    prompt = prompt_part(length_ref[0], half, prompt_ref, vectors)
    part = merged([prompt, suffix])
    top, total, summed_ref[...] = half_of(part, 0)
    stats_ref[...] = jnp.concatenate([top, total, jnp.zeros((6, VECS), jnp.float32)], axis=0)
    store_unit(out_ref, *half_of(part, 1))


def final_kernel(units_ref, last_ref, summed_ref, stats_ref, out_ref):
    n_req, n_pair = units_ref.shape[:2]
    z = lax.axis_index("z")
    parts = [load_unit(units_ref.at[z ^ d, p]) for d in range(1, n_req) for p in range(n_pair)]
    parts += [load_unit(last_ref), (stats_ref[0:1], stats_ref[1:2], summed_ref[...])]
    _, total, summed = merged(parts)
    attended = (summed / total).T
    for h in range(HEADS):
        out_ref[:, h * HD : (h + 1) * HD] = attended[h * BEAMS : (h + 1) * BEAMS]


def in_hbm(value):
    return pltpu.with_memory_space_constraint(value, pltpu.HBM)


def on_device(queries, prompt_cache, pool, block_table, parents, lengths):
    n_req = lax.axis_size("z")
    n_batch = 2 * n_req
    ndist = 2 ** (SUF + 1) - 2
    capacity = 2 * ((ndist // 2 + n_batch - 1) // n_batch)
    slots, _, half, width = pool.shape
    tokens = prompt_cache.shape[2]
    rows = block_table.shape[0]
    vmem = pl.BlockSpec(memory_space=pltpu.VMEM)
    params = pltpu.CompilerParams(vmem_limit_bytes=40 * 2**20)

    hbm = pl.BlockSpec(memory_space=pltpu.HBM)
    near = pool.reshape(slots, half, width)
    far = swapped(near, "core")
    sent = []
    for d in request_order(n_req):
        piece = swapped(queries, "z", d)
        sent += [piece, swapped(piece, "pair")]
    other = swapped(queries, "pair")

    home_keys, home_values, keys, values, member, prompt, own = pl.pallas_call(
        functools.partial(prepare_kernel, capacity),
        out_shape=(
            pltpu.VMEM((1, 2 * capacity * half, HD), jnp.bfloat16),
            pltpu.VMEM((1, HD, 2 * capacity * half), jnp.bfloat16),
            pltpu.VMEM((n_req - 1, 2 * capacity * half, HD), jnp.bfloat16),
            pltpu.VMEM((n_req - 1, HD, 2 * capacity * half), jnp.bfloat16),
            pltpu.VMEM((n_req, 2 * capacity, 2 * VECS), jnp.float32),
            pltpu.VMEM((tokens, width), jnp.bfloat16),
            pltpu.VMEM(queries.shape, jnp.bfloat16),
        ),
        in_specs=[hbm] * 5 + [vmem],
        out_specs=(vmem,) * 7,
        scratch_shapes=[
            pltpu.VMEM((2 * slots + 8, 2 * VECS), jnp.float32),
            pltpu.VMEM((SUF, rows), jnp.int32),
            pltpu.VMEM((1, rows), jnp.int32),
            pltpu.VMEM((slots, half, width), jnp.bfloat16),
            pltpu.SemaphoreType.DMA((5,)),
        ],
        compiler_params=params,
        name="prepare",
    )(
        in_hbm(block_table.T),
        in_hbm(parents.reshape(1, rows)),
        in_hbm(near),
        in_hbm(prompt_cache.reshape(tokens, width)),
        in_hbm(queries),
        far,
    )

    units, after = pl.pallas_call(
        away_kernel,
        out_shape=(
            pltpu.HBM((n_req, 2, UNIT_ROWS, VECS), jnp.bfloat16),
            pltpu.VMEM((8, VECS), jnp.float32),
        ),
        in_specs=[vmem] * (4 + len(sent)),
        out_specs=(hbm, vmem),
        scratch_shapes=[
            pltpu.VMEM((n_req - 1, 2, UNIT_ROWS, VECS), jnp.bfloat16),
            pltpu.SemaphoreType.DMA((n_req - 1, 2)),
        ],
        compiler_params=params,
        name="suffix_away",
    )(keys, values, member, *sent, other)
    units = units.reshape(2 * n_req, UNIT_ROWS, VECS)
    units = lax.all_to_all(units, ("z", "pair"), split_axis=0, concat_axis=0, tiled=True)

    summed, stats, given = pl.pallas_call(
        functools.partial(home_kernel, half),
        out_shape=(
            pltpu.VMEM((HD, VECS), jnp.float32),
            pltpu.VMEM((8, VECS), jnp.float32),
            pltpu.VMEM((UNIT_ROWS, VECS), jnp.bfloat16),
        ),
        in_specs=[pl.BlockSpec(memory_space=pltpu.SMEM)] + [vmem] * 7,
        out_specs=(vmem,) * 3,
        compiler_params=params,
        cost_estimate=pl.CostEstimate(
            flops=8 * tokens * VECS * HD, bytes_accessed=2 * tokens * width, transcendentals=0
        ),
        name="home_part",
    )(lengths, home_keys, home_values, member, own, other, prompt, after)
    last = swapped(given, "pair")

    return pl.pallas_call(
        final_kernel,
        out_shape=jax.ShapeDtypeStruct((BEAMS, HEADS * HD), jnp.float32),
        in_specs=[vmem] * 4,
        out_specs=vmem,
        compiler_params=params,
        name="combine",
    )(units.reshape(n_req, 2, UNIT_ROWS, VECS), last, summed, stats)


def solution(mesh):
    n_batch, n_mp = mesh.devices.shape
    split = jax.sharding.Mesh(
        mesh.devices.reshape(n_batch // 2, 2, n_mp // 2, 2), ("z", "core", "group", "pair")
    )
    batch, mp = ("z", "core"), ("group", "pair")
    return jax.shard_map(
        on_device,
        mesh=split,
        in_specs=(
            P(batch, mp),
            P(batch, mp, None, None),
            P(batch, mp, None, None),
            P(),
            P(),
            P(batch),
        ),
        out_specs=P(batch, mp),
        check_vma=False,
    )
```

```python
import functools

import jax
import jax.numpy as jnp
from jax import lax
from jax.experimental import pallas as pl
from jax.experimental.pallas import tpu as pltpu
from jax.sharding import PartitionSpec as P

HD = 128
GROUP = 16
BEAMS = 16
SUF = 4
HEADS = GROUP // 2
VECS = HEADS * BEAMS
STAT_ROWS = 16
UNIT_ROWS = HD + STAT_ROWS
CHUNK = 512

big_negative = -1e30
to_exp2 = HD ** (-0.5) * 1.4426950408889634


def swapped(value, axis, mask=1):
    size = lax.axis_size(axis)
    return lax.ppermute(value, axis, [(i, i ^ mask) for i in range(size)])


def request_order(n_req):
    masks = list(range(n_req - 1, 0, -1))
    return [2, 3, 1] if masks == [3, 2, 1] else masks


def stacked_heads(q):
    return jnp.concatenate([q[:, h * HD : (h + 1) * HD] for h in range(HEADS)], axis=0)


def scores_of(keys, vectors):
    return lax.dot_general(
        keys, vectors, (((1,), (1,)), ((), ())), preferred_element_type=jnp.float32
    )


def summed_of(values, weights):
    return lax.dot_general(
        values,
        weights.astype(jnp.bfloat16),
        (((0,), (0,)), ((), ())),
        preferred_element_type=jnp.float32,
    )


def merged(parts):
    top = functools.reduce(jnp.maximum, [p[0] for p in parts])
    total = 0.0
    summed = 0.0
    for part_top, part_total, part_summed in parts:
        factor = jnp.exp2((part_top - top) * to_exp2)
        total = total + part_total * factor
        summed = summed + part_summed * factor
    return top, total, summed


def weighted(scores):
    top = jnp.max(scores, axis=0, keepdims=True)
    weights = jnp.exp2((scores - top) * to_exp2)
    return top, jnp.sum(weights, axis=0, keepdims=True), weights


def three_pieces(x):
    first = x.astype(jnp.bfloat16).astype(jnp.float32)
    rest = x - first
    second = rest.astype(jnp.bfloat16).astype(jnp.float32)
    return [first, second, rest - second]


def store_unit(ref, top, total, summed):
    ref[:HD, :] = summed.astype(jnp.bfloat16)
    rows = three_pieces(top) + three_pieces(total)
    rows.append(jnp.zeros((STAT_ROWS - len(rows), VECS), jnp.float32))
    ref[HD:, :] = jnp.concatenate(rows, axis=0).astype(jnp.bfloat16)


def load_unit(ref):
    stats = ref[HD:, :].astype(jnp.float32)
    top = stats[0:1] + stats[1:2] + stats[2:3]
    total = stats[3:4] + stats[4:5] + stats[5:6]
    return top, total, ref[:HD, :].astype(jnp.float32)


def count(left, right):
    return jnp.dot(
        left.astype(jnp.bfloat16), right.astype(jnp.bfloat16), preferred_element_type=jnp.float32
    )


def iota(shape, axis):
    return lax.broadcasted_iota(jnp.int32, shape, axis)


def prompt_part(valid, prompt_ref, vectors):
    chunks = [slice(i, i + CHUNK) for i in range(0, prompt_ref.shape[0], CHUNK)]
    scores = [scores_of(prompt_ref[chunk, :HD], vectors) for chunk in chunks]
    place = iota(scores[0].shape, 0)
    scores = [
        jnp.where(place < valid - chunk.start, score, big_negative)
        for chunk, score in zip(chunks, scores)
    ]
    tops = [jnp.max(score, axis=0, keepdims=True) for score in scores]
    top = functools.reduce(jnp.maximum, tops)
    total, summed = 0.0, 0.0
    for chunk, score in zip(chunks, scores):
        weights = jnp.exp2((score - top) * to_exp2)
        total = total + jnp.sum(weights, axis=0, keepdims=True)
        summed = summed + summed_of(prompt_ref[chunk, HD:], weights)
    return top, total, summed


def prepare_kernel(
    capacity, length_ref, table_ref, parents_ref, near_ref, prompt_ref, own_ref, far_ref,
    home_keys_ref, home_values_ref, keys_ref, values_ref, member_ref, held_ref, own, valid_ref,
    rows_ref, table, parents, near, sems,
):
    n_req = keys_ref.shape[0] + 1
    slots, half, _ = near.shape
    rows = table.shape[1]
    n_batch = rows // BEAMS
    z, core = lax.axis_index("z"), lax.axis_index("core")

    small = [
        pltpu.make_async_copy(source, target, sems.at[i])
        for i, (source, target) in enumerate(
            [
                (table_ref, table),
                (parents_ref, parents),
                (near_ref, near),
                (prompt_ref, held_ref),
                (own_ref, own),
            ]
        )
    ]
    for copy in small:
        copy.start()

    length = length_ref[0]
    whole = lax.div(length, 2 * half)
    parity = lax.axis_index("pair")
    valid = whole * half + jnp.clip(length - whole * (2 * half) - parity * half, 0, half)
    valid_ref[...] = jnp.full(valid_ref.shape, valid, jnp.int32)

    small[0].wait()
    slot = iota((2 * slots, rows), 0)
    mine = slot < slots
    block = jnp.where(mine, slot, slot - slots) + jnp.where(mine, 2 * z + core, 2 * z + 1 - core) * slots
    named = functools.reduce(
        jnp.logical_or, [table[j : j + 1, :] == block for j in range(SUF)]
    ).astype(jnp.float32)
    group = (iota((rows, n_batch), 0) // BEAMS == iota((rows, n_batch), 1)).astype(jnp.float32)
    hit = jnp.where(count(named, group) > 0.0, 1.0, 0.0)
    left, right = iota((2 * slots, 2 * slots), 0), iota((2 * slots, 2 * slots), 1)
    before = (left // slots == right // slots) & (right < left)
    rank = count(before.astype(jnp.float32), hit)
    small[1].wait()
    taken = (iota((rows, rows), 0) == parents[...]).astype(jnp.float32)
    continued = count(named, taken)

    place = iota((2 * slots, n_batch), 0)
    found = []
    for k in range(2 * capacity):
        holder = k // capacity
        chosen = (hit > 0.0) & (rank == float(k % capacity)) & (place // slots == holder)
        found.append(jnp.sum(jnp.where(chosen, place + 1, 0), axis=0, keepdims=True))
    found = jnp.concatenate(found, axis=0)

    small[2].wait()
    for d in range(n_req):
        request = (z ^ d) * 2 + core
        lane = iota((rows, 2 * VECS), 1)
        spread = iota((rows, 2 * VECS), 0) == request * BEAMS + lane % BEAMS
        rows_ref[: 2 * slots, :] = count(continued, spread.astype(jnp.float32))
        rows_ref[2 * slots :, :] = jnp.zeros((8, 2 * VECS), jnp.float32)
        mask = iota(found.shape, 1) == request
        picked = jnp.sum(jnp.where(mask, found, 0), axis=1, keepdims=True)
        values = []
        for k in range(2 * capacity):
            index = picked[k, 0]
            row = jnp.where(index > 0, index - 1, 2 * slots)
            member_ref[d, k : k + 1, :] = rows_ref[pl.ds(row, 1), :]
            pool_ref = near if k < capacity else far_ref
            base = 0 if k < capacity else slots
            content = pool_ref[jnp.maximum(index - 1 - base, 0)]
            tokens = slice(k * half, (k + 1) * half)
            if d == 0:
                home_keys_ref[0, tokens, :] = content[:, :HD]
            else:
                keys_ref[d - 1, tokens, :] = content[:, :HD]
            values.append(content[:, HD:])
        values = jnp.concatenate(values, axis=0).T
        if d == 0:
            home_values_ref[0] = values
        else:
            values_ref[d - 1] = values
    small[3].wait()
    small[4].wait()


def all_vectors(own_ref, pair_ref):
    return jnp.concatenate([stacked_heads(own_ref[...]), stacked_heads(pair_ref[...])], axis=0)


def suffix_parts(vectors, keys_ref, values_ref, members, places):
    n_slots = members[0].shape[0]
    half = keys_ref.shape[1] // n_slots
    scores = [scores_of(keys_ref[i], each) for i, each in zip(places, vectors)]
    softmaxes = []
    for member, score in zip(members, scores):
        pieces = [
            jnp.where(
                member[k : k + 1, :] > 0.0, score[k * half : (k + 1) * half], big_negative
            )
            for k in range(n_slots)
        ]
        softmaxes.append(weighted(jnp.concatenate(pieces, axis=0)))
    return [
        (
            top,
            total,
            jnp.dot(
                values_ref[i], weights.astype(jnp.bfloat16), preferred_element_type=jnp.float32
            ),
        )
        for i, (top, total, weights) in zip(places, softmaxes)
    ]


def half_of(part, side):
    lanes = slice(side * VECS, (side + 1) * VECS)
    return [x[:, lanes] for x in part]


def away_kernel(keys_ref, values_ref, member_ref, *rest):
    queries, (_, out_ref, after_ref, units, sems) = rest[:-5], rest[-5:]
    after_ref[...] = jnp.zeros(after_ref.shape, jnp.float32)
    requests = request_order(keys_ref.shape[0] + 1)
    z, parity = lax.axis_index("z"), lax.axis_index("pair")
    vectors = [all_vectors(*queries[2 * i : 2 * i + 2]) for i in range(len(requests))]
    members = [member_ref[d] for d in requests]
    copies = []
    parts = suffix_parts(vectors, keys_ref, values_ref, members, [d - 1 for d in requests])
    for i, (d, part) in enumerate(zip(requests, parts)):
        for side in range(2):
            store_unit(units.at[i, side], *half_of(part, side))
            owner = parity if side == 0 else 1 - parity
            copy = pltpu.make_async_copy(
                units.at[i, side], out_ref.at[z ^ d, owner], sems.at[i, side]
            )
            copy.start()
            copies.append(copy)
    for copy in copies:
        copy.wait()


def home_kernel(
    valid_ref, keys_ref, values_ref, member_ref, own_ref, pair_ref, prompt_ref, after_ref,
    summed_ref, stats_ref, out_ref,
):
    vectors = all_vectors(own_ref, pair_ref)
    (suffix,) = suffix_parts([vectors], keys_ref, values_ref, [member_ref[0]], [0])
    prompt = prompt_part(valid_ref[0:1, :], prompt_ref, vectors)
    part = merged([prompt, suffix])
    top, total, summed_ref[...] = half_of(part, 0)
    stats_ref[...] = jnp.concatenate([top, total, jnp.zeros((6, VECS), jnp.float32)], axis=0)
    store_unit(out_ref, *half_of(part, 1))


def final_kernel(units_ref, last_ref, summed_ref, stats_ref, out_ref):
    n_req, n_pair = units_ref.shape[:2]
    z = lax.axis_index("z")
    parts = [load_unit(units_ref.at[z ^ d, p]) for d in range(1, n_req) for p in range(n_pair)]
    parts += [load_unit(last_ref), (stats_ref[0:1], stats_ref[1:2], summed_ref[...])]
    _, total, summed = merged(parts)
    attended = (summed / total).T
    for h in range(HEADS):
        out_ref[:, h * HD : (h + 1) * HD] = attended[h * BEAMS : (h + 1) * BEAMS]


def in_hbm(value):
    return pltpu.with_memory_space_constraint(value, pltpu.HBM)


def on_device(queries, prompt_cache, pool, block_table, parents, lengths):
    n_req = lax.axis_size("z")
    n_batch = 2 * n_req
    ndist = 2 ** (SUF + 1) - 2
    capacity = 2 * ((ndist // 2 + n_batch - 1) // n_batch)
    slots, _, half, width = pool.shape
    tokens = prompt_cache.shape[2]
    rows = block_table.shape[0]
    vmem = pl.BlockSpec(memory_space=pltpu.VMEM)
    params = pltpu.CompilerParams(vmem_limit_bytes=40 * 2**20)

    hbm = pl.BlockSpec(memory_space=pltpu.HBM)
    near = pool.reshape(slots, half, width)
    far = swapped(near, "core")
    sent = []
    for d in request_order(n_req):
        piece = swapped(queries, "z", d)
        sent += [piece, swapped(piece, "pair")]
    other = swapped(queries, "pair")

    home_keys, home_values, keys, values, member, prompt, own, valid = pl.pallas_call(
        functools.partial(prepare_kernel, capacity),
        out_shape=(
            pltpu.VMEM((1, 2 * capacity * half, HD), jnp.bfloat16),
            pltpu.VMEM((1, HD, 2 * capacity * half), jnp.bfloat16),
            pltpu.VMEM((n_req - 1, 2 * capacity * half, HD), jnp.bfloat16),
            pltpu.VMEM((n_req - 1, HD, 2 * capacity * half), jnp.bfloat16),
            pltpu.VMEM((n_req, 2 * capacity, 2 * VECS), jnp.float32),
            pltpu.VMEM((tokens, width), jnp.bfloat16),
            pltpu.VMEM(queries.shape, jnp.bfloat16),
            pltpu.VMEM((8, 2 * VECS), jnp.int32),
        ),
        in_specs=[pl.BlockSpec(memory_space=pltpu.SMEM)] + [hbm] * 5 + [vmem],
        out_specs=(vmem,) * 8,
        scratch_shapes=[
            pltpu.VMEM((2 * slots + 8, 2 * VECS), jnp.float32),
            pltpu.VMEM((SUF, rows), jnp.int32),
            pltpu.VMEM((1, rows), jnp.int32),
            pltpu.VMEM((slots, half, width), jnp.bfloat16),
            pltpu.SemaphoreType.DMA((5,)),
        ],
        compiler_params=params,
        name="prepare",
    )(
        lengths,
        in_hbm(block_table.T),
        in_hbm(parents.reshape(1, rows)),
        in_hbm(near),
        in_hbm(prompt_cache.reshape(tokens, width)),
        in_hbm(queries),
        far,
    )

    units, after = pl.pallas_call(
        away_kernel,
        out_shape=(
            pltpu.HBM((n_req, 2, UNIT_ROWS, VECS), jnp.bfloat16),
            pltpu.VMEM((8, VECS), jnp.float32),
        ),
        in_specs=[vmem] * (4 + len(sent)),
        out_specs=(hbm, vmem),
        scratch_shapes=[
            pltpu.VMEM((n_req - 1, 2, UNIT_ROWS, VECS), jnp.bfloat16),
            pltpu.SemaphoreType.DMA((n_req - 1, 2)),
        ],
        compiler_params=params,
        name="suffix_away",
    )(keys, values, member, *sent, other)
    units = units.reshape(2 * n_req, UNIT_ROWS, VECS)
    units = lax.all_to_all(units, ("z", "pair"), split_axis=0, concat_axis=0, tiled=True)

    summed, stats, given = pl.pallas_call(
        home_kernel,
        out_shape=(
            pltpu.VMEM((HD, VECS), jnp.float32),
            pltpu.VMEM((8, VECS), jnp.float32),
            pltpu.VMEM((UNIT_ROWS, VECS), jnp.bfloat16),
        ),
        in_specs=[vmem] * 8,
        out_specs=(vmem,) * 3,
        compiler_params=params,
        cost_estimate=pl.CostEstimate(
            flops=8 * tokens * VECS * HD, bytes_accessed=2 * tokens * width, transcendentals=0
        ),
        name="home_part",
    )(valid, home_keys, home_values, member, own, other, prompt, after)
    last = swapped(given, "pair")

    return pl.pallas_call(
        final_kernel,
        out_shape=jax.ShapeDtypeStruct((BEAMS, HEADS * HD), jnp.float32),
        in_specs=[vmem] * 4,
        out_specs=vmem,
        compiler_params=params,
        name="combine",
    )(units.reshape(n_req, 2, UNIT_ROWS, VECS), last, summed, stats)


def solution(mesh):
    n_batch, n_mp = mesh.devices.shape
    split = jax.sharding.Mesh(
        mesh.devices.reshape(n_batch // 2, 2, n_mp // 2, 2), ("z", "core", "group", "pair")
    )
    batch, mp = ("z", "core"), ("group", "pair")
    return jax.shard_map(
        on_device,
        mesh=split,
        in_specs=(
            P(batch, mp),
            P(batch, mp, None, None),
            P(batch, mp, None, None),
            P(),
            P(),
            P(batch),
        ),
        out_specs=P(batch, mp),
        check_vma=False,
    )
```

```python
import functools

import jax
import jax.numpy as jnp
from jax import lax
from jax.experimental import pallas as pl
from jax.experimental.pallas import tpu as pltpu
from jax.sharding import PartitionSpec as P

HD = 128
GROUP = 16
BEAMS = 16
SUF = 4
HEADS = GROUP // 2
VECS = HEADS * BEAMS
STAT_ROWS = 16
UNIT_ROWS = HD + STAT_ROWS
CHUNK = 512

big_negative = -1e30
to_exp2 = HD ** (-0.5) * 1.4426950408889634


def swapped(value, axis):
    return lax.ppermute(value, axis, [(0, 1), (1, 0)])


def shares(n_req):
    both = n_req // 2
    rest = [d for d in range(1, n_req) if d != both]
    return both, (rest[: len(rest) // 2], rest[len(rest) // 2 :])


def exchanged(value, message):
    n_req = lax.axis_size("z")
    both, own = shares(n_req)
    pairs = []
    for z in range(n_req):
        for core in range(2):
            for pair in range(2):
                if message == 0:
                    mask, side = both, core
                else:
                    mask, side = own[core][(message - 1) // 2], (message - 1) % 2
                target = ((z ^ mask) * 2 + core) * 2 + (pair ^ side)
                pairs.append(((z * 2 + core) * 2 + pair, target))
    return lax.ppermute(value, ("z", "core", "pair"), pairs)


def masks_here(n_req):
    both, own = shares(n_req)
    core = lax.axis_index("core")
    return [both] + [jnp.where(core == 0, d0, d1) for d0, d1 in zip(*own)]


def pack_kernel(own_ref, sibling_ref, out_ref):
    core = lax.axis_index("core")
    out_ref[core] = own_ref[...]
    out_ref[1 - core] = sibling_ref[...]


def stacked_heads(q):
    return jnp.concatenate([q[:, h * HD : (h + 1) * HD] for h in range(HEADS)], axis=0)


def scores_of(keys, vectors):
    return lax.dot_general(
        keys, vectors, (((1,), (1,)), ((), ())), preferred_element_type=jnp.float32
    )


def summed_of(values, weights):
    return lax.dot_general(
        values,
        weights.astype(jnp.bfloat16),
        (((0,), (0,)), ((), ())),
        preferred_element_type=jnp.float32,
    )


def merged(parts):
    top = functools.reduce(jnp.maximum, [p[0] for p in parts])
    total = 0.0
    summed = 0.0
    for part_top, part_total, part_summed in parts:
        factor = jnp.exp2((part_top - top) * to_exp2)
        total = total + part_total * factor
        summed = summed + part_summed * factor
    return top, total, summed


def weighted(scores):
    top = jnp.max(scores, axis=0, keepdims=True)
    weights = jnp.exp2((scores - top) * to_exp2)
    return top, jnp.sum(weights, axis=0, keepdims=True), weights


def three_pieces(x):
    first = x.astype(jnp.bfloat16).astype(jnp.float32)
    rest = x - first
    second = rest.astype(jnp.bfloat16).astype(jnp.float32)
    return [first, second, rest - second]


def store_unit(ref, top, total, summed):
    ref[:HD, :] = summed.astype(jnp.bfloat16)
    rows = three_pieces(top) + three_pieces(total)
    rows.append(jnp.zeros((STAT_ROWS - len(rows), VECS), jnp.float32))
    ref[HD:, :] = jnp.concatenate(rows, axis=0).astype(jnp.bfloat16)


def load_unit(ref):
    stats = ref[HD:, :].astype(jnp.float32)
    top = stats[0:1] + stats[1:2] + stats[2:3]
    total = stats[3:4] + stats[4:5] + stats[5:6]
    return top, total, ref[:HD, :].astype(jnp.float32)


def count(left, right):
    return jnp.dot(
        left.astype(jnp.bfloat16), right.astype(jnp.bfloat16), preferred_element_type=jnp.float32
    )


def iota(shape, axis):
    return lax.broadcasted_iota(jnp.int32, shape, axis)


def prompt_part(valid, prompt_ref, vectors):
    chunks = [slice(i, i + CHUNK) for i in range(0, prompt_ref.shape[0], CHUNK)]
    scores = [scores_of(prompt_ref[chunk, :HD], vectors) for chunk in chunks]
    place = iota(scores[0].shape, 0)
    scores = [
        jnp.where(place < valid - chunk.start, score, big_negative)
        for chunk, score in zip(chunks, scores)
    ]
    tops = [jnp.max(score, axis=0, keepdims=True) for score in scores]
    top = functools.reduce(jnp.maximum, tops)
    total, summed = 0.0, 0.0
    for chunk, score in zip(chunks, scores):
        weights = jnp.exp2((score - top) * to_exp2)
        total = total + jnp.sum(weights, axis=0, keepdims=True)
        summed = summed + summed_of(prompt_ref[chunk, HD:], weights)
    return top, total, summed


def prepare_kernel(
    capacity, length_ref, table_ref, parents_ref, near_ref, prompt_ref, own_ref, far_ref,
    home_keys_ref, home_values_ref, keys_ref, values_ref, member_ref, held_ref, own, valid_ref,
    rows_ref, table, parents, near, sems,
):
    n_req = lax.axis_size("z")
    slots, half, _ = near.shape
    rows = table.shape[1]
    n_batch = rows // BEAMS
    z, core = lax.axis_index("z"), lax.axis_index("core")

    small = [
        pltpu.make_async_copy(source, target, sems.at[i])
        for i, (source, target) in enumerate(
            [
                (table_ref, table),
                (parents_ref, parents),
                (near_ref, near),
                (prompt_ref, held_ref),
                (own_ref, own),
            ]
        )
    ]
    for copy in small:
        copy.start()

    length = length_ref[0]
    whole = lax.div(length, 2 * half)
    parity = lax.axis_index("pair")
    valid = whole * half + jnp.clip(length - whole * (2 * half) - parity * half, 0, half)
    valid_ref[...] = jnp.full(valid_ref.shape, valid, jnp.int32)

    small[0].wait()
    slot = iota((2 * slots, rows), 0)
    mine = slot < slots
    block = jnp.where(mine, slot, slot - slots) + jnp.where(mine, 2 * z + core, 2 * z + 1 - core) * slots
    named = functools.reduce(
        jnp.logical_or, [table[j : j + 1, :] == block for j in range(SUF)]
    ).astype(jnp.float32)
    group = (iota((rows, n_batch), 0) // BEAMS == iota((rows, n_batch), 1)).astype(jnp.float32)
    hit = jnp.where(count(named, group) > 0.0, 1.0, 0.0)
    left, right = iota((2 * slots, 2 * slots), 0), iota((2 * slots, 2 * slots), 1)
    before = (left // slots == right // slots) & (right < left)
    rank = count(before.astype(jnp.float32), hit)
    small[1].wait()
    taken = (iota((rows, rows), 0) == parents[...]).astype(jnp.float32)
    continued = count(named, taken)

    place = iota((2 * slots, n_batch), 0)
    found = []
    for k in range(2 * capacity):
        holder = k // capacity
        chosen = (hit > 0.0) & (rank == float(k % capacity)) & (place // slots == holder)
        found.append(jnp.sum(jnp.where(chosen, place + 1, 0), axis=0, keepdims=True))
    found = jnp.concatenate(found, axis=0)

    small[2].wait()
    requests = [z * 2 + core]
    for mask in masks_here(n_req):
        requests += [(z ^ mask) * 2, (z ^ mask) * 2 + 1]
    for i, request in enumerate(requests):
        lane = iota((rows, VECS), 1)
        spread = iota((rows, VECS), 0) == request * BEAMS + lane % BEAMS
        rows_ref[: 2 * slots, :] = count(continued, spread.astype(jnp.float32))
        rows_ref[2 * slots :, :] = jnp.zeros((8, VECS), jnp.float32)
        mask = iota(found.shape, 1) == request
        picked = jnp.sum(jnp.where(mask, found, 0), axis=1, keepdims=True)
        values = []
        for k in range(2 * capacity):
            index = picked[k, 0]
            row = jnp.where(index > 0, index - 1, 2 * slots)
            member_ref[i, k : k + 1, :] = rows_ref[pl.ds(row, 1), :]
            pool_ref = near if k < capacity else far_ref
            base = 0 if k < capacity else slots
            content = pool_ref[jnp.maximum(index - 1 - base, 0)]
            tokens = slice(k * half, (k + 1) * half)
            if i == 0:
                home_keys_ref[0, tokens, :] = content[:, :HD]
            else:
                keys_ref[i - 1, tokens, :] = content[:, :HD]
            values.append(content[:, HD:])
        values = jnp.concatenate(values, axis=0).T
        if i == 0:
            home_values_ref[0] = values
        else:
            values_ref[i - 1] = values

    small[3].wait()
    small[4].wait()


def all_vectors(own_ref, pair_ref):
    return jnp.concatenate([stacked_heads(own_ref[...]), stacked_heads(pair_ref[...])], axis=0)


def suffix_parts(vectors, keys_ref, values_ref, members):
    n_slots = members[0].shape[0]
    half = keys_ref.shape[1] // n_slots
    scores = [scores_of(keys_ref[i], each) for i, each in enumerate(vectors)]
    softmaxes = []
    for member, score in zip(members, scores):
        member = jnp.concatenate([member] * (score.shape[1] // VECS), axis=1)
        pieces = [
            jnp.where(
                member[k : k + 1, :] > 0.0, score[k * half : (k + 1) * half], big_negative
            )
            for k in range(n_slots)
        ]
        softmaxes.append(weighted(jnp.concatenate(pieces, axis=0)))
    return [
        (
            top,
            total,
            jnp.dot(
                values_ref[i], weights.astype(jnp.bfloat16), preferred_element_type=jnp.float32
            ),
        )
        for i, (top, total, weights) in enumerate(softmaxes)
    ]


def half_of(part, side):
    lanes = slice(side * VECS, (side + 1) * VECS)
    return [x[:, lanes] for x in part]


def away_kernel(n_messages, keys_ref, values_ref, member_ref, *rest):
    messages, units, after_ref = rest[:n_messages], rest[-n_messages - 1 : -1], rest[-1]
    after_ref[...] = jnp.zeros(after_ref.shape, jnp.float32)
    vectors = [stacked_heads(messages[0][core]) for core in range(2)]
    for k in range(1, n_messages, 2):
        for core in range(2):
            halves = [stacked_heads(messages[k + side][core]) for side in range(2)]
            vectors.append(jnp.concatenate(halves, axis=0))
    members = [member_ref[1 + i] for i in range(len(vectors))]
    parts = suffix_parts(vectors, keys_ref, values_ref, members)
    for i, part in enumerate(parts):
        core = i % 2
        if i < 2:
            store_unit(units[0].at[core], *part)
        else:
            for side in range(2):
                store_unit(units[i // 2 * 2 - 1 + side].at[core], *half_of(part, side))


def home_kernel(
    valid_ref, keys_ref, values_ref, member_ref, own_ref, pair_ref, prompt_ref, after_ref,
    summed_ref, stats_ref, out_ref,
):
    vectors = all_vectors(own_ref, pair_ref)
    (suffix,) = suffix_parts([vectors], keys_ref, values_ref, [member_ref[0]])
    prompt = prompt_part(valid_ref[0:1, :], prompt_ref, vectors)
    part = merged([prompt, suffix])
    top, total, summed_ref[...] = half_of(part, 0)
    stats_ref[...] = jnp.concatenate([top, total, jnp.zeros((6, VECS), jnp.float32)], axis=0)
    store_unit(out_ref, *half_of(part, 1))


def sibling_kernel(*rest):
    units, out_ref = rest[:-1], rest[-1]
    core = lax.axis_index("core")
    store_unit(out_ref, *merged([load_unit(unit.at[1 - core]) for unit in units]))


def final_kernel(*rest):
    units, (last_ref, shared_ref, summed_ref, stats_ref, out_ref) = rest[:-5], rest[-5:]
    core = lax.axis_index("core")
    parts = [load_unit(unit.at[core]) for unit in units]
    parts += [load_unit(last_ref), load_unit(shared_ref)]
    parts.append((stats_ref[0:1], stats_ref[1:2], summed_ref[...]))
    _, total, summed = merged(parts)
    attended = (summed / total).T
    for h in range(HEADS):
        out_ref[:, h * HD : (h + 1) * HD] = attended[h * BEAMS : (h + 1) * BEAMS]


def in_hbm(value):
    return pltpu.with_memory_space_constraint(value, pltpu.HBM)


def on_device(queries, prompt_cache, pool, block_table, parents, lengths):
    n_req = lax.axis_size("z")
    n_batch = 2 * n_req
    ndist = 2 ** (SUF + 1) - 2
    capacity = 2 * ((ndist // 2 + n_batch - 1) // n_batch)
    slots, _, half, width = pool.shape
    tokens = prompt_cache.shape[2]
    rows = block_table.shape[0]
    vmem = pl.BlockSpec(memory_space=pltpu.VMEM)
    params = pltpu.CompilerParams(vmem_limit_bytes=40 * 2**20)

    hbm = pl.BlockSpec(memory_space=pltpu.HBM)
    near = pool.reshape(slots, half, width)
    far = swapped(near, "core")
    other = swapped(queries, "pair")
    both = pl.pallas_call(
        pack_kernel,
        out_shape=pltpu.VMEM((2,) + queries.shape, jnp.bfloat16),
        in_specs=[vmem] * 2,
        out_specs=vmem,
        name="both_cores",
    )(queries, swapped(queries, "core"))
    n_messages = n_req - 1
    messages = [exchanged(both, k) for k in range(n_messages)]

    home_keys, home_values, keys, values, member, prompt, own, valid = pl.pallas_call(
        functools.partial(prepare_kernel, capacity),
        out_shape=(
            pltpu.VMEM((1, 2 * capacity * half, HD), jnp.bfloat16),
            pltpu.VMEM((1, HD, 2 * capacity * half), jnp.bfloat16),
            pltpu.VMEM((n_req, 2 * capacity * half, HD), jnp.bfloat16),
            pltpu.VMEM((n_req, HD, 2 * capacity * half), jnp.bfloat16),
            pltpu.VMEM((1 + n_req, 2 * capacity, VECS), jnp.float32),
            pltpu.VMEM((tokens, width), jnp.bfloat16),
            pltpu.VMEM(queries.shape, jnp.bfloat16),
            pltpu.VMEM((8, 2 * VECS), jnp.int32),
        ),
        in_specs=[pl.BlockSpec(memory_space=pltpu.SMEM)] + [hbm] * 5 + [vmem],
        out_specs=(vmem,) * 8,
        scratch_shapes=[
            pltpu.VMEM((2 * slots + 8, VECS), jnp.float32),
            pltpu.VMEM((SUF, rows), jnp.int32),
            pltpu.VMEM((1, rows), jnp.int32),
            pltpu.VMEM((slots, half, width), jnp.bfloat16),
            pltpu.SemaphoreType.DMA((5,)),
        ],
        compiler_params=params,
        name="prepare",
    )(
        lengths,
        in_hbm(block_table.T),
        in_hbm(parents.reshape(1, rows)),
        in_hbm(near),
        in_hbm(prompt_cache.reshape(tokens, width)),
        in_hbm(queries),
        far,
    )

    unit = pltpu.VMEM((UNIT_ROWS, VECS), jnp.bfloat16)
    *units, after = pl.pallas_call(
        functools.partial(away_kernel, n_messages),
        out_shape=(pltpu.VMEM((2, UNIT_ROWS, VECS), jnp.bfloat16),) * n_messages
        + (pltpu.VMEM((8, VECS), jnp.float32),),
        in_specs=[vmem] * (4 + n_messages),
        out_specs=(vmem,) * (n_messages + 1),
        compiler_params=params,
        name="suffix_away",
    )(keys, values, member, *messages, other)
    received = [exchanged(each, k) for k, each in enumerate(units)]

    summed, stats, given = pl.pallas_call(
        home_kernel,
        out_shape=(
            pltpu.VMEM((HD, VECS), jnp.float32),
            pltpu.VMEM((8, VECS), jnp.float32),
            pltpu.VMEM((UNIT_ROWS, VECS), jnp.bfloat16),
        ),
        in_specs=[vmem] * 8,
        out_specs=(vmem,) * 3,
        compiler_params=params,
        cost_estimate=pl.CostEstimate(
            flops=8 * tokens * VECS * HD, bytes_accessed=2 * tokens * width, transcendentals=0
        ),
        name="home_part",
    )(valid, home_keys, home_values, member, own, other, prompt, after)
    last = swapped(given, "pair")

    share = pl.pallas_call(
        sibling_kernel,
        out_shape=unit,
        in_specs=[vmem] * n_messages,
        out_specs=vmem,
        compiler_params=params,
        name="sibling_share",
    )(*received)

    return pl.pallas_call(
        final_kernel,
        out_shape=jax.ShapeDtypeStruct((BEAMS, HEADS * HD), jnp.float32),
        in_specs=[vmem] * (4 + n_messages),
        out_specs=vmem,
        compiler_params=params,
        name="combine",
    )(*received, last, swapped(share, "core"), summed, stats)


def solution(mesh):
    n_batch, n_mp = mesh.devices.shape
    split = jax.sharding.Mesh(
        mesh.devices.reshape(n_batch // 2, 2, n_mp // 2, 2), ("z", "core", "group", "pair")
    )
    batch, mp = ("z", "core"), ("group", "pair")
    return jax.shard_map(
        on_device,
        mesh=split,
        in_specs=(
            P(batch, mp),
            P(batch, mp, None, None),
            P(batch, mp, None, None),
            P(),
            P(),
            P(batch),
        ),
        out_specs=P(batch, mp),
        check_vma=False,
    )
```

```python
import functools

import jax
import jax.numpy as jnp
from jax import lax
from jax.experimental import pallas as pl
from jax.experimental.pallas import tpu as pltpu
from jax.sharding import PartitionSpec as P

HD = 128
GROUP = 16
BEAMS = 16
SUF = 4
HEADS = GROUP // 2
VECS = HEADS * BEAMS
STAT_ROWS = 16
UNIT_ROWS = HD + STAT_ROWS
CHUNK = 512

big_negative = -1e30
to_exp2 = HD ** (-0.5) * 1.4426950408889634


def swapped(value, axis):
    return lax.ppermute(value, axis, [(0, 1), (1, 0)])


def shares(n_req):
    both = n_req // 2
    rest = [d for d in range(1, n_req) if d != both]
    return both, (rest[: len(rest) // 2], rest[len(rest) // 2 :])


def exchanged(value, message):
    n_req = lax.axis_size("z")
    both, own = shares(n_req)
    pairs = []
    for z in range(n_req):
        for core in range(2):
            for pair in range(2):
                if message == 0:
                    mask, side = both, core
                else:
                    mask, side = own[core][(message - 1) // 2], (message - 1) % 2
                target = ((z ^ mask) * 2 + core) * 2 + (pair ^ side)
                pairs.append(((z * 2 + core) * 2 + pair, target))
    return lax.ppermute(value, ("z", "core", "pair"), pairs)


def masks_here(n_req):
    both, own = shares(n_req)
    core = lax.axis_index("core")
    return [both] + [jnp.where(core == 0, d0, d1) for d0, d1 in zip(*own)]


def stage_kernel(*refs):
    half = (len(refs) - 1) // 2
    sources, targets, sems = refs[:half], refs[half:-1], refs[-1]
    copies = [
        pltpu.make_async_copy(source, target, sems.at[i])
        for i, (source, target) in enumerate(zip(sources, targets))
    ]
    for copy in copies:
        copy.start()
    for copy in copies:
        copy.wait()


def pack_kernel(own_ref, sibling_ref, out_ref):
    core = lax.axis_index("core")
    out_ref[core] = own_ref[...]
    out_ref[1 - core] = sibling_ref[...]


def stacked_heads(q):
    return jnp.concatenate([q[:, h * HD : (h + 1) * HD] for h in range(HEADS)], axis=0)


def scores_of(keys, vectors):
    return lax.dot_general(
        keys, vectors, (((1,), (1,)), ((), ())), preferred_element_type=jnp.float32
    )


def summed_of(values, weights):
    return lax.dot_general(
        values,
        weights.astype(jnp.bfloat16),
        (((0,), (0,)), ((), ())),
        preferred_element_type=jnp.float32,
    )


def merged(parts):
    top = functools.reduce(jnp.maximum, [p[0] for p in parts])
    total = 0.0
    summed = 0.0
    for part_top, part_total, part_summed in parts:
        factor = jnp.exp2((part_top - top) * to_exp2)
        total = total + part_total * factor
        summed = summed + part_summed * factor
    return top, total, summed


def weighted(scores):
    top = jnp.max(scores, axis=0, keepdims=True)
    weights = jnp.exp2((scores - top) * to_exp2)
    return top, jnp.sum(weights, axis=0, keepdims=True), weights


def three_pieces(x):
    first = x.astype(jnp.bfloat16).astype(jnp.float32)
    rest = x - first
    second = rest.astype(jnp.bfloat16).astype(jnp.float32)
    return [first, second, rest - second]


def store_unit(ref, top, total, summed):
    ref[:HD, :] = summed.astype(jnp.bfloat16)
    rows = three_pieces(top) + three_pieces(total)
    rows.append(jnp.zeros((STAT_ROWS - len(rows), VECS), jnp.float32))
    ref[HD:, :] = jnp.concatenate(rows, axis=0).astype(jnp.bfloat16)


def load_unit(ref):
    stats = ref[HD:, :].astype(jnp.float32)
    top = stats[0:1] + stats[1:2] + stats[2:3]
    total = stats[3:4] + stats[4:5] + stats[5:6]
    return top, total, ref[:HD, :].astype(jnp.float32)


def count(left, right):
    return jnp.dot(
        left.astype(jnp.bfloat16), right.astype(jnp.bfloat16), preferred_element_type=jnp.float32
    )


def iota(shape, axis):
    return lax.broadcasted_iota(jnp.int32, shape, axis)


def prompt_part(valid, prompt_ref, vectors):
    chunks = [slice(i, i + CHUNK) for i in range(0, prompt_ref.shape[0], CHUNK)]
    scores = [scores_of(prompt_ref[chunk, :HD], vectors) for chunk in chunks]
    place = iota(scores[0].shape, 0)
    scores = [
        jnp.where(place < valid - chunk.start, score, big_negative)
        for chunk, score in zip(chunks, scores)
    ]
    tops = [jnp.max(score, axis=0, keepdims=True) for score in scores]
    top = functools.reduce(jnp.maximum, tops)
    total, summed = 0.0, 0.0
    for chunk, score in zip(chunks, scores):
        weights = jnp.exp2((score - top) * to_exp2)
        total = total + jnp.sum(weights, axis=0, keepdims=True)
        summed = summed + summed_of(prompt_ref[chunk, HD:], weights)
    return top, total, summed


def prepare_kernel(
    capacity, length_ref, prompt_ref, table, parents, near, far_ref,
    home_keys_ref, home_values_ref, keys_ref, values_ref, member_ref, held_ref, valid_ref,
    rows_ref, sem,
):
    n_req = lax.axis_size("z")
    slots, half, _ = near.shape
    rows = table.shape[1]
    n_batch = rows // BEAMS
    z, core = lax.axis_index("z"), lax.axis_index("core")

    copy = pltpu.make_async_copy(prompt_ref, held_ref, sem)
    copy.start()

    length = length_ref[0]
    whole = lax.div(length, 2 * half)
    parity = lax.axis_index("pair")
    valid = whole * half + jnp.clip(length - whole * (2 * half) - parity * half, 0, half)
    valid_ref[...] = jnp.full(valid_ref.shape, valid, jnp.int32)

    slot = iota((2 * slots, rows), 0)
    mine = slot < slots
    block = jnp.where(mine, slot, slot - slots) + jnp.where(mine, 2 * z + core, 2 * z + 1 - core) * slots
    named = functools.reduce(
        jnp.logical_or, [table[j : j + 1, :] == block for j in range(SUF)]
    ).astype(jnp.float32)
    group = (iota((rows, n_batch), 0) // BEAMS == iota((rows, n_batch), 1)).astype(jnp.float32)
    hit = jnp.where(count(named, group) > 0.0, 1.0, 0.0)
    left, right = iota((2 * slots, 2 * slots), 0), iota((2 * slots, 2 * slots), 1)
    before = (left // slots == right // slots) & (right < left)
    rank = count(before.astype(jnp.float32), hit)
    taken = (iota((rows, rows), 0) == parents[...]).astype(jnp.float32)
    continued = count(named, taken)

    place = iota((2 * slots, n_batch), 0)
    found = []
    for k in range(2 * capacity):
        holder = k // capacity
        chosen = (hit > 0.0) & (rank == float(k % capacity)) & (place // slots == holder)
        found.append(jnp.sum(jnp.where(chosen, place + 1, 0), axis=0, keepdims=True))
    found = jnp.concatenate(found, axis=0)

    requests = [z * 2 + core]
    for mask in masks_here(n_req):
        requests += [(z ^ mask) * 2, (z ^ mask) * 2 + 1]
    for i, request in enumerate(requests):
        lane = iota((rows, VECS), 1)
        spread = iota((rows, VECS), 0) == request * BEAMS + lane % BEAMS
        rows_ref[: 2 * slots, :] = count(continued, spread.astype(jnp.float32))
        rows_ref[2 * slots :, :] = jnp.zeros((8, VECS), jnp.float32)
        mask = iota(found.shape, 1) == request
        picked = jnp.sum(jnp.where(mask, found, 0), axis=1, keepdims=True)
        values = []
        for k in range(2 * capacity):
            index = picked[k, 0]
            row = jnp.where(index > 0, index - 1, 2 * slots)
            member_ref[i, k : k + 1, :] = rows_ref[pl.ds(row, 1), :]
            pool_ref = near if k < capacity else far_ref
            base = 0 if k < capacity else slots
            content = pool_ref[jnp.maximum(index - 1 - base, 0)]
            tokens = slice(k * half, (k + 1) * half)
            if i == 0:
                home_keys_ref[0, tokens, :] = content[:, :HD]
            else:
                keys_ref[i - 1, tokens, :] = content[:, :HD]
            values.append(content[:, HD:])
        values = jnp.concatenate(values, axis=0).T
        if i == 0:
            home_values_ref[0] = values
        else:
            values_ref[i - 1] = values

    copy.wait()


def all_vectors(own_ref, pair_ref):
    return jnp.concatenate([stacked_heads(own_ref[...]), stacked_heads(pair_ref[...])], axis=0)


def suffix_parts(vectors, keys_ref, values_ref, members):
    n_slots = members[0].shape[0]
    half = keys_ref.shape[1] // n_slots
    scores = [scores_of(keys_ref[i], each) for i, each in enumerate(vectors)]
    softmaxes = []
    for member, score in zip(members, scores):
        member = jnp.concatenate([member] * (score.shape[1] // VECS), axis=1)
        pieces = [
            jnp.where(
                member[k : k + 1, :] > 0.0, score[k * half : (k + 1) * half], big_negative
            )
            for k in range(n_slots)
        ]
        softmaxes.append(weighted(jnp.concatenate(pieces, axis=0)))
    return [
        (
            top,
            total,
            jnp.dot(
                values_ref[i], weights.astype(jnp.bfloat16), preferred_element_type=jnp.float32
            ),
        )
        for i, (top, total, weights) in enumerate(softmaxes)
    ]


def half_of(part, side):
    lanes = slice(side * VECS, (side + 1) * VECS)
    return [x[:, lanes] for x in part]


def away_kernel(n_messages, keys_ref, values_ref, member_ref, *rest):
    messages, units, after_ref = rest[:n_messages], rest[-n_messages - 1 : -1], rest[-1]
    after_ref[...] = jnp.zeros(after_ref.shape, jnp.float32)
    vectors = [stacked_heads(messages[0][core]) for core in range(2)]
    for k in range(1, n_messages, 2):
        for core in range(2):
            halves = [stacked_heads(messages[k + side][core]) for side in range(2)]
            vectors.append(jnp.concatenate(halves, axis=0))
    members = [member_ref[1 + i] for i in range(len(vectors))]
    parts = suffix_parts(vectors, keys_ref, values_ref, members)
    for i, part in enumerate(parts):
        core = i % 2
        if i < 2:
            store_unit(units[0].at[core], *part)
        else:
            for side in range(2):
                store_unit(units[i // 2 * 2 - 1 + side].at[core], *half_of(part, side))


def home_kernel(
    valid_ref, keys_ref, values_ref, member_ref, own_ref, pair_ref, prompt_ref, after_ref,
    summed_ref, stats_ref, out_ref,
):
    vectors = all_vectors(own_ref, pair_ref)
    (suffix,) = suffix_parts([vectors], keys_ref, values_ref, [member_ref[0]])
    prompt = prompt_part(valid_ref[0:1, :], prompt_ref, vectors)
    part = merged([prompt, suffix])
    top, total, summed_ref[...] = half_of(part, 0)
    stats_ref[...] = jnp.concatenate([top, total, jnp.zeros((6, VECS), jnp.float32)], axis=0)
    store_unit(out_ref, *half_of(part, 1))


def sibling_kernel(*rest):
    units, out_ref = rest[:-1], rest[-1]
    core = lax.axis_index("core")
    store_unit(out_ref, *merged([load_unit(unit.at[1 - core]) for unit in units]))


def final_kernel(*rest):
    units, (last_ref, shared_ref, summed_ref, stats_ref, out_ref) = rest[:-5], rest[-5:]
    core = lax.axis_index("core")
    parts = [load_unit(unit.at[core]) for unit in units]
    parts += [load_unit(last_ref), load_unit(shared_ref)]
    parts.append((stats_ref[0:1], stats_ref[1:2], summed_ref[...]))
    _, total, summed = merged(parts)
    attended = (summed / total).T
    for h in range(HEADS):
        out_ref[:, h * HD : (h + 1) * HD] = attended[h * BEAMS : (h + 1) * BEAMS]


def in_hbm(value):
    return pltpu.with_memory_space_constraint(value, pltpu.HBM)


def on_device(queries, prompt_cache, pool, block_table, parents, lengths):
    n_req = lax.axis_size("z")
    n_batch = 2 * n_req
    ndist = 2 ** (SUF + 1) - 2
    capacity = 2 * ((ndist // 2 + n_batch - 1) // n_batch)
    slots, _, half, width = pool.shape
    tokens = prompt_cache.shape[2]
    rows = block_table.shape[0]
    vmem = pl.BlockSpec(memory_space=pltpu.VMEM)
    params = pltpu.CompilerParams(vmem_limit_bytes=40 * 2**20)

    hbm = pl.BlockSpec(memory_space=pltpu.HBM)
    sibling = swapped(queries, "core")
    staged = [queries, pool.reshape(slots, half, width), block_table.T, parents.reshape(1, rows)]
    own, near, table, row_parents = pl.pallas_call(
        stage_kernel,
        out_shape=tuple(pltpu.VMEM(each.shape, each.dtype) for each in staged),
        in_specs=[hbm] * len(staged),
        out_specs=(vmem,) * len(staged),
        scratch_shapes=[pltpu.SemaphoreType.DMA((len(staged),))],
        compiler_params=params,
        name="stage",
    )(*[in_hbm(each) for each in staged])
    far = swapped(near, "core")
    other = swapped(queries, "pair")
    both = pl.pallas_call(
        pack_kernel,
        out_shape=pltpu.VMEM((2,) + queries.shape, jnp.bfloat16),
        in_specs=[vmem] * 2,
        out_specs=vmem,
        name="both_cores",
    )(own, sibling)
    n_messages = n_req - 1
    messages = [exchanged(both, k) for k in range(n_messages)]

    home_keys, home_values, keys, values, member, prompt, valid = pl.pallas_call(
        functools.partial(prepare_kernel, capacity),
        out_shape=(
            pltpu.VMEM((1, 2 * capacity * half, HD), jnp.bfloat16),
            pltpu.VMEM((1, HD, 2 * capacity * half), jnp.bfloat16),
            pltpu.VMEM((n_req, 2 * capacity * half, HD), jnp.bfloat16),
            pltpu.VMEM((n_req, HD, 2 * capacity * half), jnp.bfloat16),
            pltpu.VMEM((1 + n_req, 2 * capacity, VECS), jnp.float32),
            pltpu.VMEM((tokens, width), jnp.bfloat16),
            pltpu.VMEM((8, 2 * VECS), jnp.int32),
        ),
        in_specs=[pl.BlockSpec(memory_space=pltpu.SMEM), hbm] + [vmem] * 4,
        out_specs=(vmem,) * 7,
        scratch_shapes=[
            pltpu.VMEM((2 * slots + 8, VECS), jnp.float32),
            pltpu.SemaphoreType.DMA,
        ],
        compiler_params=params,
        name="prepare",
    )(
        lengths,
        in_hbm(prompt_cache.reshape(tokens, width)),
        table,
        row_parents,
        near,
        far,
    )

    unit = pltpu.VMEM((UNIT_ROWS, VECS), jnp.bfloat16)
    *units, after = pl.pallas_call(
        functools.partial(away_kernel, n_messages),
        out_shape=(pltpu.VMEM((2, UNIT_ROWS, VECS), jnp.bfloat16),) * n_messages
        + (pltpu.VMEM((8, VECS), jnp.float32),),
        in_specs=[vmem] * (3 + n_messages),
        out_specs=(vmem,) * (n_messages + 1),
        compiler_params=params,
        name="suffix_away",
    )(keys, values, member, *messages)
    received = [exchanged(each, k) for k, each in enumerate(units)]

    summed, stats, given = pl.pallas_call(
        home_kernel,
        out_shape=(
            pltpu.VMEM((HD, VECS), jnp.float32),
            pltpu.VMEM((8, VECS), jnp.float32),
            pltpu.VMEM((UNIT_ROWS, VECS), jnp.bfloat16),
        ),
        in_specs=[vmem] * 8,
        out_specs=(vmem,) * 3,
        compiler_params=params,
        cost_estimate=pl.CostEstimate(
            flops=8 * tokens * VECS * HD, bytes_accessed=2 * tokens * width, transcendentals=0
        ),
        name="home_part",
    )(valid, home_keys, home_values, member, own, other, prompt, after)
    last = swapped(given, "pair")

    share = pl.pallas_call(
        sibling_kernel,
        out_shape=unit,
        in_specs=[vmem] * n_messages,
        out_specs=vmem,
        compiler_params=params,
        name="sibling_share",
    )(*received)

    return pl.pallas_call(
        final_kernel,
        out_shape=jax.ShapeDtypeStruct((BEAMS, HEADS * HD), jnp.float32),
        in_specs=[vmem] * (4 + n_messages),
        out_specs=vmem,
        compiler_params=params,
        name="combine",
    )(*received, last, swapped(share, "core"), summed, stats)


def solution(mesh):
    n_batch, n_mp = mesh.devices.shape
    split = jax.sharding.Mesh(
        mesh.devices.reshape(n_batch // 2, 2, n_mp // 2, 2), ("z", "core", "group", "pair")
    )
    batch, mp = ("z", "core"), ("group", "pair")
    return jax.shard_map(
        on_device,
        mesh=split,
        in_specs=(
            P(batch, mp),
            P(batch, mp, None, None),
            P(batch, mp, None, None),
            P(),
            P(),
            P(batch),
        ),
        out_specs=P(batch, mp),
        check_vma=False,
    )
```

```python
import functools

import jax
import jax.numpy as jnp
from jax import lax
from jax.experimental import pallas as pl
from jax.experimental.pallas import tpu as pltpu
from jax.sharding import PartitionSpec as P

HD = 128
GROUP = 16
BEAMS = 16
SUF = 4
HEADS = GROUP // 2
VECS = HEADS * BEAMS
STAT_ROWS = 16
UNIT_ROWS = HD + STAT_ROWS
CHUNK = 512

big_negative = -1e30
to_exp2 = HD ** (-0.5) * 1.4426950408889634


def swapped(value, axis):
    return lax.ppermute(value, axis, [(0, 1), (1, 0)])


def shares(n_req):
    both = n_req // 2
    rest = [d for d in range(1, n_req) if d != both]
    return both, (rest[: len(rest) // 2], rest[len(rest) // 2 :])


def exchanged(value, message):
    n_req = lax.axis_size("z")
    both, own = shares(n_req)
    pairs = []
    for z in range(n_req):
        for core in range(2):
            for pair in range(2):
                if message == 0:
                    mask, side = both, core
                else:
                    mask, side = own[core][(message - 1) // 2], (message - 1) % 2
                target = ((z ^ mask) * 2 + core) * 2 + (pair ^ side)
                pairs.append(((z * 2 + core) * 2 + pair, target))
    return lax.ppermute(value, ("z", "core", "pair"), pairs)


def masks_here(n_req):
    both, own = shares(n_req)
    core = lax.axis_index("core")
    return [both] + [jnp.where(core == 0, d0, d1) for d0, d1 in zip(*own)]


def pack_kernel(own_ref, sibling_ref, out_ref):
    core = lax.axis_index("core")
    out_ref[core] = own_ref[...]
    out_ref[1 - core] = sibling_ref[...]


def stacked_heads(q):
    return jnp.concatenate([q[:, h * HD : (h + 1) * HD] for h in range(HEADS)], axis=0)


def scores_of(keys, vectors):
    return lax.dot_general(
        keys, vectors, (((1,), (1,)), ((), ())), preferred_element_type=jnp.float32
    )


def summed_of(values, weights):
    return lax.dot_general(
        values,
        weights.astype(jnp.bfloat16),
        (((0,), (0,)), ((), ())),
        preferred_element_type=jnp.float32,
    )


def merged(parts):
    top = functools.reduce(jnp.maximum, [p[0] for p in parts])
    total = 0.0
    summed = 0.0
    for part_top, part_total, part_summed in parts:
        factor = jnp.exp2((part_top - top) * to_exp2)
        total = total + part_total * factor
        summed = summed + part_summed * factor
    return top, total, summed


def weighted(scores):
    top = jnp.max(scores, axis=0, keepdims=True)
    weights = jnp.exp2((scores - top) * to_exp2)
    return top, jnp.sum(weights, axis=0, keepdims=True), weights


def three_pieces(x):
    first = x.astype(jnp.bfloat16).astype(jnp.float32)
    rest = x - first
    second = rest.astype(jnp.bfloat16).astype(jnp.float32)
    return [first, second, rest - second]


def store_unit(ref, top, total, summed):
    ref[:HD, :] = summed.astype(jnp.bfloat16)
    rows = three_pieces(top) + three_pieces(total)
    rows.append(jnp.zeros((STAT_ROWS - len(rows), VECS), jnp.float32))
    ref[HD:, :] = jnp.concatenate(rows, axis=0).astype(jnp.bfloat16)


def load_unit(ref):
    stats = ref[HD:, :].astype(jnp.float32)
    top = stats[0:1] + stats[1:2] + stats[2:3]
    total = stats[3:4] + stats[4:5] + stats[5:6]
    return top, total, ref[:HD, :].astype(jnp.float32)


def count(left, right):
    return jnp.dot(
        left.astype(jnp.bfloat16), right.astype(jnp.bfloat16), preferred_element_type=jnp.float32
    )


def iota(shape, axis):
    return lax.broadcasted_iota(jnp.int32, shape, axis)


def prompt_part(valid, prompt_ref, vectors):
    chunks = [slice(i, i + CHUNK) for i in range(0, prompt_ref.shape[0], CHUNK)]
    scores = [scores_of(prompt_ref[chunk, :HD], vectors) for chunk in chunks]
    place = iota(scores[0].shape, 0)
    scores = [
        jnp.where(place < valid - chunk.start, score, big_negative)
        for chunk, score in zip(chunks, scores)
    ]
    tops = [jnp.max(score, axis=0, keepdims=True) for score in scores]
    top = functools.reduce(jnp.maximum, tops)
    total, summed = 0.0, 0.0
    for chunk, score in zip(chunks, scores):
        weights = jnp.exp2((score - top) * to_exp2)
        total = total + jnp.sum(weights, axis=0, keepdims=True)
        summed = summed + summed_of(prompt_ref[chunk, HD:], weights)
    return top, total, summed


def prepare_kernel(
    capacity, length_ref, table_ref, parents_ref, near_ref, prompt_ref, own_ref, far_ref,
    home_keys_ref, home_values_ref, keys_ref, values_ref, member_ref, held_ref, own, valid_ref,
    rows_ref, table, parents, near, sems,
):
    n_req = lax.axis_size("z")
    slots, half, _ = near.shape
    rows = table.shape[1]
    n_batch = rows // BEAMS
    z, core = lax.axis_index("z"), lax.axis_index("core")

    small = [
        pltpu.make_async_copy(source, target, sems.at[i])
        for i, (source, target) in enumerate(
            [
                (table_ref, table),
                (parents_ref, parents),
                (near_ref, near),
                (prompt_ref, held_ref),
                (own_ref, own),
            ]
        )
    ]
    for copy in small:
        copy.start()

    length = length_ref[0]
    whole = lax.div(length, 2 * half)
    parity = lax.axis_index("pair")
    valid = whole * half + jnp.clip(length - whole * (2 * half) - parity * half, 0, half)
    valid_ref[...] = jnp.full(valid_ref.shape, valid, jnp.int32)

    small[0].wait()
    slot = iota((2 * slots, rows), 0)
    mine = slot < slots
    block = jnp.where(mine, slot, slot - slots) + jnp.where(mine, 2 * z + core, 2 * z + 1 - core) * slots
    named = functools.reduce(
        jnp.logical_or, [table[j : j + 1, :] == block for j in range(SUF)]
    ).astype(jnp.float32)
    group = (iota((rows, n_batch), 0) // BEAMS == iota((rows, n_batch), 1)).astype(jnp.float32)
    hit = jnp.where(count(named, group) > 0.0, 1.0, 0.0)
    left, right = iota((2 * slots, 2 * slots), 0), iota((2 * slots, 2 * slots), 1)
    before = (left // slots == right // slots) & (right < left)
    rank = count(before.astype(jnp.float32), hit)
    small[1].wait()
    taken = (iota((rows, rows), 0) == parents[...]).astype(jnp.float32)
    continued = count(named, taken)

    place = iota((2 * slots, n_batch), 0)
    found = []
    for k in range(2 * capacity):
        holder = k // capacity
        chosen = (hit > 0.0) & (rank == float(k % capacity)) & (place // slots == holder)
        found.append(jnp.sum(jnp.where(chosen, place + 1, 0), axis=0, keepdims=True))
    found = jnp.concatenate(found, axis=0)

    small[2].wait()
    requests = [z * 2 + core]
    for mask in masks_here(n_req):
        requests += [(z ^ mask) * 2, (z ^ mask) * 2 + 1]
    for i, request in enumerate(requests):
        lane = iota((rows, VECS), 1)
        spread = iota((rows, VECS), 0) == request * BEAMS + lane % BEAMS
        rows_ref[: 2 * slots, :] = count(continued, spread.astype(jnp.float32))
        rows_ref[2 * slots :, :] = jnp.zeros((8, VECS), jnp.float32)
        mask = iota(found.shape, 1) == request
        picked = jnp.sum(jnp.where(mask, found, 0), axis=1, keepdims=True)
        values = []
        for k in range(2 * capacity):
            index = picked[k, 0]
            row = jnp.where(index > 0, index - 1, 2 * slots)
            member_ref[i, k : k + 1, :] = rows_ref[pl.ds(row, 1), :]
            pool_ref = near if k < capacity else far_ref
            base = 0 if k < capacity else slots
            content = pool_ref[jnp.maximum(index - 1 - base, 0)]
            tokens = slice(k * half, (k + 1) * half)
            if i == 0:
                home_keys_ref[0, tokens, :] = content[:, :HD]
            else:
                keys_ref[i - 1, tokens, :] = content[:, :HD]
            values.append(content[:, HD:])
        values = jnp.concatenate(values, axis=0).T
        if i == 0:
            home_values_ref[0] = values
        else:
            values_ref[i - 1] = values

    small[3].wait()
    small[4].wait()


def all_vectors(own_ref, pair_ref):
    return jnp.concatenate([stacked_heads(own_ref[...]), stacked_heads(pair_ref[...])], axis=0)


def suffix_parts(vectors, keys_ref, values_ref, members):
    n_slots = members[0].shape[0]
    half = keys_ref.shape[1] // n_slots
    scores = [scores_of(keys_ref[i], each) for i, each in enumerate(vectors)]
    softmaxes = []
    for member, score in zip(members, scores):
        member = jnp.concatenate([member] * (score.shape[1] // VECS), axis=1)
        pieces = [
            jnp.where(
                member[k : k + 1, :] > 0.0, score[k * half : (k + 1) * half], big_negative
            )
            for k in range(n_slots)
        ]
        softmaxes.append(weighted(jnp.concatenate(pieces, axis=0)))
    return [
        (
            top,
            total,
            jnp.dot(
                values_ref[i], weights.astype(jnp.bfloat16), preferred_element_type=jnp.float32
            ),
        )
        for i, (top, total, weights) in enumerate(softmaxes)
    ]


def half_of(part, side):
    lanes = slice(side * VECS, (side + 1) * VECS)
    return [x[:, lanes] for x in part]


def away_kernel(n_messages, keys_ref, values_ref, member_ref, *rest):
    messages, units, after_ref = rest[:n_messages], rest[-n_messages - 1 : -1], rest[-1]
    after_ref[...] = jnp.zeros(after_ref.shape, jnp.float32)
    vectors = [stacked_heads(messages[0][core]) for core in range(2)]
    for k in range(1, n_messages, 2):
        for core in range(2):
            halves = [stacked_heads(messages[k + side][core]) for side in range(2)]
            vectors.append(jnp.concatenate(halves, axis=0))
    members = [member_ref[1 + i] for i in range(len(vectors))]
    parts = suffix_parts(vectors, keys_ref, values_ref, members)
    for i, part in enumerate(parts):
        core = i % 2
        if i < 2:
            store_unit(units[0].at[core], *part)
        else:
            for side in range(2):
                store_unit(units[i // 2 * 2 - 1 + side].at[core], *half_of(part, side))


def home_kernel(
    valid_ref, keys_ref, values_ref, member_ref, own_ref, pair_ref, prompt_ref, after_ref,
    summed_ref, stats_ref, out_ref,
):
    vectors = all_vectors(own_ref, pair_ref)
    (suffix,) = suffix_parts([vectors], keys_ref, values_ref, [member_ref[0]])
    prompt = prompt_part(valid_ref[0:1, :], prompt_ref, vectors)
    part = merged([prompt, suffix])
    top, total, summed_ref[...] = half_of(part, 0)
    stats_ref[...] = jnp.concatenate([top, total, jnp.zeros((6, VECS), jnp.float32)], axis=0)
    store_unit(out_ref, *half_of(part, 1))


def sibling_kernel(*rest):
    units, out_ref = rest[:-1], rest[-1]
    core = lax.axis_index("core")
    store_unit(out_ref, *merged([load_unit(unit.at[1 - core]) for unit in units]))


def final_kernel(*rest):
    units, (last_ref, shared_ref, summed_ref, stats_ref, out_ref) = rest[:-5], rest[-5:]
    core = lax.axis_index("core")
    parts = [load_unit(unit.at[core]) for unit in units]
    parts += [load_unit(last_ref), load_unit(shared_ref)]
    parts.append((stats_ref[0:1], stats_ref[1:2], summed_ref[...]))
    _, total, summed = merged(parts)
    attended = (summed / total).T
    for h in range(HEADS):
        out_ref[:, h * HD : (h + 1) * HD] = attended[h * BEAMS : (h + 1) * BEAMS]


def in_hbm(value):
    return pltpu.with_memory_space_constraint(value, pltpu.HBM)


def on_device(queries, prompt_cache, pool, block_table, parents, lengths):
    n_req = lax.axis_size("z")
    n_batch = 2 * n_req
    ndist = 2 ** (SUF + 1) - 2
    capacity = 2 * ((ndist // 2 + n_batch - 1) // n_batch)
    slots, _, half, width = pool.shape
    tokens = prompt_cache.shape[2]
    rows = block_table.shape[0]
    vmem = pl.BlockSpec(memory_space=pltpu.VMEM)
    params = pltpu.CompilerParams(vmem_limit_bytes=32 * 2**20)
    early = pl.CostEstimate(flops=2 * 10**10, bytes_accessed=0, transcendentals=0)

    hbm = pl.BlockSpec(memory_space=pltpu.HBM)
    near = pool.reshape(slots, half, width)
    far = swapped(near, "core")
    other = swapped(queries, "pair")
    both = pl.pallas_call(
        pack_kernel,
        out_shape=pltpu.VMEM((2,) + queries.shape, jnp.bfloat16),
        in_specs=[vmem] * 2,
        out_specs=vmem,
        compiler_params=params,
        cost_estimate=early,
        name="both_cores",
    )(queries, swapped(queries, "core"))
    n_messages = n_req - 1
    messages = [exchanged(both, k) for k in range(n_messages)]

    home_keys, home_values, keys, values, member, prompt, own, valid = pl.pallas_call(
        functools.partial(prepare_kernel, capacity),
        out_shape=(
            pltpu.VMEM((1, 2 * capacity * half, HD), jnp.bfloat16),
            pltpu.VMEM((1, HD, 2 * capacity * half), jnp.bfloat16),
            pltpu.VMEM((n_req, 2 * capacity * half, HD), jnp.bfloat16),
            pltpu.VMEM((n_req, HD, 2 * capacity * half), jnp.bfloat16),
            pltpu.VMEM((1 + n_req, 2 * capacity, VECS), jnp.float32),
            pltpu.VMEM((tokens, width), jnp.bfloat16),
            pltpu.VMEM(queries.shape, jnp.bfloat16),
            pltpu.VMEM((8, 2 * VECS), jnp.int32),
        ),
        in_specs=[pl.BlockSpec(memory_space=pltpu.SMEM)] + [hbm] * 5 + [vmem],
        out_specs=(vmem,) * 8,
        scratch_shapes=[
            pltpu.VMEM((2 * slots + 8, VECS), jnp.float32),
            pltpu.VMEM((SUF, rows), jnp.int32),
            pltpu.VMEM((1, rows), jnp.int32),
            pltpu.VMEM((slots, half, width), jnp.bfloat16),
            pltpu.SemaphoreType.DMA((5,)),
        ],
        compiler_params=params,
        name="prepare",
    )(
        lengths,
        in_hbm(block_table.T),
        in_hbm(parents.reshape(1, rows)),
        in_hbm(near),
        in_hbm(prompt_cache.reshape(tokens, width)),
        in_hbm(queries),
        far,
    )

    unit = pltpu.VMEM((UNIT_ROWS, VECS), jnp.bfloat16)
    *units, after = pl.pallas_call(
        functools.partial(away_kernel, n_messages),
        out_shape=(pltpu.VMEM((2, UNIT_ROWS, VECS), jnp.bfloat16),) * n_messages
        + (pltpu.VMEM((8, VECS), jnp.float32),),
        in_specs=[vmem] * (3 + n_messages),
        out_specs=(vmem,) * (n_messages + 1),
        compiler_params=params,
        name="suffix_away",
    )(keys, values, member, *messages)
    received = [exchanged(each, k) for k, each in enumerate(units)]

    summed, stats, given = pl.pallas_call(
        home_kernel,
        out_shape=(
            pltpu.VMEM((HD, VECS), jnp.float32),
            pltpu.VMEM((8, VECS), jnp.float32),
            pltpu.VMEM((UNIT_ROWS, VECS), jnp.bfloat16),
        ),
        in_specs=[vmem] * 8,
        out_specs=(vmem,) * 3,
        compiler_params=params,
        cost_estimate=pl.CostEstimate(
            flops=8 * tokens * VECS * HD, bytes_accessed=2 * tokens * width, transcendentals=0
        ),
        name="home_part",
    )(valid, home_keys, home_values, member, own, other, prompt, after)
    last = swapped(given, "pair")

    share = pl.pallas_call(
        sibling_kernel,
        out_shape=unit,
        in_specs=[vmem] * n_messages,
        out_specs=vmem,
        compiler_params=params,
        name="sibling_share",
    )(*received)

    return pl.pallas_call(
        final_kernel,
        out_shape=jax.ShapeDtypeStruct((BEAMS, HEADS * HD), jnp.float32),
        in_specs=[vmem] * (4 + n_messages),
        out_specs=vmem,
        compiler_params=params,
        name="combine",
    )(*received, last, swapped(share, "core"), summed, stats)


def solution(mesh):
    n_batch, n_mp = mesh.devices.shape
    split = jax.sharding.Mesh(
        mesh.devices.reshape(n_batch // 2, 2, n_mp // 2, 2), ("z", "core", "group", "pair")
    )
    batch, mp = ("z", "core"), ("group", "pair")
    return jax.shard_map(
        on_device,
        mesh=split,
        in_specs=(
            P(batch, mp),
            P(batch, mp, None, None),
            P(batch, mp, None, None),
            P(),
            P(),
            P(batch),
        ),
        out_specs=P(batch, mp),
        check_vma=False,
    )
```

```python
import functools

import jax
import jax.numpy as jnp
from jax import lax
from jax.experimental import pallas as pl
from jax.experimental.pallas import tpu as pltpu
from jax.sharding import PartitionSpec as P

HD = 128
GROUP = 16
BEAMS = 16
SUF = 4
HEADS = GROUP // 2
VECS = HEADS * BEAMS
STAT_ROWS = 16
CHUNK = 512

big_negative = -1e30
to_exp2 = HD ** (-0.5) * 1.4426950408889634


def swapped(value, axis):
    return lax.ppermute(value, axis, [(0, 1), (1, 0)])


def shares(n_req):
    both = n_req // 2
    rest = [d for d in range(1, n_req) if d != both]
    return both, (rest[: len(rest) // 2], rest[len(rest) // 2 :])


def exchanged(value, message):
    n_req = lax.axis_size("z")
    both, own = shares(n_req)
    pairs = []
    for z in range(n_req):
        for core in range(2):
            for pair in range(2):
                if message == 0:
                    mask, side = both, core
                else:
                    mask, side = own[core][(message - 1) // 2], (message - 1) % 2
                target = ((z ^ mask) * 2 + core) * 2 + (pair ^ side)
                pairs.append(((z * 2 + core) * 2 + pair, target))
    return lax.ppermute(value, ("z", "core", "pair"), pairs)


def masks_here(n_req):
    both, own = shares(n_req)
    core = lax.axis_index("core")
    return [both] + [jnp.where(core == 0, d0, d1) for d0, d1 in zip(*own)]


def stage_kernel(*refs):
    n = (len(refs) - 1) // 2
    copies = [
        pltpu.make_async_copy(refs[i], refs[n + i], refs[-1].at[i]) for i in range(n)
    ]
    for copy in copies:
        copy.start()
    for copy in copies:
        copy.wait()


def pack_kernel(own_ref, sibling_ref, out_ref):
    core = lax.axis_index("core")
    out_ref[core] = own_ref[...]
    out_ref[1 - core] = sibling_ref[...]


def stacked_heads(q):
    return jnp.concatenate([q[:, h * HD : (h + 1) * HD] for h in range(HEADS)], axis=0)


def scores_of(keys, vectors):
    return lax.dot_general(
        keys, vectors, (((1,), (1,)), ((), ())), preferred_element_type=jnp.float32
    )


def summed_of(values, weights):
    return lax.dot_general(
        values,
        weights.astype(jnp.bfloat16),
        (((0,), (0,)), ((), ())),
        preferred_element_type=jnp.float32,
    )


def merged(parts):
    top = functools.reduce(jnp.maximum, [p[0] for p in parts])
    total = 0.0
    summed = 0.0
    for part_top, part_total, part_summed in parts:
        factor = jnp.exp2((part_top - top) * to_exp2)
        total = total + part_total * factor
        summed = summed + part_summed * factor
    return top, total, summed


def weighted(scores):
    top = jnp.max(scores, axis=0, keepdims=True)
    weights = jnp.exp2((scores - top) * to_exp2)
    return top, jnp.sum(weights, axis=0, keepdims=True), weights


def three_pieces(x):
    first = x.astype(jnp.bfloat16).astype(jnp.float32)
    rest = x - first
    second = rest.astype(jnp.bfloat16).astype(jnp.float32)
    return [first, second, rest - second]


def store_units(ref, parts):
    rows = []
    for i, (top, total, summed) in enumerate(parts):
        ref[i * HD : (i + 1) * HD, :] = summed.astype(jnp.bfloat16)
        rows += three_pieces(top) + three_pieces(total)
    rows.append(jnp.zeros((STAT_ROWS - len(rows), VECS), jnp.float32))
    ref[len(parts) * HD :, :] = jnp.concatenate(rows, axis=0).astype(jnp.bfloat16)


def load_unit(ref, i=0):
    sums = ref.shape[0] - STAT_ROWS
    stats = ref[sums:, :].astype(jnp.float32)
    if isinstance(i, int):
        rows = [stats[6 * i + k : 6 * i + k + 1] for k in range(6)]
    else:
        rows = [jnp.where(i == 0, stats[k : k + 1], stats[6 + k : 7 + k]) for k in range(6)]
    part = ref[pl.ds(pl.multiple_of(i * HD, HD), HD), :]
    return rows[0] + rows[1] + rows[2], rows[3] + rows[4] + rows[5], part.astype(jnp.float32)


def count(left, right):
    return jnp.dot(
        left.astype(jnp.bfloat16), right.astype(jnp.bfloat16), preferred_element_type=jnp.float32
    )


def iota(shape, axis):
    return lax.broadcasted_iota(jnp.int32, shape, axis)


def prompt_part(length, half, prompt_ref, vectors):
    parity = lax.axis_index("pair")
    whole = lax.div(length, 2 * half)
    valid = whole * half + jnp.clip(length - whole * (2 * half) - parity * half, 0, half)
    chunks = [slice(i, i + CHUNK) for i in range(0, prompt_ref.shape[0], CHUNK)]
    scores = [scores_of(prompt_ref[chunk, :HD], vectors) for chunk in chunks]
    place = iota(scores[0].shape, 0)
    scores = [
        jnp.where(place < valid - chunk.start, score, big_negative)
        for chunk, score in zip(chunks, scores)
    ]
    tops = [jnp.max(score, axis=0, keepdims=True) for score in scores]
    top = functools.reduce(jnp.maximum, tops)
    total, summed = 0.0, 0.0
    for chunk, score in zip(chunks, scores):
        weights = jnp.exp2((score - top) * to_exp2)
        total = total + jnp.sum(weights, axis=0, keepdims=True)
        summed = summed + summed_of(prompt_ref[chunk, HD:], weights)
    return top, total, summed


def prepare_kernel(
    capacity, near_ref, prompt_ref, table, parents, far_ref,
    home_keys_ref, home_values_ref, keys_ref, values_ref, member_ref, held_ref,
    rows_ref, near, sems,
):
    n_req = lax.axis_size("z")
    slots, half, _ = near.shape
    rows = table.shape[1]
    n_batch = rows // BEAMS
    z, core = lax.axis_index("z"), lax.axis_index("core")

    copies = [
        pltpu.make_async_copy(near_ref, near, sems.at[0]),
        pltpu.make_async_copy(prompt_ref, held_ref, sems.at[1]),
    ]
    for copy in copies:
        copy.start()

    slot = iota((2 * slots, rows), 0)
    mine = slot < slots
    block = jnp.where(mine, slot, slot - slots) + jnp.where(mine, 2 * z + core, 2 * z + 1 - core) * slots
    named = functools.reduce(
        jnp.logical_or, [table[j : j + 1, :] == block for j in range(SUF)]
    ).astype(jnp.float32)
    group = (iota((rows, n_batch), 0) // BEAMS == iota((rows, n_batch), 1)).astype(jnp.float32)
    hit = jnp.where(count(named, group) > 0.0, 1.0, 0.0)
    left, right = iota((2 * slots, 2 * slots), 0), iota((2 * slots, 2 * slots), 1)
    before = (left // slots == right // slots) & (right < left)
    rank = count(before.astype(jnp.float32), hit)
    taken = (iota((rows, rows), 0) == parents[...]).astype(jnp.float32)
    continued = count(named, taken)

    place = iota((2 * slots, n_batch), 0)
    found = []
    for k in range(2 * capacity):
        holder = k // capacity
        chosen = (hit > 0.0) & (rank == float(k % capacity)) & (place // slots == holder)
        found.append(jnp.sum(jnp.where(chosen, place + 1, 0), axis=0, keepdims=True))
    found = jnp.concatenate(found, axis=0)

    copies[0].wait()
    requests = [z * 2 + core]
    for mask in masks_here(n_req):
        requests += [(z ^ mask) * 2, (z ^ mask) * 2 + 1]
    for i, request in enumerate(requests):
        lane = iota((rows, VECS), 1)
        spread = iota((rows, VECS), 0) == request * BEAMS + lane % BEAMS
        rows_ref[: 2 * slots, :] = count(continued, spread.astype(jnp.float32))
        rows_ref[2 * slots :, :] = jnp.zeros((8, VECS), jnp.float32)
        mask = iota(found.shape, 1) == request
        picked = jnp.sum(jnp.where(mask, found, 0), axis=1, keepdims=True)
        values = []
        for k in range(2 * capacity):
            index = picked[k, 0]
            row = jnp.where(index > 0, index - 1, 2 * slots)
            member_ref[i, k : k + 1, :] = rows_ref[pl.ds(row, 1), :]
            pool_ref = near if k < capacity else far_ref
            base = 0 if k < capacity else slots
            content = pool_ref[jnp.maximum(index - 1 - base, 0)]
            tokens = slice(k * half, (k + 1) * half)
            if i == 0:
                home_keys_ref[0, tokens, :] = content[:, :HD]
            else:
                keys_ref[i - 1, tokens, :] = content[:, :HD]
            values.append(content[:, HD:])
        values = jnp.concatenate(values, axis=0).T
        if i == 0:
            home_values_ref[0] = values
        else:
            values_ref[i - 1] = values

    copies[1].wait()


def all_vectors(own_ref, pair_ref):
    return jnp.concatenate([stacked_heads(own_ref[...]), stacked_heads(pair_ref[...])], axis=0)


def suffix_parts(vectors, keys_ref, values_ref, members, place=0):
    n_slots = members[0].shape[0]
    half = keys_ref.shape[1] // n_slots
    scores = [scores_of(keys_ref[place + i], each) for i, each in enumerate(vectors)]
    softmaxes = []
    for member, score in zip(members, scores):
        member = jnp.concatenate([member] * (score.shape[1] // VECS), axis=1)
        pieces = [
            jnp.where(
                member[k : k + 1, :] > 0.0, score[k * half : (k + 1) * half], big_negative
            )
            for k in range(n_slots)
        ]
        softmaxes.append(weighted(jnp.concatenate(pieces, axis=0)))
    return [
        (
            top,
            total,
            jnp.dot(
                values_ref[place + i], weights.astype(jnp.bfloat16), preferred_element_type=jnp.float32
            ),
        )
        for i, (top, total, weights) in enumerate(softmaxes)
    ]


def half_of(part, side):
    lanes = slice(side * VECS, (side + 1) * VECS)
    return [x[:, lanes] for x in part]


def away_kernel(place, keys_ref, values_ref, member_ref, message_ref, out_ref, after_ref):
    after_ref[...] = jnp.zeros(after_ref.shape, jnp.float32)
    vectors = [stacked_heads(message_ref[core]) for core in range(2)]
    members = [member_ref[1 + place + core] for core in range(2)]
    store_units(out_ref, suffix_parts(vectors, keys_ref, values_ref, members, place))


def home_kernel(
    length_ref, keys_ref, values_ref, member_ref, own_ref, pair_ref, prompt_ref, after_ref,
    summed_ref, stats_ref, out_ref,
):
    vectors = all_vectors(own_ref, pair_ref)
    half = keys_ref.shape[1] // member_ref.shape[1]
    (suffix,) = suffix_parts([vectors], keys_ref, values_ref, [member_ref[0]])
    prompt = prompt_part(length_ref[0], half, prompt_ref, vectors)
    part = merged([prompt, suffix])
    top, total, summed_ref[...] = half_of(part, 0)
    stats_ref[...] = jnp.concatenate([top, total, jnp.zeros((6, VECS), jnp.float32)], axis=0)
    store_units(out_ref, [half_of(part, 1)])


def sibling_kernel(*rest):
    units, out_ref = rest[:-1], rest[-1]
    core = lax.axis_index("core")
    store_units(out_ref, [merged([load_unit(unit, 1 - core) for unit in units])])


def final_kernel(*rest):
    units, (last_ref, shared_ref, summed_ref, stats_ref, out_ref) = rest[:-5], rest[-5:]
    core = lax.axis_index("core")
    parts = [load_unit(unit, core) for unit in units]
    parts += [load_unit(last_ref), load_unit(shared_ref)]
    parts.append((stats_ref[0:1], stats_ref[1:2], summed_ref[...]))
    _, total, summed = merged(parts)
    attended = (summed / total).T
    for h in range(HEADS):
        out_ref[:, h * HD : (h + 1) * HD] = attended[h * BEAMS : (h + 1) * BEAMS]


def in_hbm(value):
    return pltpu.with_memory_space_constraint(value, pltpu.HBM)


def on_device(queries, prompt_cache, pool, block_table, parents, lengths):
    n_req = lax.axis_size("z")
    n_batch = 2 * n_req
    ndist = 2 ** (SUF + 1) - 2
    capacity = 2 * ((ndist // 2 + n_batch - 1) // n_batch)
    slots, _, half, width = pool.shape
    tokens = prompt_cache.shape[2]
    rows = block_table.shape[0]
    vmem = pl.BlockSpec(memory_space=pltpu.VMEM)
    params = pltpu.CompilerParams(vmem_limit_bytes=32 * 2**20)
    early = pl.CostEstimate(flops=2 * 10**10, bytes_accessed=0, transcendentals=0)

    hbm = pl.BlockSpec(memory_space=pltpu.HBM)
    near = pool.reshape(slots, half, width)
    far = swapped(near, "core")
    other = swapped(queries, "pair")
    staged = [queries, block_table.T, parents.reshape(1, rows)]
    own, table, row_parents = pl.pallas_call(
        stage_kernel,
        out_shape=tuple(pltpu.VMEM(each.shape, each.dtype) for each in staged),
        in_specs=[hbm] * len(staged),
        out_specs=(vmem,) * len(staged),
        scratch_shapes=[pltpu.SemaphoreType.DMA((len(staged),))],
        compiler_params=params,
        name="stage",
    )(*[in_hbm(each) for each in staged])
    both = pl.pallas_call(
        pack_kernel,
        out_shape=pltpu.VMEM((2,) + queries.shape, jnp.bfloat16),
        in_specs=[vmem] * 2,
        out_specs=vmem,
        compiler_params=params,
        cost_estimate=early,
        name="both_cores",
    )(own, swapped(queries, "core"))
    n_messages = n_req - 1
    messages = [exchanged(both, k) for k in range(n_messages)]

    home_keys, home_values, keys, values, member, prompt = pl.pallas_call(
        functools.partial(prepare_kernel, capacity),
        out_shape=(
            pltpu.VMEM((1, 2 * capacity * half, HD), jnp.bfloat16),
            pltpu.VMEM((1, HD, 2 * capacity * half), jnp.bfloat16),
            pltpu.VMEM((n_req, 2 * capacity * half, HD), jnp.bfloat16),
            pltpu.VMEM((n_req, HD, 2 * capacity * half), jnp.bfloat16),
            pltpu.VMEM((1 + n_req, 2 * capacity, VECS), jnp.float32),
            pltpu.VMEM((tokens, width), jnp.bfloat16),
        ),
        in_specs=[hbm] * 2 + [vmem] * 3,
        out_specs=(vmem,) * 6,
        scratch_shapes=[
            pltpu.VMEM((2 * slots + 8, VECS), jnp.float32),
            pltpu.VMEM((slots, half, width), jnp.bfloat16),
            pltpu.SemaphoreType.DMA((2,)),
        ],
        compiler_params=params,
        name="prepare",
    )(
        in_hbm(near),
        in_hbm(prompt_cache.reshape(tokens, width)),
        table,
        row_parents,
        far,
    )

    received = []
    for k, message in reversed(list(enumerate(messages))):
        units, after = pl.pallas_call(
            functools.partial(away_kernel, 2 * ((k + 1) // 2)),
            out_shape=(
                pltpu.VMEM((2 * HD + STAT_ROWS, VECS), jnp.bfloat16),
                pltpu.VMEM((8, VECS), jnp.float32),
            ),
            in_specs=[vmem] * 4,
            out_specs=(vmem,) * 2,
            compiler_params=params,
            name="suffix_away",
        )(keys, values, member, message)
        received.append(exchanged(units, k))

    summed, stats, given = pl.pallas_call(
        home_kernel,
        out_shape=(
            pltpu.VMEM((HD, VECS), jnp.float32),
            pltpu.VMEM((8, VECS), jnp.float32),
            pltpu.VMEM((HD + STAT_ROWS, VECS), jnp.bfloat16),
        ),
        in_specs=[pl.BlockSpec(memory_space=pltpu.SMEM)] + [vmem] * 7,
        out_specs=(vmem,) * 3,
        compiler_params=params,
        cost_estimate=pl.CostEstimate(
            flops=8 * tokens * VECS * HD, bytes_accessed=2 * tokens * width, transcendentals=0
        ),
        name="home_part",
    )(lengths, home_keys, home_values, member, own, other, prompt, after)
    last = swapped(given, "pair")

    share = pl.pallas_call(
        sibling_kernel,
        out_shape=pltpu.VMEM((HD + STAT_ROWS, VECS), jnp.bfloat16),
        in_specs=[vmem] * n_messages,
        out_specs=vmem,
        compiler_params=params,
        name="sibling_share",
    )(*received)

    return pl.pallas_call(
        final_kernel,
        out_shape=jax.ShapeDtypeStruct((BEAMS, HEADS * HD), jnp.float32),
        in_specs=[vmem] * (4 + n_messages),
        out_specs=vmem,
        compiler_params=params,
        name="combine",
    )(*received, last, swapped(share, "core"), summed, stats)


def solution(mesh):
    n_batch, n_mp = mesh.devices.shape
    split = jax.sharding.Mesh(
        mesh.devices.reshape(n_batch // 2, 2, n_mp // 2, 2), ("z", "core", "group", "pair")
    )
    batch, mp = ("z", "core"), ("group", "pair")
    return jax.shard_map(
        on_device,
        mesh=split,
        in_specs=(
            P(batch, mp),
            P(batch, mp, None, None),
            P(batch, mp, None, None),
            P(),
            P(),
            P(batch),
        ),
        out_specs=P(batch, mp),
        check_vma=False,
    )
```

```python
import functools

import jax
import jax.numpy as jnp
from jax import lax
from jax.experimental import pallas as pl
from jax.experimental.pallas import tpu as pltpu
from jax.sharding import PartitionSpec as P

HD = 128
GROUP = 16
BEAMS = 16
SUF = 4
HEADS = GROUP // 2
VECS = HEADS * BEAMS
STAT_ROWS = 16
CHUNK = 512

big_negative = -1e30
to_exp2 = HD ** (-0.5) * 1.4426950408889634


def swapped(value, axis):
    return lax.ppermute(value, axis, [(0, 1), (1, 0)])


def shares(n_req):
    both = n_req // 2
    rest = [d for d in range(1, n_req) if d != both]
    return both, (rest[: len(rest) // 2], rest[len(rest) // 2 :])


def exchanged(value, message):
    n_req = lax.axis_size("z")
    both, own = shares(n_req)
    pairs = []
    for z in range(n_req):
        for core in range(2):
            for pair in range(2):
                if message == 0:
                    mask, side = both, core
                else:
                    mask, side = own[core][(message - 1) // 2], (message - 1) % 2
                target = ((z ^ mask) * 2 + core) * 2 + (pair ^ side)
                pairs.append(((z * 2 + core) * 2 + pair, target))
    return lax.ppermute(value, ("z", "core", "pair"), pairs)


def masks_here(n_req):
    both, own = shares(n_req)
    core = lax.axis_index("core")
    return [both] + [jnp.where(core == 0, d0, d1) for d0, d1 in zip(*own)]


def stage_kernel(*refs):
    n = (len(refs) - 1) // 2
    copies = [
        pltpu.make_async_copy(refs[i], refs[n + i], refs[-1].at[i]) for i in range(n)
    ]
    for copy in copies:
        copy.start()
    for copy in copies:
        copy.wait()


def pack_kernel(own_ref, sibling_ref, out_ref):
    core = lax.axis_index("core")
    out_ref[core] = own_ref[...]
    out_ref[1 - core] = sibling_ref[...]


def stacked_heads(q):
    return jnp.concatenate([q[:, h * HD : (h + 1) * HD] for h in range(HEADS)], axis=0)


def scores_of(keys, vectors):
    return lax.dot_general(
        keys, vectors, (((1,), (1,)), ((), ())), preferred_element_type=jnp.float32
    )


def summed_of(values, weights):
    return lax.dot_general(
        values,
        weights.astype(jnp.bfloat16),
        (((0,), (0,)), ((), ())),
        preferred_element_type=jnp.float32,
    )


def merged(parts):
    top = functools.reduce(jnp.maximum, [p[0] for p in parts])
    total = 0.0
    summed = 0.0
    for part_top, part_total, part_summed in parts:
        factor = jnp.exp2((part_top - top) * to_exp2)
        total = total + part_total * factor
        summed = summed + part_summed * factor
    return top, total, summed


def weighted(scores):
    top = jnp.max(scores, axis=0, keepdims=True)
    weights = jnp.exp2((scores - top) * to_exp2)
    return top, jnp.sum(weights, axis=0, keepdims=True), weights


def three_pieces(x):
    first = x.astype(jnp.bfloat16).astype(jnp.float32)
    rest = x - first
    second = rest.astype(jnp.bfloat16).astype(jnp.float32)
    return [first, second, rest - second]


def store_units(ref, parts):
    rows = []
    for i, (top, total, summed) in enumerate(parts):
        ref[i * HD : (i + 1) * HD, :] = summed.astype(jnp.bfloat16)
        rows += three_pieces(top) + three_pieces(total)
    rows.append(jnp.zeros((STAT_ROWS - len(rows), VECS), jnp.float32))
    ref[len(parts) * HD :, :] = jnp.concatenate(rows, axis=0).astype(jnp.bfloat16)


def load_unit(ref, i=0):
    sums = ref.shape[0] - STAT_ROWS
    stats = ref[sums:, :].astype(jnp.float32)
    if isinstance(i, int):
        rows = [stats[6 * i + k : 6 * i + k + 1] for k in range(6)]
    else:
        rows = [jnp.where(i == 0, stats[k : k + 1], stats[6 + k : 7 + k]) for k in range(6)]
    part = ref[pl.ds(pl.multiple_of(i * HD, HD), HD), :]
    return rows[0] + rows[1] + rows[2], rows[3] + rows[4] + rows[5], part.astype(jnp.float32)


def count(left, right):
    return jnp.dot(
        left.astype(jnp.bfloat16), right.astype(jnp.bfloat16), preferred_element_type=jnp.float32
    )


def iota(shape, axis):
    return lax.broadcasted_iota(jnp.int32, shape, axis)


def prompt_part(length, half, prompt_ref, vectors):
    parity = lax.axis_index("pair")
    whole = lax.div(length, 2 * half)
    valid = whole * half + jnp.clip(length - whole * (2 * half) - parity * half, 0, half)
    chunks = [slice(i, i + CHUNK) for i in range(0, prompt_ref.shape[0], CHUNK)]
    scores = [scores_of(prompt_ref[chunk, :HD], vectors) for chunk in chunks]
    place = iota(scores[0].shape, 0)
    scores = [
        jnp.where(place < valid - chunk.start, score, big_negative)
        for chunk, score in zip(chunks, scores)
    ]
    tops = [jnp.max(score, axis=0, keepdims=True) for score in scores]
    top = functools.reduce(jnp.maximum, tops)
    total, summed = 0.0, 0.0
    for chunk, score in zip(chunks, scores):
        weights = jnp.exp2((score - top) * to_exp2)
        total = total + jnp.sum(weights, axis=0, keepdims=True)
        summed = summed + summed_of(prompt_ref[chunk, HD:], weights)
    return top, total, summed


def prepare_kernel(
    capacity, near_ref, table, parents, far_ref,
    home_keys_ref, home_values_ref, keys_ref, values_ref, member_ref, rows_ref, near, sem,
):
    n_req = lax.axis_size("z")
    slots, half, _ = near.shape
    rows = table.shape[1]
    n_batch = rows // BEAMS
    z, core = lax.axis_index("z"), lax.axis_index("core")

    copy = pltpu.make_async_copy(near_ref, near, sem)
    copy.start()

    slot = iota((2 * slots, rows), 0)
    mine = slot < slots
    block = jnp.where(mine, slot, slot - slots) + jnp.where(mine, 2 * z + core, 2 * z + 1 - core) * slots
    named = functools.reduce(
        jnp.logical_or, [table[j : j + 1, :] == block for j in range(SUF)]
    ).astype(jnp.float32)
    group = (iota((rows, n_batch), 0) // BEAMS == iota((rows, n_batch), 1)).astype(jnp.float32)
    hit = jnp.where(count(named, group) > 0.0, 1.0, 0.0)
    left, right = iota((2 * slots, 2 * slots), 0), iota((2 * slots, 2 * slots), 1)
    before = (left // slots == right // slots) & (right < left)
    rank = count(before.astype(jnp.float32), hit)
    taken = (iota((rows, rows), 0) == parents[...]).astype(jnp.float32)
    continued = count(named, taken)

    place = iota((2 * slots, n_batch), 0)
    found = []
    for k in range(2 * capacity):
        holder = k // capacity
        chosen = (hit > 0.0) & (rank == float(k % capacity)) & (place // slots == holder)
        found.append(jnp.sum(jnp.where(chosen, place + 1, 0), axis=0, keepdims=True))
    found = jnp.concatenate(found, axis=0)

    copy.wait()
    requests = [z * 2 + core]
    for mask in masks_here(n_req):
        requests += [(z ^ mask) * 2, (z ^ mask) * 2 + 1]
    for i, request in enumerate(requests):
        lane = iota((rows, VECS), 1)
        spread = iota((rows, VECS), 0) == request * BEAMS + lane % BEAMS
        rows_ref[: 2 * slots, :] = count(continued, spread.astype(jnp.float32))
        rows_ref[2 * slots :, :] = jnp.zeros((8, VECS), jnp.float32)
        mask = iota(found.shape, 1) == request
        picked = jnp.sum(jnp.where(mask, found, 0), axis=1, keepdims=True)
        values = []
        for k in range(2 * capacity):
            index = picked[k, 0]
            row = jnp.where(index > 0, index - 1, 2 * slots)
            member_ref[i, k : k + 1, :] = rows_ref[pl.ds(row, 1), :]
            pool_ref = near if k < capacity else far_ref
            base = 0 if k < capacity else slots
            content = pool_ref[jnp.maximum(index - 1 - base, 0)]
            tokens = slice(k * half, (k + 1) * half)
            if i == 0:
                home_keys_ref[0, tokens, :] = content[:, :HD]
            else:
                keys_ref[i - 1, tokens, :] = content[:, :HD]
            values.append(content[:, HD:])
        values = jnp.concatenate(values, axis=0).T
        if i == 0:
            home_values_ref[0] = values
        else:
            values_ref[i - 1] = values


def all_vectors(own_ref, pair_ref):
    return jnp.concatenate([stacked_heads(own_ref[...]), stacked_heads(pair_ref[...])], axis=0)


def suffix_parts(vectors, keys_ref, values_ref, members, place=0):
    n_slots = members[0].shape[0]
    half = keys_ref.shape[1] // n_slots
    scores = [scores_of(keys_ref[place + i], each) for i, each in enumerate(vectors)]
    softmaxes = []
    for member, score in zip(members, scores):
        member = jnp.concatenate([member] * (score.shape[1] // VECS), axis=1)
        pieces = [
            jnp.where(
                member[k : k + 1, :] > 0.0, score[k * half : (k + 1) * half], big_negative
            )
            for k in range(n_slots)
        ]
        softmaxes.append(weighted(jnp.concatenate(pieces, axis=0)))
    return [
        (
            top,
            total,
            jnp.dot(
                values_ref[place + i], weights.astype(jnp.bfloat16), preferred_element_type=jnp.float32
            ),
        )
        for i, (top, total, weights) in enumerate(softmaxes)
    ]


def half_of(part, side):
    lanes = slice(side * VECS, (side + 1) * VECS)
    return [x[:, lanes] for x in part]


def away_kernel(place, keys_ref, values_ref, member_ref, message_ref, out_ref, *after_ref):
    for ref in after_ref:
        ref[...] = jnp.zeros(ref.shape, jnp.float32)
    vectors = [stacked_heads(message_ref[core]) for core in range(2)]
    members = [member_ref[1 + place + core] for core in range(2)]
    store_units(out_ref, suffix_parts(vectors, keys_ref, values_ref, members, place))


def home_kernel(
    length_ref, keys_ref, values_ref, member_ref, own_ref, pair_ref, prompt_ref, after_ref,
    summed_ref, stats_ref, out_ref,
):
    vectors = all_vectors(own_ref, pair_ref)
    half = keys_ref.shape[1] // member_ref.shape[1]
    (suffix,) = suffix_parts([vectors], keys_ref, values_ref, [member_ref[0]])
    prompt = prompt_part(length_ref[0], half, prompt_ref, vectors)
    part = merged([prompt, suffix])
    top, total, summed_ref[...] = half_of(part, 0)
    stats_ref[...] = jnp.concatenate([top, total, jnp.zeros((6, VECS), jnp.float32)], axis=0)
    store_units(out_ref, [half_of(part, 1)])


def sibling_kernel(*rest):
    units, out_ref = rest[:-1], rest[-1]
    core = lax.axis_index("core")
    store_units(out_ref, [merged([load_unit(unit, 1 - core) for unit in units])])


def final_kernel(*rest):
    units, (last_ref, shared_ref, summed_ref, stats_ref, out_ref) = rest[:-5], rest[-5:]
    core = lax.axis_index("core")
    parts = [load_unit(unit, core) for unit in units]
    parts += [load_unit(last_ref), load_unit(shared_ref)]
    parts.append((stats_ref[0:1], stats_ref[1:2], summed_ref[...]))
    _, total, summed = merged(parts)
    attended = (summed / total).T
    for h in range(HEADS):
        out_ref[:, h * HD : (h + 1) * HD] = attended[h * BEAMS : (h + 1) * BEAMS]


def in_hbm(value):
    return pltpu.with_memory_space_constraint(value, pltpu.HBM)


def on_device(queries, prompt_cache, pool, block_table, parents, lengths):
    n_req = lax.axis_size("z")
    n_batch = 2 * n_req
    ndist = 2 ** (SUF + 1) - 2
    capacity = 2 * ((ndist // 2 + n_batch - 1) // n_batch)
    slots, _, half, width = pool.shape
    tokens = prompt_cache.shape[2]
    rows = block_table.shape[0]
    vmem = pl.BlockSpec(memory_space=pltpu.VMEM)
    params = pltpu.CompilerParams(vmem_limit_bytes=32 * 2**20)
    some = pl.CostEstimate(flops=2 * 10**8, bytes_accessed=2**21, transcendentals=0)
    early = pl.CostEstimate(flops=2 * 10**10, bytes_accessed=0, transcendentals=0)

    hbm = pl.BlockSpec(memory_space=pltpu.HBM)
    near = pool.reshape(slots, half, width)
    far = swapped(near, "core")
    other = swapped(queries, "pair")
    staged = [queries, block_table.T, parents.reshape(1, rows)]
    own, table, row_parents = pl.pallas_call(
        stage_kernel,
        out_shape=tuple(pltpu.VMEM(each.shape, each.dtype) for each in staged),
        in_specs=[hbm] * len(staged),
        out_specs=(vmem,) * len(staged),
        scratch_shapes=[pltpu.SemaphoreType.DMA((len(staged),))],
        compiler_params=params,
        name="stage",
    )(*[in_hbm(each) for each in staged])
    both = pl.pallas_call(
        pack_kernel,
        out_shape=pltpu.VMEM((2,) + queries.shape, jnp.bfloat16),
        in_specs=[vmem] * 2,
        out_specs=vmem,
        compiler_params=params,
        cost_estimate=early,
        name="both_cores",
    )(own, swapped(queries, "core"))
    n_messages = n_req - 1
    order = [1, 0] + list(range(n_messages - 1, 1, -1)) if n_messages > 1 else [0]
    messages = {k: exchanged(both, k) for k in order}

    home_keys, home_values, keys, values, member = pl.pallas_call(
        functools.partial(prepare_kernel, capacity),
        out_shape=(
            pltpu.VMEM((1, 2 * capacity * half, HD), jnp.bfloat16),
            pltpu.VMEM((1, HD, 2 * capacity * half), jnp.bfloat16),
            pltpu.VMEM((n_req, 2 * capacity * half, HD), jnp.bfloat16),
            pltpu.VMEM((n_req, HD, 2 * capacity * half), jnp.bfloat16),
            pltpu.VMEM((1 + n_req, 2 * capacity, VECS), jnp.float32),
        ),
        in_specs=[hbm] + [vmem] * 3,
        out_specs=(vmem,) * 5,
        scratch_shapes=[
            pltpu.VMEM((2 * slots + 8, VECS), jnp.float32),
            pltpu.VMEM((slots, half, width), jnp.bfloat16),
            pltpu.SemaphoreType.DMA,
        ],
        compiler_params=params,
        cost_estimate=some,
        name="prepare",
    )(
        in_hbm(near),
        table,
        row_parents,
        far,
    )

    received, after = [], []
    for k in order:
        out = [pltpu.VMEM((2 * HD + STAT_ROWS, VECS), jnp.bfloat16)]
        if k == 0:
            out.append(pltpu.VMEM((8, VECS), jnp.float32))
        units, *token = pl.pallas_call(
            functools.partial(away_kernel, 2 * ((k + 1) // 2)),
            out_shape=out,
            in_specs=[vmem] * 4,
            out_specs=[vmem] * len(out),
            compiler_params=params,
            cost_estimate=some,
            name="suffix_away",
        )(keys, values, member, messages[k])
        received.append(exchanged(units, k))
        after += token

    summed, stats, given = pl.pallas_call(
        home_kernel,
        out_shape=(
            pltpu.VMEM((HD, VECS), jnp.float32),
            pltpu.VMEM((8, VECS), jnp.float32),
            pltpu.VMEM((HD + STAT_ROWS, VECS), jnp.bfloat16),
        ),
        in_specs=[pl.BlockSpec(memory_space=pltpu.SMEM)] + [vmem] * 7,
        out_specs=(vmem,) * 3,
        compiler_params=params,
        cost_estimate=pl.CostEstimate(
            flops=8 * tokens * VECS * HD, bytes_accessed=2 * tokens * width, transcendentals=0
        ),
        name="home_part",
    )(lengths, home_keys, home_values, member, own, other, prompt_cache.reshape(tokens, width), *after)
    last = swapped(given, "pair")

    share = pl.pallas_call(
        sibling_kernel,
        out_shape=pltpu.VMEM((HD + STAT_ROWS, VECS), jnp.bfloat16),
        in_specs=[vmem] * n_messages,
        out_specs=vmem,
        compiler_params=params,
        name="sibling_share",
    )(*received)

    return pl.pallas_call(
        final_kernel,
        out_shape=jax.ShapeDtypeStruct((BEAMS, HEADS * HD), jnp.float32),
        in_specs=[vmem] * (4 + n_messages),
        out_specs=vmem,
        compiler_params=params,
        name="combine",
    )(*received, last, swapped(share, "core"), summed, stats)


def solution(mesh):
    n_batch, n_mp = mesh.devices.shape
    split = jax.sharding.Mesh(
        mesh.devices.reshape(n_batch // 2, 2, n_mp // 2, 2), ("z", "core", "group", "pair")
    )
    batch, mp = ("z", "core"), ("group", "pair")
    return jax.shard_map(
        on_device,
        mesh=split,
        in_specs=(
            P(batch, mp),
            P(batch, mp, None, None),
            P(batch, mp, None, None),
            P(),
            P(),
            P(batch),
        ),
        out_specs=P(batch, mp),
        check_vma=False,
    )
```

```python
import functools

import jax
import jax.numpy as jnp
from jax import lax
from jax.experimental import pallas as pl
from jax.experimental.pallas import tpu as pltpu
from jax.sharding import PartitionSpec as P

HD = 128
GROUP = 16
BEAMS = 16
SUF = 4
HEADS = GROUP // 2
VECS = HEADS * BEAMS
STAT_ROWS = 16
CHUNK = 512

big_negative = -1e30
to_exp2 = HD ** (-0.5) * 1.4426950408889634


def swapped(value, axis):
    return lax.ppermute(value, axis, [(0, 1), (1, 0)])


def shares(n_req):
    both = n_req // 2
    rest = [d for d in range(1, n_req) if d != both]
    return both, (rest[: len(rest) // 2], rest[len(rest) // 2 :])


def exchanged(value, message):
    n_req = lax.axis_size("z")
    both, own = shares(n_req)
    pairs = []
    for z in range(n_req):
        for core in range(2):
            for pair in range(2):
                if message == 0:
                    mask, side = both, core
                else:
                    mask, side = own[core][(message - 1) // 2], (message - 1) % 2
                target = ((z ^ mask) * 2 + core) * 2 + (pair ^ side)
                pairs.append(((z * 2 + core) * 2 + pair, target))
    return lax.ppermute(value, ("z", "core", "pair"), pairs)


def masks_here(n_req):
    both, own = shares(n_req)
    core = lax.axis_index("core")
    return [both] + [jnp.where(core == 0, d0, d1) for d0, d1 in zip(*own)]


def stage_kernel(*refs):
    n = (len(refs) - 1) // 2
    copies = [
        pltpu.make_async_copy(refs[i], refs[n + i], refs[-1].at[i]) for i in range(n)
    ]
    for copy in copies:
        copy.start()
    for copy in copies:
        copy.wait()


def pack_kernel(own_ref, sibling_ref, out_ref):
    core = lax.axis_index("core")
    out_ref[core] = own_ref[...]
    out_ref[1 - core] = sibling_ref[...]


def stacked_heads(q):
    return jnp.concatenate([q[:, h * HD : (h + 1) * HD] for h in range(HEADS)], axis=0)


def scores_of(keys, vectors):
    return lax.dot_general(
        keys, vectors, (((1,), (1,)), ((), ())), preferred_element_type=jnp.float32
    )


def summed_of(values, weights):
    return lax.dot_general(
        values,
        weights.astype(jnp.bfloat16),
        (((0,), (0,)), ((), ())),
        preferred_element_type=jnp.float32,
    )


def merged(parts):
    top = functools.reduce(jnp.maximum, [p[0] for p in parts])
    total = 0.0
    summed = 0.0
    for part_top, part_total, part_summed in parts:
        factor = jnp.exp2((part_top - top) * to_exp2)
        total = total + part_total * factor
        summed = summed + part_summed * factor
    return top, total, summed


def weighted(scores):
    top = jnp.max(scores, axis=0, keepdims=True)
    weights = jnp.exp2((scores - top) * to_exp2)
    return top, jnp.sum(weights, axis=0, keepdims=True), weights


def three_pieces(x):
    first = x.astype(jnp.bfloat16).astype(jnp.float32)
    rest = x - first
    second = rest.astype(jnp.bfloat16).astype(jnp.float32)
    return [first, second, rest - second]


def store_units(ref, parts):
    rows = []
    for i, (top, total, summed) in enumerate(parts):
        ref[i * HD : (i + 1) * HD, :] = summed.astype(jnp.bfloat16)
        rows += three_pieces(top) + three_pieces(total)
    rows.append(jnp.zeros((STAT_ROWS - len(rows), VECS), jnp.float32))
    ref[len(parts) * HD :, :] = jnp.concatenate(rows, axis=0).astype(jnp.bfloat16)


def load_unit(ref, i=0):
    sums = ref.shape[0] - STAT_ROWS
    stats = ref[sums:, :].astype(jnp.float32)
    if isinstance(i, int):
        rows = [stats[6 * i + k : 6 * i + k + 1] for k in range(6)]
    else:
        rows = [jnp.where(i == 0, stats[k : k + 1], stats[6 + k : 7 + k]) for k in range(6)]
    part = ref[pl.ds(pl.multiple_of(i * HD, HD), HD), :]
    return rows[0] + rows[1] + rows[2], rows[3] + rows[4] + rows[5], part.astype(jnp.float32)


def count(left, right):
    return jnp.dot(
        left.astype(jnp.bfloat16), right.astype(jnp.bfloat16), preferred_element_type=jnp.float32
    )


def iota(shape, axis):
    return lax.broadcasted_iota(jnp.int32, shape, axis)


def prompt_part(length, half, prompt_ref, vectors):
    parity = lax.axis_index("pair")
    whole = lax.div(length, 2 * half)
    valid = whole * half + jnp.clip(length - whole * (2 * half) - parity * half, 0, half)
    chunks = [slice(i, i + CHUNK) for i in range(0, prompt_ref.shape[0], CHUNK)]
    scores = [scores_of(prompt_ref[chunk, :HD], vectors) for chunk in chunks]
    place = iota(scores[0].shape, 0)
    scores = [
        jnp.where(place < valid - chunk.start, score, big_negative)
        for chunk, score in zip(chunks, scores)
    ]
    tops = [jnp.max(score, axis=0, keepdims=True) for score in scores]
    top = functools.reduce(jnp.maximum, tops)
    total, summed = 0.0, 0.0
    for chunk, score in zip(chunks, scores):
        weights = jnp.exp2((score - top) * to_exp2)
        total = total + jnp.sum(weights, axis=0, keepdims=True)
        summed = summed + summed_of(prompt_ref[chunk, HD:], weights)
    return top, total, summed


def prepare_kernel(
    capacity, near_ref, table, parents, far_ref,
    home_keys_ref, home_values_ref, keys_ref, values_ref, member_ref, rows_ref, near, sem,
):
    n_req = lax.axis_size("z")
    slots, half, _ = near.shape
    rows = table.shape[1]
    n_batch = rows // BEAMS
    z, core = lax.axis_index("z"), lax.axis_index("core")

    copy = pltpu.make_async_copy(near_ref, near, sem)
    copy.start()

    slot = iota((2 * slots, rows), 0)
    mine = slot < slots
    block = jnp.where(mine, slot, slot - slots) + jnp.where(mine, 2 * z + core, 2 * z + 1 - core) * slots
    named = functools.reduce(
        jnp.logical_or, [table[j : j + 1, :] == block for j in range(SUF)]
    ).astype(jnp.float32)
    group = (iota((rows, n_batch), 0) // BEAMS == iota((rows, n_batch), 1)).astype(jnp.float32)
    hit = jnp.where(count(named, group) > 0.0, 1.0, 0.0)
    left, right = iota((2 * slots, 2 * slots), 0), iota((2 * slots, 2 * slots), 1)
    before = (left // slots == right // slots) & (right < left)
    rank = count(before.astype(jnp.float32), hit)
    taken = (iota((rows, rows), 0) == parents[...]).astype(jnp.float32)
    continued = count(named, taken)

    place = iota((2 * slots, n_batch), 0)
    found = []
    for k in range(2 * capacity):
        holder = k // capacity
        chosen = (hit > 0.0) & (rank == float(k % capacity)) & (place // slots == holder)
        found.append(jnp.sum(jnp.where(chosen, place + 1, 0), axis=0, keepdims=True))
    found = jnp.concatenate(found, axis=0)

    copy.wait()
    requests = [z * 2 + core]
    for mask in masks_here(n_req):
        requests += [(z ^ mask) * 2, (z ^ mask) * 2 + 1]
    for i, request in enumerate(requests):
        lane = iota((rows, VECS), 1)
        spread = iota((rows, VECS), 0) == request * BEAMS + lane % BEAMS
        rows_ref[: 2 * slots, :] = count(continued, spread.astype(jnp.float32))
        rows_ref[2 * slots :, :] = jnp.zeros((8, VECS), jnp.float32)
        mask = iota(found.shape, 1) == request
        picked = jnp.sum(jnp.where(mask, found, 0), axis=1, keepdims=True)
        values = []
        for k in range(2 * capacity):
            index = picked[k, 0]
            row = jnp.where(index > 0, index - 1, 2 * slots)
            member_ref[i, k : k + 1, :] = rows_ref[pl.ds(row, 1), :]
            pool_ref = near if k < capacity else far_ref
            base = 0 if k < capacity else slots
            content = pool_ref[jnp.maximum(index - 1 - base, 0)]
            tokens = slice(k * half, (k + 1) * half)
            if i == 0:
                home_keys_ref[0, tokens, :] = content[:, :HD]
            else:
                keys_ref[i - 1, tokens, :] = content[:, :HD]
            values.append(content[:, HD:])
        values = jnp.concatenate(values, axis=0).T
        if i == 0:
            home_values_ref[0] = values
        else:
            values_ref[i - 1] = values


def all_vectors(own_ref, pair_ref):
    return jnp.concatenate([stacked_heads(own_ref[...]), stacked_heads(pair_ref[...])], axis=0)


def suffix_parts(vectors, keys_ref, values_ref, members, place=0):
    n_slots = members[0].shape[0]
    half = keys_ref.shape[1] // n_slots
    scores = [scores_of(keys_ref[place + i], each) for i, each in enumerate(vectors)]
    softmaxes = []
    for member, score in zip(members, scores):
        member = jnp.concatenate([member] * (score.shape[1] // VECS), axis=1)
        pieces = [
            jnp.where(
                member[k : k + 1, :] > 0.0, score[k * half : (k + 1) * half], big_negative
            )
            for k in range(n_slots)
        ]
        softmaxes.append(weighted(jnp.concatenate(pieces, axis=0)))
    return [
        (
            top,
            total,
            jnp.dot(
                values_ref[place + i], weights.astype(jnp.bfloat16), preferred_element_type=jnp.float32
            ),
        )
        for i, (top, total, weights) in enumerate(softmaxes)
    ]


def half_of(part, side):
    lanes = slice(side * VECS, (side + 1) * VECS)
    return [x[:, lanes] for x in part]


def away_kernel(place, keys_ref, values_ref, member_ref, message_ref, out_ref, *after_ref):
    for ref in after_ref:
        ref[...] = jnp.zeros(ref.shape, jnp.float32)
    vectors = [stacked_heads(message_ref[core]) for core in range(2)]
    members = [member_ref[1 + place + core] for core in range(2)]
    store_units(out_ref, suffix_parts(vectors, keys_ref, values_ref, members, place))


def home_kernel(
    length_ref, keys_ref, values_ref, member_ref, own_ref, pair_ref, prompt_ref, after_ref,
    summed_ref, stats_ref, out_ref,
):
    vectors = all_vectors(own_ref, pair_ref)
    half = keys_ref.shape[1] // member_ref.shape[1]
    (suffix,) = suffix_parts([vectors], keys_ref, values_ref, [member_ref[0]])
    prompt = prompt_part(length_ref[0], half, prompt_ref, vectors)
    part = merged([prompt, suffix])
    top, total, summed_ref[...] = half_of(part, 0)
    stats_ref[...] = jnp.concatenate([top, total, jnp.zeros((6, VECS), jnp.float32)], axis=0)
    store_units(out_ref, [half_of(part, 1)])


def sibling_kernel(*rest):
    units, out_ref = rest[:-1], rest[-1]
    core = lax.axis_index("core")
    store_units(out_ref, [merged([load_unit(unit, 1 - core) for unit in units])])


def final_kernel(*rest):
    units, (last_ref, shared_ref, summed_ref, stats_ref, out_ref) = rest[:-5], rest[-5:]
    core = lax.axis_index("core")
    parts = [load_unit(unit, core) for unit in units]
    parts += [load_unit(last_ref), load_unit(shared_ref)]
    parts.append((stats_ref[0:1], stats_ref[1:2], summed_ref[...]))
    _, total, summed = merged(parts)
    attended = (summed / total).T
    for h in range(HEADS):
        out_ref[:, h * HD : (h + 1) * HD] = attended[h * BEAMS : (h + 1) * BEAMS]


def in_hbm(value):
    return pltpu.with_memory_space_constraint(value, pltpu.HBM)


def on_device(queries, prompt_cache, pool, block_table, parents, lengths):
    n_req = lax.axis_size("z")
    n_batch = 2 * n_req
    ndist = 2 ** (SUF + 1) - 2
    capacity = 2 * ((ndist // 2 + n_batch - 1) // n_batch)
    slots, _, half, width = pool.shape
    tokens = prompt_cache.shape[2]
    rows = block_table.shape[0]
    vmem = pl.BlockSpec(memory_space=pltpu.VMEM)
    params = pltpu.CompilerParams(vmem_limit_bytes=32 * 2**20)
    some = pl.CostEstimate(flops=2 * 10**8, bytes_accessed=2**21, transcendentals=0)
    early = pl.CostEstimate(flops=2 * 10**10, bytes_accessed=0, transcendentals=0)

    hbm = pl.BlockSpec(memory_space=pltpu.HBM)
    near = pool.reshape(slots, half, width)
    far = swapped(near, "core")
    other = swapped(queries, "pair")
    staged = [queries, block_table.T, parents.reshape(1, rows)]
    own, table, row_parents = pl.pallas_call(
        stage_kernel,
        out_shape=tuple(pltpu.VMEM(each.shape, each.dtype) for each in staged),
        in_specs=[hbm] * len(staged),
        out_specs=(vmem,) * len(staged),
        scratch_shapes=[pltpu.SemaphoreType.DMA((len(staged),))],
        compiler_params=params,
        name="stage",
    )(*[in_hbm(each) for each in staged])
    both = pl.pallas_call(
        pack_kernel,
        out_shape=pltpu.VMEM((2,) + queries.shape, jnp.bfloat16),
        in_specs=[vmem] * 2,
        out_specs=vmem,
        compiler_params=params,
        cost_estimate=early,
        name="both_cores",
    )(own, swapped(queries, "core"))
    n_messages = n_req - 1
    order = [1, 0] + list(range(n_messages - 1, 1, -1)) if n_messages > 1 else [0]
    messages = {k: exchanged(both, k) for k in order}

    home_keys, home_values, keys, values, member = pl.pallas_call(
        functools.partial(prepare_kernel, capacity),
        out_shape=(
            pltpu.VMEM((1, 2 * capacity * half, HD), jnp.bfloat16),
            pltpu.VMEM((1, HD, 2 * capacity * half), jnp.bfloat16),
            pltpu.VMEM((n_req, 2 * capacity * half, HD), jnp.bfloat16),
            pltpu.VMEM((n_req, HD, 2 * capacity * half), jnp.bfloat16),
            pltpu.VMEM((1 + n_req, 2 * capacity, VECS), jnp.float32),
        ),
        in_specs=[hbm] + [vmem] * 3,
        out_specs=(vmem,) * 5,
        scratch_shapes=[
            pltpu.VMEM((2 * slots + 8, VECS), jnp.float32),
            pltpu.VMEM((slots, half, width), jnp.bfloat16),
            pltpu.SemaphoreType.DMA,
        ],
        compiler_params=params,
        cost_estimate=some,
        name="prepare",
    )(
        in_hbm(near),
        table,
        row_parents,
        far,
    )

    received, after = [], []
    for k in order:
        out = [pltpu.VMEM((2 * HD + STAT_ROWS, VECS), jnp.bfloat16)]
        if k == order[0]:
            out.append(pltpu.VMEM((8, VECS), jnp.float32))
        units, *token = pl.pallas_call(
            functools.partial(away_kernel, 2 * ((k + 1) // 2)),
            out_shape=out,
            in_specs=[vmem] * 4,
            out_specs=[vmem] * len(out),
            compiler_params=params,
            cost_estimate=some,
            name="suffix_away",
        )(keys, values, member, messages[k])
        received.append(exchanged(units, k))
        after += token

    summed, stats, given = pl.pallas_call(
        home_kernel,
        out_shape=(
            pltpu.VMEM((HD, VECS), jnp.float32),
            pltpu.VMEM((8, VECS), jnp.float32),
            pltpu.VMEM((HD + STAT_ROWS, VECS), jnp.bfloat16),
        ),
        in_specs=[pl.BlockSpec(memory_space=pltpu.SMEM)] + [vmem] * 7,
        out_specs=(vmem,) * 3,
        compiler_params=params,
        cost_estimate=pl.CostEstimate(
            flops=8 * tokens * VECS * HD, bytes_accessed=2 * tokens * width, transcendentals=0
        ),
        name="home_part",
    )(lengths, home_keys, home_values, member, own, other, prompt_cache.reshape(tokens, width), *after)
    last = swapped(given, "pair")

    share = pl.pallas_call(
        sibling_kernel,
        out_shape=pltpu.VMEM((HD + STAT_ROWS, VECS), jnp.bfloat16),
        in_specs=[vmem] * n_messages,
        out_specs=vmem,
        compiler_params=params,
        name="sibling_share",
    )(*received)

    return pl.pallas_call(
        final_kernel,
        out_shape=jax.ShapeDtypeStruct((BEAMS, HEADS * HD), jnp.float32),
        in_specs=[vmem] * (4 + n_messages),
        out_specs=vmem,
        compiler_params=params,
        name="combine",
    )(*received, last, swapped(share, "core"), summed, stats)


def solution(mesh):
    n_batch, n_mp = mesh.devices.shape
    split = jax.sharding.Mesh(
        mesh.devices.reshape(n_batch // 2, 2, n_mp // 2, 2), ("z", "core", "group", "pair")
    )
    batch, mp = ("z", "core"), ("group", "pair")
    return jax.shard_map(
        on_device,
        mesh=split,
        in_specs=(
            P(batch, mp),
            P(batch, mp, None, None),
            P(batch, mp, None, None),
            P(),
            P(),
            P(batch),
        ),
        out_specs=P(batch, mp),
        check_vma=False,
    )
```

```python
import functools

import jax
import jax.numpy as jnp
from jax import lax
from jax.experimental import pallas as pl
from jax.experimental.pallas import tpu as pltpu
from jax.sharding import PartitionSpec as P

HD = 128
GROUP = 16
BEAMS = 16
SUF = 4
HEADS = GROUP // 2
VECS = HEADS * BEAMS
STAT_ROWS = 16
CHUNK = 512
SURELY_VALID = 1024

big_negative = -1e30
to_exp2 = HD ** (-0.5) * 1.4426950408889634


def swapped(value, axis):
    return lax.ppermute(value, axis, [(0, 1), (1, 0)])


def shares(n_req):
    both = n_req // 2
    rest = [d for d in range(1, n_req) if d != both]
    return both, (rest[: len(rest) // 2], rest[len(rest) // 2 :])


def exchanged(value, message):
    n_req = lax.axis_size("z")
    both, own = shares(n_req)
    pairs = []
    for z in range(n_req):
        for core in range(2):
            for pair in range(2):
                if message == 0:
                    mask, side = both, core
                else:
                    mask, side = own[core][(message - 1) // 2], (message - 1) % 2
                target = ((z ^ mask) * 2 + core) * 2 + (pair ^ side)
                pairs.append(((z * 2 + core) * 2 + pair, target))
    return lax.ppermute(value, ("z", "core", "pair"), pairs)


def masks_here(n_req):
    both, own = shares(n_req)
    core = lax.axis_index("core")
    return [both] + [jnp.where(core == 0, d0, d1) for d0, d1 in zip(*own)]


def stage_kernel(*refs):
    n = (len(refs) - 1) // 2
    copies = [
        pltpu.make_async_copy(refs[i], refs[n + i], refs[-1].at[i]) for i in range(n)
    ]
    for copy in copies:
        copy.start()
    for copy in copies:
        copy.wait()


def pack_kernel(own_ref, sibling_ref, out_ref):
    core = lax.axis_index("core")
    out_ref[core] = own_ref[...]
    out_ref[1 - core] = sibling_ref[...]


def stacked_heads(q):
    return jnp.concatenate([q[:, h * HD : (h + 1) * HD] for h in range(HEADS)], axis=0)


def scores_of(keys, vectors):
    return lax.dot_general(
        keys, vectors, (((1,), (1,)), ((), ())), preferred_element_type=jnp.float32
    )


def summed_of(values, weights):
    return lax.dot_general(
        values,
        weights.astype(jnp.bfloat16),
        (((0,), (0,)), ((), ())),
        preferred_element_type=jnp.float32,
    )


def merged(parts):
    top = functools.reduce(jnp.maximum, [p[0] for p in parts])
    total = 0.0
    summed = 0.0
    for part_top, part_total, part_summed in parts:
        factor = jnp.exp2((part_top - top) * to_exp2)
        total = total + part_total * factor
        summed = summed + part_summed * factor
    return top, total, summed


def weighted(scores):
    top = jnp.max(scores, axis=0, keepdims=True)
    weights = jnp.exp2((scores - top) * to_exp2)
    return top, jnp.sum(weights, axis=0, keepdims=True), weights


def three_pieces(x):
    first = x.astype(jnp.bfloat16).astype(jnp.float32)
    rest = x - first
    second = rest.astype(jnp.bfloat16).astype(jnp.float32)
    return [first, second, rest - second]


def store_units(ref, parts):
    rows = []
    for i, (top, total, summed) in enumerate(parts):
        ref[i * HD : (i + 1) * HD, :] = summed.astype(jnp.bfloat16)
        rows += three_pieces(top) + three_pieces(total)
    rows.append(jnp.zeros((STAT_ROWS - len(rows), VECS), jnp.float32))
    ref[len(parts) * HD :, :] = jnp.concatenate(rows, axis=0).astype(jnp.bfloat16)


def load_unit(ref, i=0):
    sums = ref.shape[0] - STAT_ROWS
    stats = ref[sums:, :].astype(jnp.float32)
    if isinstance(i, int):
        rows = [stats[6 * i + k : 6 * i + k + 1] for k in range(6)]
    else:
        rows = [jnp.where(i == 0, stats[k : k + 1], stats[6 + k : 7 + k]) for k in range(6)]
    part = ref[pl.ds(pl.multiple_of(i * HD, HD), HD), :]
    return rows[0] + rows[1] + rows[2], rows[3] + rows[4] + rows[5], part.astype(jnp.float32)


def count(left, right):
    return jnp.dot(
        left.astype(jnp.bfloat16), right.astype(jnp.bfloat16), preferred_element_type=jnp.float32
    )


def iota(shape, axis):
    return lax.broadcasted_iota(jnp.int32, shape, axis)


def prompt_part(length, half, prompt_ref, vectors):
    parity = lax.axis_index("pair")
    whole = lax.div(length, 2 * half)
    valid = whole * half + jnp.clip(length - whole * (2 * half) - parity * half, 0, half)
    chunks = [slice(i, i + CHUNK) for i in range(0, prompt_ref.shape[0], CHUNK)]
    scores = [scores_of(prompt_ref[chunk, :HD], vectors) for chunk in chunks]
    place = iota(scores[0].shape, 0)
    scores = [
        score
        if chunk.stop <= SURELY_VALID
        else jnp.where(place < valid - chunk.start, score, big_negative)
        for chunk, score in zip(chunks, scores)
    ]
    tops = [jnp.max(score, axis=0, keepdims=True) for score in scores]
    top = functools.reduce(jnp.maximum, tops)
    total, summed = 0.0, 0.0
    for chunk, score in zip(chunks, scores):
        weights = jnp.exp2((score - top) * to_exp2)
        total = total + jnp.sum(weights, axis=0, keepdims=True)
        summed = summed + summed_of(prompt_ref[chunk, HD:], weights)
    return top, total, summed


def prepare_kernel(
    capacity, near, table, parents, far_ref,
    home_keys_ref, home_values_ref, keys_ref, values_ref, member_ref, rows_ref,
):
    n_req = lax.axis_size("z")
    slots, half, _ = near.shape
    rows = table.shape[1]
    n_batch = rows // BEAMS
    z, core = lax.axis_index("z"), lax.axis_index("core")

    slot = iota((2 * slots, rows), 0)
    mine = slot < slots
    block = jnp.where(mine, slot, slot - slots) + jnp.where(mine, 2 * z + core, 2 * z + 1 - core) * slots
    named = functools.reduce(
        jnp.logical_or, [table[j : j + 1, :] == block for j in range(SUF)]
    ).astype(jnp.float32)
    group = (iota((rows, n_batch), 0) // BEAMS == iota((rows, n_batch), 1)).astype(jnp.float32)
    hit = jnp.where(count(named, group) > 0.0, 1.0, 0.0)
    left, right = iota((2 * slots, 2 * slots), 0), iota((2 * slots, 2 * slots), 1)
    before = (left // slots == right // slots) & (right < left)
    rank = count(before.astype(jnp.float32), hit)
    taken = (iota((rows, rows), 0) == parents[...]).astype(jnp.float32)
    continued = count(named, taken)

    place = iota((2 * slots, n_batch), 0)
    found = []
    for k in range(2 * capacity):
        holder = k // capacity
        chosen = (hit > 0.0) & (rank == float(k % capacity)) & (place // slots == holder)
        found.append(jnp.sum(jnp.where(chosen, place + 1, 0), axis=0, keepdims=True))
    found = jnp.concatenate(found, axis=0)

    requests = [z * 2 + core]
    for mask in masks_here(n_req):
        requests += [(z ^ mask) * 2, (z ^ mask) * 2 + 1]
    for i, request in enumerate(requests):
        lane = iota((rows, VECS), 1)
        spread = iota((rows, VECS), 0) == request * BEAMS + lane % BEAMS
        rows_ref[: 2 * slots, :] = count(continued, spread.astype(jnp.float32))
        rows_ref[2 * slots :, :] = jnp.zeros((8, VECS), jnp.float32)
        mask = iota(found.shape, 1) == request
        picked = jnp.sum(jnp.where(mask, found, 0), axis=1, keepdims=True)
        values = []
        for k in range(2 * capacity):
            index = picked[k, 0]
            row = jnp.where(index > 0, index - 1, 2 * slots)
            member_ref[i, k : k + 1, :] = rows_ref[pl.ds(row, 1), :]
            pool_ref = near if k < capacity else far_ref
            base = 0 if k < capacity else slots
            content = pool_ref[jnp.maximum(index - 1 - base, 0)]
            tokens = slice(k * half, (k + 1) * half)
            if i == 0:
                home_keys_ref[0, tokens, :] = content[:, :HD]
            else:
                keys_ref[i - 1, tokens, :] = content[:, :HD]
            values.append(content[:, HD:])
        values = jnp.concatenate(values, axis=0).T
        if i == 0:
            home_values_ref[0] = values
        else:
            values_ref[i - 1] = values


def all_vectors(own_ref, pair_ref):
    return jnp.concatenate([stacked_heads(own_ref[...]), stacked_heads(pair_ref[...])], axis=0)


def suffix_parts(vectors, keys_ref, values_ref, members, place=0):
    n_slots = members[0].shape[0]
    half = keys_ref.shape[1] // n_slots
    scores = [scores_of(keys_ref[place + i], each) for i, each in enumerate(vectors)]
    softmaxes = []
    for member, score in zip(members, scores):
        member = jnp.concatenate([member] * (score.shape[1] // VECS), axis=1)
        pieces = [
            jnp.where(
                member[k : k + 1, :] > 0.0, score[k * half : (k + 1) * half], big_negative
            )
            for k in range(n_slots)
        ]
        softmaxes.append(weighted(jnp.concatenate(pieces, axis=0)))
    return [
        (
            top,
            total,
            jnp.dot(
                values_ref[place + i], weights.astype(jnp.bfloat16), preferred_element_type=jnp.float32
            ),
        )
        for i, (top, total, weights) in enumerate(softmaxes)
    ]


def half_of(part, side):
    lanes = slice(side * VECS, (side + 1) * VECS)
    return [x[:, lanes] for x in part]


def away_kernel(place, keys_ref, values_ref, member_ref, message_ref, out_ref, *after_ref):
    for ref in after_ref:
        ref[...] = jnp.zeros(ref.shape, jnp.float32)
    vectors = [stacked_heads(message_ref[core]) for core in range(2)]
    members = [member_ref[1 + place + core] for core in range(2)]
    store_units(out_ref, suffix_parts(vectors, keys_ref, values_ref, members, place))


def home_kernel(
    length_ref, keys_ref, values_ref, member_ref, own_ref, pair_ref, prompt_ref, after_ref,
    summed_ref, stats_ref, out_ref,
):
    vectors = all_vectors(own_ref, pair_ref)
    half = keys_ref.shape[1] // member_ref.shape[1]
    (suffix,) = suffix_parts([vectors], keys_ref, values_ref, [member_ref[0]])
    prompt = prompt_part(length_ref[0], half, prompt_ref, vectors)
    part = merged([prompt, suffix])
    top, total, summed_ref[...] = half_of(part, 0)
    stats_ref[...] = jnp.concatenate([top, total, jnp.zeros((6, VECS), jnp.float32)], axis=0)
    store_units(out_ref, [half_of(part, 1)])


def sibling_kernel(*rest):
    units, out_ref = rest[:-1], rest[-1]
    core = lax.axis_index("core")
    store_units(out_ref, [merged([load_unit(unit, 1 - core) for unit in units])])


def final_kernel(*rest):
    units, (last_ref, shared_ref, summed_ref, stats_ref, out_ref) = rest[:-5], rest[-5:]
    core = lax.axis_index("core")
    parts = [load_unit(unit, core) for unit in units]
    parts += [load_unit(last_ref), load_unit(shared_ref)]
    parts.append((stats_ref[0:1], stats_ref[1:2], summed_ref[...]))
    _, total, summed = merged(parts)
    attended = (summed / total).T
    for h in range(HEADS):
        out_ref[:, h * HD : (h + 1) * HD] = attended[h * BEAMS : (h + 1) * BEAMS]


def in_hbm(value):
    return pltpu.with_memory_space_constraint(value, pltpu.HBM)


def on_device(queries, prompt_cache, pool, block_table, parents, lengths):
    n_req = lax.axis_size("z")
    n_batch = 2 * n_req
    ndist = 2 ** (SUF + 1) - 2
    capacity = 2 * ((ndist // 2 + n_batch - 1) // n_batch)
    slots, _, half, width = pool.shape
    tokens = prompt_cache.shape[2]
    rows = block_table.shape[0]
    vmem = pl.BlockSpec(memory_space=pltpu.VMEM)
    params = pltpu.CompilerParams(vmem_limit_bytes=32 * 2**20)
    some = pl.CostEstimate(flops=2 * 10**8, bytes_accessed=2**21, transcendentals=0)
    early = pl.CostEstimate(flops=2 * 10**10, bytes_accessed=0, transcendentals=0)

    hbm = pl.BlockSpec(memory_space=pltpu.HBM)
    near = pool.reshape(slots, half, width)
    far = swapped(near, "core")
    other = swapped(queries, "pair")
    staged = [queries, block_table.T, parents.reshape(1, rows)]
    own, table, row_parents = pl.pallas_call(
        stage_kernel,
        out_shape=tuple(pltpu.VMEM(each.shape, each.dtype) for each in staged),
        in_specs=[hbm] * len(staged),
        out_specs=(vmem,) * len(staged),
        scratch_shapes=[pltpu.SemaphoreType.DMA((len(staged),))],
        compiler_params=params,
        name="stage",
    )(*[in_hbm(each) for each in staged])
    both = pl.pallas_call(
        pack_kernel,
        out_shape=pltpu.VMEM((2,) + queries.shape, jnp.bfloat16),
        in_specs=[vmem] * 2,
        out_specs=vmem,
        compiler_params=params,
        cost_estimate=early,
        name="both_cores",
    )(own, swapped(queries, "core"))
    n_messages = n_req - 1
    order = [1, 0] + list(range(n_messages - 1, 1, -1)) if n_messages > 1 else [0]
    messages = {k: exchanged(both, k) for k in order}

    home_keys, home_values, keys, values, member = pl.pallas_call(
        functools.partial(prepare_kernel, capacity),
        out_shape=(
            pltpu.VMEM((1, 2 * capacity * half, HD), jnp.bfloat16),
            pltpu.VMEM((1, HD, 2 * capacity * half), jnp.bfloat16),
            pltpu.VMEM((n_req, 2 * capacity * half, HD), jnp.bfloat16),
            pltpu.VMEM((n_req, HD, 2 * capacity * half), jnp.bfloat16),
            pltpu.VMEM((1 + n_req, 2 * capacity, VECS), jnp.float32),
        ),
        in_specs=[vmem] * 4,
        out_specs=(vmem,) * 5,
        scratch_shapes=[pltpu.VMEM((2 * slots + 8, VECS), jnp.float32)],
        compiler_params=params,
        cost_estimate=some,
        name="prepare",
    )(
        near,
        table,
        row_parents,
        far,
    )

    received, after = [], []
    for k in order:
        out = [pltpu.VMEM((2 * HD + STAT_ROWS, VECS), jnp.bfloat16)]
        if k == order[0]:
            out.append(pltpu.VMEM((8, VECS), jnp.float32))
        units, *token = pl.pallas_call(
            functools.partial(away_kernel, 2 * ((k + 1) // 2)),
            out_shape=out,
            in_specs=[vmem] * 4,
            out_specs=[vmem] * len(out),
            compiler_params=params,
            cost_estimate=some,
            name="suffix_away",
        )(keys, values, member, messages[k])
        received.append(exchanged(units, k))
        after += token

    summed, stats, given = pl.pallas_call(
        home_kernel,
        out_shape=(
            pltpu.VMEM((HD, VECS), jnp.float32),
            pltpu.VMEM((8, VECS), jnp.float32),
            pltpu.VMEM((HD + STAT_ROWS, VECS), jnp.bfloat16),
        ),
        in_specs=[pl.BlockSpec(memory_space=pltpu.SMEM)] + [vmem] * 7,
        out_specs=(vmem,) * 3,
        compiler_params=params,
        cost_estimate=pl.CostEstimate(
            flops=8 * tokens * VECS * HD, bytes_accessed=2 * tokens * width, transcendentals=0
        ),
        name="home_part",
    )(lengths, home_keys, home_values, member, own, other, prompt_cache.reshape(tokens, width), *after)
    last = swapped(given, "pair")

    share = pl.pallas_call(
        sibling_kernel,
        out_shape=pltpu.VMEM((HD + STAT_ROWS, VECS), jnp.bfloat16),
        in_specs=[vmem] * n_messages,
        out_specs=vmem,
        compiler_params=params,
        name="sibling_share",
    )(*received)

    return pl.pallas_call(
        final_kernel,
        out_shape=jax.ShapeDtypeStruct((BEAMS, HEADS * HD), jnp.float32),
        in_specs=[vmem] * (4 + n_messages),
        out_specs=vmem,
        compiler_params=params,
        name="combine",
    )(*received, last, swapped(share, "core"), summed, stats)


def solution(mesh):
    n_batch, n_mp = mesh.devices.shape
    split = jax.sharding.Mesh(
        mesh.devices.reshape(n_batch // 2, 2, n_mp // 2, 2), ("z", "core", "group", "pair")
    )
    batch, mp = ("z", "core"), ("group", "pair")
    return jax.shard_map(
        on_device,
        mesh=split,
        in_specs=(
            P(batch, mp),
            P(batch, mp, None, None),
            P(batch, mp, None, None),
            P(),
            P(),
            P(batch),
        ),
        out_specs=P(batch, mp),
        check_vma=False,
    )
```

```python
import functools

import jax
import jax.numpy as jnp
from jax import lax
from jax.experimental import pallas as pl
from jax.experimental.pallas import tpu as pltpu
from jax.sharding import PartitionSpec as P

HD = 128
GROUP = 16
BEAMS = 16
SUF = 4
HEADS = GROUP // 2
VECS = HEADS * BEAMS
STAT_ROWS = 16
CHUNK = 512
SURELY_VALID = 1024

big_negative = -1e30
to_exp2 = HD ** (-0.5) * 1.4426950408889634


def swapped(value, axis):
    return lax.ppermute(value, axis, [(0, 1), (1, 0)])


def shares(n_req):
    both = n_req - 1
    rest = [d for d in range(1, n_req) if d != both]
    return both, (rest[: len(rest) // 2], rest[len(rest) // 2 :])


def exchanged(value, message):
    n_req = lax.axis_size("z")
    both, own = shares(n_req)
    pairs = []
    for z in range(n_req):
        for core in range(2):
            for pair in range(2):
                if message == 0:
                    mask, side = both, core
                else:
                    mask, side = own[core][(message - 1) // 2], (message - 1) % 2
                target = ((z ^ mask) * 2 + core) * 2 + (pair ^ side)
                pairs.append(((z * 2 + core) * 2 + pair, target))
    return lax.ppermute(value, ("z", "core", "pair"), pairs)


def masks_here(n_req):
    both, own = shares(n_req)
    core = lax.axis_index("core")
    return [both] + [jnp.where(core == 0, d0, d1) for d0, d1 in zip(*own)]


def stage_kernel(*refs):
    n = (len(refs) - 1) // 2
    copies = [
        pltpu.make_async_copy(refs[i], refs[n + i], refs[-1].at[i]) for i in range(n)
    ]
    for copy in copies:
        copy.start()
    for copy in copies:
        copy.wait()


def pack_kernel(own_ref, sibling_ref, out_ref):
    core = lax.axis_index("core")
    out_ref[core] = own_ref[...]
    out_ref[1 - core] = sibling_ref[...]


def stacked_heads(q):
    return jnp.concatenate([q[:, h * HD : (h + 1) * HD] for h in range(HEADS)], axis=0)


def scores_of(keys, vectors):
    return lax.dot_general(
        keys, vectors, (((1,), (1,)), ((), ())), preferred_element_type=jnp.float32
    )


def summed_of(values, weights):
    return lax.dot_general(
        values,
        weights.astype(jnp.bfloat16),
        (((0,), (0,)), ((), ())),
        preferred_element_type=jnp.float32,
    )


def merged(parts):
    top = functools.reduce(jnp.maximum, [p[0] for p in parts])
    total = 0.0
    summed = 0.0
    for part_top, part_total, part_summed in parts:
        factor = jnp.exp2((part_top - top) * to_exp2)
        total = total + part_total * factor
        summed = summed + part_summed * factor
    return top, total, summed


def weighted(scores):
    top = jnp.max(scores, axis=0, keepdims=True)
    weights = jnp.exp2((scores - top) * to_exp2)
    return top, jnp.sum(weights, axis=0, keepdims=True), weights


def three_pieces(x):
    first = x.astype(jnp.bfloat16).astype(jnp.float32)
    rest = x - first
    second = rest.astype(jnp.bfloat16).astype(jnp.float32)
    return [first, second, rest - second]


def store_units(ref, parts):
    rows = []
    for i, (top, total, summed) in enumerate(parts):
        ref[i * HD : (i + 1) * HD, :] = summed.astype(jnp.bfloat16)
        rows += three_pieces(top) + three_pieces(total)
    rows.append(jnp.zeros((STAT_ROWS - len(rows), VECS), jnp.float32))
    ref[len(parts) * HD :, :] = jnp.concatenate(rows, axis=0).astype(jnp.bfloat16)


def load_unit(ref, i=0):
    sums = ref.shape[0] - STAT_ROWS
    stats = ref[sums:, :].astype(jnp.float32)
    if isinstance(i, int):
        rows = [stats[6 * i + k : 6 * i + k + 1] for k in range(6)]
    else:
        rows = [jnp.where(i == 0, stats[k : k + 1], stats[6 + k : 7 + k]) for k in range(6)]
    part = ref[pl.ds(pl.multiple_of(i * HD, HD), HD), :]
    return rows[0] + rows[1] + rows[2], rows[3] + rows[4] + rows[5], part.astype(jnp.float32)


def count(left, right):
    return jnp.dot(
        left.astype(jnp.bfloat16), right.astype(jnp.bfloat16), preferred_element_type=jnp.float32
    )


def iota(shape, axis):
    return lax.broadcasted_iota(jnp.int32, shape, axis)


def prompt_part(length, half, prompt_ref, vectors):
    parity = lax.axis_index("pair")
    whole = lax.div(length, 2 * half)
    valid = whole * half + jnp.clip(length - whole * (2 * half) - parity * half, 0, half)
    chunks = [slice(i, i + CHUNK) for i in range(0, prompt_ref.shape[0], CHUNK)]
    scores = [scores_of(prompt_ref[chunk, :HD], vectors) for chunk in chunks]
    place = iota(scores[0].shape, 0)
    scores = [
        score
        if chunk.stop <= SURELY_VALID
        else jnp.where(place < valid - chunk.start, score, big_negative)
        for chunk, score in zip(chunks, scores)
    ]
    tops = [jnp.max(score, axis=0, keepdims=True) for score in scores]
    top = functools.reduce(jnp.maximum, tops)
    total, summed = 0.0, 0.0
    for chunk, score in zip(chunks, scores):
        weights = jnp.exp2((score - top) * to_exp2)
        total = total + jnp.sum(weights, axis=0, keepdims=True)
        summed = summed + summed_of(prompt_ref[chunk, HD:], weights)
    return top, total, summed


def prepare_kernel(
    capacity, near, table, parents, far_ref,
    home_keys_ref, home_values_ref, keys_ref, values_ref, member_ref, rows_ref,
):
    n_req = lax.axis_size("z")
    slots, half, _ = near.shape
    rows = table.shape[1]
    n_batch = rows // BEAMS
    z, core = lax.axis_index("z"), lax.axis_index("core")

    slot = iota((2 * slots, rows), 0)
    mine = slot < slots
    block = jnp.where(mine, slot, slot - slots) + jnp.where(mine, 2 * z + core, 2 * z + 1 - core) * slots
    named = functools.reduce(
        jnp.logical_or, [table[j : j + 1, :] == block for j in range(SUF)]
    ).astype(jnp.float32)
    group = (iota((rows, n_batch), 0) // BEAMS == iota((rows, n_batch), 1)).astype(jnp.float32)
    hit = jnp.where(count(named, group) > 0.0, 1.0, 0.0)
    left, right = iota((2 * slots, 2 * slots), 0), iota((2 * slots, 2 * slots), 1)
    before = (left // slots == right // slots) & (right < left)
    rank = count(before.astype(jnp.float32), hit)
    taken = (iota((rows, rows), 0) == parents[...]).astype(jnp.float32)
    continued = count(named, taken)

    place = iota((2 * slots, n_batch), 0)
    found = []
    for k in range(2 * capacity):
        holder = k // capacity
        chosen = (hit > 0.0) & (rank == float(k % capacity)) & (place // slots == holder)
        found.append(jnp.sum(jnp.where(chosen, place + 1, 0), axis=0, keepdims=True))
    found = jnp.concatenate(found, axis=0)

    requests = [z * 2 + core]
    for mask in masks_here(n_req):
        requests += [(z ^ mask) * 2, (z ^ mask) * 2 + 1]
    for i, request in enumerate(requests):
        lane = iota((rows, VECS), 1)
        spread = iota((rows, VECS), 0) == request * BEAMS + lane % BEAMS
        rows_ref[: 2 * slots, :] = count(continued, spread.astype(jnp.float32))
        rows_ref[2 * slots :, :] = jnp.zeros((8, VECS), jnp.float32)
        mask = iota(found.shape, 1) == request
        picked = jnp.sum(jnp.where(mask, found, 0), axis=1, keepdims=True)
        values = []
        for k in range(2 * capacity):
            index = picked[k, 0]
            row = jnp.where(index > 0, index - 1, 2 * slots)
            member_ref[i, k : k + 1, :] = rows_ref[pl.ds(row, 1), :]
            pool_ref = near if k < capacity else far_ref
            base = 0 if k < capacity else slots
            content = pool_ref[jnp.maximum(index - 1 - base, 0)]
            tokens = slice(k * half, (k + 1) * half)
            if i == 0:
                home_keys_ref[0, tokens, :] = content[:, :HD]
            else:
                keys_ref[i - 1, tokens, :] = content[:, :HD]
            values.append(content[:, HD:])
        values = jnp.concatenate(values, axis=0).T
        if i == 0:
            home_values_ref[0] = values
        else:
            values_ref[i - 1] = values


def all_vectors(own_ref, pair_ref):
    return jnp.concatenate([stacked_heads(own_ref[...]), stacked_heads(pair_ref[...])], axis=0)


def suffix_parts(vectors, keys_ref, values_ref, members, place=0):
    n_slots = members[0].shape[0]
    half = keys_ref.shape[1] // n_slots
    scores = [scores_of(keys_ref[place + i], each) for i, each in enumerate(vectors)]
    softmaxes = []
    for member, score in zip(members, scores):
        member = jnp.concatenate([member] * (score.shape[1] // VECS), axis=1)
        pieces = [
            jnp.where(
                member[k : k + 1, :] > 0.0, score[k * half : (k + 1) * half], big_negative
            )
            for k in range(n_slots)
        ]
        softmaxes.append(weighted(jnp.concatenate(pieces, axis=0)))
    return [
        (
            top,
            total,
            jnp.dot(
                values_ref[place + i], weights.astype(jnp.bfloat16), preferred_element_type=jnp.float32
            ),
        )
        for i, (top, total, weights) in enumerate(softmaxes)
    ]


def half_of(part, side):
    lanes = slice(side * VECS, (side + 1) * VECS)
    return [x[:, lanes] for x in part]


def away_kernel(place, keys_ref, values_ref, member_ref, message_ref, out_ref, *after_ref):
    for ref in after_ref:
        ref[...] = jnp.zeros(ref.shape, jnp.float32)
    vectors = [stacked_heads(message_ref[core]) for core in range(2)]
    members = [member_ref[1 + place + core] for core in range(2)]
    store_units(out_ref, suffix_parts(vectors, keys_ref, values_ref, members, place))


def home_kernel(
    length_ref, keys_ref, values_ref, member_ref, own_ref, pair_ref, prompt_ref, after_ref,
    summed_ref, stats_ref, out_ref,
):
    vectors = all_vectors(own_ref, pair_ref)
    half = keys_ref.shape[1] // member_ref.shape[1]
    (suffix,) = suffix_parts([vectors], keys_ref, values_ref, [member_ref[0]])
    prompt = prompt_part(length_ref[0], half, prompt_ref, vectors)
    part = merged([prompt, suffix])
    top, total, summed_ref[...] = half_of(part, 0)
    stats_ref[...] = jnp.concatenate([top, total, jnp.zeros((6, VECS), jnp.float32)], axis=0)
    store_units(out_ref, [half_of(part, 1)])


def sibling_kernel(*rest):
    units, out_ref = rest[:-1], rest[-1]
    core = lax.axis_index("core")
    store_units(out_ref, [merged([load_unit(unit, 1 - core) for unit in units])])


def final_kernel(*rest):
    units, (last_ref, shared_ref, summed_ref, stats_ref, out_ref) = rest[:-5], rest[-5:]
    core = lax.axis_index("core")
    parts = [load_unit(unit, core) for unit in units]
    parts += [load_unit(last_ref), load_unit(shared_ref)]
    parts.append((stats_ref[0:1], stats_ref[1:2], summed_ref[...]))
    _, total, summed = merged(parts)
    attended = (summed / total).T
    for h in range(HEADS):
        out_ref[:, h * HD : (h + 1) * HD] = attended[h * BEAMS : (h + 1) * BEAMS]


def in_hbm(value):
    return pltpu.with_memory_space_constraint(value, pltpu.HBM)


def on_device(queries, prompt_cache, pool, block_table, parents, lengths):
    n_req = lax.axis_size("z")
    n_batch = 2 * n_req
    ndist = 2 ** (SUF + 1) - 2
    capacity = 2 * ((ndist // 2 + n_batch - 1) // n_batch)
    slots, _, half, width = pool.shape
    tokens = prompt_cache.shape[2]
    rows = block_table.shape[0]
    vmem = pl.BlockSpec(memory_space=pltpu.VMEM)
    params = pltpu.CompilerParams(vmem_limit_bytes=32 * 2**20)
    some = pl.CostEstimate(flops=2 * 10**8, bytes_accessed=2**21, transcendentals=0)
    early = pl.CostEstimate(flops=2 * 10**10, bytes_accessed=0, transcendentals=0)

    hbm = pl.BlockSpec(memory_space=pltpu.HBM)
    near = pool.reshape(slots, half, width)
    far = swapped(near, "core")
    other = swapped(queries, "pair")
    staged = [queries, block_table.T, parents.reshape(1, rows)]
    own, table, row_parents = pl.pallas_call(
        stage_kernel,
        out_shape=tuple(pltpu.VMEM(each.shape, each.dtype) for each in staged),
        in_specs=[hbm] * len(staged),
        out_specs=(vmem,) * len(staged),
        scratch_shapes=[pltpu.SemaphoreType.DMA((len(staged),))],
        compiler_params=params,
        name="stage",
    )(*[in_hbm(each) for each in staged])
    both = pl.pallas_call(
        pack_kernel,
        out_shape=pltpu.VMEM((2,) + queries.shape, jnp.bfloat16),
        in_specs=[vmem] * 2,
        out_specs=vmem,
        compiler_params=params,
        cost_estimate=early,
        name="both_cores",
    )(own, swapped(queries, "core"))
    n_messages = n_req - 1
    order = [1, 0] + list(range(n_messages - 1, 1, -1)) if n_messages > 1 else [0]
    messages = {k: exchanged(both, k) for k in order}

    home_keys, home_values, keys, values, member = pl.pallas_call(
        functools.partial(prepare_kernel, capacity),
        out_shape=(
            pltpu.VMEM((1, 2 * capacity * half, HD), jnp.bfloat16),
            pltpu.VMEM((1, HD, 2 * capacity * half), jnp.bfloat16),
            pltpu.VMEM((n_req, 2 * capacity * half, HD), jnp.bfloat16),
            pltpu.VMEM((n_req, HD, 2 * capacity * half), jnp.bfloat16),
            pltpu.VMEM((1 + n_req, 2 * capacity, VECS), jnp.float32),
        ),
        in_specs=[vmem] * 4,
        out_specs=(vmem,) * 5,
        scratch_shapes=[pltpu.VMEM((2 * slots + 8, VECS), jnp.float32)],
        compiler_params=params,
        cost_estimate=some,
        name="prepare",
    )(
        near,
        table,
        row_parents,
        far,
    )

    received, after = [], []
    for k in order:
        out = [pltpu.VMEM((2 * HD + STAT_ROWS, VECS), jnp.bfloat16)]
        if k == order[0]:
            out.append(pltpu.VMEM((8, VECS), jnp.float32))
        units, *token = pl.pallas_call(
            functools.partial(away_kernel, 2 * ((k + 1) // 2)),
            out_shape=out,
            in_specs=[vmem] * 4,
            out_specs=[vmem] * len(out),
            compiler_params=params,
            cost_estimate=some,
            name="suffix_away",
        )(keys, values, member, messages[k])
        received.append(exchanged(units, k))
        after += token

    summed, stats, given = pl.pallas_call(
        home_kernel,
        out_shape=(
            pltpu.VMEM((HD, VECS), jnp.float32),
            pltpu.VMEM((8, VECS), jnp.float32),
            pltpu.VMEM((HD + STAT_ROWS, VECS), jnp.bfloat16),
        ),
        in_specs=[pl.BlockSpec(memory_space=pltpu.SMEM)] + [vmem] * 7,
        out_specs=(vmem,) * 3,
        compiler_params=params,
        cost_estimate=pl.CostEstimate(
            flops=8 * tokens * VECS * HD, bytes_accessed=2 * tokens * width, transcendentals=0
        ),
        name="home_part",
    )(lengths, home_keys, home_values, member, own, other, prompt_cache.reshape(tokens, width), *after)
    last = swapped(given, "pair")

    share = pl.pallas_call(
        sibling_kernel,
        out_shape=pltpu.VMEM((HD + STAT_ROWS, VECS), jnp.bfloat16),
        in_specs=[vmem] * n_messages,
        out_specs=vmem,
        compiler_params=params,
        name="sibling_share",
    )(*received)

    return pl.pallas_call(
        final_kernel,
        out_shape=jax.ShapeDtypeStruct((BEAMS, HEADS * HD), jnp.float32),
        in_specs=[vmem] * (4 + n_messages),
        out_specs=vmem,
        compiler_params=params,
        name="combine",
    )(*received, last, swapped(share, "core"), summed, stats)


def solution(mesh):
    n_batch, n_mp = mesh.devices.shape
    split = jax.sharding.Mesh(
        mesh.devices.reshape(n_batch // 2, 2, n_mp // 2, 2), ("z", "core", "group", "pair")
    )
    batch, mp = ("z", "core"), ("group", "pair")
    return jax.shard_map(
        on_device,
        mesh=split,
        in_specs=(
            P(batch, mp),
            P(batch, mp, None, None),
            P(batch, mp, None, None),
            P(),
            P(),
            P(batch),
        ),
        out_specs=P(batch, mp),
        check_vma=False,
    )
```

```python
import functools

import jax
import jax.numpy as jnp
from jax import lax
from jax.experimental import pallas as pl
from jax.experimental.pallas import tpu as pltpu
from jax.sharding import PartitionSpec as P

HD = 128
GROUP = 16
BEAMS = 16
SUF = 4
HEADS = GROUP // 2
VECS = HEADS * BEAMS
STAT_ROWS = 16
CHUNK = 512
SURELY_VALID = 1024

big_negative = -1e30
to_exp2 = HD ** (-0.5) * 1.4426950408889634


def swapped(value, axis):
    return lax.ppermute(value, axis, [(0, 1), (1, 0)])


def shares(n_req):
    both = n_req // 2
    rest = [d for d in range(1, n_req) if d != both]
    return both, (rest[: len(rest) // 2], rest[len(rest) // 2 :])


def exchanged(value, message):
    n_req = lax.axis_size("z")
    both, own = shares(n_req)
    pairs = []
    for z in range(n_req):
        for core in range(2):
            for pair in range(2):
                if message == 0:
                    mask, side = both, core
                else:
                    mask, side = own[core][(message - 1) // 2], (message - 1) % 2
                target = ((z ^ mask) * 2 + core) * 2 + (pair ^ side)
                pairs.append(((z * 2 + core) * 2 + pair, target))
    return lax.ppermute(value, ("z", "core", "pair"), pairs)


def masks_here(n_req):
    both, own = shares(n_req)
    core = lax.axis_index("core")
    return [both] + [jnp.where(core == 0, d0, d1) for d0, d1 in zip(*own)]


def stage_kernel(*refs):
    n = (len(refs) - 1) // 2
    copies = [
        pltpu.make_async_copy(refs[i], refs[n + i], refs[-1].at[i]) for i in range(n)
    ]
    for copy in copies:
        copy.start()
    for copy in copies:
        copy.wait()


def pack_kernel(own_ref, sibling_ref, out_ref):
    core = lax.axis_index("core")
    out_ref[core] = own_ref[...]
    out_ref[1 - core] = sibling_ref[...]


def stacked_heads(q):
    return jnp.concatenate([q[:, h * HD : (h + 1) * HD] for h in range(HEADS)], axis=0)


def scores_of(keys, vectors):
    return lax.dot_general(
        keys, vectors, (((1,), (1,)), ((), ())), preferred_element_type=jnp.float32
    )


def summed_of(values, weights):
    return lax.dot_general(
        values,
        weights.astype(jnp.bfloat16),
        (((0,), (0,)), ((), ())),
        preferred_element_type=jnp.float32,
    )


def merged(parts):
    top = functools.reduce(jnp.maximum, [p[0] for p in parts])
    total = 0.0
    summed = 0.0
    for part_top, part_total, part_summed in parts:
        factor = jnp.exp2((part_top - top) * to_exp2)
        total = total + part_total * factor
        summed = summed + part_summed * factor
    return top, total, summed


def weighted(scores):
    top = jnp.max(scores, axis=0, keepdims=True)
    weights = jnp.exp2((scores - top) * to_exp2)
    return top, jnp.sum(weights, axis=0, keepdims=True), weights


def three_pieces(x):
    first = x.astype(jnp.bfloat16).astype(jnp.float32)
    rest = x - first
    second = rest.astype(jnp.bfloat16).astype(jnp.float32)
    return [first, second, rest - second]


def store_units(ref, parts):
    rows = []
    for i, (top, total, summed) in enumerate(parts):
        ref[i * HD : (i + 1) * HD, :] = summed.astype(jnp.bfloat16)
        rows += three_pieces(top) + three_pieces(total)
    rows.append(jnp.zeros((STAT_ROWS - len(rows), VECS), jnp.float32))
    ref[len(parts) * HD :, :] = jnp.concatenate(rows, axis=0).astype(jnp.bfloat16)


def load_unit(ref, i=0):
    sums = ref.shape[0] - STAT_ROWS
    stats = ref[sums:, :].astype(jnp.float32)
    if isinstance(i, int):
        rows = [stats[6 * i + k : 6 * i + k + 1] for k in range(6)]
    else:
        rows = [jnp.where(i == 0, stats[k : k + 1], stats[6 + k : 7 + k]) for k in range(6)]
    part = ref[pl.ds(pl.multiple_of(i * HD, HD), HD), :]
    return rows[0] + rows[1] + rows[2], rows[3] + rows[4] + rows[5], part.astype(jnp.float32)


def count(left, right):
    return jnp.dot(
        left.astype(jnp.bfloat16), right.astype(jnp.bfloat16), preferred_element_type=jnp.float32
    )


def iota(shape, axis):
    return lax.broadcasted_iota(jnp.int32, shape, axis)


def prompt_part(length, half, prompt_ref, vectors):
    parity = lax.axis_index("pair")
    whole = lax.div(length, 2 * half)
    valid = whole * half + jnp.clip(length - whole * (2 * half) - parity * half, 0, half)
    chunks = [slice(i, i + CHUNK) for i in range(0, prompt_ref.shape[0], CHUNK)]
    scores = [scores_of(vectors, prompt_ref[chunk, :HD]) for chunk in chunks]
    place = iota(scores[0].shape, 1)
    scores = [
        score
        if chunk.stop <= SURELY_VALID
        else jnp.where(place < valid - chunk.start, score, big_negative)
        for chunk, score in zip(chunks, scores)
    ]
    top = jnp.max(functools.reduce(jnp.maximum, scores), axis=1, keepdims=True)
    totals, summed = 0.0, 0.0
    for chunk, score in zip(chunks, scores):
        weights = jnp.exp2((score - top) * to_exp2)
        totals = totals + weights
        summed = summed + jnp.dot(
            weights.astype(jnp.bfloat16), prompt_ref[chunk, HD:], preferred_element_type=jnp.float32
        )
    total = jnp.sum(totals, axis=1, keepdims=True)
    stats = jnp.where(iota(summed.shape, 1) == 0, top, total).T
    return stats[0:1], stats[1:2], summed.T


def prepare_kernel(
    capacity, near, table, parents, far_ref,
    home_keys_ref, home_values_ref, keys_ref, values_ref, member_ref, rows_ref,
):
    n_req = lax.axis_size("z")
    slots, half, _ = near.shape
    rows = table.shape[1]
    n_batch = rows // BEAMS
    z, core = lax.axis_index("z"), lax.axis_index("core")

    slot = iota((2 * slots, rows), 0)
    mine = slot < slots
    block = jnp.where(mine, slot, slot - slots) + jnp.where(mine, 2 * z + core, 2 * z + 1 - core) * slots
    named = functools.reduce(
        jnp.logical_or, [table[j : j + 1, :] == block for j in range(SUF)]
    ).astype(jnp.float32)
    group = (iota((rows, n_batch), 0) // BEAMS == iota((rows, n_batch), 1)).astype(jnp.float32)
    hit = jnp.where(count(named, group) > 0.0, 1.0, 0.0)
    left, right = iota((2 * slots, 2 * slots), 0), iota((2 * slots, 2 * slots), 1)
    before = (left // slots == right // slots) & (right < left)
    rank = count(before.astype(jnp.float32), hit)
    taken = (iota((rows, rows), 0) == parents[...]).astype(jnp.float32)
    continued = count(named, taken)

    place = iota((2 * slots, n_batch), 0)
    found = []
    for k in range(2 * capacity):
        holder = k // capacity
        chosen = (hit > 0.0) & (rank == float(k % capacity)) & (place // slots == holder)
        found.append(jnp.sum(jnp.where(chosen, place + 1, 0), axis=0, keepdims=True))
    found = jnp.concatenate(found, axis=0)

    requests = [z * 2 + core]
    for mask in masks_here(n_req):
        requests += [(z ^ mask) * 2, (z ^ mask) * 2 + 1]
    for i, request in enumerate(requests):
        lane = iota((rows, VECS), 1)
        spread = iota((rows, VECS), 0) == request * BEAMS + lane % BEAMS
        rows_ref[: 2 * slots, :] = count(continued, spread.astype(jnp.float32))
        rows_ref[2 * slots :, :] = jnp.zeros((8, VECS), jnp.float32)
        mask = iota(found.shape, 1) == request
        picked = jnp.sum(jnp.where(mask, found, 0), axis=1, keepdims=True)
        values = []
        for k in range(2 * capacity):
            index = picked[k, 0]
            row = jnp.where(index > 0, index - 1, 2 * slots)
            member_ref[i, k : k + 1, :] = rows_ref[pl.ds(row, 1), :]
            pool_ref = near if k < capacity else far_ref
            base = 0 if k < capacity else slots
            content = pool_ref[jnp.maximum(index - 1 - base, 0)]
            tokens = slice(k * half, (k + 1) * half)
            if i == 0:
                home_keys_ref[0, tokens, :] = content[:, :HD]
            else:
                keys_ref[i - 1, tokens, :] = content[:, :HD]
            values.append(content[:, HD:])
        values = jnp.concatenate(values, axis=0).T
        if i == 0:
            home_values_ref[0] = values
        else:
            values_ref[i - 1] = values


def all_vectors(own_ref, pair_ref):
    return jnp.concatenate([stacked_heads(own_ref[...]), stacked_heads(pair_ref[...])], axis=0)


def suffix_parts(vectors, keys_ref, values_ref, members, place=0):
    n_slots = members[0].shape[0]
    half = keys_ref.shape[1] // n_slots
    scores = [scores_of(keys_ref[place + i], each) for i, each in enumerate(vectors)]
    softmaxes = []
    for member, score in zip(members, scores):
        member = jnp.concatenate([member] * (score.shape[1] // VECS), axis=1)
        pieces = [
            jnp.where(
                member[k : k + 1, :] > 0.0, score[k * half : (k + 1) * half], big_negative
            )
            for k in range(n_slots)
        ]
        softmaxes.append(weighted(jnp.concatenate(pieces, axis=0)))
    return [
        (
            top,
            total,
            jnp.dot(
                values_ref[place + i], weights.astype(jnp.bfloat16), preferred_element_type=jnp.float32
            ),
        )
        for i, (top, total, weights) in enumerate(softmaxes)
    ]


def half_of(part, side):
    lanes = slice(side * VECS, (side + 1) * VECS)
    return [x[:, lanes] for x in part]


def away_kernel(place, keys_ref, values_ref, member_ref, message_ref, out_ref, *after_ref):
    for ref in after_ref:
        ref[...] = jnp.zeros(ref.shape, jnp.float32)
    vectors = [stacked_heads(message_ref[core]) for core in range(2)]
    members = [member_ref[1 + place + core] for core in range(2)]
    store_units(out_ref, suffix_parts(vectors, keys_ref, values_ref, members, place))


def home_kernel(
    length_ref, keys_ref, values_ref, member_ref, own_ref, pair_ref, prompt_ref, after_ref,
    summed_ref, stats_ref, out_ref,
):
    vectors = all_vectors(own_ref, pair_ref)
    half = keys_ref.shape[1] // member_ref.shape[1]
    (suffix,) = suffix_parts([vectors], keys_ref, values_ref, [member_ref[0]])
    prompt = prompt_part(length_ref[0], half, prompt_ref, vectors)
    part = merged([prompt, suffix])
    top, total, summed_ref[...] = half_of(part, 0)
    stats_ref[...] = jnp.concatenate([top, total, jnp.zeros((6, VECS), jnp.float32)], axis=0)
    store_units(out_ref, [half_of(part, 1)])


def sibling_kernel(*rest):
    units, out_ref = rest[:-1], rest[-1]
    core = lax.axis_index("core")
    store_units(out_ref, [merged([load_unit(unit, 1 - core) for unit in units])])


def final_kernel(*rest):
    units, (last_ref, shared_ref, summed_ref, stats_ref, out_ref) = rest[:-5], rest[-5:]
    core = lax.axis_index("core")
    parts = [load_unit(unit, core) for unit in units]
    parts += [load_unit(last_ref), load_unit(shared_ref)]
    parts.append((stats_ref[0:1], stats_ref[1:2], summed_ref[...]))
    _, total, summed = merged(parts)
    attended = (summed / total).T
    for h in range(HEADS):
        out_ref[:, h * HD : (h + 1) * HD] = attended[h * BEAMS : (h + 1) * BEAMS]


def in_hbm(value):
    return pltpu.with_memory_space_constraint(value, pltpu.HBM)


def on_device(queries, prompt_cache, pool, block_table, parents, lengths):
    n_req = lax.axis_size("z")
    n_batch = 2 * n_req
    ndist = 2 ** (SUF + 1) - 2
    capacity = 2 * ((ndist // 2 + n_batch - 1) // n_batch)
    slots, _, half, width = pool.shape
    tokens = prompt_cache.shape[2]
    rows = block_table.shape[0]
    vmem = pl.BlockSpec(memory_space=pltpu.VMEM)
    params = pltpu.CompilerParams(vmem_limit_bytes=32 * 2**20)
    some = pl.CostEstimate(flops=2 * 10**8, bytes_accessed=2**21, transcendentals=0)
    early = pl.CostEstimate(flops=2 * 10**10, bytes_accessed=0, transcendentals=0)

    hbm = pl.BlockSpec(memory_space=pltpu.HBM)
    near = pool.reshape(slots, half, width)
    far = swapped(near, "core")
    other = swapped(queries, "pair")
    staged = [queries, block_table.T, parents.reshape(1, rows)]
    own, table, row_parents = pl.pallas_call(
        stage_kernel,
        out_shape=tuple(pltpu.VMEM(each.shape, each.dtype) for each in staged),
        in_specs=[hbm] * len(staged),
        out_specs=(vmem,) * len(staged),
        scratch_shapes=[pltpu.SemaphoreType.DMA((len(staged),))],
        compiler_params=params,
        name="stage",
    )(*[in_hbm(each) for each in staged])
    both = pl.pallas_call(
        pack_kernel,
        out_shape=pltpu.VMEM((2,) + queries.shape, jnp.bfloat16),
        in_specs=[vmem] * 2,
        out_specs=vmem,
        compiler_params=params,
        cost_estimate=early,
        name="both_cores",
    )(own, swapped(queries, "core"))
    n_messages = n_req - 1
    order = [1, 0] + list(range(n_messages - 1, 1, -1)) if n_messages > 1 else [0]
    messages = {k: exchanged(both, k) for k in order}

    home_keys, home_values, keys, values, member = pl.pallas_call(
        functools.partial(prepare_kernel, capacity),
        out_shape=(
            pltpu.VMEM((1, 2 * capacity * half, HD), jnp.bfloat16),
            pltpu.VMEM((1, HD, 2 * capacity * half), jnp.bfloat16),
            pltpu.VMEM((n_req, 2 * capacity * half, HD), jnp.bfloat16),
            pltpu.VMEM((n_req, HD, 2 * capacity * half), jnp.bfloat16),
            pltpu.VMEM((1 + n_req, 2 * capacity, VECS), jnp.float32),
        ),
        in_specs=[vmem] * 4,
        out_specs=(vmem,) * 5,
        scratch_shapes=[pltpu.VMEM((2 * slots + 8, VECS), jnp.float32)],
        compiler_params=params,
        cost_estimate=some,
        name="prepare",
    )(
        near,
        table,
        row_parents,
        far,
    )

    received, after = [], []
    for k in order:
        out = [pltpu.VMEM((2 * HD + STAT_ROWS, VECS), jnp.bfloat16)]
        if k == order[0]:
            out.append(pltpu.VMEM((8, VECS), jnp.float32))
        units, *token = pl.pallas_call(
            functools.partial(away_kernel, 2 * ((k + 1) // 2)),
            out_shape=out,
            in_specs=[vmem] * 4,
            out_specs=[vmem] * len(out),
            compiler_params=params,
            cost_estimate=some,
            name="suffix_away",
        )(keys, values, member, messages[k])
        received.append(exchanged(units, k))
        after += token

    summed, stats, given = pl.pallas_call(
        home_kernel,
        out_shape=(
            pltpu.VMEM((HD, VECS), jnp.float32),
            pltpu.VMEM((8, VECS), jnp.float32),
            pltpu.VMEM((HD + STAT_ROWS, VECS), jnp.bfloat16),
        ),
        in_specs=[pl.BlockSpec(memory_space=pltpu.SMEM)] + [vmem] * 7,
        out_specs=(vmem,) * 3,
        compiler_params=params,
        cost_estimate=pl.CostEstimate(
            flops=8 * tokens * VECS * HD, bytes_accessed=2 * tokens * width, transcendentals=0
        ),
        name="home_part",
    )(lengths, home_keys, home_values, member, own, other, prompt_cache.reshape(tokens, width), *after)
    last = swapped(given, "pair")

    share = pl.pallas_call(
        sibling_kernel,
        out_shape=pltpu.VMEM((HD + STAT_ROWS, VECS), jnp.bfloat16),
        in_specs=[vmem] * n_messages,
        out_specs=vmem,
        compiler_params=params,
        name="sibling_share",
    )(*received)

    return pl.pallas_call(
        final_kernel,
        out_shape=jax.ShapeDtypeStruct((BEAMS, HEADS * HD), jnp.float32),
        in_specs=[vmem] * (4 + n_messages),
        out_specs=vmem,
        compiler_params=params,
        name="combine",
    )(*received, last, swapped(share, "core"), summed, stats)


def solution(mesh):
    n_batch, n_mp = mesh.devices.shape
    split = jax.sharding.Mesh(
        mesh.devices.reshape(n_batch // 2, 2, n_mp // 2, 2), ("z", "core", "group", "pair")
    )
    batch, mp = ("z", "core"), ("group", "pair")
    return jax.shard_map(
        on_device,
        mesh=split,
        in_specs=(
            P(batch, mp),
            P(batch, mp, None, None),
            P(batch, mp, None, None),
            P(),
            P(),
            P(batch),
        ),
        out_specs=P(batch, mp),
        check_vma=False,
    )
```

```python
import functools

import jax
import jax.numpy as jnp
from jax import lax
from jax.experimental import pallas as pl
from jax.experimental.pallas import tpu as pltpu
from jax.sharding import PartitionSpec as P

HD = 128
GROUP = 16
BEAMS = 16
SUF = 4
HEADS = GROUP // 2
VECS = HEADS * BEAMS
STAT_ROWS = 16
CHUNK = 512
SURELY_VALID = 1024

big_negative = -1e30
to_exp2 = HD ** (-0.5) * 1.4426950408889634


def swapped(value, axis):
    return lax.ppermute(value, axis, [(0, 1), (1, 0)])


def shares(n_req):
    both = n_req // 2
    rest = [d for d in range(1, n_req) if d != both]
    return both, (rest[: len(rest) // 2], rest[len(rest) // 2 :])


def exchanged(value, message):
    n_req = lax.axis_size("z")
    both, own = shares(n_req)
    pairs = []
    for z in range(n_req):
        for core in range(2):
            for pair in range(2):
                if message == 0:
                    mask, side = both, core
                else:
                    mask, side = own[core][(message - 1) // 2], (message - 1) % 2
                target = ((z ^ mask) * 2 + core) * 2 + (pair ^ side)
                pairs.append(((z * 2 + core) * 2 + pair, target))
    return lax.ppermute(value, ("z", "core", "pair"), pairs)


def masks_here(n_req):
    both, own = shares(n_req)
    core = lax.axis_index("core")
    return [both] + [jnp.where(core == 0, d0, d1) for d0, d1 in zip(*own)]


def stage_kernel(*refs):
    n = (len(refs) - 1) // 2
    copies = [
        pltpu.make_async_copy(refs[i], refs[n + i], refs[-1].at[i]) for i in range(n)
    ]
    for copy in copies:
        copy.start()
    for copy in copies:
        copy.wait()


def pack_kernel(own_ref, sibling_ref, out_ref):
    core = lax.axis_index("core")
    out_ref[core] = own_ref[...]
    out_ref[1 - core] = sibling_ref[...]


def stacked_heads(q):
    return jnp.concatenate([q[:, h * HD : (h + 1) * HD] for h in range(HEADS)], axis=0)


def scores_of(keys, vectors):
    return lax.dot_general(
        keys, vectors, (((1,), (1,)), ((), ())), preferred_element_type=jnp.float32
    )


def summed_of(values, weights):
    return lax.dot_general(
        values,
        weights.astype(jnp.bfloat16),
        (((0,), (0,)), ((), ())),
        preferred_element_type=jnp.float32,
    )


def merged(parts):
    top = functools.reduce(jnp.maximum, [p[0] for p in parts])
    total = 0.0
    summed = 0.0
    for part_top, part_total, part_summed in parts:
        factor = jnp.exp2((part_top - top) * to_exp2)
        total = total + part_total * factor
        summed = summed + part_summed * factor
    return top, total, summed


def weighted(scores):
    top = jnp.max(scores, axis=0, keepdims=True)
    weights = jnp.exp2((scores - top) * to_exp2)
    return top, jnp.sum(weights, axis=0, keepdims=True), weights


def three_pieces(x):
    first = x.astype(jnp.bfloat16).astype(jnp.float32)
    rest = x - first
    second = rest.astype(jnp.bfloat16).astype(jnp.float32)
    return [first, second, rest - second]


def store_units(ref, parts):
    rows = []
    for i, (top, total, summed) in enumerate(parts):
        ref[i * HD : (i + 1) * HD, :] = summed.astype(jnp.bfloat16)
        rows += three_pieces(top) + three_pieces(total)
    rows.append(jnp.zeros((STAT_ROWS - len(rows), VECS), jnp.float32))
    ref[len(parts) * HD :, :] = jnp.concatenate(rows, axis=0).astype(jnp.bfloat16)


def load_unit(ref, i=0):
    sums = ref.shape[0] - STAT_ROWS
    stats = ref[sums:, :].astype(jnp.float32)
    if isinstance(i, int):
        rows = [stats[6 * i + k : 6 * i + k + 1] for k in range(6)]
    else:
        rows = [jnp.where(i == 0, stats[k : k + 1], stats[6 + k : 7 + k]) for k in range(6)]
    part = ref[pl.ds(pl.multiple_of(i * HD, HD), HD), :]
    return rows[0] + rows[1] + rows[2], rows[3] + rows[4] + rows[5], part.astype(jnp.float32)


def count(left, right):
    return jnp.dot(
        left.astype(jnp.bfloat16), right.astype(jnp.bfloat16), preferred_element_type=jnp.float32
    )


def iota(shape, axis):
    return lax.broadcasted_iota(jnp.int32, shape, axis)


def prompt_part(length, half, prompt_ref, vectors):
    parity = lax.axis_index("pair")
    whole = lax.div(length, 2 * half)
    valid = whole * half + jnp.clip(length - whole * (2 * half) - parity * half, 0, half)
    chunks = [slice(i, i + CHUNK) for i in range(0, prompt_ref.shape[0], CHUNK)]
    scores = [scores_of(vectors, prompt_ref[chunk, :HD]) for chunk in chunks]
    place = iota(scores[0].shape, 1)
    scores = [
        score
        if chunk.stop <= SURELY_VALID
        else jnp.where(place < valid - chunk.start, score, big_negative)
        for chunk, score in zip(chunks, scores)
    ]
    top = jnp.max(functools.reduce(jnp.maximum, scores), axis=1, keepdims=True)
    totals, summed = 0.0, 0.0
    for chunk, score in zip(chunks, scores):
        weights = jnp.exp2((score - top) * to_exp2)
        totals = totals + weights
        summed = summed + jnp.dot(
            weights.astype(jnp.bfloat16), prompt_ref[chunk, HD:], preferred_element_type=jnp.float32
        )
    total = jnp.sum(totals, axis=1, keepdims=True)
    stats = jnp.where(iota(summed.shape, 1) == 0, top, total).T
    return stats[0:1], stats[1:2], summed.T


def prepare_kernel(
    capacity, near, table, parents, far_ref,
    home_keys_ref, home_values_ref, keys_ref, values_ref, member_ref, rows_ref,
):
    n_req = lax.axis_size("z")
    slots, half, _ = near.shape
    rows = table.shape[1]
    n_batch = rows // BEAMS
    z, core = lax.axis_index("z"), lax.axis_index("core")

    slot = iota((2 * slots, rows), 0)
    mine = slot < slots
    block = jnp.where(mine, slot, slot - slots) + jnp.where(mine, 2 * z + core, 2 * z + 1 - core) * slots
    named = functools.reduce(
        jnp.logical_or, [table[j : j + 1, :] == block for j in range(SUF)]
    ).astype(jnp.float32)
    group = (iota((rows, n_batch), 0) // BEAMS == iota((rows, n_batch), 1)).astype(jnp.float32)
    hit = jnp.where(count(named, group) > 0.0, 1.0, 0.0)
    left, right = iota((2 * slots, 2 * slots), 0), iota((2 * slots, 2 * slots), 1)
    before = (left // slots == right // slots) & (right < left)
    rank = count(before.astype(jnp.float32), hit)
    taken = (iota((rows, rows), 0) == parents[...]).astype(jnp.float32)
    continued = count(named, taken)

    place = iota((2 * slots, n_batch), 0)
    found = []
    for k in range(2 * capacity):
        holder = k // capacity
        chosen = (hit > 0.0) & (rank == float(k % capacity)) & (place // slots == holder)
        found.append(jnp.sum(jnp.where(chosen, place + 1, 0), axis=0, keepdims=True))
    found = jnp.concatenate(found, axis=0)

    requests = [z * 2 + core]
    for mask in masks_here(n_req):
        requests += [(z ^ mask) * 2, (z ^ mask) * 2 + 1]
    for i, request in enumerate(requests):
        lane = iota((rows, VECS), 1)
        spread = iota((rows, VECS), 0) == request * BEAMS + lane % BEAMS
        rows_ref[: 2 * slots, :] = count(continued, spread.astype(jnp.float32))
        rows_ref[2 * slots :, :] = jnp.zeros((8, VECS), jnp.float32)
        mask = iota(found.shape, 1) == request
        picked = jnp.sum(jnp.where(mask, found, 0), axis=1, keepdims=True)
        values = []
        for k in range(2 * capacity):
            index = picked[k, 0]
            row = jnp.where(index > 0, index - 1, 2 * slots)
            member_ref[i, k : k + 1, :] = rows_ref[pl.ds(row, 1), :]
            pool_ref = near if k < capacity else far_ref
            base = 0 if k < capacity else slots
            content = pool_ref[jnp.maximum(index - 1 - base, 0)]
            tokens = slice(k * half, (k + 1) * half)
            if i == 0:
                home_keys_ref[0, tokens, :] = content[:, :HD]
            else:
                keys_ref[i - 1, tokens, :] = content[:, :HD]
            values.append(content[:, HD:])
        values = jnp.concatenate(values, axis=0).T
        if i == 0:
            home_values_ref[0] = values
        else:
            values_ref[i - 1] = values


def all_vectors(own_ref, pair_ref):
    return jnp.concatenate([stacked_heads(own_ref[...]), stacked_heads(pair_ref[...])], axis=0)


def suffix_parts(vectors, keys_ref, values_ref, members, place=0):
    n_slots = members[0].shape[0]
    half = keys_ref.shape[1] // n_slots
    scores = [scores_of(keys_ref[place + i], each) for i, each in enumerate(vectors)]
    softmaxes = []
    for member, score in zip(members, scores):
        member = jnp.concatenate([member] * (score.shape[1] // VECS), axis=1)
        pieces = [
            jnp.where(
                member[k : k + 1, :] > 0.0, score[k * half : (k + 1) * half], big_negative
            )
            for k in range(n_slots)
        ]
        softmaxes.append(weighted(jnp.concatenate(pieces, axis=0)))
    return [
        (
            top,
            total,
            jnp.dot(
                values_ref[place + i], weights.astype(jnp.bfloat16), preferred_element_type=jnp.float32
            ),
        )
        for i, (top, total, weights) in enumerate(softmaxes)
    ]


def half_of(part, side):
    lanes = slice(side * VECS, (side + 1) * VECS)
    return [x[:, lanes] for x in part]


def away_kernel(place, keys_ref, values_ref, member_ref, message_ref, out_ref, *after_ref):
    for ref in after_ref:
        ref[...] = jnp.zeros(ref.shape, jnp.float32)
    vectors = [stacked_heads(message_ref[core]) for core in range(2)]
    members = [member_ref[1 + place + core] for core in range(2)]
    store_units(out_ref, suffix_parts(vectors, keys_ref, values_ref, members, place))


def home_kernel(
    length_ref, keys_ref, values_ref, member_ref, own_ref, pair_ref, prompt_ref, after_ref,
    summed_ref, stats_ref, out_ref,
):
    vectors = all_vectors(own_ref, pair_ref)
    half = keys_ref.shape[1] // member_ref.shape[1]
    (suffix,) = suffix_parts([vectors], keys_ref, values_ref, [member_ref[0]])
    prompt = prompt_part(length_ref[0], half, prompt_ref, vectors)
    part = merged([prompt, suffix])
    top, total, summed_ref[...] = half_of(part, 0)
    stats_ref[...] = jnp.concatenate([top, total, jnp.zeros((6, VECS), jnp.float32)], axis=0)
    store_units(out_ref, [half_of(part, 1)])


def sibling_kernel(*rest):
    units, out_ref = rest[:-1], rest[-1]
    core = lax.axis_index("core")
    store_units(out_ref, [merged([load_unit(unit, 1 - core) for unit in units])])


def final_kernel(*rest):
    units, (last_ref, shared_ref, summed_ref, stats_ref, out_ref) = rest[:-5], rest[-5:]
    core = lax.axis_index("core")
    parts = [load_unit(unit, core) for unit in units]
    parts += [load_unit(last_ref), load_unit(shared_ref)]
    parts.append((stats_ref[0:1], stats_ref[1:2], summed_ref[...]))
    _, total, summed = merged(parts)
    attended = (summed / total).T
    for h in range(HEADS):
        out_ref[:, h * HD : (h + 1) * HD] = attended[h * BEAMS : (h + 1) * BEAMS]


def in_hbm(value):
    return pltpu.with_memory_space_constraint(value, pltpu.HBM)


def on_device(queries, prompt_cache, pool, block_table, parents, lengths):
    n_req = lax.axis_size("z")
    n_batch = 2 * n_req
    ndist = 2 ** (SUF + 1) - 2
    capacity = 2 * ((ndist // 2 + n_batch - 1) // n_batch)
    slots, _, half, width = pool.shape
    tokens = prompt_cache.shape[2]
    rows = block_table.shape[0]
    vmem = pl.BlockSpec(memory_space=pltpu.VMEM)
    params = pltpu.CompilerParams(vmem_limit_bytes=32 * 2**20)
    some = pl.CostEstimate(flops=2 * 10**8, bytes_accessed=2**21, transcendentals=0)
    early = pl.CostEstimate(flops=2 * 10**10, bytes_accessed=0, transcendentals=0)

    hbm = pl.BlockSpec(memory_space=pltpu.HBM)
    near = pool.reshape(slots, half, width)
    far = swapped(near, "core")
    other = swapped(queries, "pair")
    staged = [queries, block_table.T, parents.reshape(1, rows)]
    own, table, row_parents = pl.pallas_call(
        stage_kernel,
        out_shape=tuple(pltpu.VMEM(each.shape, each.dtype) for each in staged),
        in_specs=[hbm] * len(staged),
        out_specs=(vmem,) * len(staged),
        scratch_shapes=[pltpu.SemaphoreType.DMA((len(staged),))],
        compiler_params=params,
        name="stage",
    )(*[in_hbm(each) for each in staged])
    both = pl.pallas_call(
        pack_kernel,
        out_shape=pltpu.VMEM((2,) + queries.shape, jnp.bfloat16),
        in_specs=[vmem] * 2,
        out_specs=vmem,
        compiler_params=params,
        cost_estimate=early,
        name="both_cores",
    )(own, swapped(queries, "core"))
    n_messages = n_req - 1
    order = list(range(1, n_messages)) + [0]
    messages = {k: exchanged(both, k) for k in order}

    home_keys, home_values, keys, values, member = pl.pallas_call(
        functools.partial(prepare_kernel, capacity),
        out_shape=(
            pltpu.VMEM((1, 2 * capacity * half, HD), jnp.bfloat16),
            pltpu.VMEM((1, HD, 2 * capacity * half), jnp.bfloat16),
            pltpu.VMEM((n_req, 2 * capacity * half, HD), jnp.bfloat16),
            pltpu.VMEM((n_req, HD, 2 * capacity * half), jnp.bfloat16),
            pltpu.VMEM((1 + n_req, 2 * capacity, VECS), jnp.float32),
        ),
        in_specs=[vmem] * 4,
        out_specs=(vmem,) * 5,
        scratch_shapes=[pltpu.VMEM((2 * slots + 8, VECS), jnp.float32)],
        compiler_params=params,
        cost_estimate=some,
        name="prepare",
    )(
        near,
        table,
        row_parents,
        far,
    )

    received, after = [], []
    for k in order:
        out = [pltpu.VMEM((2 * HD + STAT_ROWS, VECS), jnp.bfloat16)]
        if k == order[0]:
            out.append(pltpu.VMEM((8, VECS), jnp.float32))
        units, *token = pl.pallas_call(
            functools.partial(away_kernel, 2 * ((k + 1) // 2)),
            out_shape=out,
            in_specs=[vmem] * 4,
            out_specs=[vmem] * len(out),
            compiler_params=params,
            cost_estimate=some,
            name="suffix_away",
        )(keys, values, member, messages[k])
        received.append(exchanged(units, k))
        after += token

    summed, stats, given = pl.pallas_call(
        home_kernel,
        out_shape=(
            pltpu.VMEM((HD, VECS), jnp.float32),
            pltpu.VMEM((8, VECS), jnp.float32),
            pltpu.VMEM((HD + STAT_ROWS, VECS), jnp.bfloat16),
        ),
        in_specs=[pl.BlockSpec(memory_space=pltpu.SMEM)] + [vmem] * 7,
        out_specs=(vmem,) * 3,
        compiler_params=params,
        cost_estimate=pl.CostEstimate(
            flops=8 * tokens * VECS * HD, bytes_accessed=2 * tokens * width, transcendentals=0
        ),
        name="home_part",
    )(lengths, home_keys, home_values, member, own, other, prompt_cache.reshape(tokens, width), *after)
    last = swapped(given, "pair")

    share = pl.pallas_call(
        sibling_kernel,
        out_shape=pltpu.VMEM((HD + STAT_ROWS, VECS), jnp.bfloat16),
        in_specs=[vmem] * n_messages,
        out_specs=vmem,
        compiler_params=params,
        name="sibling_share",
    )(*received)

    return pl.pallas_call(
        final_kernel,
        out_shape=jax.ShapeDtypeStruct((BEAMS, HEADS * HD), jnp.float32),
        in_specs=[vmem] * (4 + n_messages),
        out_specs=vmem,
        compiler_params=params,
        name="combine",
    )(*received, last, swapped(share, "core"), summed, stats)


def solution(mesh):
    n_batch, n_mp = mesh.devices.shape
    split = jax.sharding.Mesh(
        mesh.devices.reshape(n_batch // 2, 2, n_mp // 2, 2), ("z", "core", "group", "pair")
    )
    batch, mp = ("z", "core"), ("group", "pair")
    return jax.shard_map(
        on_device,
        mesh=split,
        in_specs=(
            P(batch, mp),
            P(batch, mp, None, None),
            P(batch, mp, None, None),
            P(),
            P(),
            P(batch),
        ),
        out_specs=P(batch, mp),
        check_vma=False,
    )
```

```python
import functools

import jax
import jax.numpy as jnp
from jax import lax
from jax.experimental import pallas as pl
from jax.experimental.pallas import tpu as pltpu
from jax.sharding import PartitionSpec as P

HD = 128
GROUP = 16
BEAMS = 16
SUF = 4
HEADS = GROUP // 2
VECS = HEADS * BEAMS
STAT_ROWS = 16
CHUNK = 512
SURELY_VALID = 1024

big_negative = -1e30
to_exp2 = HD ** (-0.5) * 1.4426950408889634


def swapped(value, axis):
    return lax.ppermute(value, axis, [(0, 1), (1, 0)])


def shares(n_req):
    both = n_req // 2
    rest = [d for d in range(1, n_req) if d != both]
    return both, (rest[: len(rest) // 2], rest[len(rest) // 2 :])


def exchanged(value, message):
    n_req = lax.axis_size("z")
    both, own = shares(n_req)
    pairs = []
    for z in range(n_req):
        for core in range(2):
            for pair in range(2):
                if message == 0:
                    mask, side = both, core
                else:
                    mask, side = own[core][(message - 1) // 2], (message - 1) % 2
                target = ((z ^ mask) * 2 + core) * 2 + (pair ^ side)
                pairs.append(((z * 2 + core) * 2 + pair, target))
    return lax.ppermute(value, ("z", "core", "pair"), pairs)


def masks_here(n_req):
    both, own = shares(n_req)
    core = lax.axis_index("core")
    return [both] + [jnp.where(core == 0, d0, d1) for d0, d1 in zip(*own)]


def stage_kernel(*refs):
    n = (len(refs) - 1) // 2
    copies = [
        pltpu.make_async_copy(refs[i], refs[n + i], refs[-1].at[i]) for i in range(n)
    ]
    for copy in copies:
        copy.start()
    for copy in copies:
        copy.wait()


def pack_kernel(own_ref, sibling_ref, out_ref):
    core = lax.axis_index("core")
    out_ref[core] = own_ref[...]
    out_ref[1 - core] = sibling_ref[...]


def stacked_heads(q):
    return jnp.concatenate([q[:, h * HD : (h + 1) * HD] for h in range(HEADS)], axis=0)


def scores_of(keys, vectors):
    return lax.dot_general(
        keys, vectors, (((1,), (1,)), ((), ())), preferred_element_type=jnp.float32
    )


def summed_of(values, weights):
    return lax.dot_general(
        values,
        weights.astype(jnp.bfloat16),
        (((0,), (0,)), ((), ())),
        preferred_element_type=jnp.float32,
    )


def merged(parts):
    top = functools.reduce(jnp.maximum, [p[0] for p in parts])
    total = 0.0
    summed = 0.0
    for part_top, part_total, part_summed in parts:
        factor = jnp.exp2((part_top - top) * to_exp2)
        total = total + part_total * factor
        summed = summed + part_summed * factor
    return top, total, summed


def weighted(scores):
    top = jnp.max(scores, axis=0, keepdims=True)
    weights = jnp.exp2((scores - top) * to_exp2)
    return top, jnp.sum(weights, axis=0, keepdims=True), weights


def three_pieces(x):
    first = x.astype(jnp.bfloat16).astype(jnp.float32)
    rest = x - first
    second = rest.astype(jnp.bfloat16).astype(jnp.float32)
    return [first, second, rest - second]


def store_units(ref, parts):
    rows = []
    for i, (top, total, summed) in enumerate(parts):
        ref[i * HD : (i + 1) * HD, :] = summed.astype(jnp.bfloat16)
        rows += three_pieces(top) + three_pieces(total)
    rows.append(jnp.zeros((STAT_ROWS - len(rows), VECS), jnp.float32))
    ref[len(parts) * HD :, :] = jnp.concatenate(rows, axis=0).astype(jnp.bfloat16)


def load_unit(ref, i=0):
    sums = ref.shape[0] - STAT_ROWS
    stats = ref[sums:, :].astype(jnp.float32)
    if isinstance(i, int):
        rows = [stats[6 * i + k : 6 * i + k + 1] for k in range(6)]
    else:
        rows = [jnp.where(i == 0, stats[k : k + 1], stats[6 + k : 7 + k]) for k in range(6)]
    part = ref[pl.ds(pl.multiple_of(i * HD, HD), HD), :]
    return rows[0] + rows[1] + rows[2], rows[3] + rows[4] + rows[5], part.astype(jnp.float32)


def count(left, right):
    return jnp.dot(
        left.astype(jnp.bfloat16), right.astype(jnp.bfloat16), preferred_element_type=jnp.float32
    )


def iota(shape, axis):
    return lax.broadcasted_iota(jnp.int32, shape, axis)


def prompt_part(length, half, prompt_ref, vectors):
    parity = lax.axis_index("pair")
    whole = lax.div(length, 2 * half)
    valid = whole * half + jnp.clip(length - whole * (2 * half) - parity * half, 0, half)
    chunks = [slice(i, i + CHUNK) for i in range(0, prompt_ref.shape[0], CHUNK)]
    scores = [scores_of(vectors, prompt_ref[chunk, :HD]) for chunk in chunks]
    place = iota(scores[0].shape, 1)
    scores = [
        score
        if chunk.stop <= SURELY_VALID
        else jnp.where(place < valid - chunk.start, score, big_negative)
        for chunk, score in zip(chunks, scores)
    ]
    top = jnp.max(functools.reduce(jnp.maximum, scores), axis=1, keepdims=True)
    totals, summed = 0.0, 0.0
    for chunk, score in zip(chunks, scores):
        weights = jnp.exp2((score - top) * to_exp2)
        totals = totals + weights
        summed = summed + jnp.dot(
            weights.astype(jnp.bfloat16), prompt_ref[chunk, HD:], preferred_element_type=jnp.float32
        )
    total = jnp.sum(totals, axis=1, keepdims=True)
    stats = jnp.where(iota(summed.shape, 1) == 0, top, total).T
    return stats[0:1], stats[1:2], summed.T


def prepare_kernel(
    capacity, near, table, parents, far_ref,
    home_keys_ref, home_values_ref, keys_ref, values_ref, member_ref, rows_ref,
):
    n_req = lax.axis_size("z")
    slots, half, _ = near.shape
    rows = table.shape[1]
    n_batch = rows // BEAMS
    z, core = lax.axis_index("z"), lax.axis_index("core")

    slot = iota((2 * slots, rows), 0)
    mine = slot < slots
    block = jnp.where(mine, slot, slot - slots) + jnp.where(mine, 2 * z + core, 2 * z + 1 - core) * slots
    named = functools.reduce(
        jnp.logical_or, [table[j : j + 1, :] == block for j in range(SUF)]
    ).astype(jnp.float32)
    group = (iota((rows, n_batch), 0) // BEAMS == iota((rows, n_batch), 1)).astype(jnp.float32)
    hit = jnp.where(count(named, group) > 0.0, 1.0, 0.0)
    left, right = iota((2 * slots, 2 * slots), 0), iota((2 * slots, 2 * slots), 1)
    before = (left // slots == right // slots) & (right < left)
    rank = count(before.astype(jnp.float32), hit)
    taken = (iota((rows, rows), 0) == parents[...]).astype(jnp.float32)
    continued = count(named, taken)

    place = iota((2 * slots, n_batch), 0)
    found = []
    for k in range(2 * capacity):
        holder = k // capacity
        chosen = (hit > 0.0) & (rank == float(k % capacity)) & (place // slots == holder)
        found.append(jnp.sum(jnp.where(chosen, place + 1, 0), axis=0, keepdims=True))
    found = jnp.concatenate(found, axis=0)

    requests = [z * 2 + core]
    for mask in masks_here(n_req):
        requests += [(z ^ mask) * 2, (z ^ mask) * 2 + 1]
    for i, request in enumerate(requests):
        lane = iota((rows, VECS), 1)
        spread = iota((rows, VECS), 0) == request * BEAMS + lane % BEAMS
        rows_ref[: 2 * slots, :] = count(continued, spread.astype(jnp.float32))
        rows_ref[2 * slots :, :] = jnp.zeros((8, VECS), jnp.float32)
        mask = iota(found.shape, 1) == request
        picked = jnp.sum(jnp.where(mask, found, 0), axis=1, keepdims=True)
        values = []
        for k in range(2 * capacity):
            index = picked[k, 0]
            row = jnp.where(index > 0, index - 1, 2 * slots)
            member_ref[i, k : k + 1, :] = rows_ref[pl.ds(row, 1), :]
            pool_ref = near if k < capacity else far_ref
            base = 0 if k < capacity else slots
            content = pool_ref[jnp.maximum(index - 1 - base, 0)]
            tokens = slice(k * half, (k + 1) * half)
            if i == 0:
                home_keys_ref[0, tokens, :] = content[:, :HD]
            else:
                keys_ref[i - 1, tokens, :] = content[:, :HD]
            values.append(content[:, HD:])
        values = jnp.concatenate(values, axis=0).T
        if i == 0:
            home_values_ref[0] = values
        else:
            values_ref[i - 1] = values


def suffix_parts(vectors, keys_ref, values_ref, members, place=0):
    n_slots = members[0].shape[0]
    half = keys_ref.shape[1] // n_slots
    scores = [scores_of(keys_ref[place + i], each) for i, each in enumerate(vectors)]
    softmaxes = []
    for member, score in zip(members, scores):
        pieces = [
            jnp.where(
                member[k : k + 1, :] > 0.0, score[k * half : (k + 1) * half], big_negative
            )
            for k in range(n_slots)
        ]
        softmaxes.append(weighted(jnp.concatenate(pieces, axis=0)))
    return [
        (
            top,
            total,
            jnp.dot(
                values_ref[place + i], weights.astype(jnp.bfloat16), preferred_element_type=jnp.float32
            ),
        )
        for i, (top, total, weights) in enumerate(softmaxes)
    ]


def away_kernel(place, keys_ref, values_ref, member_ref, message_ref, out_ref, *after_ref):
    for ref in after_ref:
        ref[...] = jnp.zeros(ref.shape, jnp.float32)
    vectors = [stacked_heads(message_ref[core]) for core in range(2)]
    members = [member_ref[1 + place + core] for core in range(2)]
    store_units(out_ref, suffix_parts(vectors, keys_ref, values_ref, members, place))


def home_part(length_ref, keys_ref, values_ref, member_ref, queries_ref, prompt_ref):
    vectors = stacked_heads(queries_ref[...])
    half = keys_ref.shape[1] // member_ref.shape[1]
    (suffix,) = suffix_parts([vectors], keys_ref, values_ref, [member_ref[0]])
    return merged([prompt_part(length_ref[0], half, prompt_ref, vectors), suffix])


def pair_heads_kernel(*refs):
    *inputs, _, out_ref = refs
    store_units(out_ref, [home_part(*inputs)])


def own_heads_kernel(*refs):
    *inputs, _, summed_ref, stats_ref = refs
    top, total, summed_ref[...] = home_part(*inputs)
    stats_ref[...] = jnp.concatenate([top, total, jnp.zeros((6, VECS), jnp.float32)], axis=0)


def sibling_kernel(*rest):
    units, out_ref = rest[:-2], rest[-1]
    core = lax.axis_index("core")
    store_units(out_ref, [merged([load_unit(unit, 1 - core) for unit in units])])


def final_kernel(*rest):
    units, (last_ref, shared_ref, summed_ref, stats_ref, out_ref) = rest[:-5], rest[-5:]
    core = lax.axis_index("core")
    parts = [load_unit(unit, core) for unit in units]
    parts += [load_unit(last_ref), load_unit(shared_ref)]
    parts.append((stats_ref[0:1], stats_ref[1:2], summed_ref[...]))
    _, total, summed = merged(parts)
    attended = (summed / total).T
    for h in range(HEADS):
        out_ref[:, h * HD : (h + 1) * HD] = attended[h * BEAMS : (h + 1) * BEAMS]


def in_hbm(value):
    return pltpu.with_memory_space_constraint(value, pltpu.HBM)


def on_device(queries, prompt_cache, pool, block_table, parents, lengths):
    n_req = lax.axis_size("z")
    n_batch = 2 * n_req
    ndist = 2 ** (SUF + 1) - 2
    capacity = 2 * ((ndist // 2 + n_batch - 1) // n_batch)
    slots, _, half, width = pool.shape
    tokens = prompt_cache.shape[2]
    rows = block_table.shape[0]
    vmem = pl.BlockSpec(memory_space=pltpu.VMEM)
    params = pltpu.CompilerParams(vmem_limit_bytes=32 * 2**20)
    some = pl.CostEstimate(flops=2 * 10**8, bytes_accessed=2**21, transcendentals=0)
    early = pl.CostEstimate(flops=2 * 10**10, bytes_accessed=0, transcendentals=0)

    hbm = pl.BlockSpec(memory_space=pltpu.HBM)
    near = pool.reshape(slots, half, width)
    far = swapped(near, "core")
    other = swapped(queries, "pair")
    staged = [queries, block_table.T, parents.reshape(1, rows)]
    own, table, row_parents = pl.pallas_call(
        stage_kernel,
        out_shape=tuple(pltpu.VMEM(each.shape, each.dtype) for each in staged),
        in_specs=[hbm] * len(staged),
        out_specs=(vmem,) * len(staged),
        scratch_shapes=[pltpu.SemaphoreType.DMA((len(staged),))],
        compiler_params=params,
        name="stage",
    )(*[in_hbm(each) for each in staged])
    both = pl.pallas_call(
        pack_kernel,
        out_shape=pltpu.VMEM((2,) + queries.shape, jnp.bfloat16),
        in_specs=[vmem] * 2,
        out_specs=vmem,
        compiler_params=params,
        cost_estimate=early,
        name="both_cores",
    )(own, swapped(queries, "core"))
    n_messages = n_req - 1
    order = [1, 0] + list(range(n_messages - 1, 1, -1)) if n_messages > 1 else [0]
    messages = {k: exchanged(both, k) for k in order}

    home_keys, home_values, keys, values, member = pl.pallas_call(
        functools.partial(prepare_kernel, capacity),
        out_shape=(
            pltpu.VMEM((1, 2 * capacity * half, HD), jnp.bfloat16),
            pltpu.VMEM((1, HD, 2 * capacity * half), jnp.bfloat16),
            pltpu.VMEM((n_req, 2 * capacity * half, HD), jnp.bfloat16),
            pltpu.VMEM((n_req, HD, 2 * capacity * half), jnp.bfloat16),
            pltpu.VMEM((1 + n_req, 2 * capacity, VECS), jnp.float32),
        ),
        in_specs=[vmem] * 4,
        out_specs=(vmem,) * 5,
        scratch_shapes=[pltpu.VMEM((2 * slots + 8, VECS), jnp.float32)],
        compiler_params=params,
        cost_estimate=some,
        name="prepare",
    )(
        near,
        table,
        row_parents,
        far,
    )

    received, after = [], []
    for k in order:
        out = [pltpu.VMEM((2 * HD + STAT_ROWS, VECS), jnp.bfloat16)]
        if k == order[0]:
            out.append(pltpu.VMEM((8, VECS), jnp.float32))
        units, *token = pl.pallas_call(
            functools.partial(away_kernel, 2 * ((k + 1) // 2)),
            out_shape=out,
            in_specs=[vmem] * 4,
            out_specs=[vmem] * len(out),
            compiler_params=params,
            cost_estimate=some,
            name="suffix_away",
        )(keys, values, member, messages[k])
        received.append(exchanged(units, k))
        after += token

    home = pl.CostEstimate(
        flops=5 * tokens * VECS * HD, bytes_accessed=2 * tokens * width, transcendentals=0
    )
    home_specs = [pl.BlockSpec(memory_space=pltpu.SMEM)] + [vmem] * 6
    prompt = prompt_cache.reshape(tokens, width)
    given = pl.pallas_call(
        pair_heads_kernel,
        out_shape=pltpu.VMEM((HD + STAT_ROWS, VECS), jnp.bfloat16),
        in_specs=home_specs,
        out_specs=vmem,
        compiler_params=params,
        cost_estimate=home,
        name="home_pair_heads",
    )(lengths, home_keys, home_values, member, other, prompt, *after)
    last = swapped(given, "pair")
    summed, stats = pl.pallas_call(
        own_heads_kernel,
        out_shape=(pltpu.VMEM((HD, VECS), jnp.float32), pltpu.VMEM((8, VECS), jnp.float32)),
        in_specs=home_specs,
        out_specs=(vmem,) * 2,
        compiler_params=params,
        cost_estimate=home,
        name="home_own_heads",
    )(lengths, home_keys, home_values, member, own, prompt, *after)

    share = pl.pallas_call(
        sibling_kernel,
        out_shape=pltpu.VMEM((HD + STAT_ROWS, VECS), jnp.bfloat16),
        in_specs=[vmem] * (n_messages + 1),
        out_specs=vmem,
        compiler_params=params,
        name="sibling_share",
    )(*received, stats)

    return pl.pallas_call(
        final_kernel,
        out_shape=jax.ShapeDtypeStruct((BEAMS, HEADS * HD), jnp.float32),
        in_specs=[vmem] * (4 + n_messages),
        out_specs=vmem,
        compiler_params=params,
        name="combine",
    )(*received, last, swapped(share, "core"), summed, stats)


def solution(mesh):
    n_batch, n_mp = mesh.devices.shape
    split = jax.sharding.Mesh(
        mesh.devices.reshape(n_batch // 2, 2, n_mp // 2, 2), ("z", "core", "group", "pair")
    )
    batch, mp = ("z", "core"), ("group", "pair")
    return jax.shard_map(
        on_device,
        mesh=split,
        in_specs=(
            P(batch, mp),
            P(batch, mp, None, None),
            P(batch, mp, None, None),
            P(),
            P(),
            P(batch),
        ),
        out_specs=P(batch, mp),
        check_vma=False,
    )
```

```python
import functools

import jax
import jax.numpy as jnp
from jax import lax
from jax.experimental import pallas as pl
from jax.experimental.pallas import tpu as pltpu
from jax.sharding import PartitionSpec as P

HD = 128
GROUP = 16
BEAMS = 16
SUF = 4
HEADS = GROUP // 2
VECS = HEADS * BEAMS
STAT_ROWS = 16
CHUNK = 512
FIRST_MASKS = (2, 3, 1)
SURELY_VALID = 1024

big_negative = -1e30
to_exp2 = HD ** (-0.5) * 1.4426950408889634


def swapped(value, axis):
    return lax.ppermute(value, axis, [(0, 1), (1, 0)])


def exchanged(value, mask):
    pairs = []
    for z in range(lax.axis_size("z")):
        for core in range(2):
            for pair in range(2):
                target = ((z ^ mask) * 2 + core) * 2 + (pair ^ core)
                pairs.append(((z * 2 + core) * 2 + pair, target))
    return lax.ppermute(value, ("z", "core", "pair"), pairs)


def mask_order(n_req):
    return FIRST_MASKS if n_req == 4 else tuple(range(n_req - 1, 0, -1))


def stage_kernel(*refs):
    n = (len(refs) - 1) // 2
    copies = [
        pltpu.make_async_copy(refs[i], refs[n + i], refs[-1].at[i]) for i in range(n)
    ]
    for copy in copies:
        copy.start()
    for copy in copies:
        copy.wait()


def pack_kernel(own_ref, sibling_ref, out_ref):
    core = lax.axis_index("core")
    out_ref[core] = own_ref[...]
    out_ref[1 - core] = sibling_ref[...]


def stacked_heads(q):
    return jnp.concatenate([q[:, h * HD : (h + 1) * HD] for h in range(HEADS)], axis=0)


def scores_of(keys, vectors):
    return lax.dot_general(
        keys, vectors, (((1,), (1,)), ((), ())), preferred_element_type=jnp.float32
    )


def summed_of(values, weights):
    return lax.dot_general(
        values,
        weights.astype(jnp.bfloat16),
        (((0,), (0,)), ((), ())),
        preferred_element_type=jnp.float32,
    )


def merged(parts):
    top = functools.reduce(jnp.maximum, [p[0] for p in parts])
    total = 0.0
    summed = 0.0
    for part_top, part_total, part_summed in parts:
        factor = jnp.exp2((part_top - top) * to_exp2)
        total = total + part_total * factor
        summed = summed + part_summed * factor
    return top, total, summed


def weighted(scores):
    top = jnp.max(scores, axis=0, keepdims=True)
    weights = jnp.exp2((scores - top) * to_exp2)
    return top, jnp.sum(weights, axis=0, keepdims=True), weights


def three_pieces(x):
    first = x.astype(jnp.bfloat16).astype(jnp.float32)
    rest = x - first
    second = rest.astype(jnp.bfloat16).astype(jnp.float32)
    return [first, second, rest - second]


def store_units(ref, parts):
    rows = []
    for i, (top, total, summed) in enumerate(parts):
        ref[i * HD : (i + 1) * HD, :] = summed.astype(jnp.bfloat16)
        rows += three_pieces(top) + three_pieces(total)
    rows.append(jnp.zeros((STAT_ROWS - len(rows), VECS), jnp.float32))
    ref[len(parts) * HD :, :] = jnp.concatenate(rows, axis=0).astype(jnp.bfloat16)


def load_unit(ref, i=0):
    sums = ref.shape[0] - STAT_ROWS
    stats = ref[sums:, :].astype(jnp.float32)
    if isinstance(i, int):
        rows = [stats[6 * i + k : 6 * i + k + 1] for k in range(6)]
    else:
        rows = [jnp.where(i == 0, stats[k : k + 1], stats[6 + k : 7 + k]) for k in range(6)]
    part = ref[pl.ds(pl.multiple_of(i * HD, HD), HD), :]
    return rows[0] + rows[1] + rows[2], rows[3] + rows[4] + rows[5], part.astype(jnp.float32)


def count(left, right):
    return jnp.dot(
        left.astype(jnp.bfloat16), right.astype(jnp.bfloat16), preferred_element_type=jnp.float32
    )


def iota(shape, axis):
    return lax.broadcasted_iota(jnp.int32, shape, axis)


def prompt_part(length, half, prompt_ref, vectors):
    parity = lax.axis_index("pair")
    whole = lax.div(length, 2 * half)
    valid = whole * half + jnp.clip(length - whole * (2 * half) - parity * half, 0, half)
    chunks = [slice(i, i + CHUNK) for i in range(0, prompt_ref.shape[0], CHUNK)]
    scores = [scores_of(vectors, prompt_ref[chunk, :HD]) for chunk in chunks]
    place = iota(scores[0].shape, 1)
    scores = [
        score
        if chunk.stop <= SURELY_VALID
        else jnp.where(place < valid - chunk.start, score, big_negative)
        for chunk, score in zip(chunks, scores)
    ]
    top = jnp.max(functools.reduce(jnp.maximum, scores), axis=1, keepdims=True)
    totals, summed = 0.0, 0.0
    for chunk, score in zip(chunks, scores):
        weights = jnp.exp2((score - top) * to_exp2)
        totals = totals + weights
        summed = summed + jnp.dot(
            weights.astype(jnp.bfloat16), prompt_ref[chunk, HD:], preferred_element_type=jnp.float32
        )
    total = jnp.sum(totals, axis=1, keepdims=True)
    stats = jnp.where(iota(summed.shape, 1) == 0, top, total).T
    return stats[0:1], stats[1:2], summed.T


def prepare_kernel(
    capacity, near, table, parents, far_ref,
    home_keys_ref, home_values_ref, keys_ref, values_ref, member_ref, rows_ref,
):
    n_req = lax.axis_size("z")
    slots, half, _ = near.shape
    rows = table.shape[1]
    n_batch = rows // BEAMS
    z, core = lax.axis_index("z"), lax.axis_index("core")

    slot = iota((2 * slots, rows), 0)
    mine = slot < slots
    block = jnp.where(mine, slot, slot - slots) + jnp.where(mine, 2 * z + core, 2 * z + 1 - core) * slots
    named = functools.reduce(
        jnp.logical_or, [table[j : j + 1, :] == block for j in range(SUF)]
    ).astype(jnp.float32)
    group = (iota((rows, n_batch), 0) // BEAMS == iota((rows, n_batch), 1)).astype(jnp.float32)
    hit = jnp.where(count(named, group) > 0.0, 1.0, 0.0)
    left, right = iota((2 * slots, 2 * slots), 0), iota((2 * slots, 2 * slots), 1)
    before = (left // slots == right // slots) & (right < left)
    rank = count(before.astype(jnp.float32), hit)
    taken = (iota((rows, rows), 0) == parents[...]).astype(jnp.float32)
    continued = count(named, taken)

    place = iota((2 * slots, n_batch), 0)
    found = []
    for k in range(2 * capacity):
        holder = k // capacity
        chosen = (hit > 0.0) & (rank == float(k % capacity)) & (place // slots == holder)
        found.append(jnp.sum(jnp.where(chosen, place + 1, 0), axis=0, keepdims=True))
    found = jnp.concatenate(found, axis=0)

    requests = [z * 2 + core]
    for mask in range(1, n_req):
        requests += [(z ^ mask) * 2, (z ^ mask) * 2 + 1]
    for i, request in enumerate(requests):
        lane = iota((rows, VECS), 1)
        spread = iota((rows, VECS), 0) == request * BEAMS + lane % BEAMS
        rows_ref[: 2 * slots, :] = count(continued, spread.astype(jnp.float32))
        rows_ref[2 * slots :, :] = jnp.zeros((8, VECS), jnp.float32)
        mask = iota(found.shape, 1) == request
        picked = jnp.sum(jnp.where(mask, found, 0), axis=1, keepdims=True)
        values = []
        for k in range(2 * capacity):
            index = picked[k, 0]
            row = jnp.where(index > 0, index - 1, 2 * slots)
            member_ref[i, k : k + 1, :] = rows_ref[pl.ds(row, 1), :]
            pool_ref = near if k < capacity else far_ref
            base = 0 if k < capacity else slots
            content = pool_ref[jnp.maximum(index - 1 - base, 0)]
            tokens = slice(k * half, (k + 1) * half)
            if i == 0:
                home_keys_ref[0, tokens, :] = content[:, :HD]
            else:
                keys_ref[i - 1, tokens, :] = content[:, :HD]
            values.append(content[:, HD:])
        values = jnp.concatenate(values, axis=0).T
        if i == 0:
            home_values_ref[0] = values
        else:
            values_ref[i - 1] = values


def suffix_parts(vectors, keys_ref, values_ref, members, place=0):
    n_slots = members[0].shape[0]
    half = keys_ref.shape[1] // n_slots
    scores = [scores_of(keys_ref[place + i], each) for i, each in enumerate(vectors)]
    softmaxes = []
    for member, score in zip(members, scores):
        pieces = [
            jnp.where(
                member[k : k + 1, :] > 0.0, score[k * half : (k + 1) * half], big_negative
            )
            for k in range(n_slots)
        ]
        softmaxes.append(weighted(jnp.concatenate(pieces, axis=0)))
    return [
        (
            top,
            total,
            jnp.dot(
                values_ref[place + i], weights.astype(jnp.bfloat16), preferred_element_type=jnp.float32
            ),
        )
        for i, (top, total, weights) in enumerate(softmaxes)
    ]


def away_kernel(place, keys_ref, values_ref, member_ref, message_ref, out_ref, *after_ref):
    for ref in after_ref:
        ref[...] = jnp.zeros(ref.shape, jnp.float32)
    vectors = [stacked_heads(message_ref[core]) for core in range(2)]
    members = [member_ref[1 + place + core] for core in range(2)]
    store_units(out_ref, suffix_parts(vectors, keys_ref, values_ref, members, place))


def home_part(length_ref, keys_ref, values_ref, member_ref, queries_ref, prompt_ref):
    vectors = stacked_heads(queries_ref[...])
    half = keys_ref.shape[1] // member_ref.shape[1]
    (suffix,) = suffix_parts([vectors], keys_ref, values_ref, [member_ref[0]])
    return merged([prompt_part(length_ref[0], half, prompt_ref, vectors), suffix])


def pair_heads_kernel(*refs):
    *inputs, _, out_ref = refs
    store_units(out_ref, [home_part(*inputs)])


def own_heads_kernel(*refs):
    *inputs, _, summed_ref, stats_ref = refs
    top, total, summed_ref[...] = home_part(*inputs)
    stats_ref[...] = jnp.concatenate([top, total, jnp.zeros((6, VECS), jnp.float32)], axis=0)


def sibling_kernel(*rest):
    units, out_ref = rest[:-2], rest[-1]
    core = lax.axis_index("core")
    store_units(out_ref, [merged([load_unit(unit, 1 - core) for unit in units])])


def final_kernel(*rest):
    units, (last_ref, shared_ref, summed_ref, stats_ref, out_ref) = rest[:-5], rest[-5:]
    core = lax.axis_index("core")
    parts = [load_unit(unit, core) for unit in units]
    parts += [load_unit(last_ref), load_unit(shared_ref)]
    parts.append((stats_ref[0:1], stats_ref[1:2], summed_ref[...]))
    _, total, summed = merged(parts)
    attended = (summed / total).T
    for h in range(HEADS):
        out_ref[:, h * HD : (h + 1) * HD] = attended[h * BEAMS : (h + 1) * BEAMS]


def in_hbm(value):
    return pltpu.with_memory_space_constraint(value, pltpu.HBM)


def on_device(queries, prompt_cache, pool, block_table, parents, lengths):
    n_req = lax.axis_size("z")
    n_batch = 2 * n_req
    ndist = 2 ** (SUF + 1) - 2
    capacity = 2 * ((ndist // 2 + n_batch - 1) // n_batch)
    slots, _, half, width = pool.shape
    tokens = prompt_cache.shape[2]
    rows = block_table.shape[0]
    vmem = pl.BlockSpec(memory_space=pltpu.VMEM)
    params = pltpu.CompilerParams(vmem_limit_bytes=32 * 2**20)
    some = pl.CostEstimate(flops=2 * 10**8, bytes_accessed=2**21, transcendentals=0)
    early = pl.CostEstimate(flops=2 * 10**10, bytes_accessed=0, transcendentals=0)

    hbm = pl.BlockSpec(memory_space=pltpu.HBM)
    near = pool.reshape(slots, half, width)
    far = swapped(near, "core")
    other = swapped(queries, "pair")
    staged = [queries, block_table.T, parents.reshape(1, rows)]
    own, table, row_parents = pl.pallas_call(
        stage_kernel,
        out_shape=tuple(pltpu.VMEM(each.shape, each.dtype) for each in staged),
        in_specs=[hbm] * len(staged),
        out_specs=(vmem,) * len(staged),
        scratch_shapes=[pltpu.SemaphoreType.DMA((len(staged),))],
        compiler_params=params,
        name="stage",
    )(*[in_hbm(each) for each in staged])
    both = pl.pallas_call(
        pack_kernel,
        out_shape=pltpu.VMEM((2,) + queries.shape, jnp.bfloat16),
        in_specs=[vmem] * 2,
        out_specs=vmem,
        compiler_params=params,
        cost_estimate=early,
        name="both_cores",
    )(own, swapped(queries, "core"))
    first, *others = mask_order(n_req)
    order = [first] + others[::-1]
    messages = {mask: exchanged(both, mask) for mask in order}

    home_keys, home_values, keys, values, member = pl.pallas_call(
        functools.partial(prepare_kernel, capacity),
        out_shape=(
            pltpu.VMEM((1, 2 * capacity * half, HD), jnp.bfloat16),
            pltpu.VMEM((1, HD, 2 * capacity * half), jnp.bfloat16),
            pltpu.VMEM((2 * n_req - 2, 2 * capacity * half, HD), jnp.bfloat16),
            pltpu.VMEM((2 * n_req - 2, HD, 2 * capacity * half), jnp.bfloat16),
            pltpu.VMEM((2 * n_req - 1, 2 * capacity, VECS), jnp.float32),
        ),
        in_specs=[vmem] * 4,
        out_specs=(vmem,) * 5,
        scratch_shapes=[pltpu.VMEM((2 * slots + 8, VECS), jnp.float32)],
        compiler_params=params,
        cost_estimate=some,
        name="prepare",
    )(
        near,
        table,
        row_parents,
        far,
    )

    received, after = [], []
    for mask in order:
        out = [pltpu.VMEM((2 * HD + STAT_ROWS, VECS), jnp.bfloat16)]
        if mask == first:
            out.append(pltpu.VMEM((8, VECS), jnp.float32))
        units, *token = pl.pallas_call(
            functools.partial(away_kernel, 2 * mask - 2),
            out_shape=out,
            in_specs=[vmem] * 4,
            out_specs=[vmem] * len(out),
            compiler_params=params,
            cost_estimate=some,
            name="suffix_away",
        )(keys, values, member, messages[mask])
        received.append(exchanged(units, mask))
        after += token

    home = pl.CostEstimate(
        flops=5 * tokens * VECS * HD, bytes_accessed=2 * tokens * width, transcendentals=0
    )
    home_specs = [pl.BlockSpec(memory_space=pltpu.SMEM)] + [vmem] * 6
    prompt = prompt_cache.reshape(tokens, width)
    given = pl.pallas_call(
        pair_heads_kernel,
        out_shape=pltpu.VMEM((HD + STAT_ROWS, VECS), jnp.bfloat16),
        in_specs=home_specs,
        out_specs=vmem,
        compiler_params=params,
        cost_estimate=home,
        name="home_pair_heads",
    )(lengths, home_keys, home_values, member, other, prompt, *after)
    last = swapped(given, "pair")
    summed, stats = pl.pallas_call(
        own_heads_kernel,
        out_shape=(pltpu.VMEM((HD, VECS), jnp.float32), pltpu.VMEM((8, VECS), jnp.float32)),
        in_specs=home_specs,
        out_specs=(vmem,) * 2,
        compiler_params=params,
        cost_estimate=home,
        name="home_own_heads",
    )(lengths, home_keys, home_values, member, own, prompt, *after)

    share = pl.pallas_call(
        sibling_kernel,
        out_shape=pltpu.VMEM((HD + STAT_ROWS, VECS), jnp.bfloat16),
        in_specs=[vmem] * n_req,
        out_specs=vmem,
        compiler_params=params,
        name="sibling_share",
    )(*received, stats)

    return pl.pallas_call(
        final_kernel,
        out_shape=jax.ShapeDtypeStruct((BEAMS, HEADS * HD), jnp.float32),
        in_specs=[vmem] * (3 + n_req),
        out_specs=vmem,
        compiler_params=params,
        name="combine",
    )(*received, last, swapped(share, "core"), summed, stats)


def solution(mesh):
    n_batch, n_mp = mesh.devices.shape
    split = jax.sharding.Mesh(
        mesh.devices.reshape(n_batch // 2, 2, n_mp // 2, 2), ("z", "core", "group", "pair")
    )
    batch, mp = ("z", "core"), ("group", "pair")
    return jax.shard_map(
        on_device,
        mesh=split,
        in_specs=(
            P(batch, mp),
            P(batch, mp, None, None),
            P(batch, mp, None, None),
            P(),
            P(),
            P(batch),
        ),
        out_specs=P(batch, mp),
        check_vma=False,
    )
```

```python
import functools

import jax
import jax.numpy as jnp
from jax import lax
from jax.experimental import pallas as pl
from jax.experimental.pallas import tpu as pltpu
from jax.sharding import PartitionSpec as P

HD = 128
GROUP = 16
BEAMS = 16
SUF = 4
HEADS = GROUP // 2
VECS = HEADS * BEAMS
STAT_ROWS = 16
CHUNK = 512
FIRST_MASKS = (2, 3, 1)
SURELY_VALID = 1024

big_negative = -1e30
to_exp2 = HD ** (-0.5) * 1.4426950408889634


def swapped(value, axis):
    return lax.ppermute(value, axis, [(0, 1), (1, 0)])


def exchanged(value, mask):
    pairs = []
    for z in range(lax.axis_size("z")):
        for core in range(2):
            for pair in range(2):
                target = ((z ^ mask) * 2 + core) * 2 + (pair ^ core)
                pairs.append(((z * 2 + core) * 2 + pair, target))
    return lax.ppermute(value, ("z", "core", "pair"), pairs)


def mask_order(n_req):
    return FIRST_MASKS if n_req == 4 else tuple(range(n_req - 1, 0, -1))


def stage_kernel(*refs):
    n = (len(refs) - 1) // 2
    copies = [
        pltpu.make_async_copy(refs[i], refs[n + i], refs[-1].at[i]) for i in range(n)
    ]
    for copy in copies:
        copy.start()
    for copy in copies:
        copy.wait()


def pack_kernel(own_ref, sibling_ref, out_ref):
    core = lax.axis_index("core")
    out_ref[core] = own_ref[...]
    out_ref[1 - core] = sibling_ref[...]


def stacked_heads(q):
    return jnp.concatenate([q[:, h * HD : (h + 1) * HD] for h in range(HEADS)], axis=0)


def scores_of(keys, vectors):
    return lax.dot_general(
        keys, vectors, (((1,), (1,)), ((), ())), preferred_element_type=jnp.float32
    )


def summed_of(values, weights):
    return lax.dot_general(
        values,
        weights.astype(jnp.bfloat16),
        (((0,), (0,)), ((), ())),
        preferred_element_type=jnp.float32,
    )


def merged(parts):
    top = functools.reduce(jnp.maximum, [p[0] for p in parts])
    total = 0.0
    summed = 0.0
    for part_top, part_total, part_summed in parts:
        factor = jnp.exp2((part_top - top) * to_exp2)
        total = total + part_total * factor
        summed = summed + part_summed * factor
    return top, total, summed


def weighted(scores):
    top = jnp.max(scores, axis=0, keepdims=True)
    weights = jnp.exp2((scores - top) * to_exp2)
    return top, jnp.sum(weights, axis=0, keepdims=True), weights


def three_pieces(x):
    first = x.astype(jnp.bfloat16).astype(jnp.float32)
    rest = x - first
    second = rest.astype(jnp.bfloat16).astype(jnp.float32)
    return [first, second, rest - second]


def store_units(ref, parts):
    rows = []
    for i, (top, total, summed) in enumerate(parts):
        ref[i * HD : (i + 1) * HD, :] = summed.astype(jnp.bfloat16)
        rows += three_pieces(top) + three_pieces(total)
    rows.append(jnp.zeros((STAT_ROWS - len(rows), VECS), jnp.float32))
    ref[len(parts) * HD :, :] = jnp.concatenate(rows, axis=0).astype(jnp.bfloat16)


def load_unit(ref, i=0):
    sums = ref.shape[0] - STAT_ROWS
    stats = ref[sums:, :].astype(jnp.float32)
    if isinstance(i, int):
        rows = [stats[6 * i + k : 6 * i + k + 1] for k in range(6)]
    else:
        rows = [jnp.where(i == 0, stats[k : k + 1], stats[6 + k : 7 + k]) for k in range(6)]
    part = ref[pl.ds(pl.multiple_of(i * HD, HD), HD), :]
    return rows[0] + rows[1] + rows[2], rows[3] + rows[4] + rows[5], part.astype(jnp.float32)


def count(left, right):
    return jnp.dot(
        left.astype(jnp.bfloat16), right.astype(jnp.bfloat16), preferred_element_type=jnp.float32
    )


def iota(shape, axis):
    return lax.broadcasted_iota(jnp.int32, shape, axis)


def prompt_part(length, half, prompt_ref, vectors):
    parity = lax.axis_index("pair")
    whole = lax.div(length, 2 * half)
    valid = whole * half + jnp.clip(length - whole * (2 * half) - parity * half, 0, half)
    chunks = [slice(i, i + CHUNK) for i in range(0, prompt_ref.shape[0], CHUNK)]
    scores = [scores_of(vectors, prompt_ref[chunk, :HD]) for chunk in chunks]
    place = iota(scores[0].shape, 1)
    scores = [
        score
        if chunk.stop <= SURELY_VALID
        else jnp.where(place < valid - chunk.start, score, big_negative)
        for chunk, score in zip(chunks, scores)
    ]
    top = jnp.max(functools.reduce(jnp.maximum, scores), axis=1, keepdims=True)
    totals, summed = 0.0, 0.0
    for chunk, score in zip(chunks, scores):
        weights = jnp.exp2((score - top) * to_exp2)
        totals = totals + weights
        summed = summed + jnp.dot(
            weights.astype(jnp.bfloat16), prompt_ref[chunk, HD:], preferred_element_type=jnp.float32
        )
    total = jnp.sum(totals, axis=1, keepdims=True)
    stats = jnp.where(iota(summed.shape, 1) == 0, top, total).T
    return stats[0:1], stats[1:2], summed.T


def prepare_kernel(
    capacity, near, table, parents, far_ref,
    home_keys_ref, home_values_ref, keys_ref, values_ref, member_ref, rows_ref,
):
    n_req = lax.axis_size("z")
    slots, half, _ = near.shape
    rows = table.shape[1]
    n_batch = rows // BEAMS
    z, core = lax.axis_index("z"), lax.axis_index("core")

    slot = iota((2 * slots, rows), 0)
    mine = slot < slots
    block = jnp.where(mine, slot, slot - slots) + jnp.where(mine, 2 * z + core, 2 * z + 1 - core) * slots
    named = functools.reduce(
        jnp.logical_or, [table[j : j + 1, :] == block for j in range(SUF)]
    ).astype(jnp.float32)
    group = (iota((rows, n_batch), 0) // BEAMS == iota((rows, n_batch), 1)).astype(jnp.float32)
    hit = jnp.where(count(named, group) > 0.0, 1.0, 0.0)
    left, right = iota((2 * slots, 2 * slots), 0), iota((2 * slots, 2 * slots), 1)
    before = (left // slots == right // slots) & (right < left)
    rank = count(before.astype(jnp.float32), hit)
    taken = (iota((rows, rows), 0) == parents[...]).astype(jnp.float32)
    continued = count(named, taken)

    place = iota((2 * slots, n_batch), 0)
    found = []
    for k in range(2 * capacity):
        holder = k // capacity
        chosen = (hit > 0.0) & (rank == float(k % capacity)) & (place // slots == holder)
        found.append(jnp.sum(jnp.where(chosen, place + 1, 0), axis=0, keepdims=True))
    found = jnp.concatenate(found, axis=0)

    requests = [z * 2 + core]
    for mask in range(1, n_req):
        requests += [(z ^ mask) * 2, (z ^ mask) * 2 + 1]
    for i, request in enumerate(requests):
        lane = iota((rows, VECS), 1)
        spread = iota((rows, VECS), 0) == request * BEAMS + lane % BEAMS
        rows_ref[: 2 * slots, :] = count(continued, spread.astype(jnp.float32))
        rows_ref[2 * slots :, :] = jnp.zeros((8, VECS), jnp.float32)
        mask = iota(found.shape, 1) == request
        picked = jnp.sum(jnp.where(mask, found, 0), axis=1, keepdims=True)
        values = []
        for k in range(2 * capacity):
            index = picked[k, 0]
            row = jnp.where(index > 0, index - 1, 2 * slots)
            member_ref[i, k : k + 1, :] = rows_ref[pl.ds(row, 1), :]
            pool_ref = near if k < capacity else far_ref
            base = 0 if k < capacity else slots
            content = pool_ref[jnp.maximum(index - 1 - base, 0)]
            tokens = slice(k * half, (k + 1) * half)
            if i == 0:
                home_keys_ref[0, tokens, :] = content[:, :HD]
            else:
                keys_ref[i - 1, tokens, :] = content[:, :HD]
            values.append(content[:, HD:])
        values = jnp.concatenate(values, axis=0).T
        if i == 0:
            home_values_ref[0] = values
        else:
            values_ref[i - 1] = values


def suffix_parts(vectors, keys_ref, values_ref, members, place=0):
    n_slots = members[0].shape[0]
    half = keys_ref.shape[1] // n_slots
    scores = [scores_of(keys_ref[place + i], each) for i, each in enumerate(vectors)]
    softmaxes = []
    for member, score in zip(members, scores):
        pieces = [
            jnp.where(
                member[k : k + 1, :] > 0.0, score[k * half : (k + 1) * half], big_negative
            )
            for k in range(n_slots)
        ]
        softmaxes.append(weighted(jnp.concatenate(pieces, axis=0)))
    return [
        (
            top,
            total,
            jnp.dot(
                values_ref[place + i], weights.astype(jnp.bfloat16), preferred_element_type=jnp.float32
            ),
        )
        for i, (top, total, weights) in enumerate(softmaxes)
    ]


def away_kernel(place, keys_ref, values_ref, member_ref, message_ref, after_ref, out_ref, *next_ref):
    for ref in next_ref:
        ref[...] = jnp.zeros(ref.shape, jnp.float32)
    vectors = [stacked_heads(message_ref[core]) for core in range(2)]
    members = [member_ref[1 + place + core] for core in range(2)]
    store_units(out_ref, suffix_parts(vectors, keys_ref, values_ref, members, place))


def home_part(length_ref, keys_ref, values_ref, member_ref, queries_ref, prompt_ref):
    vectors = stacked_heads(queries_ref[...])
    half = keys_ref.shape[1] // member_ref.shape[1]
    (suffix,) = suffix_parts([vectors], keys_ref, values_ref, [member_ref[0]])
    return merged([prompt_part(length_ref[0], half, prompt_ref, vectors), suffix])


def pair_heads_kernel(*refs):
    *inputs, out_ref = refs
    store_units(out_ref, [home_part(*inputs)])


def own_heads_kernel(*refs):
    *inputs, _, summed_ref, stats_ref = refs
    top, total, summed_ref[...] = home_part(*inputs)
    stats_ref[...] = jnp.concatenate([top, total, jnp.zeros((6, VECS), jnp.float32)], axis=0)


def sibling_kernel(*rest):
    units, out_ref = rest[:-2], rest[-1]
    core = lax.axis_index("core")
    store_units(out_ref, [merged([load_unit(unit, 1 - core) for unit in units])])


def final_kernel(*rest):
    units, (last_ref, shared_ref, summed_ref, stats_ref, out_ref) = rest[:-5], rest[-5:]
    core = lax.axis_index("core")
    parts = [load_unit(unit, core) for unit in units]
    parts += [load_unit(last_ref), load_unit(shared_ref)]
    parts.append((stats_ref[0:1], stats_ref[1:2], summed_ref[...]))
    _, total, summed = merged(parts)
    attended = (summed / total).T
    for h in range(HEADS):
        out_ref[:, h * HD : (h + 1) * HD] = attended[h * BEAMS : (h + 1) * BEAMS]


def in_hbm(value):
    return pltpu.with_memory_space_constraint(value, pltpu.HBM)


def on_device(queries, prompt_cache, pool, block_table, parents, lengths):
    n_req = lax.axis_size("z")
    n_batch = 2 * n_req
    ndist = 2 ** (SUF + 1) - 2
    capacity = 2 * ((ndist // 2 + n_batch - 1) // n_batch)
    slots, _, half, width = pool.shape
    tokens = prompt_cache.shape[2]
    rows = block_table.shape[0]
    vmem = pl.BlockSpec(memory_space=pltpu.VMEM)
    params = pltpu.CompilerParams(vmem_limit_bytes=32 * 2**20)
    little = pl.CostEstimate(flops=10**6, bytes_accessed=0, transcendentals=0)
    some = pl.CostEstimate(flops=2 * 10**8, bytes_accessed=2**21, transcendentals=0)
    early = pl.CostEstimate(flops=2 * 10**10, bytes_accessed=0, transcendentals=0)

    hbm = pl.BlockSpec(memory_space=pltpu.HBM)
    near = pool.reshape(slots, half, width)
    far = swapped(near, "core")
    other = swapped(queries, "pair")
    staged = [queries, block_table.T, parents.reshape(1, rows)]
    own, table, row_parents = pl.pallas_call(
        stage_kernel,
        out_shape=tuple(pltpu.VMEM(each.shape, each.dtype) for each in staged),
        in_specs=[hbm] * len(staged),
        out_specs=(vmem,) * len(staged),
        scratch_shapes=[pltpu.SemaphoreType.DMA((len(staged),))],
        compiler_params=params,
        name="stage",
    )(*[in_hbm(each) for each in staged])
    both = pl.pallas_call(
        pack_kernel,
        out_shape=pltpu.VMEM((2,) + queries.shape, jnp.bfloat16),
        in_specs=[vmem] * 2,
        out_specs=vmem,
        compiler_params=params,
        cost_estimate=early,
        name="both_cores",
    )(own, swapped(queries, "core"))
    first, *others = mask_order(n_req)
    order = others[::-1] + [first]
    messages = {mask: exchanged(both, mask) for mask in order}

    home_keys, home_values, keys, values, member = pl.pallas_call(
        functools.partial(prepare_kernel, capacity),
        out_shape=(
            pltpu.VMEM((1, 2 * capacity * half, HD), jnp.bfloat16),
            pltpu.VMEM((1, HD, 2 * capacity * half), jnp.bfloat16),
            pltpu.VMEM((2 * n_req - 2, 2 * capacity * half, HD), jnp.bfloat16),
            pltpu.VMEM((2 * n_req - 2, HD, 2 * capacity * half), jnp.bfloat16),
            pltpu.VMEM((2 * n_req - 1, 2 * capacity, VECS), jnp.float32),
        ),
        in_specs=[vmem] * 4,
        out_specs=(vmem,) * 5,
        scratch_shapes=[pltpu.VMEM((2 * slots + 8, VECS), jnp.float32)],
        compiler_params=params,
        cost_estimate=some,
        name="prepare",
    )(
        near,
        table,
        row_parents,
        far,
    )

    home = pl.CostEstimate(
        flops=5 * tokens * VECS * HD, bytes_accessed=2 * tokens * width, transcendentals=0
    )
    home_specs = [pl.BlockSpec(memory_space=pltpu.SMEM)] + [vmem] * 5
    prompt = prompt_cache.reshape(tokens, width)
    given = pl.pallas_call(
        pair_heads_kernel,
        out_shape=pltpu.VMEM((HD + STAT_ROWS, VECS), jnp.bfloat16),
        in_specs=home_specs,
        out_specs=vmem,
        compiler_params=params,
        cost_estimate=little,
        name="home_pair_heads",
    )(lengths, home_keys, home_values, member, other, prompt)
    received, after = [], []
    for mask in order:
        out = [pltpu.VMEM((2 * HD + STAT_ROWS, VECS), jnp.bfloat16)]
        if mask == first:
            out.append(pltpu.VMEM((8, VECS), jnp.float32))
        units, *token = pl.pallas_call(
            functools.partial(away_kernel, 2 * mask - 2),
            out_shape=out,
            in_specs=[vmem] * 5,
            out_specs=[vmem] * len(out),
            compiler_params=params,
            cost_estimate=some,
            name="suffix_away",
        )(keys, values, member, messages[mask], given)
        received.append(exchanged(units, mask))
        after += token

    last = swapped(given, "pair")
    summed, stats = pl.pallas_call(
        own_heads_kernel,
        out_shape=(pltpu.VMEM((HD, VECS), jnp.float32), pltpu.VMEM((8, VECS), jnp.float32)),
        in_specs=home_specs + [vmem],
        out_specs=(vmem,) * 2,
        compiler_params=params,
        cost_estimate=home,
        name="home_own_heads",
    )(lengths, home_keys, home_values, member, own, prompt, *after)

    share = pl.pallas_call(
        sibling_kernel,
        out_shape=pltpu.VMEM((HD + STAT_ROWS, VECS), jnp.bfloat16),
        in_specs=[vmem] * n_req,
        out_specs=vmem,
        compiler_params=params,
        name="sibling_share",
    )(*received, stats)

    return pl.pallas_call(
        final_kernel,
        out_shape=jax.ShapeDtypeStruct((BEAMS, HEADS * HD), jnp.float32),
        in_specs=[vmem] * (3 + n_req),
        out_specs=vmem,
        compiler_params=params,
        name="combine",
    )(*received, last, swapped(share, "core"), summed, stats)


def solution(mesh):
    n_batch, n_mp = mesh.devices.shape
    split = jax.sharding.Mesh(
        mesh.devices.reshape(n_batch // 2, 2, n_mp // 2, 2), ("z", "core", "group", "pair")
    )
    batch, mp = ("z", "core"), ("group", "pair")
    return jax.shard_map(
        on_device,
        mesh=split,
        in_specs=(
            P(batch, mp),
            P(batch, mp, None, None),
            P(batch, mp, None, None),
            P(),
            P(),
            P(batch),
        ),
        out_specs=P(batch, mp),
        check_vma=False,
    )
```

```python
import functools

import jax
import jax.numpy as jnp
from jax import lax
from jax.experimental import pallas as pl
from jax.experimental.pallas import tpu as pltpu
from jax.sharding import PartitionSpec as P

HD = 128
GROUP = 16
BEAMS = 16
SUF = 4
HEADS = GROUP // 2
VECS = HEADS * BEAMS
STAT_ROWS = 16
CHUNK = 512
FIRST_MASKS = (2, 3, 1)
SURELY_VALID = 1024

big_negative = -1e30
to_exp2 = HD ** (-0.5) * 1.4426950408889634


def swapped(value, axis):
    return lax.ppermute(value, axis, [(0, 1), (1, 0)])


def exchanged(value, mask):
    pairs = []
    for z in range(lax.axis_size("z")):
        for core in range(2):
            for pair in range(2):
                target = ((z ^ mask) * 2 + core) * 2 + (pair ^ core)
                pairs.append(((z * 2 + core) * 2 + pair, target))
    return lax.ppermute(value, ("z", "core", "pair"), pairs)


def mask_order(n_req):
    return FIRST_MASKS if n_req == 4 else tuple(range(n_req - 1, 0, -1))


def stage_kernel(*refs):
    n = (len(refs) - 1) // 2
    copies = [
        pltpu.make_async_copy(refs[i], refs[n + i], refs[-1].at[i]) for i in range(n)
    ]
    for copy in copies:
        copy.start()
    for copy in copies:
        copy.wait()


def pack_kernel(own_ref, sibling_ref, out_ref):
    core = lax.axis_index("core")
    out_ref[core] = own_ref[...]
    out_ref[1 - core] = sibling_ref[...]


def stacked_heads(q):
    return jnp.concatenate([q[:, h * HD : (h + 1) * HD] for h in range(HEADS)], axis=0)


def scores_of(keys, vectors):
    return lax.dot_general(
        keys, vectors, (((1,), (1,)), ((), ())), preferred_element_type=jnp.float32
    )


def summed_of(values, weights):
    return lax.dot_general(
        values,
        weights.astype(jnp.bfloat16),
        (((0,), (0,)), ((), ())),
        preferred_element_type=jnp.float32,
    )


def merged(parts):
    top = functools.reduce(jnp.maximum, [p[0] for p in parts])
    total = 0.0
    summed = 0.0
    for part_top, part_total, part_summed in parts:
        factor = jnp.exp2((part_top - top) * to_exp2)
        total = total + part_total * factor
        summed = summed + part_summed * factor
    return top, total, summed


def weighted(scores):
    top = jnp.max(scores, axis=0, keepdims=True)
    weights = jnp.exp2((scores - top) * to_exp2)
    return top, jnp.sum(weights, axis=0, keepdims=True), weights


def three_pieces(x):
    first = x.astype(jnp.bfloat16).astype(jnp.float32)
    rest = x - first
    second = rest.astype(jnp.bfloat16).astype(jnp.float32)
    return [first, second, rest - second]


def store_units(ref, parts):
    rows = []
    for i, (top, total, summed) in enumerate(parts):
        ref[i * HD : (i + 1) * HD, :] = summed.astype(jnp.bfloat16)
        rows += three_pieces(top) + three_pieces(total)
    rows.append(jnp.zeros((STAT_ROWS - len(rows), VECS), jnp.float32))
    ref[len(parts) * HD :, :] = jnp.concatenate(rows, axis=0).astype(jnp.bfloat16)


def load_unit(ref, i=0):
    sums = ref.shape[0] - STAT_ROWS
    stats = ref[sums:, :].astype(jnp.float32)
    if isinstance(i, int):
        rows = [stats[6 * i + k : 6 * i + k + 1] for k in range(6)]
    else:
        rows = [jnp.where(i == 0, stats[k : k + 1], stats[6 + k : 7 + k]) for k in range(6)]
    part = ref[pl.ds(pl.multiple_of(i * HD, HD), HD), :]
    return rows[0] + rows[1] + rows[2], rows[3] + rows[4] + rows[5], part.astype(jnp.float32)


def count(left, right):
    return jnp.dot(
        left.astype(jnp.bfloat16), right.astype(jnp.bfloat16), preferred_element_type=jnp.float32
    )


def iota(shape, axis):
    return lax.broadcasted_iota(jnp.int32, shape, axis)


def prompt_part(length, half, prompt_ref, vectors):
    parity = lax.axis_index("pair")
    whole = lax.div(length, 2 * half)
    valid = whole * half + jnp.clip(length - whole * (2 * half) - parity * half, 0, half)
    chunks = [slice(i, i + CHUNK) for i in range(0, prompt_ref.shape[0], CHUNK)]
    scores = [scores_of(vectors, prompt_ref[chunk, :HD]) for chunk in chunks]
    place = iota(scores[0].shape, 1)
    scores = [
        score
        if chunk.stop <= SURELY_VALID
        else jnp.where(place < valid - chunk.start, score, big_negative)
        for chunk, score in zip(chunks, scores)
    ]
    top = jnp.max(functools.reduce(jnp.maximum, scores), axis=1, keepdims=True)
    totals, summed = 0.0, 0.0
    for chunk, score in zip(chunks, scores):
        weights = jnp.exp2((score - top) * to_exp2)
        totals = totals + weights
        summed = summed + jnp.dot(
            weights.astype(jnp.bfloat16), prompt_ref[chunk, HD:], preferred_element_type=jnp.float32
        )
    total = jnp.sum(totals, axis=1, keepdims=True)
    stats = jnp.where(iota(summed.shape, 1) == 0, top, total).T
    return stats[0:1], stats[1:2], summed.T


def prepare_kernel(
    capacity, near, table, parents, far_ref,
    home_keys_ref, home_values_ref, keys_ref, values_ref, member_ref, rows_ref,
):
    n_req = lax.axis_size("z")
    slots, half, _ = near.shape
    rows = table.shape[1]
    n_batch = rows // BEAMS
    z, core = lax.axis_index("z"), lax.axis_index("core")

    slot = iota((2 * slots, rows), 0)
    mine = slot < slots
    block = jnp.where(mine, slot, slot - slots) + jnp.where(mine, 2 * z + core, 2 * z + 1 - core) * slots
    named = functools.reduce(
        jnp.logical_or, [table[j : j + 1, :] == block for j in range(SUF)]
    ).astype(jnp.float32)
    group = (iota((rows, n_batch), 0) // BEAMS == iota((rows, n_batch), 1)).astype(jnp.float32)
    hit = jnp.where(count(named, group) > 0.0, 1.0, 0.0)
    left, right = iota((2 * slots, 2 * slots), 0), iota((2 * slots, 2 * slots), 1)
    before = (left // slots == right // slots) & (right < left)
    rank = count(before.astype(jnp.float32), hit)
    taken = (iota((rows, rows), 0) == parents[...]).astype(jnp.float32)
    continued = count(named, taken)

    place = iota((2 * slots, n_batch), 0)
    found = []
    for k in range(2 * capacity):
        holder = k // capacity
        chosen = (hit > 0.0) & (rank == float(k % capacity)) & (place // slots == holder)
        found.append(jnp.sum(jnp.where(chosen, place + 1, 0), axis=0, keepdims=True))
    found = jnp.concatenate(found, axis=0)

    requests = [z * 2 + core]
    for mask in range(1, n_req):
        requests += [(z ^ mask) * 2, (z ^ mask) * 2 + 1]
    for i, request in enumerate(requests):
        lane = iota((rows, VECS), 1)
        spread = iota((rows, VECS), 0) == request * BEAMS + lane % BEAMS
        rows_ref[: 2 * slots, :] = count(continued, spread.astype(jnp.float32))
        rows_ref[2 * slots :, :] = jnp.zeros((8, VECS), jnp.float32)
        mask = iota(found.shape, 1) == request
        picked = jnp.sum(jnp.where(mask, found, 0), axis=1, keepdims=True)
        values = []
        for k in range(2 * capacity):
            index = picked[k, 0]
            row = jnp.where(index > 0, index - 1, 2 * slots)
            member_ref[i, k : k + 1, :] = rows_ref[pl.ds(row, 1), :]
            pool_ref = near if k < capacity else far_ref
            base = 0 if k < capacity else slots
            content = pool_ref[jnp.maximum(index - 1 - base, 0)]
            tokens = slice(k * half, (k + 1) * half)
            if i == 0:
                home_keys_ref[0, tokens, :] = content[:, :HD]
            else:
                keys_ref[i - 1, tokens, :] = content[:, :HD]
            values.append(content[:, HD:])
        values = jnp.concatenate(values, axis=0).T
        if i == 0:
            home_values_ref[0] = values
        else:
            values_ref[i - 1] = values


def suffix_parts(vectors, keys_ref, values_ref, members, place=0):
    n_slots = members[0].shape[0]
    half = keys_ref.shape[1] // n_slots
    scores = [scores_of(keys_ref[place + i], each) for i, each in enumerate(vectors)]
    softmaxes = []
    for member, score in zip(members, scores):
        pieces = [
            jnp.where(
                member[k : k + 1, :] > 0.0, score[k * half : (k + 1) * half], big_negative
            )
            for k in range(n_slots)
        ]
        softmaxes.append(weighted(jnp.concatenate(pieces, axis=0)))
    return [
        (
            top,
            total,
            jnp.dot(
                values_ref[place + i], weights.astype(jnp.bfloat16), preferred_element_type=jnp.float32
            ),
        )
        for i, (top, total, weights) in enumerate(softmaxes)
    ]


def away_kernel(place, keys_ref, values_ref, member_ref, message_ref, out_ref, *after_ref):
    for ref in after_ref:
        ref[...] = jnp.zeros(ref.shape, jnp.float32)
    vectors = [stacked_heads(message_ref[core]) for core in range(2)]
    members = [member_ref[1 + place + core] for core in range(2)]
    store_units(out_ref, suffix_parts(vectors, keys_ref, values_ref, members, place))


def home_part(length_ref, keys_ref, values_ref, member_ref, queries_ref, prompt_ref):
    vectors = stacked_heads(queries_ref[...])
    half = keys_ref.shape[1] // member_ref.shape[1]
    (suffix,) = suffix_parts([vectors], keys_ref, values_ref, [member_ref[0]])
    return merged([prompt_part(length_ref[0], half, prompt_ref, vectors), suffix])


def pair_heads_kernel(*refs):
    *inputs, _, out_ref = refs
    store_units(out_ref, [home_part(*inputs)])


def own_heads_kernel(*refs):
    *inputs, _, summed_ref, stats_ref = refs
    top, total, summed_ref[...] = home_part(*inputs)
    stats_ref[...] = jnp.concatenate([top, total, jnp.zeros((6, VECS), jnp.float32)], axis=0)


def sibling_kernel(*rest):
    units, out_ref = rest[:-1], rest[-1]
    core = lax.axis_index("core")
    store_units(out_ref, [merged([load_unit(unit, 1 - core) for unit in units])])


def final_kernel(*rest):
    units, (last_ref, shared_ref, summed_ref, stats_ref, out_ref) = rest[:-5], rest[-5:]
    core = lax.axis_index("core")
    parts = [load_unit(unit, core) for unit in units]
    parts += [load_unit(last_ref), load_unit(shared_ref)]
    parts.append((stats_ref[0:1], stats_ref[1:2], summed_ref[...]))
    _, total, summed = merged(parts)
    attended = (summed / total).T
    for h in range(HEADS):
        out_ref[:, h * HD : (h + 1) * HD] = attended[h * BEAMS : (h + 1) * BEAMS]


def in_hbm(value):
    return pltpu.with_memory_space_constraint(value, pltpu.HBM)


def on_device(queries, prompt_cache, pool, block_table, parents, lengths):
    n_req = lax.axis_size("z")
    n_batch = 2 * n_req
    ndist = 2 ** (SUF + 1) - 2
    capacity = 2 * ((ndist // 2 + n_batch - 1) // n_batch)
    slots, _, half, width = pool.shape
    tokens = prompt_cache.shape[2]
    rows = block_table.shape[0]
    vmem = pl.BlockSpec(memory_space=pltpu.VMEM)
    params = pltpu.CompilerParams(vmem_limit_bytes=32 * 2**20)
    some = pl.CostEstimate(flops=2 * 10**8, bytes_accessed=2**21, transcendentals=0)
    early = pl.CostEstimate(flops=2 * 10**10, bytes_accessed=0, transcendentals=0)

    hbm = pl.BlockSpec(memory_space=pltpu.HBM)
    near = pool.reshape(slots, half, width)
    far = swapped(near, "core")
    other = swapped(queries, "pair")
    staged = [queries, block_table.T, parents.reshape(1, rows)]
    own, table, row_parents = pl.pallas_call(
        stage_kernel,
        out_shape=tuple(pltpu.VMEM(each.shape, each.dtype) for each in staged),
        in_specs=[hbm] * len(staged),
        out_specs=(vmem,) * len(staged),
        scratch_shapes=[pltpu.SemaphoreType.DMA((len(staged),))],
        compiler_params=params,
        name="stage",
    )(*[in_hbm(each) for each in staged])
    both = pl.pallas_call(
        pack_kernel,
        out_shape=pltpu.VMEM((2,) + queries.shape, jnp.bfloat16),
        in_specs=[vmem] * 2,
        out_specs=vmem,
        compiler_params=params,
        cost_estimate=early,
        name="both_cores",
    )(own, swapped(queries, "core"))
    first, *others = mask_order(n_req)
    order = [first] + others[::-1]
    messages = {mask: exchanged(both, mask) for mask in order}

    home_keys, home_values, keys, values, member = pl.pallas_call(
        functools.partial(prepare_kernel, capacity),
        out_shape=(
            pltpu.VMEM((1, 2 * capacity * half, HD), jnp.bfloat16),
            pltpu.VMEM((1, HD, 2 * capacity * half), jnp.bfloat16),
            pltpu.VMEM((2 * n_req - 2, 2 * capacity * half, HD), jnp.bfloat16),
            pltpu.VMEM((2 * n_req - 2, HD, 2 * capacity * half), jnp.bfloat16),
            pltpu.VMEM((2 * n_req - 1, 2 * capacity, VECS), jnp.float32),
        ),
        in_specs=[vmem] * 4,
        out_specs=(vmem,) * 5,
        scratch_shapes=[pltpu.VMEM((2 * slots + 8, VECS), jnp.float32)],
        compiler_params=params,
        cost_estimate=some,
        name="prepare",
    )(
        near,
        table,
        row_parents,
        far,
    )

    received, after = [], []
    for mask in order:
        out = [pltpu.VMEM((2 * HD + STAT_ROWS, VECS), jnp.bfloat16)]
        if mask == first:
            out.append(pltpu.VMEM((8, VECS), jnp.float32))
        units, *token = pl.pallas_call(
            functools.partial(away_kernel, 2 * mask - 2),
            out_shape=out,
            in_specs=[vmem] * 4,
            out_specs=[vmem] * len(out),
            compiler_params=params,
            cost_estimate=some,
            name="suffix_away",
        )(keys, values, member, messages[mask])
        received.append(exchanged(units, mask))
        after += token

    home = pl.CostEstimate(
        flops=12 * tokens * VECS * HD, bytes_accessed=2 * tokens * width, transcendentals=0
    )
    home_specs = [pl.BlockSpec(memory_space=pltpu.SMEM)] + [vmem] * 6
    prompt = prompt_cache.reshape(tokens, width)
    given = pl.pallas_call(
        pair_heads_kernel,
        out_shape=pltpu.VMEM((HD + STAT_ROWS, VECS), jnp.bfloat16),
        in_specs=home_specs,
        out_specs=vmem,
        compiler_params=params,
        cost_estimate=home,
        name="home_pair_heads",
    )(lengths, home_keys, home_values, member, other, prompt, *after)
    last = swapped(given, "pair")
    summed, stats = pl.pallas_call(
        own_heads_kernel,
        out_shape=(pltpu.VMEM((HD, VECS), jnp.float32), pltpu.VMEM((8, VECS), jnp.float32)),
        in_specs=home_specs,
        out_specs=(vmem,) * 2,
        compiler_params=params,
        cost_estimate=home,
        name="home_own_heads",
    )(lengths, home_keys, home_values, member, own, prompt, *after)

    share = pl.pallas_call(
        sibling_kernel,
        out_shape=pltpu.VMEM((HD + STAT_ROWS, VECS), jnp.bfloat16),
        in_specs=[vmem] * (n_req - 1),
        out_specs=vmem,
        compiler_params=params,
        name="sibling_share",
    )(*received)

    return pl.pallas_call(
        final_kernel,
        out_shape=jax.ShapeDtypeStruct((BEAMS, HEADS * HD), jnp.float32),
        in_specs=[vmem] * (3 + n_req),
        out_specs=vmem,
        compiler_params=params,
        name="combine",
    )(*received, last, swapped(share, "core"), summed, stats)


def solution(mesh):
    n_batch, n_mp = mesh.devices.shape
    split = jax.sharding.Mesh(
        mesh.devices.reshape(n_batch // 2, 2, n_mp // 2, 2), ("z", "core", "group", "pair")
    )
    batch, mp = ("z", "core"), ("group", "pair")
    return jax.shard_map(
        on_device,
        mesh=split,
        in_specs=(
            P(batch, mp),
            P(batch, mp, None, None),
            P(batch, mp, None, None),
            P(),
            P(),
            P(batch),
        ),
        out_specs=P(batch, mp),
        check_vma=False,
    )
```

```python
import functools

import jax
import jax.numpy as jnp
from jax import lax
from jax.experimental import pallas as pl
from jax.experimental.pallas import tpu as pltpu
from jax.sharding import PartitionSpec as P

HD = 128
GROUP = 16
BEAMS = 16
SUF = 4
HEADS = GROUP // 2
VECS = HEADS * BEAMS
STAT_ROWS = 16
CHUNK = 512
FIRST_MASKS = (2, 3, 1)
SURELY_VALID = 1024

big_negative = -1e30
to_exp2 = HD ** (-0.5) * 1.4426950408889634


def swapped(value, axis):
    return lax.ppermute(value, axis, [(0, 1), (1, 0)])


def exchanged(value, mask):
    pairs = []
    for z in range(lax.axis_size("z")):
        for core in range(2):
            for pair in range(2):
                target = ((z ^ mask) * 2 + core) * 2 + (pair ^ core)
                pairs.append(((z * 2 + core) * 2 + pair, target))
    return lax.ppermute(value, ("z", "core", "pair"), pairs)


def mask_order(n_req):
    return FIRST_MASKS if n_req == 4 else tuple(range(n_req - 1, 0, -1))


def stage_kernel(*refs):
    n = (len(refs) - 1) // 2
    copies = [
        pltpu.make_async_copy(refs[i], refs[n + i], refs[-1].at[i]) for i in range(n)
    ]
    for copy in copies:
        copy.start()
    for copy in copies:
        copy.wait()


def pack_kernel(own_ref, sibling_ref, out_ref):
    core = lax.axis_index("core")
    out_ref[core] = own_ref[...]
    out_ref[1 - core] = sibling_ref[...]


def stacked_heads(q):
    return jnp.concatenate([q[:, h * HD : (h + 1) * HD] for h in range(HEADS)], axis=0)


def scores_of(keys, vectors):
    return lax.dot_general(
        keys, vectors, (((1,), (1,)), ((), ())), preferred_element_type=jnp.float32
    )


def summed_of(values, weights):
    return lax.dot_general(
        values,
        weights.astype(jnp.bfloat16),
        (((0,), (0,)), ((), ())),
        preferred_element_type=jnp.float32,
    )


def merged(parts):
    top = functools.reduce(jnp.maximum, [p[0] for p in parts])
    total = 0.0
    summed = 0.0
    for part_top, part_total, part_summed in parts:
        factor = jnp.exp2((part_top - top) * to_exp2)
        total = total + part_total * factor
        summed = summed + part_summed * factor
    return top, total, summed


def weighted(scores):
    top = jnp.max(scores, axis=0, keepdims=True)
    weights = jnp.exp2((scores - top) * to_exp2)
    return top, jnp.sum(weights, axis=0, keepdims=True), weights


def three_pieces(x):
    first = x.astype(jnp.bfloat16).astype(jnp.float32)
    rest = x - first
    second = rest.astype(jnp.bfloat16).astype(jnp.float32)
    return [first, second, rest - second]


def store_units(ref, parts):
    rows = []
    for i, (top, total, summed) in enumerate(parts):
        ref[i * HD : (i + 1) * HD, :] = summed.astype(jnp.bfloat16)
        rows += three_pieces(top) + three_pieces(total)
    rows.append(jnp.zeros((STAT_ROWS - len(rows), VECS), jnp.float32))
    ref[len(parts) * HD :, :] = jnp.concatenate(rows, axis=0).astype(jnp.bfloat16)


def load_unit(ref, i=0):
    sums = ref.shape[0] - STAT_ROWS
    stats = ref[sums:, :].astype(jnp.float32)
    if isinstance(i, int):
        rows = [stats[6 * i + k : 6 * i + k + 1] for k in range(6)]
    else:
        rows = [jnp.where(i == 0, stats[k : k + 1], stats[6 + k : 7 + k]) for k in range(6)]
    part = ref[pl.ds(pl.multiple_of(i * HD, HD), HD), :]
    return rows[0] + rows[1] + rows[2], rows[3] + rows[4] + rows[5], part.astype(jnp.float32)


def count(left, right):
    return jnp.dot(
        left.astype(jnp.bfloat16), right.astype(jnp.bfloat16), preferred_element_type=jnp.float32
    )


def iota(shape, axis):
    return lax.broadcasted_iota(jnp.int32, shape, axis)


def prompt_part(length, half, prompt_ref, vectors):
    parity = lax.axis_index("pair")
    whole = lax.div(length, 2 * half)
    valid = whole * half + jnp.clip(length - whole * (2 * half) - parity * half, 0, half)
    chunks = [slice(i, i + CHUNK) for i in range(0, prompt_ref.shape[0], CHUNK)]
    scores = [scores_of(vectors, prompt_ref[chunk, :HD]) for chunk in chunks]
    place = iota(scores[0].shape, 1)
    scores = [
        score
        if chunk.stop <= SURELY_VALID
        else jnp.where(place < valid - chunk.start, score, big_negative)
        for chunk, score in zip(chunks, scores)
    ]
    top = jnp.max(functools.reduce(jnp.maximum, scores), axis=1, keepdims=True)
    totals, summed = 0.0, 0.0
    for chunk, score in zip(chunks, scores):
        weights = jnp.exp2((score - top) * to_exp2)
        totals = totals + weights
        summed = summed + jnp.dot(
            weights.astype(jnp.bfloat16), prompt_ref[chunk, HD:], preferred_element_type=jnp.float32
        )
    total = jnp.sum(totals, axis=1, keepdims=True)
    stats = jnp.where(iota(summed.shape, 1) == 0, top, total).T
    return stats[0:1], stats[1:2], summed.T


def prepare_kernel(
    capacity, near, table, parents, far_ref,
    home_keys_ref, home_values_ref, keys_ref, values_ref, member_ref, rows_ref,
):
    n_req = lax.axis_size("z")
    slots, half, _ = near.shape
    rows = table.shape[1]
    n_batch = rows // BEAMS
    z, core = lax.axis_index("z"), lax.axis_index("core")

    slot = iota((2 * slots, rows), 0)
    mine = slot < slots
    block = jnp.where(mine, slot, slot - slots) + jnp.where(mine, 2 * z + core, 2 * z + 1 - core) * slots
    named = functools.reduce(
        jnp.logical_or, [table[j : j + 1, :] == block for j in range(SUF)]
    ).astype(jnp.float32)
    group = (iota((rows, n_batch), 0) // BEAMS == iota((rows, n_batch), 1)).astype(jnp.float32)
    hit = jnp.where(count(named, group) > 0.0, 1.0, 0.0)
    left, right = iota((2 * slots, 2 * slots), 0), iota((2 * slots, 2 * slots), 1)
    before = (left // slots == right // slots) & (right < left)
    rank = count(before.astype(jnp.float32), hit)
    taken = (iota((rows, rows), 0) == parents[...]).astype(jnp.float32)
    continued = count(named, taken)

    place = iota((2 * slots, n_batch), 0)
    found = []
    for k in range(2 * capacity):
        holder = k // capacity
        chosen = (hit > 0.0) & (rank == float(k % capacity)) & (place // slots == holder)
        found.append(jnp.sum(jnp.where(chosen, place + 1, 0), axis=0, keepdims=True))
    found = jnp.concatenate(found, axis=0)

    requests = [z * 2 + core]
    for mask in range(1, n_req):
        requests += [(z ^ mask) * 2, (z ^ mask) * 2 + 1]
    for i, request in enumerate(requests):
        lane = iota((rows, VECS), 1)
        spread = iota((rows, VECS), 0) == request * BEAMS + lane % BEAMS
        rows_ref[: 2 * slots, :] = count(continued, spread.astype(jnp.float32))
        rows_ref[2 * slots :, :] = jnp.zeros((8, VECS), jnp.float32)
        mask = iota(found.shape, 1) == request
        picked = jnp.sum(jnp.where(mask, found, 0), axis=1, keepdims=True)
        values = []
        for k in range(2 * capacity):
            index = picked[k, 0]
            row = jnp.where(index > 0, index - 1, 2 * slots)
            member_ref[i, k : k + 1, :] = rows_ref[pl.ds(row, 1), :]
            pool_ref = near if k < capacity else far_ref
            base = 0 if k < capacity else slots
            content = pool_ref[jnp.maximum(index - 1 - base, 0)]
            tokens = slice(k * half, (k + 1) * half)
            if i == 0:
                home_keys_ref[0, tokens, :] = content[:, :HD]
            else:
                keys_ref[i - 1, tokens, :] = content[:, :HD]
            values.append(content[:, HD:])
        values = jnp.concatenate(values, axis=0).T
        if i == 0:
            home_values_ref[0] = values
        else:
            values_ref[i - 1] = values


def suffix_parts(vectors, keys_ref, values_ref, members, place=0):
    n_slots = members[0].shape[0]
    half = keys_ref.shape[1] // n_slots
    scores = [scores_of(keys_ref[place + i], each) for i, each in enumerate(vectors)]
    softmaxes = []
    for member, score in zip(members, scores):
        pieces = [
            jnp.where(
                member[k : k + 1, :] > 0.0, score[k * half : (k + 1) * half], big_negative
            )
            for k in range(n_slots)
        ]
        softmaxes.append(weighted(jnp.concatenate(pieces, axis=0)))
    return [
        (
            top,
            total,
            jnp.dot(
                values_ref[place + i], weights.astype(jnp.bfloat16), preferred_element_type=jnp.float32
            ),
        )
        for i, (top, total, weights) in enumerate(softmaxes)
    ]


def away_kernel(place, keys_ref, values_ref, member_ref, message_ref, out_ref, *after_ref):
    for ref in after_ref:
        ref[...] = jnp.zeros(ref.shape, jnp.float32)
    vectors = [stacked_heads(message_ref[core]) for core in range(2)]
    members = [member_ref[1 + place + core] for core in range(2)]
    store_units(out_ref, suffix_parts(vectors, keys_ref, values_ref, members, place))


def home_part(length_ref, keys_ref, values_ref, member_ref, queries_ref, prompt_ref):
    vectors = stacked_heads(queries_ref[...])
    half = keys_ref.shape[1] // member_ref.shape[1]
    (suffix,) = suffix_parts([vectors], keys_ref, values_ref, [member_ref[0]])
    return merged([prompt_part(length_ref[0], half, prompt_ref, vectors), suffix])


def pair_heads_kernel(*refs):
    *inputs, _, out_ref = refs
    store_units(out_ref, [home_part(*inputs)])


def own_heads_kernel(*refs):
    *inputs, _, summed_ref, stats_ref = refs
    top, total, summed_ref[...] = home_part(*inputs)
    stats_ref[...] = jnp.concatenate([top, total, jnp.zeros((6, VECS), jnp.float32)], axis=0)


def sibling_kernel(*rest):
    units, out_ref = rest[:-2], rest[-1]
    core = lax.axis_index("core")
    store_units(out_ref, [merged([load_unit(unit, 1 - core) for unit in units])])


def final_kernel(*rest):
    units, (last_ref, shared_ref, summed_ref, stats_ref, out_ref) = rest[:-5], rest[-5:]
    core = lax.axis_index("core")
    parts = [load_unit(unit, core) for unit in units]
    parts += [load_unit(last_ref), load_unit(shared_ref)]
    parts.append((stats_ref[0:1], stats_ref[1:2], summed_ref[...]))
    _, total, summed = merged(parts)
    attended = (summed / total).T
    for h in range(HEADS):
        out_ref[:, h * HD : (h + 1) * HD] = attended[h * BEAMS : (h + 1) * BEAMS]


def in_hbm(value):
    return pltpu.with_memory_space_constraint(value, pltpu.HBM)


def on_device(queries, prompt_cache, pool, block_table, parents, lengths):
    n_req = lax.axis_size("z")
    n_batch = 2 * n_req
    ndist = 2 ** (SUF + 1) - 2
    capacity = 2 * ((ndist // 2 + n_batch - 1) // n_batch)
    slots, _, half, width = pool.shape
    tokens = prompt_cache.shape[2]
    rows = block_table.shape[0]
    vmem = pl.BlockSpec(memory_space=pltpu.VMEM)
    params = pltpu.CompilerParams(vmem_limit_bytes=32 * 2**20)
    some = pl.CostEstimate(flops=2 * 10**8, bytes_accessed=2**21, transcendentals=0)
    early = pl.CostEstimate(flops=2 * 10**10, bytes_accessed=0, transcendentals=0)

    hbm = pl.BlockSpec(memory_space=pltpu.HBM)
    near = pool.reshape(slots, half, width)
    far = swapped(near, "core")
    other = swapped(queries, "pair")
    staged = [queries, block_table.T, parents.reshape(1, rows)]
    own, table, row_parents = pl.pallas_call(
        stage_kernel,
        out_shape=tuple(pltpu.VMEM(each.shape, each.dtype) for each in staged),
        in_specs=[hbm] * len(staged),
        out_specs=(vmem,) * len(staged),
        scratch_shapes=[pltpu.SemaphoreType.DMA((len(staged),))],
        compiler_params=params,
        name="stage",
    )(*[in_hbm(each) for each in staged])
    both = pl.pallas_call(
        pack_kernel,
        out_shape=pltpu.VMEM((2,) + queries.shape, jnp.bfloat16),
        in_specs=[vmem] * 2,
        out_specs=vmem,
        compiler_params=params,
        cost_estimate=early,
        name="both_cores",
    )(own, swapped(queries, "core"))
    first, *others = mask_order(n_req)
    order = [first] + others[::-1]
    messages = {mask: exchanged(both, mask) for mask in order}

    home_keys, home_values, keys, values, member = pl.pallas_call(
        functools.partial(prepare_kernel, capacity),
        out_shape=(
            pltpu.VMEM((1, 2 * capacity * half, HD), jnp.bfloat16),
            pltpu.VMEM((1, HD, 2 * capacity * half), jnp.bfloat16),
            pltpu.VMEM((2 * n_req - 2, 2 * capacity * half, HD), jnp.bfloat16),
            pltpu.VMEM((2 * n_req - 2, HD, 2 * capacity * half), jnp.bfloat16),
            pltpu.VMEM((2 * n_req - 1, 2 * capacity, VECS), jnp.float32),
        ),
        in_specs=[vmem] * 4,
        out_specs=(vmem,) * 5,
        scratch_shapes=[pltpu.VMEM((2 * slots + 8, VECS), jnp.float32)],
        compiler_params=params,
        cost_estimate=some,
        name="prepare",
    )(
        near,
        table,
        row_parents,
        far,
    )

    received, after = [], []
    for mask in order:
        out = [pltpu.VMEM((2 * HD + STAT_ROWS, VECS), jnp.bfloat16)]
        if mask == first:
            out.append(pltpu.VMEM((8, VECS), jnp.float32))
        units, *token = pl.pallas_call(
            functools.partial(away_kernel, 2 * mask - 2),
            out_shape=out,
            in_specs=[vmem] * 4,
            out_specs=[vmem] * len(out),
            compiler_params=params,
            cost_estimate=some,
            name="suffix_away",
        )(keys, values, member, messages[mask])
        received.append(exchanged(units, mask))
        after += token

    home = pl.CostEstimate(
        flops=8 * tokens * VECS * HD, bytes_accessed=2 * tokens * width, transcendentals=0
    )
    home_specs = [pl.BlockSpec(memory_space=pltpu.SMEM)] + [vmem] * 6
    prompt = prompt_cache.reshape(tokens, width)
    given = pl.pallas_call(
        pair_heads_kernel,
        out_shape=pltpu.VMEM((HD + STAT_ROWS, VECS), jnp.bfloat16),
        in_specs=home_specs,
        out_specs=vmem,
        compiler_params=params,
        cost_estimate=home,
        name="home_pair_heads",
    )(lengths, home_keys, home_values, member, other, prompt, *after)
    last = swapped(given, "pair")
    summed, stats = pl.pallas_call(
        own_heads_kernel,
        out_shape=(pltpu.VMEM((HD, VECS), jnp.float32), pltpu.VMEM((8, VECS), jnp.float32)),
        in_specs=home_specs,
        out_specs=(vmem,) * 2,
        compiler_params=params,
        cost_estimate=home,
        name="home_own_heads",
    )(lengths, home_keys, home_values, member, own, prompt, *after)

    share = pl.pallas_call(
        sibling_kernel,
        out_shape=pltpu.VMEM((HD + STAT_ROWS, VECS), jnp.bfloat16),
        in_specs=[vmem] * n_req,
        out_specs=vmem,
        compiler_params=params,
        name="sibling_share",
    )(*received, stats)

    return pl.pallas_call(
        final_kernel,
        out_shape=jax.ShapeDtypeStruct((BEAMS, HEADS * HD), jnp.float32),
        in_specs=[vmem] * (3 + n_req),
        out_specs=vmem,
        compiler_params=params,
        name="combine",
    )(*received, last, swapped(share, "core"), summed, stats)


def solution(mesh):
    n_batch, n_mp = mesh.devices.shape
    split = jax.sharding.Mesh(
        mesh.devices.reshape(n_batch // 2, 2, n_mp // 2, 2), ("z", "core", "group", "pair")
    )
    batch, mp = ("z", "core"), ("group", "pair")
    return jax.shard_map(
        on_device,
        mesh=split,
        in_specs=(
            P(batch, mp),
            P(batch, mp, None, None),
            P(batch, mp, None, None),
            P(),
            P(),
            P(batch),
        ),
        out_specs=P(batch, mp),
        check_vma=False,
    )
```

```python
import functools

import jax
import jax.numpy as jnp
from jax import lax
from jax.experimental import pallas as pl
from jax.experimental.pallas import tpu as pltpu
from jax.sharding import PartitionSpec as P

HD = 128
GROUP = 16
BEAMS = 16
SUF = 4
HEADS = GROUP // 2
VECS = HEADS * BEAMS
STAT_ROWS = 16
CHUNK = 512
FIRST_MASKS = (3, 1, 2)
SURELY_VALID = 1024

big_negative = -1e30
to_exp2 = HD ** (-0.5) * 1.4426950408889634


def swapped(value, axis):
    return lax.ppermute(value, axis, [(0, 1), (1, 0)])


def exchanged(value, mask):
    pairs = []
    for z in range(lax.axis_size("z")):
        for core in range(2):
            for pair in range(2):
                target = ((z ^ mask) * 2 + core) * 2 + (pair ^ core)
                pairs.append(((z * 2 + core) * 2 + pair, target))
    return lax.ppermute(value, ("z", "core", "pair"), pairs)


def mask_order(n_req):
    return FIRST_MASKS if n_req == 4 else tuple(range(n_req - 1, 0, -1))


def stage_kernel(*refs):
    n = (len(refs) - 1) // 2
    copies = [
        pltpu.make_async_copy(refs[i], refs[n + i], refs[-1].at[i]) for i in range(n)
    ]
    for copy in copies:
        copy.start()
    for copy in copies:
        copy.wait()


def pack_kernel(own_ref, sibling_ref, out_ref):
    core = lax.axis_index("core")
    out_ref[core] = own_ref[...]
    out_ref[1 - core] = sibling_ref[...]


def stacked_heads(q):
    return jnp.concatenate([q[:, h * HD : (h + 1) * HD] for h in range(HEADS)], axis=0)


def scores_of(keys, vectors):
    return lax.dot_general(
        keys, vectors, (((1,), (1,)), ((), ())), preferred_element_type=jnp.float32
    )


def summed_of(values, weights):
    return lax.dot_general(
        values,
        weights.astype(jnp.bfloat16),
        (((0,), (0,)), ((), ())),
        preferred_element_type=jnp.float32,
    )


def merged(parts):
    top = functools.reduce(jnp.maximum, [p[0] for p in parts])
    total = 0.0
    summed = 0.0
    for part_top, part_total, part_summed in parts:
        factor = jnp.exp2((part_top - top) * to_exp2)
        total = total + part_total * factor
        summed = summed + part_summed * factor
    return top, total, summed


def weighted(scores):
    top = jnp.max(scores, axis=0, keepdims=True)
    weights = jnp.exp2((scores - top) * to_exp2)
    return top, jnp.sum(weights, axis=0, keepdims=True), weights


def three_pieces(x):
    first = x.astype(jnp.bfloat16).astype(jnp.float32)
    rest = x - first
    second = rest.astype(jnp.bfloat16).astype(jnp.float32)
    return [first, second, rest - second]


def store_units(ref, parts):
    rows = []
    for i, (top, total, summed) in enumerate(parts):
        ref[i * HD : (i + 1) * HD, :] = summed.astype(jnp.bfloat16)
        rows += three_pieces(top) + three_pieces(total)
    rows.append(jnp.zeros((STAT_ROWS - len(rows), VECS), jnp.float32))
    ref[len(parts) * HD :, :] = jnp.concatenate(rows, axis=0).astype(jnp.bfloat16)


def load_unit(ref, i=0):
    sums = ref.shape[0] - STAT_ROWS
    stats = ref[sums:, :].astype(jnp.float32)
    if isinstance(i, int):
        rows = [stats[6 * i + k : 6 * i + k + 1] for k in range(6)]
    else:
        rows = [jnp.where(i == 0, stats[k : k + 1], stats[6 + k : 7 + k]) for k in range(6)]
    part = ref[pl.ds(pl.multiple_of(i * HD, HD), HD), :]
    return rows[0] + rows[1] + rows[2], rows[3] + rows[4] + rows[5], part.astype(jnp.float32)


def count(left, right):
    return jnp.dot(
        left.astype(jnp.bfloat16), right.astype(jnp.bfloat16), preferred_element_type=jnp.float32
    )


def iota(shape, axis):
    return lax.broadcasted_iota(jnp.int32, shape, axis)


def prompt_part(length, half, prompt_ref, vectors):
    parity = lax.axis_index("pair")
    whole = lax.div(length, 2 * half)
    valid = whole * half + jnp.clip(length - whole * (2 * half) - parity * half, 0, half)
    chunks = [slice(i, i + CHUNK) for i in range(0, prompt_ref.shape[0], CHUNK)]
    scores = [scores_of(vectors, prompt_ref[chunk, :HD]) for chunk in chunks]
    place = iota(scores[0].shape, 1)
    scores = [
        score
        if chunk.stop <= SURELY_VALID
        else jnp.where(place < valid - chunk.start, score, big_negative)
        for chunk, score in zip(chunks, scores)
    ]
    top = jnp.max(functools.reduce(jnp.maximum, scores), axis=1, keepdims=True)
    totals, summed = 0.0, 0.0
    for chunk, score in zip(chunks, scores):
        weights = jnp.exp2((score - top) * to_exp2)
        totals = totals + weights
        summed = summed + jnp.dot(
            weights.astype(jnp.bfloat16), prompt_ref[chunk, HD:], preferred_element_type=jnp.float32
        )
    total = jnp.sum(totals, axis=1, keepdims=True)
    stats = jnp.where(iota(summed.shape, 1) == 0, top, total).T
    return stats[0:1], stats[1:2], summed.T


def prepare_kernel(
    capacity, near, table, parents, far_ref,
    home_keys_ref, home_values_ref, keys_ref, values_ref, member_ref, rows_ref,
):
    n_req = lax.axis_size("z")
    slots, half, _ = near.shape
    rows = table.shape[1]
    n_batch = rows // BEAMS
    z, core = lax.axis_index("z"), lax.axis_index("core")

    slot = iota((2 * slots, rows), 0)
    mine = slot < slots
    block = jnp.where(mine, slot, slot - slots) + jnp.where(mine, 2 * z + core, 2 * z + 1 - core) * slots
    named = functools.reduce(
        jnp.logical_or, [table[j : j + 1, :] == block for j in range(SUF)]
    ).astype(jnp.float32)
    group = (iota((rows, n_batch), 0) // BEAMS == iota((rows, n_batch), 1)).astype(jnp.float32)
    hit = jnp.where(count(named, group) > 0.0, 1.0, 0.0)
    left, right = iota((2 * slots, 2 * slots), 0), iota((2 * slots, 2 * slots), 1)
    before = (left // slots == right // slots) & (right < left)
    rank = count(before.astype(jnp.float32), hit)
    taken = (iota((rows, rows), 0) == parents[...]).astype(jnp.float32)
    continued = count(named, taken)

    place = iota((2 * slots, n_batch), 0)
    found = []
    for k in range(2 * capacity):
        holder = k // capacity
        chosen = (hit > 0.0) & (rank == float(k % capacity)) & (place // slots == holder)
        found.append(jnp.sum(jnp.where(chosen, place + 1, 0), axis=0, keepdims=True))
    found = jnp.concatenate(found, axis=0)

    requests = [z * 2 + core]
    for mask in range(1, n_req):
        requests += [(z ^ mask) * 2, (z ^ mask) * 2 + 1]
    for i, request in enumerate(requests):
        lane = iota((rows, VECS), 1)
        spread = iota((rows, VECS), 0) == request * BEAMS + lane % BEAMS
        rows_ref[: 2 * slots, :] = count(continued, spread.astype(jnp.float32))
        rows_ref[2 * slots :, :] = jnp.zeros((8, VECS), jnp.float32)
        mask = iota(found.shape, 1) == request
        picked = jnp.sum(jnp.where(mask, found, 0), axis=1, keepdims=True)
        values = []
        for k in range(2 * capacity):
            index = picked[k, 0]
            row = jnp.where(index > 0, index - 1, 2 * slots)
            member_ref[i, k : k + 1, :] = rows_ref[pl.ds(row, 1), :]
            pool_ref = near if k < capacity else far_ref
            base = 0 if k < capacity else slots
            content = pool_ref[jnp.maximum(index - 1 - base, 0)]
            tokens = slice(k * half, (k + 1) * half)
            if i == 0:
                home_keys_ref[0, tokens, :] = content[:, :HD]
            else:
                keys_ref[i - 1, tokens, :] = content[:, :HD]
            values.append(content[:, HD:])
        values = jnp.concatenate(values, axis=0).T
        if i == 0:
            home_values_ref[0] = values
        else:
            values_ref[i - 1] = values


def suffix_parts(vectors, keys_ref, values_ref, members, place=0):
    n_slots = members[0].shape[0]
    half = keys_ref.shape[1] // n_slots
    scores = [scores_of(keys_ref[place + i], each) for i, each in enumerate(vectors)]
    softmaxes = []
    for member, score in zip(members, scores):
        pieces = [
            jnp.where(
                member[k : k + 1, :] > 0.0, score[k * half : (k + 1) * half], big_negative
            )
            for k in range(n_slots)
        ]
        softmaxes.append(weighted(jnp.concatenate(pieces, axis=0)))
    return [
        (
            top,
            total,
            jnp.dot(
                values_ref[place + i], weights.astype(jnp.bfloat16), preferred_element_type=jnp.float32
            ),
        )
        for i, (top, total, weights) in enumerate(softmaxes)
    ]


def away_kernel(place, keys_ref, values_ref, member_ref, message_ref, out_ref, *after_ref):
    for ref in after_ref:
        ref[...] = jnp.zeros(ref.shape, jnp.float32)
    vectors = [stacked_heads(message_ref[core]) for core in range(2)]
    members = [member_ref[1 + place + core] for core in range(2)]
    store_units(out_ref, suffix_parts(vectors, keys_ref, values_ref, members, place))


def home_part(length_ref, keys_ref, values_ref, member_ref, queries_ref, prompt_ref):
    vectors = stacked_heads(queries_ref[...])
    half = keys_ref.shape[1] // member_ref.shape[1]
    (suffix,) = suffix_parts([vectors], keys_ref, values_ref, [member_ref[0]])
    return merged([prompt_part(length_ref[0], half, prompt_ref, vectors), suffix])


def pair_heads_kernel(*refs):
    *inputs, _, out_ref = refs
    store_units(out_ref, [home_part(*inputs)])


def own_heads_kernel(*refs):
    *inputs, _, summed_ref, stats_ref = refs
    top, total, summed_ref[...] = home_part(*inputs)
    stats_ref[...] = jnp.concatenate([top, total, jnp.zeros((6, VECS), jnp.float32)], axis=0)


def sibling_kernel(*rest):
    units, out_ref = rest[:-2], rest[-1]
    core = lax.axis_index("core")
    store_units(out_ref, [merged([load_unit(unit, 1 - core) for unit in units])])


def final_kernel(*rest):
    units, (last_ref, shared_ref, summed_ref, stats_ref, out_ref) = rest[:-5], rest[-5:]
    core = lax.axis_index("core")
    parts = [load_unit(unit, core) for unit in units]
    parts += [load_unit(last_ref), load_unit(shared_ref)]
    parts.append((stats_ref[0:1], stats_ref[1:2], summed_ref[...]))
    _, total, summed = merged(parts)
    attended = (summed / total).T
    for h in range(HEADS):
        out_ref[:, h * HD : (h + 1) * HD] = attended[h * BEAMS : (h + 1) * BEAMS]


def in_hbm(value):
    return pltpu.with_memory_space_constraint(value, pltpu.HBM)


def on_device(queries, prompt_cache, pool, block_table, parents, lengths):
    n_req = lax.axis_size("z")
    n_batch = 2 * n_req
    ndist = 2 ** (SUF + 1) - 2
    capacity = 2 * ((ndist // 2 + n_batch - 1) // n_batch)
    slots, _, half, width = pool.shape
    tokens = prompt_cache.shape[2]
    rows = block_table.shape[0]
    vmem = pl.BlockSpec(memory_space=pltpu.VMEM)
    params = pltpu.CompilerParams(vmem_limit_bytes=32 * 2**20)
    some = pl.CostEstimate(flops=2 * 10**8, bytes_accessed=2**21, transcendentals=0)
    early = pl.CostEstimate(flops=2 * 10**10, bytes_accessed=0, transcendentals=0)

    hbm = pl.BlockSpec(memory_space=pltpu.HBM)
    near = pool.reshape(slots, half, width)
    far = swapped(near, "core")
    other = swapped(queries, "pair")
    staged = [queries, block_table.T, parents.reshape(1, rows)]
    own, table, row_parents = pl.pallas_call(
        stage_kernel,
        out_shape=tuple(pltpu.VMEM(each.shape, each.dtype) for each in staged),
        in_specs=[hbm] * len(staged),
        out_specs=(vmem,) * len(staged),
        scratch_shapes=[pltpu.SemaphoreType.DMA((len(staged),))],
        compiler_params=params,
        name="stage",
    )(*[in_hbm(each) for each in staged])
    both = pl.pallas_call(
        pack_kernel,
        out_shape=pltpu.VMEM((2,) + queries.shape, jnp.bfloat16),
        in_specs=[vmem] * 2,
        out_specs=vmem,
        compiler_params=params,
        cost_estimate=early,
        name="both_cores",
    )(own, swapped(queries, "core"))
    first, *others = mask_order(n_req)
    order = [first] + others[::-1]
    messages = {mask: exchanged(both, mask) for mask in order}

    home_keys, home_values, keys, values, member = pl.pallas_call(
        functools.partial(prepare_kernel, capacity),
        out_shape=(
            pltpu.VMEM((1, 2 * capacity * half, HD), jnp.bfloat16),
            pltpu.VMEM((1, HD, 2 * capacity * half), jnp.bfloat16),
            pltpu.VMEM((2 * n_req - 2, 2 * capacity * half, HD), jnp.bfloat16),
            pltpu.VMEM((2 * n_req - 2, HD, 2 * capacity * half), jnp.bfloat16),
            pltpu.VMEM((2 * n_req - 1, 2 * capacity, VECS), jnp.float32),
        ),
        in_specs=[vmem] * 4,
        out_specs=(vmem,) * 5,
        scratch_shapes=[pltpu.VMEM((2 * slots + 8, VECS), jnp.float32)],
        compiler_params=params,
        cost_estimate=some,
        name="prepare",
    )(
        near,
        table,
        row_parents,
        far,
    )

    received, after = [], []
    for mask in order:
        out = [pltpu.VMEM((2 * HD + STAT_ROWS, VECS), jnp.bfloat16)]
        if mask == first:
            out.append(pltpu.VMEM((8, VECS), jnp.float32))
        units, *token = pl.pallas_call(
            functools.partial(away_kernel, 2 * mask - 2),
            out_shape=out,
            in_specs=[vmem] * 4,
            out_specs=[vmem] * len(out),
            compiler_params=params,
            cost_estimate=some,
            name="suffix_away",
        )(keys, values, member, messages[mask])
        received.append(exchanged(units, mask))
        after += token

    home = pl.CostEstimate(
        flops=8 * tokens * VECS * HD, bytes_accessed=2 * tokens * width, transcendentals=0
    )
    home_specs = [pl.BlockSpec(memory_space=pltpu.SMEM)] + [vmem] * 6
    prompt = prompt_cache.reshape(tokens, width)
    given = pl.pallas_call(
        pair_heads_kernel,
        out_shape=pltpu.VMEM((HD + STAT_ROWS, VECS), jnp.bfloat16),
        in_specs=home_specs,
        out_specs=vmem,
        compiler_params=params,
        cost_estimate=home,
        name="home_pair_heads",
    )(lengths, home_keys, home_values, member, other, prompt, *after)
    last = swapped(given, "pair")
    summed, stats = pl.pallas_call(
        own_heads_kernel,
        out_shape=(pltpu.VMEM((HD, VECS), jnp.float32), pltpu.VMEM((8, VECS), jnp.float32)),
        in_specs=home_specs,
        out_specs=(vmem,) * 2,
        compiler_params=params,
        cost_estimate=home,
        name="home_own_heads",
    )(lengths, home_keys, home_values, member, own, prompt, *after)

    share = pl.pallas_call(
        sibling_kernel,
        out_shape=pltpu.VMEM((HD + STAT_ROWS, VECS), jnp.bfloat16),
        in_specs=[vmem] * n_req,
        out_specs=vmem,
        compiler_params=params,
        name="sibling_share",
    )(*received, stats)

    return pl.pallas_call(
        final_kernel,
        out_shape=jax.ShapeDtypeStruct((BEAMS, HEADS * HD), jnp.float32),
        in_specs=[vmem] * (3 + n_req),
        out_specs=vmem,
        compiler_params=params,
        name="combine",
    )(*received, last, swapped(share, "core"), summed, stats)


def solution(mesh):
    n_batch, n_mp = mesh.devices.shape
    split = jax.sharding.Mesh(
        mesh.devices.reshape(n_batch // 2, 2, n_mp // 2, 2), ("z", "core", "group", "pair")
    )
    batch, mp = ("z", "core"), ("group", "pair")
    return jax.shard_map(
        on_device,
        mesh=split,
        in_specs=(
            P(batch, mp),
            P(batch, mp, None, None),
            P(batch, mp, None, None),
            P(),
            P(),
            P(batch),
        ),
        out_specs=P(batch, mp),
        check_vma=False,
    )
```

```python
import functools

import jax
import jax.numpy as jnp
from jax import lax
from jax.experimental import pallas as pl
from jax.experimental.pallas import tpu as pltpu
from jax.sharding import PartitionSpec as P

HD = 128
GROUP = 16
BEAMS = 16
SUF = 4
HEADS = GROUP // 2
VECS = HEADS * BEAMS
STAT_ROWS = 16
CHUNK = 512
FIRST_MASKS = (2, 1, 3)
SURELY_VALID = 1024

big_negative = -1e30
to_exp2 = HD ** (-0.5) * 1.4426950408889634


def swapped(value, axis):
    return lax.ppermute(value, axis, [(0, 1), (1, 0)])


def exchanged(value, mask):
    pairs = []
    for z in range(lax.axis_size("z")):
        for core in range(2):
            for pair in range(2):
                target = ((z ^ mask) * 2 + core) * 2 + (pair ^ core)
                pairs.append(((z * 2 + core) * 2 + pair, target))
    return lax.ppermute(value, ("z", "core", "pair"), pairs)


def mask_order(n_req):
    return FIRST_MASKS if n_req == 4 else tuple(range(n_req - 1, 0, -1))


def stage_kernel(*refs):
    n = (len(refs) - 1) // 2
    copies = [
        pltpu.make_async_copy(refs[i], refs[n + i], refs[-1].at[i]) for i in range(n)
    ]
    for copy in copies:
        copy.start()
    for copy in copies:
        copy.wait()


def pack_kernel(own_ref, sibling_ref, out_ref):
    core = lax.axis_index("core")
    out_ref[core] = own_ref[...]
    out_ref[1 - core] = sibling_ref[...]


def stacked_heads(q):
    return jnp.concatenate([q[:, h * HD : (h + 1) * HD] for h in range(HEADS)], axis=0)


def scores_of(keys, vectors):
    return lax.dot_general(
        keys, vectors, (((1,), (1,)), ((), ())), preferred_element_type=jnp.float32
    )


def summed_of(values, weights):
    return lax.dot_general(
        values,
        weights.astype(jnp.bfloat16),
        (((0,), (0,)), ((), ())),
        preferred_element_type=jnp.float32,
    )


def merged(parts):
    top = functools.reduce(jnp.maximum, [p[0] for p in parts])
    total = 0.0
    summed = 0.0
    for part_top, part_total, part_summed in parts:
        factor = jnp.exp2((part_top - top) * to_exp2)
        total = total + part_total * factor
        summed = summed + part_summed * factor
    return top, total, summed


def weighted(scores):
    top = jnp.max(scores, axis=0, keepdims=True)
    weights = jnp.exp2((scores - top) * to_exp2)
    return top, jnp.sum(weights, axis=0, keepdims=True), weights


def three_pieces(x):
    first = x.astype(jnp.bfloat16).astype(jnp.float32)
    rest = x - first
    second = rest.astype(jnp.bfloat16).astype(jnp.float32)
    return [first, second, rest - second]


def store_units(ref, parts):
    rows = []
    for i, (top, total, summed) in enumerate(parts):
        ref[i * HD : (i + 1) * HD, :] = summed.astype(jnp.bfloat16)
        rows += three_pieces(top) + three_pieces(total)
    rows.append(jnp.zeros((STAT_ROWS - len(rows), VECS), jnp.float32))
    ref[len(parts) * HD :, :] = jnp.concatenate(rows, axis=0).astype(jnp.bfloat16)


def load_unit(ref, i=0):
    sums = ref.shape[0] - STAT_ROWS
    stats = ref[sums:, :].astype(jnp.float32)
    if isinstance(i, int):
        rows = [stats[6 * i + k : 6 * i + k + 1] for k in range(6)]
    else:
        rows = [jnp.where(i == 0, stats[k : k + 1], stats[6 + k : 7 + k]) for k in range(6)]
    part = ref[pl.ds(pl.multiple_of(i * HD, HD), HD), :]
    return rows[0] + rows[1] + rows[2], rows[3] + rows[4] + rows[5], part.astype(jnp.float32)


def count(left, right):
    return jnp.dot(
        left.astype(jnp.bfloat16), right.astype(jnp.bfloat16), preferred_element_type=jnp.float32
    )


def iota(shape, axis):
    return lax.broadcasted_iota(jnp.int32, shape, axis)


def prompt_part(length, half, prompt_ref, vectors):
    parity = lax.axis_index("pair")
    whole = lax.div(length, 2 * half)
    valid = whole * half + jnp.clip(length - whole * (2 * half) - parity * half, 0, half)
    chunks = [slice(i, i + CHUNK) for i in range(0, prompt_ref.shape[0], CHUNK)]
    scores = [scores_of(vectors, prompt_ref[chunk, :HD]) for chunk in chunks]
    place = iota(scores[0].shape, 1)
    scores = [
        score
        if chunk.stop <= SURELY_VALID
        else jnp.where(place < valid - chunk.start, score, big_negative)
        for chunk, score in zip(chunks, scores)
    ]
    top = jnp.max(functools.reduce(jnp.maximum, scores), axis=1, keepdims=True)
    totals, summed = 0.0, 0.0
    for chunk, score in zip(chunks, scores):
        weights = jnp.exp2((score - top) * to_exp2)
        totals = totals + weights
        summed = summed + jnp.dot(
            weights.astype(jnp.bfloat16), prompt_ref[chunk, HD:], preferred_element_type=jnp.float32
        )
    total = jnp.sum(totals, axis=1, keepdims=True)
    stats = jnp.where(iota(summed.shape, 1) == 0, top, total).T
    return stats[0:1], stats[1:2], summed.T


def prepare_kernel(
    capacity, near, table, parents, far_ref,
    home_keys_ref, home_values_ref, keys_ref, values_ref, member_ref, rows_ref,
):
    n_req = lax.axis_size("z")
    slots, half, _ = near.shape
    rows = table.shape[1]
    n_batch = rows // BEAMS
    z, core = lax.axis_index("z"), lax.axis_index("core")

    slot = iota((2 * slots, rows), 0)
    mine = slot < slots
    block = jnp.where(mine, slot, slot - slots) + jnp.where(mine, 2 * z + core, 2 * z + 1 - core) * slots
    named = functools.reduce(
        jnp.logical_or, [table[j : j + 1, :] == block for j in range(SUF)]
    ).astype(jnp.float32)
    group = (iota((rows, n_batch), 0) // BEAMS == iota((rows, n_batch), 1)).astype(jnp.float32)
    hit = jnp.where(count(named, group) > 0.0, 1.0, 0.0)
    left, right = iota((2 * slots, 2 * slots), 0), iota((2 * slots, 2 * slots), 1)
    before = (left // slots == right // slots) & (right < left)
    rank = count(before.astype(jnp.float32), hit)
    taken = (iota((rows, rows), 0) == parents[...]).astype(jnp.float32)
    continued = count(named, taken)

    place = iota((2 * slots, n_batch), 0)
    found = []
    for k in range(2 * capacity):
        holder = k // capacity
        chosen = (hit > 0.0) & (rank == float(k % capacity)) & (place // slots == holder)
        found.append(jnp.sum(jnp.where(chosen, place + 1, 0), axis=0, keepdims=True))
    found = jnp.concatenate(found, axis=0)

    requests = [z * 2 + core]
    for mask in range(1, n_req):
        requests += [(z ^ mask) * 2, (z ^ mask) * 2 + 1]
    for i, request in enumerate(requests):
        lane = iota((rows, VECS), 1)
        spread = iota((rows, VECS), 0) == request * BEAMS + lane % BEAMS
        rows_ref[: 2 * slots, :] = count(continued, spread.astype(jnp.float32))
        rows_ref[2 * slots :, :] = jnp.zeros((8, VECS), jnp.float32)
        mask = iota(found.shape, 1) == request
        picked = jnp.sum(jnp.where(mask, found, 0), axis=1, keepdims=True)
        values = []
        for k in range(2 * capacity):
            index = picked[k, 0]
            row = jnp.where(index > 0, index - 1, 2 * slots)
            member_ref[i, k : k + 1, :] = rows_ref[pl.ds(row, 1), :]
            pool_ref = near if k < capacity else far_ref
            base = 0 if k < capacity else slots
            content = pool_ref[jnp.maximum(index - 1 - base, 0)]
            tokens = slice(k * half, (k + 1) * half)
            if i == 0:
                home_keys_ref[0, tokens, :] = content[:, :HD]
            else:
                keys_ref[i - 1, tokens, :] = content[:, :HD]
            values.append(content[:, HD:])
        values = jnp.concatenate(values, axis=0).T
        if i == 0:
            home_values_ref[0] = values
        else:
            values_ref[i - 1] = values


def suffix_parts(vectors, keys_ref, values_ref, members, place=0):
    n_slots = members[0].shape[0]
    half = keys_ref.shape[1] // n_slots
    scores = [scores_of(keys_ref[place + i], each) for i, each in enumerate(vectors)]
    softmaxes = []
    for member, score in zip(members, scores):
        pieces = [
            jnp.where(
                member[k : k + 1, :] > 0.0, score[k * half : (k + 1) * half], big_negative
            )
            for k in range(n_slots)
        ]
        softmaxes.append(weighted(jnp.concatenate(pieces, axis=0)))
    return [
        (
            top,
            total,
            jnp.dot(
                values_ref[place + i], weights.astype(jnp.bfloat16), preferred_element_type=jnp.float32
            ),
        )
        for i, (top, total, weights) in enumerate(softmaxes)
    ]


def away_kernel(place, keys_ref, values_ref, member_ref, message_ref, out_ref, *after_ref):
    for ref in after_ref:
        ref[...] = jnp.zeros(ref.shape, jnp.float32)
    vectors = [stacked_heads(message_ref[core]) for core in range(2)]
    members = [member_ref[1 + place + core] for core in range(2)]
    store_units(out_ref, suffix_parts(vectors, keys_ref, values_ref, members, place))


def home_part(length_ref, keys_ref, values_ref, member_ref, queries_ref, prompt_ref):
    vectors = stacked_heads(queries_ref[...])
    half = keys_ref.shape[1] // member_ref.shape[1]
    (suffix,) = suffix_parts([vectors], keys_ref, values_ref, [member_ref[0]])
    return merged([prompt_part(length_ref[0], half, prompt_ref, vectors), suffix])


def pair_heads_kernel(*refs):
    *inputs, _, out_ref = refs
    store_units(out_ref, [home_part(*inputs)])


def own_heads_kernel(*refs):
    *inputs, _, summed_ref, stats_ref = refs
    top, total, summed_ref[...] = home_part(*inputs)
    stats_ref[...] = jnp.concatenate([top, total, jnp.zeros((6, VECS), jnp.float32)], axis=0)


def sibling_kernel(*rest):
    units, out_ref = rest[:-2], rest[-1]
    core = lax.axis_index("core")
    store_units(out_ref, [merged([load_unit(unit, 1 - core) for unit in units])])


def final_kernel(*rest):
    units, (last_ref, shared_ref, summed_ref, stats_ref, out_ref) = rest[:-5], rest[-5:]
    core = lax.axis_index("core")
    parts = [load_unit(unit, core) for unit in units]
    parts += [load_unit(last_ref), load_unit(shared_ref)]
    parts.append((stats_ref[0:1], stats_ref[1:2], summed_ref[...]))
    _, total, summed = merged(parts)
    attended = (summed / total).T
    for h in range(HEADS):
        out_ref[:, h * HD : (h + 1) * HD] = attended[h * BEAMS : (h + 1) * BEAMS]


def in_hbm(value):
    return pltpu.with_memory_space_constraint(value, pltpu.HBM)


def on_device(queries, prompt_cache, pool, block_table, parents, lengths):
    n_req = lax.axis_size("z")
    n_batch = 2 * n_req
    ndist = 2 ** (SUF + 1) - 2
    capacity = 2 * ((ndist // 2 + n_batch - 1) // n_batch)
    slots, _, half, width = pool.shape
    tokens = prompt_cache.shape[2]
    rows = block_table.shape[0]
    vmem = pl.BlockSpec(memory_space=pltpu.VMEM)
    params = pltpu.CompilerParams(vmem_limit_bytes=32 * 2**20)
    some = pl.CostEstimate(flops=2 * 10**8, bytes_accessed=2**21, transcendentals=0)
    early = pl.CostEstimate(flops=2 * 10**10, bytes_accessed=0, transcendentals=0)

    hbm = pl.BlockSpec(memory_space=pltpu.HBM)
    near = pool.reshape(slots, half, width)
    far = swapped(near, "core")
    other = swapped(queries, "pair")
    staged = [queries, block_table.T, parents.reshape(1, rows)]
    own, table, row_parents = pl.pallas_call(
        stage_kernel,
        out_shape=tuple(pltpu.VMEM(each.shape, each.dtype) for each in staged),
        in_specs=[hbm] * len(staged),
        out_specs=(vmem,) * len(staged),
        scratch_shapes=[pltpu.SemaphoreType.DMA((len(staged),))],
        compiler_params=params,
        name="stage",
    )(*[in_hbm(each) for each in staged])
    both = pl.pallas_call(
        pack_kernel,
        out_shape=pltpu.VMEM((2,) + queries.shape, jnp.bfloat16),
        in_specs=[vmem] * 2,
        out_specs=vmem,
        compiler_params=params,
        cost_estimate=early,
        name="both_cores",
    )(own, swapped(queries, "core"))
    first, *others = mask_order(n_req)
    order = [first] + others[::-1]
    messages = {mask: exchanged(both, mask) for mask in order}

    home_keys, home_values, keys, values, member = pl.pallas_call(
        functools.partial(prepare_kernel, capacity),
        out_shape=(
            pltpu.VMEM((1, 2 * capacity * half, HD), jnp.bfloat16),
            pltpu.VMEM((1, HD, 2 * capacity * half), jnp.bfloat16),
            pltpu.VMEM((2 * n_req - 2, 2 * capacity * half, HD), jnp.bfloat16),
            pltpu.VMEM((2 * n_req - 2, HD, 2 * capacity * half), jnp.bfloat16),
            pltpu.VMEM((2 * n_req - 1, 2 * capacity, VECS), jnp.float32),
        ),
        in_specs=[vmem] * 4,
        out_specs=(vmem,) * 5,
        scratch_shapes=[pltpu.VMEM((2 * slots + 8, VECS), jnp.float32)],
        compiler_params=params,
        cost_estimate=some,
        name="prepare",
    )(
        near,
        table,
        row_parents,
        far,
    )

    received, after = [], []
    for mask in order:
        out = [pltpu.VMEM((2 * HD + STAT_ROWS, VECS), jnp.bfloat16)]
        if mask == first:
            out.append(pltpu.VMEM((8, VECS), jnp.float32))
        units, *token = pl.pallas_call(
            functools.partial(away_kernel, 2 * mask - 2),
            out_shape=out,
            in_specs=[vmem] * 4,
            out_specs=[vmem] * len(out),
            compiler_params=params,
            cost_estimate=some,
            name="suffix_away",
        )(keys, values, member, messages[mask])
        received.append(exchanged(units, mask))
        after += token

    home = pl.CostEstimate(
        flops=8 * tokens * VECS * HD, bytes_accessed=2 * tokens * width, transcendentals=0
    )
    home_specs = [pl.BlockSpec(memory_space=pltpu.SMEM)] + [vmem] * 6
    prompt = prompt_cache.reshape(tokens, width)
    given = pl.pallas_call(
        pair_heads_kernel,
        out_shape=pltpu.VMEM((HD + STAT_ROWS, VECS), jnp.bfloat16),
        in_specs=home_specs,
        out_specs=vmem,
        compiler_params=params,
        cost_estimate=home,
        name="home_pair_heads",
    )(lengths, home_keys, home_values, member, other, prompt, *after)
    last = swapped(given, "pair")
    summed, stats = pl.pallas_call(
        own_heads_kernel,
        out_shape=(pltpu.VMEM((HD, VECS), jnp.float32), pltpu.VMEM((8, VECS), jnp.float32)),
        in_specs=home_specs,
        out_specs=(vmem,) * 2,
        compiler_params=params,
        cost_estimate=home,
        name="home_own_heads",
    )(lengths, home_keys, home_values, member, own, prompt, *after)

    share = pl.pallas_call(
        sibling_kernel,
        out_shape=pltpu.VMEM((HD + STAT_ROWS, VECS), jnp.bfloat16),
        in_specs=[vmem] * n_req,
        out_specs=vmem,
        compiler_params=params,
        name="sibling_share",
    )(*received, stats)

    return pl.pallas_call(
        final_kernel,
        out_shape=jax.ShapeDtypeStruct((BEAMS, HEADS * HD), jnp.float32),
        in_specs=[vmem] * (3 + n_req),
        out_specs=vmem,
        compiler_params=params,
        name="combine",
    )(*received, last, swapped(share, "core"), summed, stats)


def solution(mesh):
    n_batch, n_mp = mesh.devices.shape
    split = jax.sharding.Mesh(
        mesh.devices.reshape(n_batch // 2, 2, n_mp // 2, 2), ("z", "core", "group", "pair")
    )
    batch, mp = ("z", "core"), ("group", "pair")
    return jax.shard_map(
        on_device,
        mesh=split,
        in_specs=(
            P(batch, mp),
            P(batch, mp, None, None),
            P(batch, mp, None, None),
            P(),
            P(),
            P(batch),
        ),
        out_specs=P(batch, mp),
        check_vma=False,
    )
```

```python
import functools

import jax
import jax.numpy as jnp
from jax import lax
from jax.experimental import pallas as pl
from jax.experimental.pallas import tpu as pltpu
from jax.sharding import PartitionSpec as P

HD = 128
GROUP = 16
BEAMS = 16
SUF = 4
HEADS = GROUP // 2
VECS = HEADS * BEAMS
STAT_ROWS = 16
CHUNK = 512
FIRST_MASKS = (3, 2, 1)
SURELY_VALID = 1024

big_negative = -1e30
to_exp2 = HD ** (-0.5) * 1.4426950408889634


def swapped(value, axis):
    return lax.ppermute(value, axis, [(0, 1), (1, 0)])


def exchanged(value, mask):
    pairs = []
    for z in range(lax.axis_size("z")):
        for core in range(2):
            for pair in range(2):
                target = ((z ^ mask) * 2 + core) * 2 + (pair ^ core)
                pairs.append(((z * 2 + core) * 2 + pair, target))
    return lax.ppermute(value, ("z", "core", "pair"), pairs)


def mask_order(n_req):
    return FIRST_MASKS if n_req == 4 else tuple(range(n_req - 1, 0, -1))


def stage_kernel(*refs):
    n = (len(refs) - 1) // 2
    copies = [
        pltpu.make_async_copy(refs[i], refs[n + i], refs[-1].at[i]) for i in range(n)
    ]
    for copy in copies:
        copy.start()
    for copy in copies:
        copy.wait()


def pack_kernel(own_ref, sibling_ref, out_ref):
    core = lax.axis_index("core")
    out_ref[core] = own_ref[...]
    out_ref[1 - core] = sibling_ref[...]


def stacked_heads(q):
    return jnp.concatenate([q[:, h * HD : (h + 1) * HD] for h in range(HEADS)], axis=0)


def scores_of(keys, vectors):
    return lax.dot_general(
        keys, vectors, (((1,), (1,)), ((), ())), preferred_element_type=jnp.float32
    )


def summed_of(values, weights):
    return lax.dot_general(
        values,
        weights.astype(jnp.bfloat16),
        (((0,), (0,)), ((), ())),
        preferred_element_type=jnp.float32,
    )


def merged(parts):
    top = functools.reduce(jnp.maximum, [p[0] for p in parts])
    total = 0.0
    summed = 0.0
    for part_top, part_total, part_summed in parts:
        factor = jnp.exp2((part_top - top) * to_exp2)
        total = total + part_total * factor
        summed = summed + part_summed * factor
    return top, total, summed


def weighted(scores):
    top = jnp.max(scores, axis=0, keepdims=True)
    weights = jnp.exp2((scores - top) * to_exp2)
    return top, jnp.sum(weights, axis=0, keepdims=True), weights


def three_pieces(x):
    first = x.astype(jnp.bfloat16).astype(jnp.float32)
    rest = x - first
    second = rest.astype(jnp.bfloat16).astype(jnp.float32)
    return [first, second, rest - second]


def store_units(ref, parts):
    rows = []
    for i, (top, total, summed) in enumerate(parts):
        ref[i * HD : (i + 1) * HD, :] = summed.astype(jnp.bfloat16)
        rows += three_pieces(top) + three_pieces(total)
    rows.append(jnp.zeros((STAT_ROWS - len(rows), VECS), jnp.float32))
    ref[len(parts) * HD :, :] = jnp.concatenate(rows, axis=0).astype(jnp.bfloat16)


def load_unit(ref, i=0):
    sums = ref.shape[0] - STAT_ROWS
    stats = ref[sums:, :].astype(jnp.float32)
    if isinstance(i, int):
        rows = [stats[6 * i + k : 6 * i + k + 1] for k in range(6)]
    else:
        rows = [jnp.where(i == 0, stats[k : k + 1], stats[6 + k : 7 + k]) for k in range(6)]
    part = ref[pl.ds(pl.multiple_of(i * HD, HD), HD), :]
    return rows[0] + rows[1] + rows[2], rows[3] + rows[4] + rows[5], part.astype(jnp.float32)


def count(left, right):
    return jnp.dot(
        left.astype(jnp.bfloat16), right.astype(jnp.bfloat16), preferred_element_type=jnp.float32
    )


def iota(shape, axis):
    return lax.broadcasted_iota(jnp.int32, shape, axis)


def prompt_part(length, half, prompt_ref, vectors):
    parity = lax.axis_index("pair")
    whole = lax.div(length, 2 * half)
    valid = whole * half + jnp.clip(length - whole * (2 * half) - parity * half, 0, half)
    chunks = [slice(i, i + CHUNK) for i in range(0, prompt_ref.shape[0], CHUNK)]
    scores = [scores_of(vectors, prompt_ref[chunk, :HD]) for chunk in chunks]
    place = iota(scores[0].shape, 1)
    scores = [
        score
        if chunk.stop <= SURELY_VALID
        else jnp.where(place < valid - chunk.start, score, big_negative)
        for chunk, score in zip(chunks, scores)
    ]
    top = jnp.max(functools.reduce(jnp.maximum, scores), axis=1, keepdims=True)
    totals, summed = 0.0, 0.0
    for chunk, score in zip(chunks, scores):
        weights = jnp.exp2((score - top) * to_exp2)
        totals = totals + weights
        summed = summed + jnp.dot(
            weights.astype(jnp.bfloat16), prompt_ref[chunk, HD:], preferred_element_type=jnp.float32
        )
    total = jnp.sum(totals, axis=1, keepdims=True)
    stats = jnp.where(iota(summed.shape, 1) == 0, top, total).T
    return stats[0:1], stats[1:2], summed.T


def prepare_kernel(
    capacity, near, table, parents, far_ref,
    home_keys_ref, home_values_ref, keys_ref, values_ref, member_ref, rows_ref,
):
    n_req = lax.axis_size("z")
    slots, half, _ = near.shape
    rows = table.shape[1]
    n_batch = rows // BEAMS
    z, core = lax.axis_index("z"), lax.axis_index("core")

    slot = iota((2 * slots, rows), 0)
    mine = slot < slots
    block = jnp.where(mine, slot, slot - slots) + jnp.where(mine, 2 * z + core, 2 * z + 1 - core) * slots
    named = functools.reduce(
        jnp.logical_or, [table[j : j + 1, :] == block for j in range(SUF)]
    ).astype(jnp.float32)
    group = (iota((rows, n_batch), 0) // BEAMS == iota((rows, n_batch), 1)).astype(jnp.float32)
    hit = jnp.where(count(named, group) > 0.0, 1.0, 0.0)
    left, right = iota((2 * slots, 2 * slots), 0), iota((2 * slots, 2 * slots), 1)
    before = (left // slots == right // slots) & (right < left)
    rank = count(before.astype(jnp.float32), hit)
    taken = (iota((rows, rows), 0) == parents[...]).astype(jnp.float32)
    continued = count(named, taken)

    place = iota((2 * slots, n_batch), 0)
    found = []
    for k in range(2 * capacity):
        holder = k // capacity
        chosen = (hit > 0.0) & (rank == float(k % capacity)) & (place // slots == holder)
        found.append(jnp.sum(jnp.where(chosen, place + 1, 0), axis=0, keepdims=True))
    found = jnp.concatenate(found, axis=0)

    requests = [z * 2 + core]
    for mask in range(1, n_req):
        requests += [(z ^ mask) * 2, (z ^ mask) * 2 + 1]
    for i, request in enumerate(requests):
        lane = iota((rows, VECS), 1)
        spread = iota((rows, VECS), 0) == request * BEAMS + lane % BEAMS
        rows_ref[: 2 * slots, :] = count(continued, spread.astype(jnp.float32))
        rows_ref[2 * slots :, :] = jnp.zeros((8, VECS), jnp.float32)
        mask = iota(found.shape, 1) == request
        picked = jnp.sum(jnp.where(mask, found, 0), axis=1, keepdims=True)
        values = []
        for k in range(2 * capacity):
            index = picked[k, 0]
            row = jnp.where(index > 0, index - 1, 2 * slots)
            member_ref[i, k : k + 1, :] = rows_ref[pl.ds(row, 1), :]
            pool_ref = near if k < capacity else far_ref
            base = 0 if k < capacity else slots
            content = pool_ref[jnp.maximum(index - 1 - base, 0)]
            tokens = slice(k * half, (k + 1) * half)
            if i == 0:
                home_keys_ref[0, tokens, :] = content[:, :HD]
            else:
                keys_ref[i - 1, tokens, :] = content[:, :HD]
            values.append(content[:, HD:])
        values = jnp.concatenate(values, axis=0).T
        if i == 0:
            home_values_ref[0] = values
        else:
            values_ref[i - 1] = values


def suffix_parts(vectors, keys_ref, values_ref, members, place=0):
    n_slots = members[0].shape[0]
    half = keys_ref.shape[1] // n_slots
    scores = [scores_of(keys_ref[place + i], each) for i, each in enumerate(vectors)]
    softmaxes = []
    for member, score in zip(members, scores):
        pieces = [
            jnp.where(
                member[k : k + 1, :] > 0.0, score[k * half : (k + 1) * half], big_negative
            )
            for k in range(n_slots)
        ]
        softmaxes.append(weighted(jnp.concatenate(pieces, axis=0)))
    return [
        (
            top,
            total,
            jnp.dot(
                values_ref[place + i], weights.astype(jnp.bfloat16), preferred_element_type=jnp.float32
            ),
        )
        for i, (top, total, weights) in enumerate(softmaxes)
    ]


def away_kernel(place, keys_ref, values_ref, member_ref, message_ref, out_ref, *after_ref):
    for ref in after_ref:
        ref[...] = jnp.zeros(ref.shape, jnp.float32)
    vectors = [stacked_heads(message_ref[core]) for core in range(2)]
    members = [member_ref[1 + place + core] for core in range(2)]
    store_units(out_ref, suffix_parts(vectors, keys_ref, values_ref, members, place))


def home_part(length_ref, keys_ref, values_ref, member_ref, queries_ref, prompt_ref):
    vectors = stacked_heads(queries_ref[...])
    half = keys_ref.shape[1] // member_ref.shape[1]
    (suffix,) = suffix_parts([vectors], keys_ref, values_ref, [member_ref[0]])
    return merged([prompt_part(length_ref[0], half, prompt_ref, vectors), suffix])


def pair_heads_kernel(*refs):
    *inputs, _, out_ref = refs
    store_units(out_ref, [home_part(*inputs)])


def own_heads_kernel(*refs):
    *inputs, _, summed_ref, stats_ref = refs
    top, total, summed_ref[...] = home_part(*inputs)
    stats_ref[...] = jnp.concatenate([top, total, jnp.zeros((6, VECS), jnp.float32)], axis=0)


def sibling_kernel(*rest):
    units, out_ref = rest[:-2], rest[-1]
    core = lax.axis_index("core")
    store_units(out_ref, [merged([load_unit(unit, 1 - core) for unit in units])])


def final_kernel(*rest):
    units, (last_ref, shared_ref, summed_ref, stats_ref, out_ref) = rest[:-5], rest[-5:]
    core = lax.axis_index("core")
    parts = [load_unit(unit, core) for unit in units]
    parts += [load_unit(last_ref), load_unit(shared_ref)]
    parts.append((stats_ref[0:1], stats_ref[1:2], summed_ref[...]))
    _, total, summed = merged(parts)
    attended = (summed / total).T
    for h in range(HEADS):
        out_ref[:, h * HD : (h + 1) * HD] = attended[h * BEAMS : (h + 1) * BEAMS]


def in_hbm(value):
    return pltpu.with_memory_space_constraint(value, pltpu.HBM)


def on_device(queries, prompt_cache, pool, block_table, parents, lengths):
    n_req = lax.axis_size("z")
    n_batch = 2 * n_req
    ndist = 2 ** (SUF + 1) - 2
    capacity = 2 * ((ndist // 2 + n_batch - 1) // n_batch)
    slots, _, half, width = pool.shape
    tokens = prompt_cache.shape[2]
    rows = block_table.shape[0]
    vmem = pl.BlockSpec(memory_space=pltpu.VMEM)
    params = pltpu.CompilerParams(vmem_limit_bytes=32 * 2**20)
    some = pl.CostEstimate(flops=2 * 10**8, bytes_accessed=2**21, transcendentals=0)
    early = pl.CostEstimate(flops=2 * 10**10, bytes_accessed=0, transcendentals=0)

    hbm = pl.BlockSpec(memory_space=pltpu.HBM)
    near = pool.reshape(slots, half, width)
    far = swapped(near, "core")
    other = swapped(queries, "pair")
    staged = [queries, block_table.T, parents.reshape(1, rows)]
    own, table, row_parents = pl.pallas_call(
        stage_kernel,
        out_shape=tuple(pltpu.VMEM(each.shape, each.dtype) for each in staged),
        in_specs=[hbm] * len(staged),
        out_specs=(vmem,) * len(staged),
        scratch_shapes=[pltpu.SemaphoreType.DMA((len(staged),))],
        compiler_params=params,
        name="stage",
    )(*[in_hbm(each) for each in staged])
    both = pl.pallas_call(
        pack_kernel,
        out_shape=pltpu.VMEM((2,) + queries.shape, jnp.bfloat16),
        in_specs=[vmem] * 2,
        out_specs=vmem,
        compiler_params=params,
        cost_estimate=early,
        name="both_cores",
    )(own, swapped(queries, "core"))
    first, *others = mask_order(n_req)
    order = [first] + others[::-1]
    messages = {mask: exchanged(both, mask) for mask in order}

    home_keys, home_values, keys, values, member = pl.pallas_call(
        functools.partial(prepare_kernel, capacity),
        out_shape=(
            pltpu.VMEM((1, 2 * capacity * half, HD), jnp.bfloat16),
            pltpu.VMEM((1, HD, 2 * capacity * half), jnp.bfloat16),
            pltpu.VMEM((2 * n_req - 2, 2 * capacity * half, HD), jnp.bfloat16),
            pltpu.VMEM((2 * n_req - 2, HD, 2 * capacity * half), jnp.bfloat16),
            pltpu.VMEM((2 * n_req - 1, 2 * capacity, VECS), jnp.float32),
        ),
        in_specs=[vmem] * 4,
        out_specs=(vmem,) * 5,
        scratch_shapes=[pltpu.VMEM((2 * slots + 8, VECS), jnp.float32)],
        compiler_params=params,
        cost_estimate=some,
        name="prepare",
    )(
        near,
        table,
        row_parents,
        far,
    )

    received, after = [], []
    for mask in order:
        out = [pltpu.VMEM((2 * HD + STAT_ROWS, VECS), jnp.bfloat16)]
        if mask == first:
            out.append(pltpu.VMEM((8, VECS), jnp.float32))
        units, *token = pl.pallas_call(
            functools.partial(away_kernel, 2 * mask - 2),
            out_shape=out,
            in_specs=[vmem] * 4,
            out_specs=[vmem] * len(out),
            compiler_params=params,
            cost_estimate=some,
            name="suffix_away",
        )(keys, values, member, messages[mask])
        received.append(exchanged(units, mask))
        after += token

    home = pl.CostEstimate(
        flops=8 * tokens * VECS * HD, bytes_accessed=2 * tokens * width, transcendentals=0
    )
    home_specs = [pl.BlockSpec(memory_space=pltpu.SMEM)] + [vmem] * 6
    prompt = prompt_cache.reshape(tokens, width)
    given = pl.pallas_call(
        pair_heads_kernel,
        out_shape=pltpu.VMEM((HD + STAT_ROWS, VECS), jnp.bfloat16),
        in_specs=home_specs,
        out_specs=vmem,
        compiler_params=params,
        cost_estimate=home,
        name="home_pair_heads",
    )(lengths, home_keys, home_values, member, other, prompt, *after)
    last = swapped(given, "pair")
    summed, stats = pl.pallas_call(
        own_heads_kernel,
        out_shape=(pltpu.VMEM((HD, VECS), jnp.float32), pltpu.VMEM((8, VECS), jnp.float32)),
        in_specs=home_specs,
        out_specs=(vmem,) * 2,
        compiler_params=params,
        cost_estimate=home,
        name="home_own_heads",
    )(lengths, home_keys, home_values, member, own, prompt, *after)

    share = pl.pallas_call(
        sibling_kernel,
        out_shape=pltpu.VMEM((HD + STAT_ROWS, VECS), jnp.bfloat16),
        in_specs=[vmem] * n_req,
        out_specs=vmem,
        compiler_params=params,
        name="sibling_share",
    )(*received, stats)

    return pl.pallas_call(
        final_kernel,
        out_shape=jax.ShapeDtypeStruct((BEAMS, HEADS * HD), jnp.float32),
        in_specs=[vmem] * (3 + n_req),
        out_specs=vmem,
        compiler_params=params,
        name="combine",
    )(*received, last, swapped(share, "core"), summed, stats)


def solution(mesh):
    n_batch, n_mp = mesh.devices.shape
    split = jax.sharding.Mesh(
        mesh.devices.reshape(n_batch // 2, 2, n_mp // 2, 2), ("z", "core", "group", "pair")
    )
    batch, mp = ("z", "core"), ("group", "pair")
    return jax.shard_map(
        on_device,
        mesh=split,
        in_specs=(
            P(batch, mp),
            P(batch, mp, None, None),
            P(batch, mp, None, None),
            P(),
            P(),
            P(batch),
        ),
        out_specs=P(batch, mp),
        check_vma=False,
    )
```

```python
import functools

import jax
import jax.numpy as jnp
from jax import lax
from jax.experimental import pallas as pl
from jax.experimental.pallas import tpu as pltpu
from jax.sharding import PartitionSpec as P

HD = 128
GROUP = 16
BEAMS = 16
SUF = 4
HEADS = GROUP // 2
VECS = HEADS * BEAMS
STAT_ROWS = 16
CHUNK = 512
FIRST_MASKS = (2, 3, 1)
SURELY_VALID = 1024

big_negative = -1e30
to_exp2 = HD ** (-0.5) * 1.4426950408889634


def swapped(value, axis):
    return lax.ppermute(value, axis, [(0, 1), (1, 0)])


def exchanged(value, mask):
    pairs = []
    for z in range(lax.axis_size("z")):
        for core in range(2):
            for pair in range(2):
                target = ((z ^ mask) * 2 + core) * 2 + (pair ^ core)
                pairs.append(((z * 2 + core) * 2 + pair, target))
    return lax.ppermute(value, ("z", "core", "pair"), pairs)


def mask_order(n_req):
    return FIRST_MASKS if n_req == 4 else tuple(range(n_req - 1, 0, -1))


def stage_kernel(*refs):
    n = (len(refs) - 1) // 2
    copies = [
        pltpu.make_async_copy(refs[i], refs[n + i], refs[-1].at[i]) for i in range(n)
    ]
    for copy in copies:
        copy.start()
    for copy in copies:
        copy.wait()


def pack_kernel(own_ref, sibling_ref, out_ref):
    core = lax.axis_index("core")
    out_ref[core] = own_ref[...]
    out_ref[1 - core] = sibling_ref[...]


def stacked_heads(q):
    return jnp.concatenate([q[:, h * HD : (h + 1) * HD] for h in range(HEADS)], axis=0)


def scores_of(keys, vectors):
    return lax.dot_general(
        keys, vectors, (((1,), (1,)), ((), ())), preferred_element_type=jnp.float32
    )


def summed_of(values, weights):
    return lax.dot_general(
        values,
        weights.astype(jnp.bfloat16),
        (((0,), (0,)), ((), ())),
        preferred_element_type=jnp.float32,
    )


def merged(parts):
    top = functools.reduce(jnp.maximum, [p[0] for p in parts])
    total = 0.0
    summed = 0.0
    for part_top, part_total, part_summed in parts:
        factor = jnp.exp2((part_top - top) * to_exp2)
        total = total + part_total * factor
        summed = summed + part_summed * factor
    return top, total, summed


def weighted(scores):
    top = jnp.max(scores, axis=0, keepdims=True)
    weights = jnp.exp2((scores - top) * to_exp2)
    return top, jnp.sum(weights, axis=0, keepdims=True), weights


def three_pieces(x):
    first = x.astype(jnp.bfloat16).astype(jnp.float32)
    rest = x - first
    second = rest.astype(jnp.bfloat16).astype(jnp.float32)
    return [first, second, rest - second]


def store_units(ref, parts):
    stats = jnp.concatenate([row for top, total, _ in parts for row in (top, total)], axis=0)
    pieces = three_pieces(stats)
    padding = jnp.zeros((STAT_ROWS - 3 * stats.shape[0], VECS), jnp.float32)
    ref[len(parts) * HD :, :] = jnp.concatenate(pieces + [padding], axis=0).astype(jnp.bfloat16)
    for i, (_, _, summed) in enumerate(parts):
        ref[i * HD : (i + 1) * HD, :] = summed.astype(jnp.bfloat16)


def load_unit(ref, i=0):
    n_parts = ref.shape[0] // HD
    pieces = ref[n_parts * HD :, :].astype(jnp.float32)
    rows = 2 * n_parts
    stats = pieces[:rows] + pieces[rows : 2 * rows] + pieces[2 * rows : 3 * rows]
    if n_parts == 1:
        top, total = stats[0:1], stats[1:2]
    else:
        top = jnp.where(i == 0, stats[0:1], stats[2:3])
        total = jnp.where(i == 0, stats[1:2], stats[3:4])
    part = ref[pl.ds(pl.multiple_of(i * HD, HD), HD), :]
    return top, total, part.astype(jnp.float32)


def count(left, right):
    return jnp.dot(
        left.astype(jnp.bfloat16), right.astype(jnp.bfloat16), preferred_element_type=jnp.float32
    )


def iota(shape, axis):
    return lax.broadcasted_iota(jnp.int32, shape, axis)


def prompt_part(length, half, prompt_ref, vectors):
    parity = lax.axis_index("pair")
    whole = lax.div(length, 2 * half)
    valid = whole * half + jnp.clip(length - whole * (2 * half) - parity * half, 0, half)
    chunks = [slice(i, i + CHUNK) for i in range(0, prompt_ref.shape[0], CHUNK)]
    scores = [scores_of(vectors, prompt_ref[chunk, :HD]) for chunk in chunks]
    place = iota(scores[0].shape, 1)
    scores = [
        score
        if chunk.stop <= SURELY_VALID
        else jnp.where(place < valid - chunk.start, score, big_negative)
        for chunk, score in zip(chunks, scores)
    ]
    top = jnp.max(functools.reduce(jnp.maximum, scores), axis=1, keepdims=True)
    totals, summed = 0.0, 0.0
    for chunk, score in zip(chunks, scores):
        weights = jnp.exp2((score - top) * to_exp2)
        totals = totals + weights
        summed = summed + jnp.dot(
            weights.astype(jnp.bfloat16), prompt_ref[chunk, HD:], preferred_element_type=jnp.float32
        )
    total = jnp.sum(totals, axis=1, keepdims=True)
    stats = jnp.where(iota(summed.shape, 1) == 0, top, total).T
    return stats[0:1], stats[1:2], summed.T


def prepare_kernel(
    capacity, near, table, parents, far_ref,
    home_keys_ref, home_values_ref, keys_ref, values_ref, member_ref, rows_ref,
):
    n_req = lax.axis_size("z")
    slots, half, _ = near.shape
    rows = table.shape[1]
    n_batch = rows // BEAMS
    z, core = lax.axis_index("z"), lax.axis_index("core")

    slot = iota((2 * slots, rows), 0)
    mine = slot < slots
    block = jnp.where(mine, slot, slot - slots) + jnp.where(mine, 2 * z + core, 2 * z + 1 - core) * slots
    named = functools.reduce(
        jnp.logical_or, [table[j : j + 1, :] == block for j in range(SUF)]
    ).astype(jnp.float32)
    group = (iota((rows, n_batch), 0) // BEAMS == iota((rows, n_batch), 1)).astype(jnp.float32)
    hit = jnp.where(count(named, group) > 0.0, 1.0, 0.0)
    left, right = iota((2 * slots, 2 * slots), 0), iota((2 * slots, 2 * slots), 1)
    before = (left // slots == right // slots) & (right < left)
    rank = count(before.astype(jnp.float32), hit)
    taken = (iota((rows, rows), 0) == parents[...]).astype(jnp.float32)
    continued = count(named, taken)

    place = iota((2 * slots, n_batch), 0)
    found = []
    for k in range(2 * capacity):
        holder = k // capacity
        chosen = (hit > 0.0) & (rank == float(k % capacity)) & (place // slots == holder)
        found.append(jnp.sum(jnp.where(chosen, place + 1, 0), axis=0, keepdims=True))
    found = jnp.concatenate(found, axis=0)

    requests = [z * 2 + core]
    for mask in range(1, n_req):
        requests += [(z ^ mask) * 2, (z ^ mask) * 2 + 1]
    for i, request in enumerate(requests):
        lane = iota((rows, VECS), 1)
        spread = iota((rows, VECS), 0) == request * BEAMS + lane % BEAMS
        rows_ref[: 2 * slots, :] = count(continued, spread.astype(jnp.float32))
        rows_ref[2 * slots :, :] = jnp.zeros((8, VECS), jnp.float32)
        mask = iota(found.shape, 1) == request
        picked = jnp.sum(jnp.where(mask, found, 0), axis=1, keepdims=True)
        values = []
        for k in range(2 * capacity):
            index = picked[k, 0]
            row = jnp.where(index > 0, index - 1, 2 * slots)
            member_ref[i, k : k + 1, :] = rows_ref[pl.ds(row, 1), :]
            pool_ref = near if k < capacity else far_ref
            base = 0 if k < capacity else slots
            content = pool_ref[jnp.maximum(index - 1 - base, 0)]
            tokens = slice(k * half, (k + 1) * half)
            if i == 0:
                home_keys_ref[0, tokens, :] = content[:, :HD]
            else:
                keys_ref[i - 1, tokens, :] = content[:, :HD]
            values.append(content[:, HD:])
        values = jnp.concatenate(values, axis=0).T
        if i == 0:
            home_values_ref[0] = values
        else:
            values_ref[i - 1] = values


def suffix_parts(vectors, keys_ref, values_ref, members, place=0):
    n_slots = members[0].shape[0]
    half = keys_ref.shape[1] // n_slots
    scores = [scores_of(keys_ref[place + i], each) for i, each in enumerate(vectors)]
    softmaxes = []
    for member, score in zip(members, scores):
        pieces = [
            jnp.where(
                member[k : k + 1, :] > 0.0, score[k * half : (k + 1) * half], big_negative
            )
            for k in range(n_slots)
        ]
        softmaxes.append(weighted(jnp.concatenate(pieces, axis=0)))
    return [
        (
            top,
            total,
            jnp.dot(
                values_ref[place + i], weights.astype(jnp.bfloat16), preferred_element_type=jnp.float32
            ),
        )
        for i, (top, total, weights) in enumerate(softmaxes)
    ]


def away_kernel(place, keys_ref, values_ref, member_ref, message_ref, out_ref, *after_ref):
    for ref in after_ref:
        ref[...] = jnp.zeros(ref.shape, jnp.float32)
    vectors = [stacked_heads(message_ref[core]) for core in range(2)]
    members = [member_ref[1 + place + core] for core in range(2)]
    store_units(out_ref, suffix_parts(vectors, keys_ref, values_ref, members, place))


def home_part(length_ref, keys_ref, values_ref, member_ref, queries_ref, prompt_ref):
    vectors = stacked_heads(queries_ref[...])
    half = keys_ref.shape[1] // member_ref.shape[1]
    (suffix,) = suffix_parts([vectors], keys_ref, values_ref, [member_ref[0]])
    return merged([prompt_part(length_ref[0], half, prompt_ref, vectors), suffix])


def pair_heads_kernel(*refs):
    *inputs, _, out_ref = refs
    store_units(out_ref, [home_part(*inputs)])


def own_heads_kernel(*refs):
    *inputs, _, summed_ref, stats_ref = refs
    top, total, summed_ref[...] = home_part(*inputs)
    stats_ref[...] = jnp.concatenate([top, total, jnp.zeros((6, VECS), jnp.float32)], axis=0)


def sibling_kernel(*rest):
    units, out_ref = rest[:-2], rest[-1]
    core = lax.axis_index("core")
    store_units(out_ref, [merged([load_unit(unit, 1 - core) for unit in units])])


def final_kernel(*rest):
    units, (last_ref, shared_ref, summed_ref, stats_ref, out_ref) = rest[:-5], rest[-5:]
    core = lax.axis_index("core")
    parts = [load_unit(unit, core) for unit in units]
    parts += [load_unit(last_ref), load_unit(shared_ref)]
    parts.append((stats_ref[0:1], stats_ref[1:2], summed_ref[...]))
    _, total, summed = merged(parts)
    attended = (summed / total).T
    for h in range(HEADS):
        out_ref[:, h * HD : (h + 1) * HD] = attended[h * BEAMS : (h + 1) * BEAMS]


def in_hbm(value):
    return pltpu.with_memory_space_constraint(value, pltpu.HBM)


def on_device(queries, prompt_cache, pool, block_table, parents, lengths):
    n_req = lax.axis_size("z")
    n_batch = 2 * n_req
    ndist = 2 ** (SUF + 1) - 2
    capacity = 2 * ((ndist // 2 + n_batch - 1) // n_batch)
    slots, _, half, width = pool.shape
    tokens = prompt_cache.shape[2]
    rows = block_table.shape[0]
    vmem = pl.BlockSpec(memory_space=pltpu.VMEM)
    params = pltpu.CompilerParams(vmem_limit_bytes=32 * 2**20)
    some = pl.CostEstimate(flops=2 * 10**8, bytes_accessed=2**21, transcendentals=0)
    early = pl.CostEstimate(flops=2 * 10**10, bytes_accessed=0, transcendentals=0)

    hbm = pl.BlockSpec(memory_space=pltpu.HBM)
    near = pool.reshape(slots, half, width)
    far = swapped(near, "core")
    other = swapped(queries, "pair")
    staged = [queries, block_table.T, parents.reshape(1, rows)]
    own, table, row_parents = pl.pallas_call(
        stage_kernel,
        out_shape=tuple(pltpu.VMEM(each.shape, each.dtype) for each in staged),
        in_specs=[hbm] * len(staged),
        out_specs=(vmem,) * len(staged),
        scratch_shapes=[pltpu.SemaphoreType.DMA((len(staged),))],
        compiler_params=params,
        name="stage",
    )(*[in_hbm(each) for each in staged])
    both = pl.pallas_call(
        pack_kernel,
        out_shape=pltpu.VMEM((2,) + queries.shape, jnp.bfloat16),
        in_specs=[vmem] * 2,
        out_specs=vmem,
        compiler_params=params,
        cost_estimate=early,
        name="both_cores",
    )(own, swapped(queries, "core"))
    first, *others = mask_order(n_req)
    order = [first] + others[::-1]
    messages = {mask: exchanged(both, mask) for mask in order}

    home_keys, home_values, keys, values, member = pl.pallas_call(
        functools.partial(prepare_kernel, capacity),
        out_shape=(
            pltpu.VMEM((1, 2 * capacity * half, HD), jnp.bfloat16),
            pltpu.VMEM((1, HD, 2 * capacity * half), jnp.bfloat16),
            pltpu.VMEM((2 * n_req - 2, 2 * capacity * half, HD), jnp.bfloat16),
            pltpu.VMEM((2 * n_req - 2, HD, 2 * capacity * half), jnp.bfloat16),
            pltpu.VMEM((2 * n_req - 1, 2 * capacity, VECS), jnp.float32),
        ),
        in_specs=[vmem] * 4,
        out_specs=(vmem,) * 5,
        scratch_shapes=[pltpu.VMEM((2 * slots + 8, VECS), jnp.float32)],
        compiler_params=params,
        cost_estimate=some,
        name="prepare",
    )(
        near,
        table,
        row_parents,
        far,
    )

    received, after = [], []
    for mask in order:
        out = [pltpu.VMEM((2 * HD + STAT_ROWS, VECS), jnp.bfloat16)]
        if mask == first:
            out.append(pltpu.VMEM((8, VECS), jnp.float32))
        units, *token = pl.pallas_call(
            functools.partial(away_kernel, 2 * mask - 2),
            out_shape=out,
            in_specs=[vmem] * 4,
            out_specs=[vmem] * len(out),
            compiler_params=params,
            cost_estimate=some,
            name="suffix_away",
        )(keys, values, member, messages[mask])
        received.append(exchanged(units, mask))
        after += token

    home = pl.CostEstimate(
        flops=8 * tokens * VECS * HD, bytes_accessed=2 * tokens * width, transcendentals=0
    )
    home_specs = [pl.BlockSpec(memory_space=pltpu.SMEM)] + [vmem] * 6
    prompt = prompt_cache.reshape(tokens, width)
    given = pl.pallas_call(
        pair_heads_kernel,
        out_shape=pltpu.VMEM((HD + STAT_ROWS, VECS), jnp.bfloat16),
        in_specs=home_specs,
        out_specs=vmem,
        compiler_params=params,
        cost_estimate=home,
        name="home_pair_heads",
    )(lengths, home_keys, home_values, member, other, prompt, *after)
    last = swapped(given, "pair")
    summed, stats = pl.pallas_call(
        own_heads_kernel,
        out_shape=(pltpu.VMEM((HD, VECS), jnp.float32), pltpu.VMEM((8, VECS), jnp.float32)),
        in_specs=home_specs,
        out_specs=(vmem,) * 2,
        compiler_params=params,
        cost_estimate=home,
        name="home_own_heads",
    )(lengths, home_keys, home_values, member, own, prompt, *after)

    share = pl.pallas_call(
        sibling_kernel,
        out_shape=pltpu.VMEM((HD + STAT_ROWS, VECS), jnp.bfloat16),
        in_specs=[vmem] * n_req,
        out_specs=vmem,
        compiler_params=params,
        name="sibling_share",
    )(*received, stats)

    return pl.pallas_call(
        final_kernel,
        out_shape=jax.ShapeDtypeStruct((BEAMS, HEADS * HD), jnp.float32),
        in_specs=[vmem] * (3 + n_req),
        out_specs=vmem,
        compiler_params=params,
        name="combine",
    )(*received, last, swapped(share, "core"), summed, stats)


def solution(mesh):
    n_batch, n_mp = mesh.devices.shape
    split = jax.sharding.Mesh(
        mesh.devices.reshape(n_batch // 2, 2, n_mp // 2, 2), ("z", "core", "group", "pair")
    )
    batch, mp = ("z", "core"), ("group", "pair")
    return jax.shard_map(
        on_device,
        mesh=split,
        in_specs=(
            P(batch, mp),
            P(batch, mp, None, None),
            P(batch, mp, None, None),
            P(),
            P(),
            P(batch),
        ),
        out_specs=P(batch, mp),
        check_vma=False,
    )
```

```python
import functools

import jax
import jax.numpy as jnp
from jax import lax
from jax.experimental import pallas as pl
from jax.experimental.pallas import tpu as pltpu
from jax.sharding import PartitionSpec as P

HD = 128
GROUP = 16
BEAMS = 16
SUF = 4
HEADS = GROUP // 2
VECS = HEADS * BEAMS
STAT_ROWS = 16
CHUNK = 512
FIRST_MASKS = (2, 3, 1)
SURELY_VALID = 1024

big_negative = -1e30
to_exp2 = HD ** (-0.5) * 1.4426950408889634


def swapped(value, axis):
    return lax.ppermute(value, axis, [(0, 1), (1, 0)])


def exchanged(value, mask):
    pairs = []
    for z in range(lax.axis_size("z")):
        for core in range(2):
            for pair in range(2):
                target = ((z ^ mask) * 2 + core) * 2 + (pair ^ core)
                pairs.append(((z * 2 + core) * 2 + pair, target))
    return lax.ppermute(value, ("z", "core", "pair"), pairs)


def mask_order(n_req):
    return FIRST_MASKS if n_req == 4 else tuple(range(n_req - 1, 0, -1))


def stage_kernel(*refs):
    n = (len(refs) - 1) // 2
    copies = [
        pltpu.make_async_copy(refs[i], refs[n + i], refs[-1].at[i]) for i in range(n)
    ]
    for copy in copies:
        copy.start()
    for copy in copies:
        copy.wait()


def pack_kernel(own_ref, sibling_ref, out_ref):
    core = lax.axis_index("core")
    out_ref[core] = own_ref[...]
    out_ref[1 - core] = sibling_ref[...]


def stacked_heads(q):
    return jnp.concatenate([q[:, h * HD : (h + 1) * HD] for h in range(HEADS)], axis=0)


def scores_of(keys, vectors):
    return lax.dot_general(
        keys, vectors, (((1,), (1,)), ((), ())), preferred_element_type=jnp.float32
    )


def summed_of(values, weights):
    return lax.dot_general(
        values,
        weights.astype(jnp.bfloat16),
        (((0,), (0,)), ((), ())),
        preferred_element_type=jnp.float32,
    )


def merged(parts):
    top = functools.reduce(jnp.maximum, [p[0] for p in parts])
    total = 0.0
    summed = 0.0
    for part_top, part_total, part_summed in parts:
        factor = jnp.exp2((part_top - top) * to_exp2)
        total = total + part_total * factor
        summed = summed + part_summed * factor
    return top, total, summed


def weighted(scores):
    top = jnp.max(scores, axis=0, keepdims=True)
    weights = jnp.exp2((scores - top) * to_exp2)
    return top, jnp.sum(weights, axis=0, keepdims=True), weights


def three_pieces(x):
    first = x.astype(jnp.bfloat16).astype(jnp.float32)
    rest = x - first
    second = rest.astype(jnp.bfloat16).astype(jnp.float32)
    return [first, second, rest - second]


def store_units(ref, parts):
    stats = jnp.concatenate([row for top, total, _ in parts for row in (top, total)], axis=0)
    pieces = three_pieces(stats)
    padding = jnp.zeros((STAT_ROWS - 3 * stats.shape[0], VECS), jnp.float32)
    ref[len(parts) * HD :, :] = jnp.concatenate(pieces + [padding], axis=0).astype(jnp.bfloat16)
    for i, (_, _, summed) in enumerate(parts):
        ref[i * HD : (i + 1) * HD, :] = summed.astype(jnp.bfloat16)


def load_unit(ref, i=0):
    n_parts = ref.shape[0] // HD
    pieces = ref[n_parts * HD :, :].astype(jnp.float32)
    rows = 2 * n_parts
    stats = pieces[:rows] + pieces[rows : 2 * rows] + pieces[2 * rows : 3 * rows]
    if n_parts == 1:
        top, total = stats[0:1], stats[1:2]
    else:
        top = jnp.where(i == 0, stats[0:1], stats[2:3])
        total = jnp.where(i == 0, stats[1:2], stats[3:4])
    part = ref[pl.ds(pl.multiple_of(i * HD, HD), HD), :]
    return top, total, part.astype(jnp.float32)


def count(left, right):
    return jnp.dot(
        left.astype(jnp.bfloat16), right.astype(jnp.bfloat16), preferred_element_type=jnp.float32
    )


def iota(shape, axis):
    return lax.broadcasted_iota(jnp.int32, shape, axis)


def prompt_part(length, half, prompt_ref, vectors):
    parity = lax.axis_index("pair")
    whole = lax.div(length, 2 * half)
    valid = whole * half + jnp.clip(length - whole * (2 * half) - parity * half, 0, half)
    chunks = [slice(i, i + CHUNK) for i in range(0, prompt_ref.shape[0], CHUNK)]
    scores = [scores_of(vectors, prompt_ref[chunk, :HD]) for chunk in chunks]
    place = iota(scores[0].shape, 1)
    scores = [
        score
        if chunk.stop <= SURELY_VALID
        else jnp.where(place < valid - chunk.start, score, big_negative)
        for chunk, score in zip(chunks, scores)
    ]
    top = jnp.max(functools.reduce(jnp.maximum, scores), axis=1, keepdims=True)
    totals, summed = 0.0, 0.0
    for chunk, score in zip(chunks, scores):
        weights = jnp.exp2((score - top) * to_exp2)
        totals = totals + weights
        summed = summed + jnp.dot(
            weights.astype(jnp.bfloat16), prompt_ref[chunk, HD:], preferred_element_type=jnp.float32
        )
    total = jnp.sum(totals, axis=1, keepdims=True)
    stats = jnp.where(iota(summed.shape, 1) == 0, top, total).T
    return stats[0:1], stats[1:2], summed.T


def prepare_kernel(
    capacity, near, table, parents, far_ref,
    home_keys_ref, home_values_ref, keys_ref, values_ref, member_ref, rows_ref,
):
    n_req = lax.axis_size("z")
    slots, half, _ = near.shape
    rows = table.shape[1]
    n_batch = rows // BEAMS
    z, core = lax.axis_index("z"), lax.axis_index("core")

    slot = iota((2 * slots, rows), 0)
    mine = slot < slots
    block = jnp.where(mine, slot, slot - slots) + jnp.where(mine, 2 * z + core, 2 * z + 1 - core) * slots
    named = functools.reduce(
        jnp.logical_or, [table[j : j + 1, :] == block for j in range(SUF)]
    ).astype(jnp.float32)
    group = (iota((rows, n_batch), 0) // BEAMS == iota((rows, n_batch), 1)).astype(jnp.float32)
    hit = jnp.where(count(named, group) > 0.0, 1.0, 0.0)
    left, right = iota((2 * slots, 2 * slots), 0), iota((2 * slots, 2 * slots), 1)
    before = (left // slots == right // slots) & (right < left)
    rank = count(before.astype(jnp.float32), hit)
    taken = (iota((rows, rows), 0) == parents[...]).astype(jnp.float32)
    continued = count(named, taken)

    place = iota((2 * slots, n_batch), 0)
    found = []
    for k in range(2 * capacity):
        holder = k // capacity
        chosen = (hit > 0.0) & (rank == float(k % capacity)) & (place // slots == holder)
        found.append(jnp.sum(jnp.where(chosen, place + 1, 0), axis=0, keepdims=True))
    found = jnp.concatenate(found, axis=0)

    requests = [z * 2 + core]
    for mask in range(1, n_req):
        requests += [(z ^ mask) * 2, (z ^ mask) * 2 + 1]
    for i, request in enumerate(requests):
        lane = iota((rows, VECS), 1)
        spread = iota((rows, VECS), 0) == request * BEAMS + lane % BEAMS
        rows_ref[: 2 * slots, :] = count(continued, spread.astype(jnp.float32))
        rows_ref[2 * slots :, :] = jnp.zeros((8, VECS), jnp.float32)
        mask = iota(found.shape, 1) == request
        picked = jnp.sum(jnp.where(mask, found, 0), axis=1, keepdims=True)
        values = []
        for k in range(2 * capacity):
            index = picked[k, 0]
            row = jnp.where(index > 0, index - 1, 2 * slots)
            member_ref[i, k : k + 1, :] = rows_ref[pl.ds(row, 1), :]
            pool_ref = near if k < capacity else far_ref
            base = 0 if k < capacity else slots
            content = pool_ref[jnp.maximum(index - 1 - base, 0)]
            tokens = slice(k * half, (k + 1) * half)
            if i == 0:
                home_keys_ref[0, tokens, :] = content[:, :HD]
            else:
                keys_ref[i - 1, tokens, :] = content[:, :HD]
            values.append(content[:, HD:])
        values = jnp.concatenate(values, axis=0).T
        if i == 0:
            home_values_ref[0] = values
        else:
            values_ref[i - 1] = values


def suffix_parts(vectors, keys_ref, values_ref, members, place=0):
    n_slots = members[0].shape[0]
    half = keys_ref.shape[1] // n_slots
    scores = [scores_of(keys_ref[place + i], each) for i, each in enumerate(vectors)]
    softmaxes = []
    for member, score in zip(members, scores):
        pieces = [
            jnp.where(
                member[k : k + 1, :] > 0.0, score[k * half : (k + 1) * half], big_negative
            )
            for k in range(n_slots)
        ]
        softmaxes.append(weighted(jnp.concatenate(pieces, axis=0)))
    return [
        (
            top,
            total,
            jnp.dot(
                values_ref[place + i], weights.astype(jnp.bfloat16), preferred_element_type=jnp.float32
            ),
        )
        for i, (top, total, weights) in enumerate(softmaxes)
    ]


def away_kernel(place, keys_ref, values_ref, member_ref, message_ref, out_ref, *after_ref):
    for ref in after_ref:
        ref[...] = jnp.zeros(ref.shape, jnp.float32)
    vectors = [stacked_heads(message_ref[core]) for core in range(2)]
    members = [member_ref[1 + place + core] for core in range(2)]
    store_units(out_ref, suffix_parts(vectors, keys_ref, values_ref, members, place))


def home_part(length_ref, keys_ref, values_ref, member_ref, queries_ref, prompt_ref):
    vectors = stacked_heads(queries_ref[...])
    half = keys_ref.shape[1] // member_ref.shape[1]
    (suffix,) = suffix_parts([vectors], keys_ref, values_ref, [member_ref[0]])
    return merged([prompt_part(length_ref[0], half, prompt_ref, vectors), suffix])


def pair_heads_kernel(*refs):
    *inputs, _, out_ref = refs
    store_units(out_ref, [home_part(*inputs)])


def own_heads_kernel(*refs):
    *inputs, _, summed_ref, stats_ref = refs
    top, total, summed_ref[...] = home_part(*inputs)
    stats_ref[...] = jnp.concatenate([top, total, jnp.zeros((6, VECS), jnp.float32)], axis=0)


def sibling_kernel(*rest):
    units, out_ref = rest[:-2], rest[-1]
    core = lax.axis_index("core")
    store_units(out_ref, [merged([load_unit(unit, 1 - core) for unit in units])])


def own_share_kernel(*rest):
    units, (summed_ref, stats_ref, out_ref, out_stats_ref) = rest[:-4], rest[-4:]
    core = lax.axis_index("core")
    parts = [load_unit(unit, core) for unit in units]
    parts.append((stats_ref[0:1], stats_ref[1:2], summed_ref[...]))
    top, total, out_ref[...] = merged(parts)
    out_stats_ref[...] = jnp.concatenate([top, total, jnp.zeros((6, VECS), jnp.float32)], axis=0)


def final_kernel(last_ref, shared_ref, summed_ref, stats_ref, out_ref):
    parts = [load_unit(last_ref), load_unit(shared_ref)]
    parts.append((stats_ref[0:1], stats_ref[1:2], summed_ref[...]))
    _, total, summed = merged(parts)
    attended = (summed / total).T
    for h in range(HEADS):
        out_ref[:, h * HD : (h + 1) * HD] = attended[h * BEAMS : (h + 1) * BEAMS]


def in_hbm(value):
    return pltpu.with_memory_space_constraint(value, pltpu.HBM)


def on_device(queries, prompt_cache, pool, block_table, parents, lengths):
    n_req = lax.axis_size("z")
    n_batch = 2 * n_req
    ndist = 2 ** (SUF + 1) - 2
    capacity = 2 * ((ndist // 2 + n_batch - 1) // n_batch)
    slots, _, half, width = pool.shape
    tokens = prompt_cache.shape[2]
    rows = block_table.shape[0]
    vmem = pl.BlockSpec(memory_space=pltpu.VMEM)
    params = pltpu.CompilerParams(vmem_limit_bytes=32 * 2**20)
    some = pl.CostEstimate(flops=2 * 10**8, bytes_accessed=2**21, transcendentals=0)
    early = pl.CostEstimate(flops=2 * 10**10, bytes_accessed=0, transcendentals=0)

    hbm = pl.BlockSpec(memory_space=pltpu.HBM)
    near = pool.reshape(slots, half, width)
    far = swapped(near, "core")
    other = swapped(queries, "pair")
    staged = [queries, block_table.T, parents.reshape(1, rows)]
    own, table, row_parents = pl.pallas_call(
        stage_kernel,
        out_shape=tuple(pltpu.VMEM(each.shape, each.dtype) for each in staged),
        in_specs=[hbm] * len(staged),
        out_specs=(vmem,) * len(staged),
        scratch_shapes=[pltpu.SemaphoreType.DMA((len(staged),))],
        compiler_params=params,
        name="stage",
    )(*[in_hbm(each) for each in staged])
    both = pl.pallas_call(
        pack_kernel,
        out_shape=pltpu.VMEM((2,) + queries.shape, jnp.bfloat16),
        in_specs=[vmem] * 2,
        out_specs=vmem,
        compiler_params=params,
        cost_estimate=early,
        name="both_cores",
    )(own, swapped(queries, "core"))
    first, *others = mask_order(n_req)
    order = [first] + others[::-1]
    messages = {mask: exchanged(both, mask) for mask in order}

    home_keys, home_values, keys, values, member = pl.pallas_call(
        functools.partial(prepare_kernel, capacity),
        out_shape=(
            pltpu.VMEM((1, 2 * capacity * half, HD), jnp.bfloat16),
            pltpu.VMEM((1, HD, 2 * capacity * half), jnp.bfloat16),
            pltpu.VMEM((2 * n_req - 2, 2 * capacity * half, HD), jnp.bfloat16),
            pltpu.VMEM((2 * n_req - 2, HD, 2 * capacity * half), jnp.bfloat16),
            pltpu.VMEM((2 * n_req - 1, 2 * capacity, VECS), jnp.float32),
        ),
        in_specs=[vmem] * 4,
        out_specs=(vmem,) * 5,
        scratch_shapes=[pltpu.VMEM((2 * slots + 8, VECS), jnp.float32)],
        compiler_params=params,
        cost_estimate=some,
        name="prepare",
    )(
        near,
        table,
        row_parents,
        far,
    )

    received, after = [], []
    for mask in order:
        out = [pltpu.VMEM((2 * HD + STAT_ROWS, VECS), jnp.bfloat16)]
        if mask == first:
            out.append(pltpu.VMEM((8, VECS), jnp.float32))
        units, *token = pl.pallas_call(
            functools.partial(away_kernel, 2 * mask - 2),
            out_shape=out,
            in_specs=[vmem] * 4,
            out_specs=[vmem] * len(out),
            compiler_params=params,
            cost_estimate=some,
            name="suffix_away",
        )(keys, values, member, messages[mask])
        received.append(exchanged(units, mask))
        after += token

    home = pl.CostEstimate(
        flops=8 * tokens * VECS * HD, bytes_accessed=2 * tokens * width, transcendentals=0
    )
    home_specs = [pl.BlockSpec(memory_space=pltpu.SMEM)] + [vmem] * 6
    prompt = prompt_cache.reshape(tokens, width)
    given = pl.pallas_call(
        pair_heads_kernel,
        out_shape=pltpu.VMEM((HD + STAT_ROWS, VECS), jnp.bfloat16),
        in_specs=home_specs,
        out_specs=vmem,
        compiler_params=params,
        cost_estimate=home,
        name="home_pair_heads",
    )(lengths, home_keys, home_values, member, other, prompt, *after)
    last = swapped(given, "pair")
    summed, stats = pl.pallas_call(
        own_heads_kernel,
        out_shape=(pltpu.VMEM((HD, VECS), jnp.float32), pltpu.VMEM((8, VECS), jnp.float32)),
        in_specs=home_specs,
        out_specs=(vmem,) * 2,
        compiler_params=params,
        cost_estimate=home,
        name="home_own_heads",
    )(lengths, home_keys, home_values, member, own, prompt, *after)

    share = pl.pallas_call(
        sibling_kernel,
        out_shape=pltpu.VMEM((HD + STAT_ROWS, VECS), jnp.bfloat16),
        in_specs=[vmem] * n_req,
        out_specs=vmem,
        compiler_params=params,
        name="sibling_share",
    )(*received, stats)

    partial = (pltpu.VMEM((HD, VECS), jnp.float32), pltpu.VMEM((8, VECS), jnp.float32))
    summed, stats = pl.pallas_call(
        own_share_kernel,
        out_shape=partial,
        in_specs=[vmem] * (n_req + 1),
        out_specs=(vmem,) * 2,
        compiler_params=params,
        name="own_share",
    )(*received, summed, stats)

    return pl.pallas_call(
        final_kernel,
        out_shape=jax.ShapeDtypeStruct((BEAMS, HEADS * HD), jnp.float32),
        in_specs=[vmem] * 4,
        out_specs=vmem,
        compiler_params=params,
        name="combine",
    )(last, swapped(share, "core"), summed, stats)


def solution(mesh):
    n_batch, n_mp = mesh.devices.shape
    split = jax.sharding.Mesh(
        mesh.devices.reshape(n_batch // 2, 2, n_mp // 2, 2), ("z", "core", "group", "pair")
    )
    batch, mp = ("z", "core"), ("group", "pair")
    return jax.shard_map(
        on_device,
        mesh=split,
        in_specs=(
            P(batch, mp),
            P(batch, mp, None, None),
            P(batch, mp, None, None),
            P(),
            P(),
            P(batch),
        ),
        out_specs=P(batch, mp),
        check_vma=False,
    )
```

```python
import functools

import jax
import jax.numpy as jnp
from jax import lax
from jax.experimental import pallas as pl
from jax.experimental.pallas import tpu as pltpu
from jax.sharding import PartitionSpec as P

HD = 128
GROUP = 16
BEAMS = 16
SUF = 4
HEADS = GROUP // 2
VECS = HEADS * BEAMS
STAT_ROWS = 16
CHUNK = 512
FIRST_MASKS = (2, 3, 1)
SURELY_VALID = 1024

big_negative = -1e30
to_exp2 = HD ** (-0.5) * 1.4426950408889634


def swapped(value, axis):
    return lax.ppermute(value, axis, [(0, 1), (1, 0)])


def exchanged(value, mask):
    pairs = []
    for z in range(lax.axis_size("z")):
        for core in range(2):
            for pair in range(2):
                target = ((z ^ mask) * 2 + core) * 2 + (pair ^ core)
                pairs.append(((z * 2 + core) * 2 + pair, target))
    return lax.ppermute(value, ("z", "core", "pair"), pairs)


def mask_order(n_req):
    return FIRST_MASKS if n_req == 4 else tuple(range(n_req - 1, 0, -1))


def stage_kernel(*refs):
    n = (len(refs) - 1) // 2
    copies = [
        pltpu.make_async_copy(refs[i], refs[n + i], refs[-1].at[i]) for i in range(n)
    ]
    for copy in copies:
        copy.start()
    for copy in copies:
        copy.wait()


def pack_kernel(own_ref, sibling_ref, out_ref):
    core = lax.axis_index("core")
    out_ref[core] = own_ref[...]
    out_ref[1 - core] = sibling_ref[...]


def stacked_heads(q):
    return jnp.concatenate([q[:, h * HD : (h + 1) * HD] for h in range(HEADS)], axis=0)


def scores_of(keys, vectors):
    return lax.dot_general(
        keys, vectors, (((1,), (1,)), ((), ())), preferred_element_type=jnp.float32
    )


def summed_of(values, weights):
    return lax.dot_general(
        values,
        weights.astype(jnp.bfloat16),
        (((0,), (0,)), ((), ())),
        preferred_element_type=jnp.float32,
    )


def merged(parts):
    top = functools.reduce(jnp.maximum, [p[0] for p in parts])
    total = 0.0
    summed = 0.0
    for part_top, part_total, part_summed in parts:
        factor = jnp.exp2((part_top - top) * to_exp2)
        total = total + part_total * factor
        summed = summed + part_summed * factor
    return top, total, summed


def weighted(scores):
    top = jnp.max(scores, axis=0, keepdims=True)
    weights = jnp.exp2((scores - top) * to_exp2)
    return top, jnp.sum(weights, axis=0, keepdims=True), weights


def three_pieces(x):
    first = x.astype(jnp.bfloat16).astype(jnp.float32)
    rest = x - first
    second = rest.astype(jnp.bfloat16).astype(jnp.float32)
    return [first, second, rest - second]


def store_units(ref, parts):
    stats = jnp.concatenate([row for top, total, _ in parts for row in (top, total)], axis=0)
    pieces = three_pieces(stats)
    padding = jnp.zeros((STAT_ROWS - 3 * stats.shape[0], VECS), jnp.float32)
    ref[len(parts) * HD :, :] = jnp.concatenate(pieces + [padding], axis=0).astype(jnp.bfloat16)
    for i, (_, _, summed) in enumerate(parts):
        ref[i * HD : (i + 1) * HD, :] = summed.astype(jnp.bfloat16)


def load_unit(ref, i=0):
    n_parts = ref.shape[0] // HD
    pieces = ref[n_parts * HD :, :].astype(jnp.float32)
    rows = 2 * n_parts
    stats = pieces[:rows] + pieces[rows : 2 * rows] + pieces[2 * rows : 3 * rows]
    if n_parts == 1:
        top, total = stats[0:1], stats[1:2]
    else:
        top = jnp.where(i == 0, stats[0:1], stats[2:3])
        total = jnp.where(i == 0, stats[1:2], stats[3:4])
    part = ref[pl.ds(pl.multiple_of(i * HD, HD), HD), :]
    return top, total, part.astype(jnp.float32)


def count(left, right):
    return jnp.dot(
        left.astype(jnp.bfloat16), right.astype(jnp.bfloat16), preferred_element_type=jnp.float32
    )


def iota(shape, axis):
    return lax.broadcasted_iota(jnp.int32, shape, axis)


def prompt_part(length, half, prompt_ref, vectors):
    parity = lax.axis_index("pair")
    whole = lax.div(length, 2 * half)
    valid = whole * half + jnp.clip(length - whole * (2 * half) - parity * half, 0, half)
    chunks = [slice(i, i + CHUNK) for i in range(0, prompt_ref.shape[0], CHUNK)]
    scores = [scores_of(vectors, prompt_ref[chunk, :HD]) for chunk in chunks]
    place = iota(scores[0].shape, 1)
    scores = [
        score
        if chunk.stop <= SURELY_VALID
        else jnp.where(place < valid - chunk.start, score, big_negative)
        for chunk, score in zip(chunks, scores)
    ]
    top = jnp.max(functools.reduce(jnp.maximum, scores), axis=1, keepdims=True)
    totals, summed = 0.0, 0.0
    for chunk, score in zip(chunks, scores):
        weights = jnp.exp2((score - top) * to_exp2)
        totals = totals + weights
        summed = summed + jnp.dot(
            weights.astype(jnp.bfloat16), prompt_ref[chunk, HD:], preferred_element_type=jnp.float32
        )
    total = jnp.sum(totals, axis=1, keepdims=True)
    stats = jnp.where(iota(summed.shape, 1) == 0, top, total).T
    return stats[0:1], stats[1:2], summed.T


def prepare_kernel(
    capacity, near, table, parents, far_ref,
    home_keys_ref, home_values_ref, keys_ref, values_ref, member_ref, rows_ref,
):
    n_req = lax.axis_size("z")
    slots, half, _ = near.shape
    rows = table.shape[1]
    n_batch = rows // BEAMS
    z, core = lax.axis_index("z"), lax.axis_index("core")

    slot = iota((2 * slots, rows), 0)
    mine = slot < slots
    block = jnp.where(mine, slot, slot - slots) + jnp.where(mine, 2 * z + core, 2 * z + 1 - core) * slots
    named = functools.reduce(
        jnp.logical_or, [table[j : j + 1, :] == block for j in range(SUF)]
    ).astype(jnp.float32)
    group = (iota((rows, n_batch), 0) // BEAMS == iota((rows, n_batch), 1)).astype(jnp.float32)
    hit = jnp.where(count(named, group) > 0.0, 1.0, 0.0)
    left, right = iota((2 * slots, 2 * slots), 0), iota((2 * slots, 2 * slots), 1)
    before = (left // slots == right // slots) & (right < left)
    rank = count(before.astype(jnp.float32), hit)
    taken = (iota((rows, rows), 0) == parents[...]).astype(jnp.float32)
    continued = count(named, taken)

    place = iota((2 * slots, n_batch), 0)
    found = []
    for k in range(2 * capacity):
        holder = k // capacity
        chosen = (hit > 0.0) & (rank == float(k % capacity)) & (place // slots == holder)
        found.append(jnp.sum(jnp.where(chosen, place + 1, 0), axis=0, keepdims=True))
    found = jnp.concatenate(found, axis=0)

    requests = [z * 2 + core]
    for mask in range(1, n_req):
        requests += [(z ^ mask) * 2, (z ^ mask) * 2 + 1]
    for i, request in enumerate(requests):
        lane = iota((rows, VECS), 1)
        spread = iota((rows, VECS), 0) == request * BEAMS + lane % BEAMS
        rows_ref[i, : 2 * slots, :] = count(continued, spread.astype(jnp.float32))
        rows_ref[i, 2 * slots :, :] = jnp.zeros((8, VECS), jnp.float32)
        mask = iota(found.shape, 1) == request
        picked = jnp.sum(jnp.where(mask, found, 0), axis=1, keepdims=True)
        values = []
        for k in range(2 * capacity):
            index = picked[k, 0]
            row = jnp.where(index > 0, index - 1, 2 * slots)
            member_ref[i, k : k + 1, :] = rows_ref[i, pl.ds(row, 1), :]
            pool_ref = near if k < capacity else far_ref
            base = 0 if k < capacity else slots
            content = pool_ref[jnp.maximum(index - 1 - base, 0)]
            tokens = slice(k * half, (k + 1) * half)
            if i == 0:
                home_keys_ref[0, tokens, :] = content[:, :HD]
            else:
                keys_ref[i - 1, tokens, :] = content[:, :HD]
            values.append(content[:, HD:])
        values = jnp.concatenate(values, axis=0).T
        if i == 0:
            home_values_ref[0] = values
        else:
            values_ref[i - 1] = values


def suffix_parts(vectors, keys_ref, values_ref, members, place=0):
    n_slots = members[0].shape[0]
    half = keys_ref.shape[1] // n_slots
    scores = [scores_of(keys_ref[place + i], each) for i, each in enumerate(vectors)]
    softmaxes = []
    for member, score in zip(members, scores):
        pieces = [
            jnp.where(
                member[k : k + 1, :] > 0.0, score[k * half : (k + 1) * half], big_negative
            )
            for k in range(n_slots)
        ]
        softmaxes.append(weighted(jnp.concatenate(pieces, axis=0)))
    return [
        (
            top,
            total,
            jnp.dot(
                values_ref[place + i], weights.astype(jnp.bfloat16), preferred_element_type=jnp.float32
            ),
        )
        for i, (top, total, weights) in enumerate(softmaxes)
    ]


def away_kernel(place, keys_ref, values_ref, member_ref, message_ref, out_ref, *after_ref):
    for ref in after_ref:
        ref[...] = jnp.zeros(ref.shape, jnp.float32)
    vectors = [stacked_heads(message_ref[core]) for core in range(2)]
    members = [member_ref[1 + place + core] for core in range(2)]
    store_units(out_ref, suffix_parts(vectors, keys_ref, values_ref, members, place))


def home_part(length_ref, keys_ref, values_ref, member_ref, queries_ref, prompt_ref):
    vectors = stacked_heads(queries_ref[...])
    half = keys_ref.shape[1] // member_ref.shape[1]
    (suffix,) = suffix_parts([vectors], keys_ref, values_ref, [member_ref[0]])
    return merged([prompt_part(length_ref[0], half, prompt_ref, vectors), suffix])


def pair_heads_kernel(*refs):
    *inputs, _, out_ref = refs
    store_units(out_ref, [home_part(*inputs)])


def own_heads_kernel(*refs):
    *inputs, _, summed_ref, stats_ref = refs
    top, total, summed_ref[...] = home_part(*inputs)
    stats_ref[...] = jnp.concatenate([top, total, jnp.zeros((6, VECS), jnp.float32)], axis=0)


def sibling_kernel(*rest):
    units, out_ref = rest[:-2], rest[-1]
    core = lax.axis_index("core")
    store_units(out_ref, [merged([load_unit(unit, 1 - core) for unit in units])])


def own_share_kernel(*rest):
    units, (summed_ref, stats_ref, out_ref, out_stats_ref) = rest[:-4], rest[-4:]
    core = lax.axis_index("core")
    parts = [load_unit(unit, core) for unit in units]
    parts.append((stats_ref[0:1], stats_ref[1:2], summed_ref[...]))
    top, total, out_ref[...] = merged(parts)
    out_stats_ref[...] = jnp.concatenate([top, total, jnp.zeros((6, VECS), jnp.float32)], axis=0)


def final_kernel(last_ref, shared_ref, summed_ref, stats_ref, out_ref):
    parts = [load_unit(last_ref), load_unit(shared_ref)]
    parts.append((stats_ref[0:1], stats_ref[1:2], summed_ref[...]))
    _, total, summed = merged(parts)
    attended = (summed / total).T
    for h in range(HEADS):
        out_ref[:, h * HD : (h + 1) * HD] = attended[h * BEAMS : (h + 1) * BEAMS]


def in_hbm(value):
    return pltpu.with_memory_space_constraint(value, pltpu.HBM)


def on_device(queries, prompt_cache, pool, block_table, parents, lengths):
    n_req = lax.axis_size("z")
    n_batch = 2 * n_req
    ndist = 2 ** (SUF + 1) - 2
    capacity = 2 * ((ndist // 2 + n_batch - 1) // n_batch)
    slots, _, half, width = pool.shape
    tokens = prompt_cache.shape[2]
    rows = block_table.shape[0]
    vmem = pl.BlockSpec(memory_space=pltpu.VMEM)
    params = pltpu.CompilerParams(vmem_limit_bytes=32 * 2**20)
    some = pl.CostEstimate(flops=2 * 10**8, bytes_accessed=2**21, transcendentals=0)
    early = pl.CostEstimate(flops=2 * 10**10, bytes_accessed=0, transcendentals=0)

    hbm = pl.BlockSpec(memory_space=pltpu.HBM)
    near = pool.reshape(slots, half, width)
    far = swapped(near, "core")
    other = swapped(queries, "pair")
    staged = [queries, block_table.T, parents.reshape(1, rows)]
    own, table, row_parents = pl.pallas_call(
        stage_kernel,
        out_shape=tuple(pltpu.VMEM(each.shape, each.dtype) for each in staged),
        in_specs=[hbm] * len(staged),
        out_specs=(vmem,) * len(staged),
        scratch_shapes=[pltpu.SemaphoreType.DMA((len(staged),))],
        compiler_params=params,
        name="stage",
    )(*[in_hbm(each) for each in staged])
    both = pl.pallas_call(
        pack_kernel,
        out_shape=pltpu.VMEM((2,) + queries.shape, jnp.bfloat16),
        in_specs=[vmem] * 2,
        out_specs=vmem,
        compiler_params=params,
        cost_estimate=early,
        name="both_cores",
    )(own, swapped(queries, "core"))
    first, *others = mask_order(n_req)
    order = [first] + others[::-1]
    messages = {mask: exchanged(both, mask) for mask in order}

    home_keys, home_values, keys, values, member = pl.pallas_call(
        functools.partial(prepare_kernel, capacity),
        out_shape=(
            pltpu.VMEM((1, 2 * capacity * half, HD), jnp.bfloat16),
            pltpu.VMEM((1, HD, 2 * capacity * half), jnp.bfloat16),
            pltpu.VMEM((2 * n_req - 2, 2 * capacity * half, HD), jnp.bfloat16),
            pltpu.VMEM((2 * n_req - 2, HD, 2 * capacity * half), jnp.bfloat16),
            pltpu.VMEM((2 * n_req - 1, 2 * capacity, VECS), jnp.float32),
        ),
        in_specs=[vmem] * 4,
        out_specs=(vmem,) * 5,
        scratch_shapes=[pltpu.VMEM((2 * n_req - 1, 2 * slots + 8, VECS), jnp.float32)],
        compiler_params=params,
        cost_estimate=some,
        name="prepare",
    )(
        near,
        table,
        row_parents,
        far,
    )

    received, after = [], []
    for mask in order:
        out = [pltpu.VMEM((2 * HD + STAT_ROWS, VECS), jnp.bfloat16)]
        if mask == first:
            out.append(pltpu.VMEM((8, VECS), jnp.float32))
        units, *token = pl.pallas_call(
            functools.partial(away_kernel, 2 * mask - 2),
            out_shape=out,
            in_specs=[vmem] * 4,
            out_specs=[vmem] * len(out),
            compiler_params=params,
            cost_estimate=some,
            name="suffix_away",
        )(keys, values, member, messages[mask])
        received.append(exchanged(units, mask))
        after += token

    home = pl.CostEstimate(
        flops=8 * tokens * VECS * HD, bytes_accessed=2 * tokens * width, transcendentals=0
    )
    home_specs = [pl.BlockSpec(memory_space=pltpu.SMEM)] + [vmem] * 6
    prompt = prompt_cache.reshape(tokens, width)
    given = pl.pallas_call(
        pair_heads_kernel,
        out_shape=pltpu.VMEM((HD + STAT_ROWS, VECS), jnp.bfloat16),
        in_specs=home_specs,
        out_specs=vmem,
        compiler_params=params,
        cost_estimate=home,
        name="home_pair_heads",
    )(lengths, home_keys, home_values, member, other, prompt, *after)
    last = swapped(given, "pair")
    summed, stats = pl.pallas_call(
        own_heads_kernel,
        out_shape=(pltpu.VMEM((HD, VECS), jnp.float32), pltpu.VMEM((8, VECS), jnp.float32)),
        in_specs=home_specs,
        out_specs=(vmem,) * 2,
        compiler_params=params,
        cost_estimate=home,
        name="home_own_heads",
    )(lengths, home_keys, home_values, member, own, prompt, *after)

    share = pl.pallas_call(
        sibling_kernel,
        out_shape=pltpu.VMEM((HD + STAT_ROWS, VECS), jnp.bfloat16),
        in_specs=[vmem] * n_req,
        out_specs=vmem,
        compiler_params=params,
        name="sibling_share",
    )(*received, stats)

    partial = (pltpu.VMEM((HD, VECS), jnp.float32), pltpu.VMEM((8, VECS), jnp.float32))
    summed, stats = pl.pallas_call(
        own_share_kernel,
        out_shape=partial,
        in_specs=[vmem] * (n_req + 1),
        out_specs=(vmem,) * 2,
        compiler_params=params,
        name="own_share",
    )(*received, summed, stats)

    return pl.pallas_call(
        final_kernel,
        out_shape=jax.ShapeDtypeStruct((BEAMS, HEADS * HD), jnp.float32),
        in_specs=[vmem] * 4,
        out_specs=vmem,
        compiler_params=params,
        name="combine",
    )(last, swapped(share, "core"), summed, stats)


def solution(mesh):
    n_batch, n_mp = mesh.devices.shape
    split = jax.sharding.Mesh(
        mesh.devices.reshape(n_batch // 2, 2, n_mp // 2, 2), ("z", "core", "group", "pair")
    )
    batch, mp = ("z", "core"), ("group", "pair")
    return jax.shard_map(
        on_device,
        mesh=split,
        in_specs=(
            P(batch, mp),
            P(batch, mp, None, None),
            P(batch, mp, None, None),
            P(),
            P(),
            P(batch),
        ),
        out_specs=P(batch, mp),
        check_vma=False,
    )
```

```python
import functools

import jax
import jax.numpy as jnp
from jax import lax
from jax.experimental import pallas as pl
from jax.experimental.pallas import tpu as pltpu
from jax.sharding import PartitionSpec as P

HD = 128
GROUP = 16
BEAMS = 16
SUF = 4
HEADS = GROUP // 2
VECS = HEADS * BEAMS
STAT_ROWS = 16
CHUNK = 512
FIRST_MASKS = (2, 3, 1)
SURELY_VALID = 1024

big_negative = -1e30
to_exp2 = HD ** (-0.5) * 1.4426950408889634


def swapped(value, axis):
    return lax.ppermute(value, axis, [(0, 1), (1, 0)])


def exchanged(value, mask):
    pairs = []
    for z in range(lax.axis_size("z")):
        for core in range(2):
            for pair in range(2):
                target = ((z ^ mask) * 2 + core) * 2 + (pair ^ core)
                pairs.append(((z * 2 + core) * 2 + pair, target))
    return lax.ppermute(value, ("z", "core", "pair"), pairs)


def mask_order(n_req):
    return FIRST_MASKS if n_req == 4 else tuple(range(n_req - 1, 0, -1))


def stage_kernel(*refs):
    n = (len(refs) - 1) // 2
    copies = [
        pltpu.make_async_copy(refs[i], refs[n + i], refs[-1].at[i]) for i in range(n)
    ]
    for copy in copies:
        copy.start()
    for copy in copies:
        copy.wait()


def pack_kernel(own_ref, sibling_ref, out_ref):
    core = lax.axis_index("core")
    out_ref[core] = own_ref[...]
    out_ref[1 - core] = sibling_ref[...]


def stacked_heads(q):
    return jnp.concatenate([q[:, h * HD : (h + 1) * HD] for h in range(HEADS)], axis=0)


def scores_of(keys, vectors):
    return lax.dot_general(
        keys, vectors, (((1,), (1,)), ((), ())), preferred_element_type=jnp.float32
    )


def summed_of(values, weights):
    return lax.dot_general(
        values,
        weights.astype(jnp.bfloat16),
        (((0,), (0,)), ((), ())),
        preferred_element_type=jnp.float32,
    )


def merged(parts):
    top = functools.reduce(jnp.maximum, [p[0] for p in parts])
    total = 0.0
    summed = 0.0
    for part_top, part_total, part_summed in parts:
        factor = jnp.exp2((part_top - top) * to_exp2)
        total = total + part_total * factor
        summed = summed + part_summed * factor
    return top, total, summed


def weighted(scores):
    top = jnp.max(scores, axis=0, keepdims=True)
    weights = jnp.exp2((scores - top) * to_exp2)
    return top, jnp.sum(weights, axis=0, keepdims=True), weights


def three_pieces(x):
    first = x.astype(jnp.bfloat16).astype(jnp.float32)
    rest = x - first
    second = rest.astype(jnp.bfloat16).astype(jnp.float32)
    return [first, second, rest - second]


def store_units(ref, parts):
    stats = jnp.concatenate([row for top, total, _ in parts for row in (top, total)], axis=0)
    pieces = three_pieces(stats)
    padding = jnp.zeros((STAT_ROWS - 3 * stats.shape[0], VECS), jnp.float32)
    ref[len(parts) * HD :, :] = jnp.concatenate(pieces + [padding], axis=0).astype(jnp.bfloat16)
    for i, (_, _, summed) in enumerate(parts):
        ref[i * HD : (i + 1) * HD, :] = summed.astype(jnp.bfloat16)


def load_unit(ref, i=0):
    n_parts = ref.shape[0] // HD
    pieces = ref[n_parts * HD :, :].astype(jnp.float32)
    rows = 2 * n_parts
    stats = pieces[:rows] + pieces[rows : 2 * rows] + pieces[2 * rows : 3 * rows]
    if n_parts == 1:
        top, total = stats[0:1], stats[1:2]
    else:
        top = jnp.where(i == 0, stats[0:1], stats[2:3])
        total = jnp.where(i == 0, stats[1:2], stats[3:4])
    part = ref[pl.ds(pl.multiple_of(i * HD, HD), HD), :]
    return top, total, part.astype(jnp.float32)


def count(left, right):
    return jnp.dot(
        left.astype(jnp.bfloat16), right.astype(jnp.bfloat16), preferred_element_type=jnp.float32
    )


def iota(shape, axis):
    return lax.broadcasted_iota(jnp.int32, shape, axis)


def prompt_part(length, half, prompt_ref, vectors):
    parity = lax.axis_index("pair")
    whole = lax.div(length, 2 * half)
    valid = whole * half + jnp.clip(length - whole * (2 * half) - parity * half, 0, half)
    chunks = [slice(i, i + CHUNK) for i in range(0, prompt_ref.shape[0], CHUNK)]
    scores = [scores_of(vectors, prompt_ref[chunk, :HD]) for chunk in chunks]
    place = iota(scores[0].shape, 1)
    scores = [
        score
        if chunk.stop <= SURELY_VALID
        else jnp.where(place < valid - chunk.start, score, big_negative)
        for chunk, score in zip(chunks, scores)
    ]
    top = jnp.max(functools.reduce(jnp.maximum, scores), axis=1, keepdims=True)
    totals, summed = 0.0, 0.0
    for chunk, score in zip(chunks, scores):
        weights = jnp.exp2((score - top) * to_exp2)
        totals = totals + weights
        summed = summed + jnp.dot(
            weights.astype(jnp.bfloat16), prompt_ref[chunk, HD:], preferred_element_type=jnp.float32
        )
    total = jnp.sum(totals, axis=1, keepdims=True)
    stats = jnp.where(iota(summed.shape, 1) == 0, top, total).T
    return stats[0:1], stats[1:2], summed.T


def prepare_kernel(
    capacity, near, table, parents, far_ref,
    home_keys_ref, home_values_ref, keys_ref, values_ref, member_ref, rows_ref,
):
    n_req = lax.axis_size("z")
    slots, half, _ = near.shape
    rows = table.shape[1]
    n_batch = rows // BEAMS
    z, core = lax.axis_index("z"), lax.axis_index("core")

    slot = iota((2 * slots, rows), 0)
    mine = slot < slots
    block = jnp.where(mine, slot, slot - slots) + jnp.where(mine, 2 * z + core, 2 * z + 1 - core) * slots
    named = functools.reduce(
        jnp.logical_or, [table[j : j + 1, :] == block for j in range(SUF)]
    ).astype(jnp.float32)
    group = (iota((rows, n_batch), 0) // BEAMS == iota((rows, n_batch), 1)).astype(jnp.float32)
    hit = jnp.where(count(named, group) > 0.0, 1.0, 0.0)
    left, right = iota((2 * slots, 2 * slots), 0), iota((2 * slots, 2 * slots), 1)
    before = (left // slots == right // slots) & (right < left)
    rank = count(before.astype(jnp.float32), hit)
    taken = (iota((rows, rows), 0) == parents[...]).astype(jnp.float32)
    continued = count(named, taken)

    place = iota((2 * slots, n_batch), 0)
    found = []
    for k in range(2 * capacity):
        holder = k // capacity
        chosen = (hit > 0.0) & (rank == float(k % capacity)) & (place // slots == holder)
        found.append(jnp.sum(jnp.where(chosen, place + 1, 0), axis=0, keepdims=True))
    found = jnp.concatenate(found, axis=0)

    requests = [z * 2 + core]
    for mask in range(1, n_req):
        requests += [(z ^ mask) * 2, (z ^ mask) * 2 + 1]
    for i, request in enumerate(requests):
        lane = iota((rows, VECS), 1)
        spread = iota((rows, VECS), 0) == request * BEAMS + lane % BEAMS
        rows_ref[: 2 * slots, :] = count(continued, spread.astype(jnp.float32))
        rows_ref[2 * slots :, :] = jnp.zeros((8, VECS), jnp.float32)
        mask = iota(found.shape, 1) == request
        picked = jnp.sum(jnp.where(mask, found, 0), axis=1, keepdims=True)
        values = []
        for k in range(2 * capacity):
            index = picked[k, 0]
            row = jnp.where(index > 0, index - 1, 2 * slots)
            member_ref[i, k : k + 1, :] = rows_ref[pl.ds(row, 1), :]
            pool_ref = near if k < capacity else far_ref
            base = 0 if k < capacity else slots
            content = pool_ref[jnp.maximum(index - 1 - base, 0)]
            tokens = slice(k * half, (k + 1) * half)
            if i == 0:
                home_keys_ref[0, tokens, :] = content[:, :HD]
            else:
                keys_ref[i - 1, tokens, :] = content[:, :HD]
            values.append(content[:, HD:])
        values = jnp.concatenate(values, axis=0).T
        if i == 0:
            home_values_ref[0] = values
        else:
            values_ref[i - 1] = values


def suffix_parts(vectors, keys_ref, values_ref, members, place=0):
    n_slots = members[0].shape[0]
    half = keys_ref.shape[1] // n_slots
    scores = [scores_of(keys_ref[place + i], each) for i, each in enumerate(vectors)]
    softmaxes = []
    for member, score in zip(members, scores):
        pieces = [
            jnp.where(
                member[k : k + 1, :] > 0.0, score[k * half : (k + 1) * half], big_negative
            )
            for k in range(n_slots)
        ]
        softmaxes.append(weighted(jnp.concatenate(pieces, axis=0)))
    return [
        (
            top,
            total,
            jnp.dot(
                values_ref[place + i], weights.astype(jnp.bfloat16), preferred_element_type=jnp.float32
            ),
        )
        for i, (top, total, weights) in enumerate(softmaxes)
    ]


def away_kernel(place, keys_ref, values_ref, member_ref, message_ref, out_ref, *after_ref):
    for ref in after_ref:
        ref[...] = jnp.zeros(ref.shape, jnp.float32)
    vectors = [stacked_heads(message_ref[core]) for core in range(2)]
    members = [member_ref[1 + place + core] for core in range(2)]
    store_units(out_ref, suffix_parts(vectors, keys_ref, values_ref, members, place))


def home_part(length_ref, keys_ref, values_ref, member_ref, queries_ref, prompt_ref):
    vectors = stacked_heads(queries_ref[...])
    half = keys_ref.shape[1] // member_ref.shape[1]
    (suffix,) = suffix_parts([vectors], keys_ref, values_ref, [member_ref[0]])
    return merged([prompt_part(length_ref[0], half, prompt_ref, vectors), suffix])


def pair_heads_kernel(*refs):
    *inputs, _, out_ref = refs
    store_units(out_ref, [home_part(*inputs)])


def own_heads_kernel(*refs):
    *inputs, _, summed_ref, stats_ref = refs
    top, total, summed_ref[...] = home_part(*inputs)
    stats_ref[...] = jnp.concatenate([top, total, jnp.zeros((6, VECS), jnp.float32)], axis=0)


def sibling_kernel(*rest):
    units, out_ref = rest[:-2], rest[-1]
    core = lax.axis_index("core")
    store_units(out_ref, [merged([load_unit(unit, 1 - core) for unit in units])])


def own_share_kernel(*rest):
    units, (summed_ref, stats_ref, out_ref, out_stats_ref) = rest[:-4], rest[-4:]
    core = lax.axis_index("core")
    parts = [load_unit(unit, core) for unit in units]
    parts.append((stats_ref[0:1], stats_ref[1:2], summed_ref[...]))
    top, total, out_ref[...] = merged(parts)
    out_stats_ref[...] = jnp.concatenate([top, total, jnp.zeros((6, VECS), jnp.float32)], axis=0)


def final_kernel(last_ref, shared_ref, summed_ref, stats_ref, out_ref, held, sems):
    parts = [load_unit(last_ref), load_unit(shared_ref)]
    parts.append((stats_ref[0:1], stats_ref[1:2], summed_ref[...]))
    _, total, summed = merged(parts)
    attended = (summed / total).T
    copies = []
    for h in range(HEADS):
        lanes = slice(h * HD, (h + 1) * HD)
        held[:, lanes] = attended[h * BEAMS : (h + 1) * BEAMS]
        copy = pltpu.make_async_copy(held.at[:, lanes], out_ref.at[:, lanes], sems.at[h])
        copy.start()
        copies.append(copy)
    for copy in copies:
        copy.wait()


def in_hbm(value):
    return pltpu.with_memory_space_constraint(value, pltpu.HBM)


def on_device(queries, prompt_cache, pool, block_table, parents, lengths):
    n_req = lax.axis_size("z")
    n_batch = 2 * n_req
    ndist = 2 ** (SUF + 1) - 2
    capacity = 2 * ((ndist // 2 + n_batch - 1) // n_batch)
    slots, _, half, width = pool.shape
    tokens = prompt_cache.shape[2]
    rows = block_table.shape[0]
    vmem = pl.BlockSpec(memory_space=pltpu.VMEM)
    params = pltpu.CompilerParams(vmem_limit_bytes=32 * 2**20)
    some = pl.CostEstimate(flops=2 * 10**8, bytes_accessed=2**21, transcendentals=0)
    early = pl.CostEstimate(flops=2 * 10**10, bytes_accessed=0, transcendentals=0)

    hbm = pl.BlockSpec(memory_space=pltpu.HBM)
    near = pool.reshape(slots, half, width)
    far = swapped(near, "core")
    other = swapped(queries, "pair")
    staged = [queries, block_table.T, parents.reshape(1, rows)]
    own, table, row_parents = pl.pallas_call(
        stage_kernel,
        out_shape=tuple(pltpu.VMEM(each.shape, each.dtype) for each in staged),
        in_specs=[hbm] * len(staged),
        out_specs=(vmem,) * len(staged),
        scratch_shapes=[pltpu.SemaphoreType.DMA((len(staged),))],
        compiler_params=params,
        name="stage",
    )(*[in_hbm(each) for each in staged])
    both = pl.pallas_call(
        pack_kernel,
        out_shape=pltpu.VMEM((2,) + queries.shape, jnp.bfloat16),
        in_specs=[vmem] * 2,
        out_specs=vmem,
        compiler_params=params,
        cost_estimate=early,
        name="both_cores",
    )(own, swapped(queries, "core"))
    first, *others = mask_order(n_req)
    order = [first] + others[::-1]
    messages = {mask: exchanged(both, mask) for mask in order}

    home_keys, home_values, keys, values, member = pl.pallas_call(
        functools.partial(prepare_kernel, capacity),
        out_shape=(
            pltpu.VMEM((1, 2 * capacity * half, HD), jnp.bfloat16),
            pltpu.VMEM((1, HD, 2 * capacity * half), jnp.bfloat16),
            pltpu.VMEM((2 * n_req - 2, 2 * capacity * half, HD), jnp.bfloat16),
            pltpu.VMEM((2 * n_req - 2, HD, 2 * capacity * half), jnp.bfloat16),
            pltpu.VMEM((2 * n_req - 1, 2 * capacity, VECS), jnp.float32),
        ),
        in_specs=[vmem] * 4,
        out_specs=(vmem,) * 5,
        scratch_shapes=[pltpu.VMEM((2 * slots + 8, VECS), jnp.float32)],
        compiler_params=params,
        cost_estimate=some,
        name="prepare",
    )(
        near,
        table,
        row_parents,
        far,
    )

    received, after = [], []
    for mask in order:
        out = [pltpu.VMEM((2 * HD + STAT_ROWS, VECS), jnp.bfloat16)]
        if mask == first:
            out.append(pltpu.VMEM((8, VECS), jnp.float32))
        units, *token = pl.pallas_call(
            functools.partial(away_kernel, 2 * mask - 2),
            out_shape=out,
            in_specs=[vmem] * 4,
            out_specs=[vmem] * len(out),
            compiler_params=params,
            cost_estimate=some,
            name="suffix_away",
        )(keys, values, member, messages[mask])
        received.append(exchanged(units, mask))
        after += token

    home = pl.CostEstimate(
        flops=8 * tokens * VECS * HD, bytes_accessed=2 * tokens * width, transcendentals=0
    )
    home_specs = [pl.BlockSpec(memory_space=pltpu.SMEM)] + [vmem] * 6
    prompt = prompt_cache.reshape(tokens, width)
    given = pl.pallas_call(
        pair_heads_kernel,
        out_shape=pltpu.VMEM((HD + STAT_ROWS, VECS), jnp.bfloat16),
        in_specs=home_specs,
        out_specs=vmem,
        compiler_params=params,
        cost_estimate=home,
        name="home_pair_heads",
    )(lengths, home_keys, home_values, member, other, prompt, *after)
    last = swapped(given, "pair")
    summed, stats = pl.pallas_call(
        own_heads_kernel,
        out_shape=(pltpu.VMEM((HD, VECS), jnp.float32), pltpu.VMEM((8, VECS), jnp.float32)),
        in_specs=home_specs,
        out_specs=(vmem,) * 2,
        compiler_params=params,
        cost_estimate=home,
        name="home_own_heads",
    )(lengths, home_keys, home_values, member, own, prompt, *after)

    share = pl.pallas_call(
        sibling_kernel,
        out_shape=pltpu.VMEM((HD + STAT_ROWS, VECS), jnp.bfloat16),
        in_specs=[vmem] * n_req,
        out_specs=vmem,
        compiler_params=params,
        name="sibling_share",
    )(*received, stats)

    partial = (pltpu.VMEM((HD, VECS), jnp.float32), pltpu.VMEM((8, VECS), jnp.float32))
    summed, stats = pl.pallas_call(
        own_share_kernel,
        out_shape=partial,
        in_specs=[vmem] * (n_req + 1),
        out_specs=(vmem,) * 2,
        compiler_params=params,
        name="own_share",
    )(*received, summed, stats)

    return pl.pallas_call(
        final_kernel,
        out_shape=jax.ShapeDtypeStruct((BEAMS, HEADS * HD), jnp.float32),
        in_specs=[vmem] * 4,
        out_specs=pl.BlockSpec(memory_space=pltpu.HBM),
        scratch_shapes=[
            pltpu.VMEM((BEAMS, HEADS * HD), jnp.float32),
            pltpu.SemaphoreType.DMA((HEADS,)),
        ],
        compiler_params=params,
        name="combine",
    )(last, swapped(share, "core"), summed, stats)


def solution(mesh):
    n_batch, n_mp = mesh.devices.shape
    split = jax.sharding.Mesh(
        mesh.devices.reshape(n_batch // 2, 2, n_mp // 2, 2), ("z", "core", "group", "pair")
    )
    batch, mp = ("z", "core"), ("group", "pair")
    return jax.shard_map(
        on_device,
        mesh=split,
        in_specs=(
            P(batch, mp),
            P(batch, mp, None, None),
            P(batch, mp, None, None),
            P(),
            P(),
            P(batch),
        ),
        out_specs=P(batch, mp),
        check_vma=False,
    )
```
